32 devices in a mesh: expert: 8 (over z, x), tensor: 4 (over y, core).
Axes of the slice: x: 2, y: 2, z: 4, core: 2. Of those that a mesh axis runs over, the one named last changes fastest.
Arguments:
- inputs: bfloat16 [8192, 1536], P('expert'), may hold values from -6 to 6
- routes: int32 [8192, 4], P('expert'), may hold values from 0 to 7, all different within a row; in each aligned block of 1024 rows (0 to 1023, 1024 to 2047, ...) at most 768 rows name the same one
- cotangent: bfloat16 [8192, 1536], P('expert'), may hold values from -6 to 6
- first_gain: float32 [1536], replicated, may hold values from 0.5 to 1.5
- second_gain: float32 [1536], replicated, may hold values from 0.5 to 1.5
- w_query: bfloat16 [1536, 1536], P(None, 'tensor'), may hold values from -0.15625 to 0.15625
- w_key: bfloat16 [1536, 256], replicated, may hold values from -0.15625 to 0.15625
- w_value: bfloat16 [1536, 256], replicated, may hold values from -0.15625 to 0.15625
- w_output: bfloat16 [1536, 1536], P('tensor'), may hold values from -0.47851562 to 0.47851562
- w_router: bfloat16 [1536, 8], replicated, may hold values from -0.076660156 to 0.076660156
- w_gate: bfloat16 [8, 1536, 768], P('expert', None, 'tensor'), may hold values from -0.15625 to 0.15625
- w_up: bfloat16 [8, 1536, 768], P('expert', None, 'tensor'), may hold values from -0.15625 to 0.15625
- w_down: bfloat16 [8, 768, 1536], P('expert', 'tensor'), may hold values from -3 to 3
Outputs:
- layer_out: bfloat16 [8192, 1536], P('expert')
- grad_inputs: bfloat16 [8192, 1536], P('expert')
- grad_first: float32 [1536], replicated
- grad_second: float32 [1536], replicated
- grad_query: float32 [1536, 1536], P(None, 'tensor')
- grad_key: float32 [1536, 256], replicated
- grad_value: float32 [1536, 256], replicated
- grad_output: float32 [1536, 1536], P('tensor')
- grad_router: float32 [1536, 8], replicated
- grad_gate: float32 [8, 1536, 768], P('expert', None, 'tensor')
- grad_up: float32 [8, 1536, 768], P('expert', None, 'tensor')
- grad_down: float32 [8, 768, 1536], P('expert', 'tensor')
The draws below stay inside these ranges and needn't reach their ends.
Inputs may be any that keep to these rules, and one draw needn't show every extreme that they name: `routes`: each row names 4 different experts. Within the rows of one device (aligned blocks of 1024 rows) no expert is named by more than 768 rows, a bound that some block reaches.
All inputs are finite; a program needn't handle non-finite values.
Results may differ from the reference program's by a relative error of at most 0.019.
Values may be sent and summed in bfloat16 or wider, within the bound.
A program may use at most 320 MiB of HBM per device.

```python
import math
import jax
import jax.numpy as jnp
import numpy as np
from jax import lax

D = 1536
HEADS = 12
KV = 2
HD = 128
FF = 768
TOP = 4
TOK_DEV = 1024
EXPERTS = 8
TOKENS = 8192
CAP = 768
N_EXPERT = 8
N_TENSOR = 4


def shard_levels(rng, shape, split, smallest, high):
    def one(position, shards_of):
        heights = jax.random.uniform(jax.random.fold_in(jax.random.fold_in(rng, 6), position), (shards_of,), jnp.float32, smallest / len(split), high / len(split))
        return jnp.repeat(jnp.exp(heights), shape[position] // shards_of).reshape((-1,) + (1,) * (len(shape) - position - 1))

    loudness = one(*split[0])
    for cut in split[1:]:
        loudness = loudness * one(*cut)
    return loudness


def deal_out(own_key, own, number, rows, amount, top, limit, lean):
    order = jax.random.permutation(own_key, amount)
    crowded, usual = portions_of(amount, rows * top, limit, lean, True), portions_of(amount, rows * top, limit, lean, False)
    places = jnp.arange(amount)

    def named(sizes, offset_by):
        used = int((sizes > 0).sum())
        fixed = max(1, used // 4)
        moved = fixed + (places - fixed + offset_by * (used - fixed)) % max(1, amount - fixed)
        return jnp.zeros((amount,), jnp.int32).at[order[jnp.where(places < fixed, places, moved)]].set(jnp.asarray(sizes, jnp.int32))

    sizes = jnp.where(number % 4 == 0, named(crowded, number // 4), named(usual, number - number // 4 - 1))
    mixed = jax.random.permutation(jax.random.fold_in(own, 3), amount)
    giver, receiver = mixed[0:amount // 2 * 2:2], mixed[1:amount // 2 * 2:2]
    room = jnp.minimum(sizes[giver] - 1, limit - sizes[receiver]) // 2
    room = jnp.where((giver == order[0]) | (receiver == order[0]) | (sizes[receiver] == 0), 0, jnp.maximum(room, 0))
    moved = jax.random.randint(jax.random.fold_in(own, 4), (amount // 2,), 0, 1 << 20) % (room + 1)
    sizes = sizes.at[giver].add(-moved).at[receiver].add(moved)
    labels = jnp.searchsorted(jnp.cumsum(sizes), jnp.arange(rows * top), side="right").astype(jnp.int32)
    table = labels.reshape(top, rows).T
    table = table[jax.random.permutation(jax.random.fold_in(own, 1), rows)]
    offset_by = jax.random.randint(jax.random.fold_in(own, 2), (rows, 1), 0, top)
    return jnp.take_along_axis(table, (jnp.arange(top)[None, :] + offset_by) % top, axis=1)


def portions_of(number_of, total, bound, slope, full):
    weights = [(1 << 20) // math.isqrt(standing ** slope) + 1 for standing in range(1, number_of + 1)]
    largest = bound if full else min(bound, max(-(-total // number_of), total * weights[0] // sum(weights)))
    least = 1 if total - largest >= number_of - 1 else 0
    counts, rest = [largest] + [least] * (number_of - 1), total - largest - least * (number_of - 1)
    while rest > 0:
        candidates = [i for i in range(1, number_of) if counts[i] < largest] or [i for i in range(1, number_of) if counts[i] < bound]
        pool, remaining = sum([weights[i] for i in candidates]), rest
        for i in candidates:
            extra = min(bound - counts[i], max(1, remaining * weights[i] // pool), rest)
            counts[i] = counts[i] + extra
            rest = rest - extra
    return np.array(counts)


def centred(own_key, extent, spread, reach, cuts=(), held_as=jnp.bfloat16):
    level = shard_levels(own_key, extent, cuts, -0.22, 0.18) if cuts else 1.0
    drawn = jax.random.normal(own_key, extent, jnp.float32) * spread * level
    return jnp.minimum(jnp.maximum(drawn, -reach), reach).astype(held_as)


def setup_inputs(seed: int = 0) -> dict:
    seeds = jax.random.split(jax.random.key(seed), 14)
    inputs = centred(seeds[0], (TOKENS, D), 1.0, 6.0, ((0, 8),))
    routes_keys = jax.random.split(jax.random.fold_in(seeds[1], 1), TOKENS // TOK_DEV)
    routes_turns = jax.random.permutation(jax.random.fold_in(seeds[1], 3), TOKENS // TOK_DEV)
    routes = jax.vmap(lambda own, number: deal_out(jax.random.fold_in(seeds[1], 2), own, number, TOK_DEV, EXPERTS, TOP, CAP, 1))(routes_keys, routes_turns).reshape((TOKENS, TOP))
    cotangent = centred(seeds[2], (TOKENS, D), 1.0, 6.0, ((0, 8),))
    first_gain = jnp.clip(1.0 + 0.1 * jax.random.normal(seeds[3], (D,), jnp.float32), 0.5, 1.5)
    second_gain = jnp.clip(1.0 + 0.1 * jax.random.normal(seeds[4], (D,), jnp.float32), 0.5, 1.5)
    w_query = centred(seeds[5], (D, HEADS * HD), D ** -0.5, 0.15625, ((1, 4),))
    w_key = centred(seeds[6], (D, KV * HD), D ** -0.5, 0.15625)
    w_value = centred(seeds[7], (D, KV * HD), D ** -0.5, 0.15625)
    w_output = centred(seeds[8], (HEADS * HD, D), 0.08, 0.47851562, ((0, 4),))
    w_router = centred(seeds[9], (D, EXPERTS), 0.0128, 0.076660156)
    w_gate = centred(seeds[10], (EXPERTS, D, FF), D ** -0.5, 0.15625, ((0, 8), (2, 4)))
    w_up = centred(seeds[11], (EXPERTS, D, FF), D ** -0.5, 0.15625, ((0, 8), (2, 4)))
    w_down = centred(seeds[12], (EXPERTS, FF, D), 0.5, 3.0, ((0, 8), (1, 4)))
    return {"inputs": inputs, "routes": routes, "cotangent": cotangent, "first_gain": first_gain, "second_gain": second_gain, "w_query": w_query, "w_key": w_key, "w_value": w_value, "w_output": w_output, "w_router": w_router, "w_gate": w_gate, "w_up": w_up, "w_down": w_down}


@jax.custom_vjp
def low(v):
    return lax.optimization_barrier(v.astype(jnp.bfloat16)).astype(jnp.float32)

@jax.custom_vjp
def low_back(v):
    return v

def low_keep(v):
    return (low(v), None)

def low_pass(kept, grad):
    return (grad,)

def back_keep(v):
    return (v, None)

def back_low(kept, grad):
    return (low(grad),)
low.defvjp(low_keep, low_pass)
low_back.defvjp(back_keep, back_low)
EPSILON = 1e-06
ROPE_BASE = 10000.0
NEGATIVE = -1e+30

def matmul(left, right):
    return jnp.dot(left, right, precision=lax.Precision.HIGHEST)

def rms_norm(values, gain):
    inverse = lax.rsqrt(lax.optimization_barrier(jnp.mean(values * values, axis=-1, keepdims=True)) + EPSILON)
    return values * inverse * gain

def rotary_tables(length, head_size):
    half_size = head_size // 2
    positions = jnp.arange(length, dtype=jnp.float32)[:, None]
    frequency = ROPE_BASE ** (-jnp.arange(half_size, dtype=jnp.float32) * 2.0 / head_size)
    angles = positions * frequency[None, :]
    return (jnp.cos(angles), jnp.sin(angles))

def rotate(values, cos_table, sin_table):
    half_size = values.shape[-1] // 2
    leading = values[..., :half_size]
    trailing = values[..., half_size:]
    return jnp.concatenate([leading * cos_table - trailing * sin_table, trailing * cos_table + leading * sin_table], axis=-1)

def softmax_rows(scores):
    row_peak = lax.optimization_barrier(jnp.max(scores, axis=-1, keepdims=True))
    exponent = jnp.exp(scores - row_peak)
    return exponent / lax.optimization_barrier(jnp.sum(exponent, axis=-1, keepdims=True))

def reference(inputs, routes, cotangent, first_gain, second_gain, w_query, w_key, w_value, w_output, w_router, w_gate, w_up, w_down):
    local_heads = HEADS // N_TENSOR
    group_size = HEADS // KV
    ff_block = FF // N_TENSOR
    score_scale = HD ** (-0.5)
    cos_table, sin_table = rotary_tables(TOK_DEV, HD)
    allowed = jnp.arange(TOK_DEV)[None, :] <= jnp.arange(TOK_DEV)[:, None]
    most_rows = N_EXPERT * CAP

    def forward(inputs_f, gain_one, gain_two, query_w, key_w, value_w, output_w, router_w, gate_w, up_w, down_w):
        tokens_all = inputs_f.shape[0]
        sequences = tokens_all // TOK_DEV
        attn_in = low(rms_norm(inputs_f, gain_one))

        def attend(seq_in):
            attn_total = jnp.zeros((TOK_DEV, D), jnp.float32)
            for group_index in range(N_TENSOR):
                head_lo = group_index * local_heads * HD
                head_hi = head_lo + local_heads * HD
                kv_head = group_index * local_heads // group_size
                kv_lo = kv_head * HD
                query_proj = low_back(matmul(seq_in, query_w[:, head_lo:head_hi])).reshape(TOK_DEV, local_heads, HD)
                query_rot = low(rotate(query_proj, cos_table[:, None, :], sin_table[:, None, :]))
                key_proj = low_back(matmul(seq_in, key_w[:, kv_lo:kv_lo + HD]))
                key_rot = low(rotate(key_proj, cos_table, sin_table))
                value_low = low_back(low(matmul(seq_in, value_w[:, kv_lo:kv_lo + HD])))
                raw_scores = jnp.einsum('qhd,kd->hqk', query_rot, key_rot, precision=lax.Precision.HIGHEST) * score_scale
                scores = jnp.where(allowed[None], low_back(raw_scores), NEGATIVE)
                weights = softmax_rows(scores)
                context = jnp.einsum('hqk,kd->qhd', low(weights), value_low, precision=lax.Precision.HIGHEST)
                context = low_back(low(context)).reshape(TOK_DEV, local_heads * HD)
                attn_total = attn_total + matmul(context, output_w[head_lo:head_hi, :])
            return low_back(attn_total)
        attn = lax.map(jax.checkpoint(attend), attn_in.reshape(sequences, TOK_DEV, D)).reshape(tokens_all, D)
        after = inputs_f + attn
        expert_in = low(rms_norm(after, gain_two))
        logits = low_back(matmul(expert_in, router_w))
        router_probs = softmax_rows(logits)
        gate_probs = jnp.take_along_axis(router_probs, routes, axis=1)

        def expert_step(moe_total, expert_index):
            hit_mask = routes == expert_index
            weight_row = lax.optimization_barrier(jnp.sum(jnp.where(hit_mask, gate_probs, 0.0), axis=1))
            chosen = jnp.any(hit_mask, axis=1)
            picked = jnp.nonzero(chosen, size=most_rows, fill_value=0)[0].astype(jnp.int32)
            valid_rows = (jnp.arange(most_rows) < jnp.sum(chosen.astype(jnp.int32))).astype(jnp.float32)
            token_rows = expert_in[picked] * valid_rows[:, None]
            gate_mat = gate_w[expert_index]
            up_mat = up_w[expert_index]
            down_mat = down_w[expert_index]
            result = jnp.zeros((most_rows, D), jnp.float32)
            for group_index in range(N_TENSOR):
                col_lo = group_index * ff_block
                rows_group = low_back(token_rows)
                gate_pre = low_back(matmul(rows_group, gate_mat[:, col_lo:col_lo + ff_block]))
                up_pre = low_back(matmul(rows_group, up_mat[:, col_lo:col_lo + ff_block]))
                hidden = low(gate_pre * jax.nn.sigmoid(gate_pre) * up_pre)
                result = result + low_back(low(matmul(hidden, down_mat[col_lo:col_lo + ff_block, :])))
            moe_total = moe_total.at[picked].add(result * (weight_row[picked] * valid_rows)[:, None])
            return (moe_total, None)
        moe, unused = lax.scan(jax.checkpoint(expert_step), jnp.zeros((tokens_all, D), jnp.float32), jnp.arange(EXPERTS, dtype=jnp.int32))
        return after + moe
    primals = (inputs.astype(jnp.float32), first_gain, second_gain, w_query.astype(jnp.float32), w_key.astype(jnp.float32), w_value.astype(jnp.float32), w_output.astype(jnp.float32), w_router.astype(jnp.float32), w_gate.astype(jnp.float32), w_up.astype(jnp.float32), w_down.astype(jnp.float32))
    layer_out, pullback = jax.vjp(forward, *primals)
    grads = pullback(cotangent.astype(jnp.float32))
    return (layer_out.astype(jnp.bfloat16), grads[0].astype(jnp.bfloat16), grads[1], grads[2], grads[3], grads[4], grads[5], grads[6], grads[7], grads[8], grads[9], grads[10])
```

```python
import jax
import jax.numpy as jnp
from jax import lax
from jax.sharding import PartitionSpec as P

HEADS = 12
KV = 2
HD = 128
EPSILON = 1e-06
ROPE_BASE = 10000.0
NEGATIVE = -1e30
F32 = jnp.float32
BF16 = jnp.bfloat16


def dot(left, right, left_dim, right_dim):
    return lax.dot_general(
        left, right, (((left_dim,), (right_dim,)), ((), ())), preferred_element_type=F32
    )


def rms_norm(values, gain):
    inverse = lax.rsqrt(jnp.mean(values * values, axis=-1, keepdims=True) + EPSILON)
    normed = values * inverse
    return normed * gain, normed, inverse


def norm_backward(upstream, normed, inverse, gain):
    scaled = upstream * gain
    through = inverse * (scaled - normed * jnp.mean(scaled * normed, axis=-1, keepdims=True))
    return through, jnp.sum(upstream * normed, axis=0)


def rotary_tables(length, head_size):
    half_size = head_size // 2
    positions = jnp.arange(length, dtype=F32)[:, None]
    frequency = ROPE_BASE ** (-jnp.arange(half_size, dtype=F32) * 2.0 / head_size)
    angles = positions * frequency[None, :]
    return jnp.cos(angles), jnp.sin(angles)


def rotate(values, cos_table, sin_table):
    half = values.shape[-1] // 2
    a, b = values[..., :half], values[..., half:]
    return jnp.concatenate([a * cos_table - b * sin_table, b * cos_table + a * sin_table], axis=-1)


def unrotate(values, cos_table, sin_table):
    half = values.shape[-1] // 2
    a, b = values[..., :half], values[..., half:]
    return jnp.concatenate([a * cos_table + b * sin_table, b * cos_table - a * sin_table], axis=-1)


def causal(scores):
    rows = lax.broadcasted_iota(jnp.int32, scores.shape[-2:], 0)
    cols = lax.broadcasted_iota(jnp.int32, scores.shape[-2:], 1)
    return jnp.where(cols <= rows, scores, NEGATIVE)


class Links:
    def __init__(self, experts, tensors):
        self.experts, self.tensors = experts, tensors
        self.line = experts // 2
        self.tensor = lax.axis_index("tensor")
        expert = lax.axis_index("expert")
        self.place, self.side = expert // 2, expert % 2

    def over_tensor(self, values, bit):
        return lax.ppermute(values, "tensor", [(i, i ^ bit) for i in range(self.tensors)])

    def over_pair(self, values):
        return lax.ppermute(values, "expert", [(i, i ^ 1) for i in range(self.experts)])

    def along(self, values, step, reach=1):
        places = [p for p in range(self.line) if 0 <= p + step * reach < self.line]
        pairs = [(2 * p + s, 2 * (p + step) + s) for p in places for s in range(2)]
        return lax.ppermute(values, "expert", pairs)

    def relative(self, values):
        rows = values.shape[0] // 4
        return jnp.concatenate(
            [lax.dynamic_slice_in_dim(values, (self.tensor ^ r) * rows, rows, 0) for r in range(4)], 0
        )

    def scatter_sum(self, pieces, sent_as=BF16):
        rows = pieces[0].shape[0]
        sent = jnp.concatenate([pieces[1], pieces[3]], 0).astype(sent_as)
        got = self.over_tensor(sent, 1)
        other = (pieces[2] + got[rows:].astype(F32)).astype(sent_as)
        mine = pieces[0] + got[:rows].astype(F32)
        return mine + self.over_tensor(other, 2).astype(F32)

    def gather(self, quarter):
        rows = quarter.shape[0]
        both = jnp.concatenate([quarter, self.over_tensor(quarter, 2)], 0)
        rest = self.over_tensor(both, 1)
        return jnp.concatenate([both[:rows], rest[:rows], both[rows:], rest[rows:]], 0)


def nearest_first(line):
    tables = []
    for place in range(line):
        offsets = [p - place for p in range(line) if p != place]
        tables.append(sorted(offsets, key=lambda o: (abs(o), -o)))
    return tables


def pick(place, options):
    chosen = options[0][0]
    for values, places in options[1:]:
        wanted = place == places[0]
        for p in places[1:]:
            wanted = jnp.logical_or(wanted, place == p)
        chosen = jnp.where(wanted, values, chosen)
    return chosen


def quarters(values):
    rows = values.shape[0] // 4
    return [values[r * rows : (r + 1) * rows] for r in range(4)]


def shards(
    experts,
    tensors,
    inputs,
    routes,
    cotangent,
    first_gain,
    second_gain,
    w_query,
    w_key,
    w_value,
    w_output,
    w_router,
    w_gate,
    w_up,
    w_down,
):
    links = Links(experts, tensors)
    line, place, side = links.line, links.place, links.side
    length, width = inputs.shape
    heads = w_query.shape[1] // HD
    hidden = w_gate.shape[2]
    group = HEADS // KV
    kv_head = links.tensor * heads // group
    scale = HD ** (-0.5)
    order = nearest_first(line)

    own_weights = jnp.concatenate([w_gate[0].T, w_up[0].T, w_down[0]], 0)
    short = line <= 4
    if short:
        arrived = {0: own_weights}
        for step in range(1, line):
            arrived[-step] = links.along(arrived[1 - step] if step > 1 else own_weights, 1)
            arrived[step] = links.along(arrived[step - 1] if step > 1 else own_weights, -1)
        weights = [own_weights]
        for slot in range(line - 1):
            takers = {}
            for p in range(line):
                takers.setdefault(order[p][slot], []).append(p)
            weights.append(pick(place, [(arrived[o], ps) for o, ps in takers.items()]))
    else:
        sides = [[2 * p + s for p in range(line)] for s in range(2)]
        weights = lax.all_gather(own_weights, "expert", axis_index_groups=sides)

    grad_rel = links.relative(cotangent)
    rows = length // 4
    half = links.over_pair(jnp.concatenate([grad_rel[:rows], grad_rel[2 * rows : 3 * rows]], 0))
    rest = links.over_tensor(half, 1)
    grad_pair = jnp.concatenate([half[:rows], rest[:rows], half[rows:], rest[rows:]], 0)
    routes_rel = links.relative(routes)
    routes_both = jnp.concatenate([routes_rel, links.over_pair(routes_rel)], 0)
    grad_both = jnp.concatenate([grad_rel, grad_pair], 0)

    cos_table, sin_table = rotary_tables(length, HD)
    residual = inputs.astype(F32)
    first_out, _, _ = rms_norm(residual, first_gain)
    attn_in = first_out.astype(BF16)
    key_weight = lax.dynamic_slice_in_dim(w_key, kv_head * HD, HD, 1)
    value_weight = lax.dynamic_slice_in_dim(w_value, kv_head * HD, HD, 1)
    query_rot = rotate(
        dot(attn_in, w_query, 1, 0).reshape(length, heads, HD), cos_table[:, None], sin_table[:, None]
    ).astype(BF16)
    key_rot = rotate(dot(attn_in, key_weight, 1, 0), cos_table, sin_table).astype(BF16)
    value_low = dot(attn_in, value_weight, 1, 0).astype(BF16)
    probs, contexts = [], []
    for head in range(heads):
        scores = causal(dot(query_rot[:, head], key_rot, 1, 1) * scale)
        peak = jnp.max(scores, axis=-1, keepdims=True)
        exponent = jnp.exp(scores - peak)
        prob = exponent / jnp.sum(exponent, axis=-1, keepdims=True)
        probs.append(prob)
        contexts.append(dot(prob.astype(BF16), value_low, 1, 0))
    context = jnp.concatenate(contexts, 1).astype(BF16)
    context_rel = links.relative(context)
    attn = links.scatter_sum([dot(piece, w_output, 1, 0) for piece in quarters(context_rel)])

    def own_quarter(values):
        return lax.dynamic_slice_in_dim(values, links.tensor * rows, rows, 0)

    after = own_quarter(inputs).astype(F32) + attn
    second_out, second_normed, second_inverse = rms_norm(after, second_gain)
    expert_in = second_out.astype(BF16)
    tokens_pair = links.over_pair(expert_in)
    tokens_own = links.gather(expert_in)
    tokens = jnp.concatenate([tokens_own, links.gather(tokens_pair)], 0)

    logits = dot(w_router, tokens, 0, 1)
    logit_exp = jnp.exp(logits - jnp.max(logits, axis=0, keepdims=True))
    router_probs = logit_exp / jnp.sum(logit_exp, axis=0, keepdims=True)
    names = jnp.arange(experts, dtype=jnp.int32)[:, None, None]
    named = jnp.any(routes_both.T[None] == names, axis=1).astype(F32)
    gates = router_probs * named

    def one_expert(weight, position):
        name = position * 2 + side
        gate = lax.dynamic_slice_in_dim(gates, name, 1, 0)
        gate_up, down = weight[: 2 * hidden], weight[2 * hidden :]
        pre = dot(gate_up, tokens, 1, 1)
        back = dot(down, grad_both, 1, 1)
        gate_pre, up_pre = pre[:hidden], pre[hidden:]
        sigmoid = jax.nn.sigmoid(gate_pre)
        activated = gate_pre * sigmoid
        hid = (activated * up_pre).astype(BF16).astype(F32)
        gate_row = jnp.sum(hid * back, axis=0, keepdims=True) * lax.dynamic_slice_in_dim(named, name, 1, 0)
        gated = (hid * gate).astype(BF16)
        grad_hidden = back * gate
        grad_pre = jnp.concatenate(
            [
                grad_hidden * up_pre * sigmoid * (1.0 + gate_pre * (1.0 - sigmoid)),
                grad_hidden * activated,
            ],
            0,
        ).astype(BF16)
        weight_grad = jnp.concatenate([dot(grad_pre, tokens, 1, 0), dot(gated, grad_both, 1, 0)], 0)
        return dot(gated, down, 0, 0), dot(grad_pre, gate_up, 0, 0), gate_row, weight_grad

    moe = jnp.zeros(tokens.shape, F32)
    grad_tokens = jnp.zeros(tokens.shape, F32)
    if short:
        gate_rows, weight_grads = [], []
        for slot in range(line):
            offsets = jnp.asarray([0 if slot == 0 else order[p][slot - 1] for p in range(line)], jnp.int32)
            moe_part, grad_part, gate_row, weight_grad = one_expert(weights[slot], place + offsets[place])
            moe, grad_tokens = moe + moe_part, grad_tokens + grad_part
            gate_rows.append(gate_row)
            weight_grads.append(weight_grad)
        gate_sums = jnp.concatenate(gate_rows, 0)
    else:

        def step(totals, weight_at):
            moe_part, grad_part, gate_row, weight_grad = one_expert(*weight_at)
            return (totals[0] + moe_part, totals[1] + grad_part), (gate_row[0], weight_grad.astype(BF16))

        (moe, grad_tokens), (gate_sums, weight_grads) = lax.scan(
            step, (moe, grad_tokens), (weights, jnp.arange(line, dtype=jnp.int32))
        )

    grad_pair_quarter = links.scatter_sum(quarters(grad_tokens[length:])).astype(BF16)
    grad_own_quarter = links.scatter_sum(quarters(grad_tokens[:length]))
    grad_expert_in = grad_own_quarter + links.over_pair(grad_pair_quarter).astype(F32)

    gate_sums = jnp.concatenate([gate_sums[:, :length], gate_sums[:, length:]], 0)
    gate_sums = links.scatter_sum([gate_sums[:, r * rows : (r + 1) * rows] for r in range(4)], F32)
    gate_own, gate_other = gate_sums[:line], links.over_pair(gate_sums[line:])
    slot_of = jnp.asarray(
        [
            [q if not short else 0 if q == p else 1 + order[p].index(q - p) for q in range(line)]
            for p in range(line)
        ],
        jnp.int32,
    )
    dprobs = []
    for q in range(line):
        slot = slot_of[place, q]
        mine = lax.dynamic_slice_in_dim(gate_own, slot, 1, 0)
        theirs = lax.dynamic_slice_in_dim(gate_other, slot, 1, 0)
        dprobs += [jnp.where(side == 0, mine, theirs), jnp.where(side == 0, theirs, mine)]
    dprobs = jnp.concatenate(dprobs, 0)
    quarter_probs = router_probs[:, :rows]
    dlogits = (
        quarter_probs * (dprobs - jnp.sum(quarter_probs * dprobs, axis=0, keepdims=True))
    ).astype(BF16)
    grad_expert_in = grad_expert_in + dot(dlogits, w_router, 0, 1)
    grad_router = dot(expert_in, dlogits, 0, 1)
    through_second, grad_second = norm_backward(
        grad_expert_in, second_normed, second_inverse, second_gain
    )
    grad_after = own_quarter(cotangent).astype(F32) + through_second
    grad_after_low = links.gather(grad_after.astype(BF16))

    moe_pair = links.scatter_sum(quarters(moe[length:])).astype(BF16)
    moe_own = links.scatter_sum(quarters(moe[:length]))
    layer_out = links.relative(
        links.gather((after + moe_own + links.over_pair(moe_pair).astype(F32)).astype(BF16))
    )

    def flow(step):
        got = None
        for reach in range(line - 1, 0, -1):
            takers = {}
            for p in range(line):
                if 0 <= p + step * reach < line:
                    takers.setdefault(1 + order[p].index(step * reach), []).append(p)
            total = pick(place, [(weight_grads[s], ps) for s, ps in takers.items()])
            if got is not None:
                total = total + got.astype(F32)
            got = links.along(total.astype(BF16), step, reach)
        return got.astype(F32)

    if short:
        expert_grads = weight_grads[0]
        if line > 1:
            expert_grads = expert_grads + flow(1) + flow(-1)
    else:
        expert_grads = lax.psum_scatter(
            weight_grads, "expert", scatter_dimension=0, axis_index_groups=sides
        ).astype(F32)

    grad_output = dot(context_rel, grad_after_low, 0, 0)
    grad_output = lax.psum(grad_output.astype(BF16), "expert").astype(F32)
    grad_context = links.relative(dot(grad_after_low, w_output, 1, 1).astype(BF16))
    grad_heads = grad_context.reshape(length, heads, HD)
    query_grads = []
    key_grad = jnp.zeros((length, HD), F32)
    value_grad = jnp.zeros((length, HD), F32)
    for head in range(heads):
        dprob = dot(grad_heads[:, head], value_low, 1, 1)
        delta = jnp.sum(probs[head] * dprob, axis=-1, keepdims=True)
        dscore = (probs[head] * (dprob - delta)).astype(BF16)
        query_grads.append(dot(dscore, key_rot, 1, 0) * scale)
        key_grad = key_grad + dot(dscore, query_rot[:, head], 0, 0) * scale
        value_grad = value_grad + dot(probs[head].astype(BF16), grad_heads[:, head], 0, 0)
    query_grad = jnp.concatenate(
        [unrotate(g, cos_table, sin_table).astype(BF16) for g in query_grads], 1
    )
    key_grad = unrotate(key_grad, cos_table, sin_table).astype(BF16)
    value_grad = value_grad.astype(BF16)
    attn_weights = jnp.concatenate([w_query, key_weight, value_weight], 1)
    attn_grads = jnp.concatenate([query_grad, key_grad, value_grad], 1)
    grad_attn_in = links.scatter_sum(
        [dot(piece, attn_weights, 1, 1) for piece in quarters(links.relative(attn_grads))]
    )
    attn_weight_grads = dot(attn_in, attn_grads, 0, 0)
    query_width = heads * HD
    kv_grads = attn_weight_grads[:, query_width:]
    kv_grads = kv_grads + links.over_tensor(kv_grads.astype(BF16), 1).astype(F32)
    kv_grads = kv_grads.astype(BF16)
    summed = lax.psum(
        jnp.concatenate([attn_weight_grads[:, :query_width].astype(BF16), kv_grads], 1), "expert"
    )
    grad_query = summed[:, :query_width].astype(F32)
    kv_mine = summed[:, query_width:]
    kv_theirs = links.over_tensor(kv_mine, 2)
    first_head = kv_head == 0
    kv_low = jnp.where(first_head, kv_mine, kv_theirs).astype(F32)
    kv_high = jnp.where(first_head, kv_theirs, kv_mine).astype(F32)
    grad_key = jnp.concatenate([kv_low[:, :HD], kv_high[:, :HD]], 1)
    grad_value = jnp.concatenate([kv_low[:, HD:], kv_high[:, HD:]], 1)

    quarter_in = own_quarter(inputs).astype(F32)
    _, first_normed, first_inverse = rms_norm(quarter_in, first_gain)
    through_first, grad_first = norm_backward(
        grad_attn_in, first_normed, first_inverse, first_gain
    )
    grad_inputs = links.relative(links.gather((grad_after + through_first).astype(BF16)))
    grad_first, grad_second, grad_router = lax.psum(
        (grad_first, grad_second, grad_router), ("expert", "tensor")
    )
    return (
        layer_out,
        grad_inputs,
        grad_first,
        grad_second,
        grad_query,
        grad_key,
        grad_value,
        grad_output,
        grad_router,
        expert_grads[:hidden].T[None],
        expert_grads[hidden : 2 * hidden].T[None],
        expert_grads[2 * hidden :][None],
    )


def solution(mesh):
    experts, tensors = mesh.shape["expert"], mesh.shape["tensor"]
    in_specs = (
        P("expert", None),
        P("expert", None),
        P("expert", None),
        P(),
        P(),
        P(None, "tensor"),
        P(),
        P(),
        P("tensor", None),
        P(),
        P("expert", None, "tensor"),
        P("expert", None, "tensor"),
        P("expert", "tensor", None),
    )
    out_specs = (
        P("expert", None),
        P("expert", None),
        P(),
        P(),
        P(None, "tensor"),
        P(),
        P(),
        P("tensor", None),
        P(),
        P("expert", None, "tensor"),
        P("expert", None, "tensor"),
        P("expert", "tensor", None),
    )

    def run(*arrays):
        return shards(experts, tensors, *arrays)

    return jax.shard_map(run, mesh=mesh, in_specs=in_specs, out_specs=out_specs, check_vma=False)
```

```python
import functools

import jax
import jax.numpy as jnp
from jax import lax
from jax.experimental import pallas as pl
from jax.experimental.pallas import tpu as pltpu
from jax.sharding import PartitionSpec as P

HEADS = 12
KV = 2
HD = 128
EPSILON = 1e-06
ROPE_BASE = 10000.0
NEGATIVE = -1e30
F32 = jnp.float32
BF16 = jnp.bfloat16


def dot(left, right, left_dim, right_dim):
    return lax.dot_general(
        left, right, (((left_dim,), (right_dim,)), ((), ())), preferred_element_type=F32
    )


def rms_norm(values, gain):
    inverse = lax.rsqrt(jnp.mean(values * values, axis=-1, keepdims=True) + EPSILON)
    normed = values * inverse
    return normed * gain, normed, inverse


def norm_backward(upstream, normed, inverse, gain):
    scaled = upstream * gain
    through = inverse * (scaled - normed * jnp.mean(scaled * normed, axis=-1, keepdims=True))
    return through, jnp.sum(upstream * normed, axis=0)


def rotary_tables(length, head_size):
    half_size = head_size // 2
    positions = jnp.arange(length, dtype=F32)[:, None]
    frequency = ROPE_BASE ** (-jnp.arange(half_size, dtype=F32) * 2.0 / head_size)
    angles = positions * frequency[None, :]
    return jnp.cos(angles), jnp.sin(angles)


def rotate(values, cos_table, sin_table):
    half = values.shape[-1] // 2
    a, b = values[..., :half], values[..., half:]
    return jnp.concatenate([a * cos_table - b * sin_table, b * cos_table + a * sin_table], axis=-1)


def unrotate(values, cos_table, sin_table):
    half = values.shape[-1] // 2
    a, b = values[..., :half], values[..., half:]
    return jnp.concatenate([a * cos_table + b * sin_table, b * cos_table - a * sin_table], axis=-1)


def causal(scores):
    rows = lax.broadcasted_iota(jnp.int32, scores.shape[-2:], 0)
    cols = lax.broadcasted_iota(jnp.int32, scores.shape[-2:], 1)
    return jnp.where(cols <= rows, scores, NEGATIVE)


class Links:
    def __init__(self, experts, tensors):
        self.experts, self.tensors = experts, tensors
        self.line = experts // 2
        self.tensor = lax.axis_index("tensor")
        expert = lax.axis_index("expert")
        self.place, self.side = expert // 2, expert % 2

    def over_tensor(self, values, bit):
        return lax.ppermute(values, "tensor", [(i, i ^ bit) for i in range(self.tensors)])

    def over_expert(self, values, bit):
        return lax.ppermute(values, "expert", [(i, i ^ bit) for i in range(self.experts)])

    def over_pair(self, values):
        return self.over_expert(values, 1)

    def along(self, values, step, reach=1):
        places = [p for p in range(self.line) if 0 <= p + step * reach < self.line]
        pairs = [(2 * p + s, 2 * (p + step) + s) for p in places for s in range(2)]
        return lax.ppermute(values, "expert", pairs)

    def relative(self, values):
        rows = values.shape[0] // 4
        return jnp.concatenate(
            [
                lax.dynamic_slice_in_dim(values, (self.tensor ^ r) * rows, rows, 0)
                for r in (0, 2, 1, 3)
            ],
            0,
        )

    def absolute(self, values):
        rows = values.shape[0] // 4
        place = jnp.asarray([0, 2, 1, 3], jnp.int32)
        return jnp.concatenate(
            [
                lax.dynamic_slice_in_dim(values, place[self.tensor ^ q] * rows, rows, 0)
                for q in range(4)
            ],
            0,
        )

    def gather(self, quarter):
        both = jnp.concatenate([quarter, self.over_tensor(quarter, 2)], 0)
        return jnp.concatenate([both, self.over_tensor(both, 1)], 0)


def nearest_first(line):
    tables = []
    for place in range(line):
        offsets = [p - place for p in range(line) if p != place]
        tables.append(sorted(offsets, key=lambda o: (abs(o), -o)))
    return tables


def pick(place, options):
    chosen = options[0][0]
    for values, places in options[1:]:
        wanted = place == places[0]
        for p in places[1:]:
            wanted = jnp.logical_or(wanted, place == p)
        chosen = jnp.where(wanted, values, chosen)
    return chosen


def expert_kernel(count, hidden, split, prior, *refs):
    names, tokens, grads, gates = refs[:4]
    weights, refs = refs[4 : 4 + count], refs[4 + count :]
    if prior:
        before, refs = refs[0], refs[1:]
    outs, (gated_out, grad_pre_out, rows_out) = refs[: 2 if split else 1], refs[2 if split else 1 :]
    tile, grad_tile = tokens[...], grads[...]
    total = before[...].astype(F32) if prior else None
    for slot in range(count):
        weight = weights[slot]
        pre = dot(weight[: 2 * hidden, :], tile, 1, 1)
        back = dot(weight[2 * hidden :, :], grad_tile, 1, 1)
        gate = gates[pl.ds(names[slot], 1), :]
        gate_pre, up_pre = pre[:hidden], pre[hidden:]
        sigmoid = jax.nn.sigmoid(gate_pre)
        activated = gate_pre * sigmoid
        hid = (activated * up_pre).astype(BF16).astype(F32)
        rows_out[slot : slot + 1, :] = jnp.sum(hid * back, axis=0, keepdims=True)
        gated_out[slot * hidden : (slot + 1) * hidden, :] = (hid * gate).astype(BF16)
        grad_hidden = back * gate
        grad_pre = jnp.concatenate(
            [
                (grad_hidden * up_pre * (sigmoid * (1.0 + gate_pre * (1.0 - sigmoid)))).astype(BF16),
                (grad_hidden * activated).astype(BF16),
            ],
            0,
        )
        grad_pre_out[2 * slot * hidden : 2 * (slot + 1) * hidden, :] = grad_pre
        part = dot(grad_pre, weight[: 2 * hidden, :], 0, 0)
        total = part if total is None else total + part
    if split:
        for step in range(2):

            @pl.when(pl.program_id(0) == step)
            def _(step=step):
                outs[step][...] = total.astype(BF16)
    else:
        outs[0][...] = total.astype(BF16)


def expert_pass(tokens, grads, gates, names, weights, before=None, split=False):
    count, length, width = len(weights), tokens.shape[0], tokens.shape[1]
    hidden = weights[0].shape[0] // 3
    tile = length // 2
    token_spec = pl.BlockSpec((tile, width), lambda i, *_: (i, 0))
    half_spec = pl.BlockSpec((tile, width), lambda i, *_: (0, 0))

    def column_spec(rows):
        return pl.BlockSpec((rows, tile), lambda i, *_: (0, i))

    weight_spec = pl.BlockSpec((3 * hidden, width), lambda i, *_: (0, 0))
    token_shape = jax.ShapeDtypeStruct((length, width), BF16)
    half_shape = jax.ShapeDtypeStruct((tile, width), BF16)
    columns = [(count * hidden, BF16), (2 * count * hidden, BF16), (count, F32)]
    return pl.pallas_call(
        functools.partial(expert_kernel, count, hidden, split, before is not None),
        grid_spec=pltpu.PrefetchScalarGridSpec(
            num_scalar_prefetch=1,
            grid=(2,),
            in_specs=[token_spec, token_spec, column_spec(gates.shape[0])]
            + [weight_spec] * count
            + [token_spec] * (before is not None),
            out_specs=([half_spec] * 2 if split else [token_spec]) + [column_spec(r) for r, _ in columns],
        ),
        out_shape=([half_shape] * 2 if split else [token_shape])
        + [jax.ShapeDtypeStruct((r, length), t) for r, t in columns],
        compiler_params=pltpu.CompilerParams(vmem_limit_bytes=48 * 2**20),
        cost_estimate=pl.CostEstimate(
            flops=2 * count * length * width * hidden * 5,
            bytes_accessed=(4 * length + 3 * hidden * count) * width * 2,
            transcendentals=0,
        ),
    )(names, tokens, grads, gates, *weights, *([before] if before is not None else []))


def weight_grad_kernel(grad_pre_own, grad_pre_pair, gated_own, gated_pair, own, pair, grad_own, grad_pair, out):
    rows = grad_pre_own.shape[0]
    out[:rows, :] = (
        dot(grad_pre_own[...], own[...], 1, 0) + dot(grad_pre_pair[...], pair[...], 1, 0)
    ).astype(out.dtype)
    out[rows:, :] = (
        dot(gated_own[...], grad_own[...], 1, 0) + dot(gated_pair[...], grad_pair[...], 1, 0)
    ).astype(out.dtype)


def weight_grad(slot, hidden, grad_pre, gated, tokens, grads, kept_as):
    length, width = tokens[0].shape
    tile = width // 3
    pre_spec = pl.BlockSpec((2 * hidden, length), lambda i: (slot, 0))
    gated_spec = pl.BlockSpec((hidden, length), lambda i: (slot, 0))
    token_spec = pl.BlockSpec((length, tile), lambda i: (0, i))
    return pl.pallas_call(
        weight_grad_kernel,
        grid=(3,),
        in_specs=[pre_spec] * 2 + [gated_spec] * 2 + [token_spec] * 4,
        out_specs=pl.BlockSpec((3 * hidden, tile), lambda i: (0, i)),
        out_shape=jax.ShapeDtypeStruct((3 * hidden, width), kept_as),
        compiler_params=pltpu.CompilerParams(vmem_limit_bytes=32 * 2**20),
        cost_estimate=pl.CostEstimate(
            flops=2 * 2 * length * width * hidden * 3,
            bytes_accessed=(4 * length + 6 * hidden) * width * 2,
            transcendentals=0,
        ),
    )(*grad_pre, *gated, *tokens, *grads)


MESH = pl.DeviceIdType.MESH


class Copies:
    def __init__(self, tensors, send, recv):
        self.send, self.recv, self.started = send, recv, []
        expert, tensor = lax.axis_index("expert"), lax.axis_index("tensor")
        self.core = (expert, tensor + 1 - 2 * (tensor % 2))
        self.far = (expert, (tensor + tensors // 2) % tensors)
        self.mate = (expert + 1 - 2 * (expert % 2), tensor)

    def across(self, bit):
        expert, tensor = lax.axis_index("expert"), lax.axis_index("tensor")
        return (expert + bit - 2 * bit * (expert // bit % 2), tensor)

    def greet(self, partners):
        barrier = pltpu.get_barrier_semaphore()
        for partner in partners:
            pl.semaphore_signal(barrier, inc=1, device_id=partner, device_id_type=MESH)
        pl.semaphore_wait(barrier, len(partners))

    def start(self, source, target, device):
        place = len(self.started)
        copy = pltpu.make_async_remote_copy(
            src_ref=source,
            dst_ref=target,
            send_sem=self.send.at[place],
            recv_sem=self.recv.at[place],
            device_id=device,
            device_id_type=MESH,
        )
        copy.start()
        self.started.append(copy)
        return copy

    def finish(self):
        for copy in self.started:
            copy.wait_send()


def sum_quarter(copies, part, sent, got, crossing, crossed):
    rows = crossing.shape[0]
    sent[rows:, :] = part(3).astype(BF16)
    last = copies.start(sent.at[pl.ds(rows, rows)], got.at[pl.ds(rows, rows)], copies.core)
    sent[:rows, :] = part(2).astype(BF16)
    first = copies.start(sent.at[pl.ds(0, rows)], got.at[pl.ds(0, rows)], copies.core)
    other = part(1)
    last.wait_recv()
    crossing[...] = (other + got[rows:, :].astype(F32)).astype(BF16)
    far = copies.start(crossing, crossed, copies.far)
    mine = part(0)
    first.wait_recv()
    mine = mine + got[:rows, :].astype(F32)
    far.wait_recv()
    return mine + crossed[...].astype(F32)


def gather_quarters(copies, whole, rows, fill=None):
    far = copies.start(whole.at[pl.ds(0, rows)], whole.at[pl.ds(rows, rows)], copies.far)
    first = copies.start(whole.at[pl.ds(0, rows)], whole.at[pl.ds(2 * rows, rows)], copies.core)
    if fill is not None:
        fill()
    far.wait_recv()
    last = copies.start(whole.at[pl.ds(rows, rows)], whole.at[pl.ds(3 * rows, rows)], copies.core)
    first.wait_recv()
    last.wait_recv()


def attend_out_kernel(
    tensors, context, weight, stream, gain, own, pair, after, sent, got, crossing, crossed, send, recv
):
    copies = Copies(tensors, send, recv)
    copies.greet([copies.core, copies.far, copies.mate])
    rows = stream.shape[0]

    def part(place):
        return dot(context[place * rows : (place + 1) * rows, :], weight[...], 1, 0)

    total = stream[...].astype(F32) + sum_quarter(copies, part, sent, got, crossing, crossed)
    after[...] = total
    own[:rows, :] = rms_norm(total, gain[...])[0].astype(BF16)
    mate = copies.start(own.at[pl.ds(0, rows)], pair.at[pl.ds(0, rows)], copies.mate)
    gather_quarters(copies, own, rows)
    mate.wait_recv()
    gather_quarters(copies, pair, rows)
    copies.finish()


def vmem():
    return pl.BlockSpec(memory_space=pltpu.VMEM)


def attend_out(tensors, context, weight, stream, gain):
    rows, width = stream.shape
    return pl.pallas_call(
        functools.partial(attend_out_kernel, tensors),
        out_shape=[
            jax.ShapeDtypeStruct((4 * rows, width), BF16),
            jax.ShapeDtypeStruct((4 * rows, width), BF16),
            jax.ShapeDtypeStruct((rows, width), F32),
        ],
        in_specs=[vmem()] * 4,
        out_specs=[vmem()] * 3,
        scratch_shapes=[
            pltpu.VMEM((2 * rows, width), BF16),
            pltpu.VMEM((2 * rows, width), BF16),
            pltpu.VMEM((rows, width), BF16),
            pltpu.VMEM((rows, width), BF16),
            pltpu.SemaphoreType.DMA((10,)),
            pltpu.SemaphoreType.DMA((10,)),
        ],
        compiler_params=pltpu.CompilerParams(
            collective_id=1, has_side_effects=True, vmem_limit_bytes=40 * 2**20
        ),
        cost_estimate=pl.CostEstimate(flops=6 * 10**10, bytes_accessed=10**7, transcendentals=0),
    )(context, weight, stream, gain)


def tokens_back_kernel(
    tensors,
    kept_pair,
    sent_pair,
    kept_own,
    sent_own,
    rows_kept,
    rows_sent,
    names,
    probs,
    named,
    router,
    after,
    gain,
    grad,
    whole,
    grad_after,
    grad_router,
    grad_second,
    got_pair,
    got_own,
    crossing_pair,
    crossed_pair,
    crossing_own,
    crossed_own,
    mate_out,
    mate_in,
    rows_got,
    rows_crossing,
    rows_crossed,
    rows_mine,
    rows_mate,
    send,
    recv,
):
    copies = Copies(tensors, send, recv)
    copies.greet([copies.core, copies.far, copies.mate])
    rows = grad.shape[0]
    low, high = pl.ds(0, rows), pl.ds(rows, rows)
    pair_last = copies.start(sent_pair.at[high], got_pair.at[high], copies.core)
    pair_first = copies.start(sent_pair.at[low], got_pair.at[low], copies.core)
    rows_core = copies.start(rows_sent, rows_got, copies.core)
    own_last = copies.start(sent_own.at[high], got_own.at[high], copies.core)
    own_first = copies.start(sent_own.at[low], got_own.at[low], copies.core)
    pair_last.wait_recv()
    crossing_pair[...] = (kept_pair[rows:, :].astype(F32) + got_pair[rows:, :].astype(F32)).astype(BF16)
    pair_far = copies.start(crossing_pair, crossed_pair, copies.far)
    rows_core.wait_recv()
    rows_crossing[...] = rows_kept[:, rows:] + rows_got[:, rows:]
    rows_far = copies.start(rows_crossing, rows_crossed, copies.far)
    pair_first.wait_recv()
    mine_pair = kept_pair[:rows, :].astype(F32) + got_pair[:rows, :].astype(F32)
    own_last.wait_recv()
    crossing_own[...] = (kept_own[rows:, :].astype(F32) + got_own[rows:, :].astype(F32)).astype(BF16)
    own_first.wait_recv()
    grad_tokens = kept_own[:rows, :].astype(F32) + got_own[:rows, :].astype(F32)
    pair_far.wait_recv()
    own_far = copies.start(crossing_own, crossed_own, copies.far)
    mate_out[...] = (mine_pair + crossed_pair[...].astype(F32)).astype(BF16)
    mate = copies.start(mate_out, mate_in, copies.mate)
    rows_far.wait_recv()
    rows_mine[...] = rows_kept[:, :rows] + rows_got[:, :rows] + rows_crossed[...]
    rows_over = copies.start(rows_mine, rows_mate, copies.mate)
    rows_over.wait_recv()
    line = rows_mine.shape[0] // 2
    slots = jnp.concatenate([rows_mine[:line, :], rows_mate[line:, :]], 0)
    dprobs = jnp.zeros(probs.shape, F32)
    for slot in range(2 * line):
        dprobs = dprobs + names[:, slot : slot + 1] * slots[slot : slot + 1, :]
    dprobs = dprobs * named[...]
    dlogits = (
        probs[...] * (dprobs - jnp.sum(probs[...] * dprobs, axis=0, keepdims=True))
    ).astype(BF16)
    second_out, normed, inverse = rms_norm(after[...], gain[...])
    grad_router[...] = dot(dlogits, second_out.astype(BF16), 1, 0)
    grad_tokens = grad_tokens + dot(dlogits, router[...], 0, 0)
    own_far.wait_recv()
    grad_tokens = grad_tokens + crossed_own[...].astype(F32)
    mate.wait_recv()
    grad_tokens = grad_tokens + mate_in[...].astype(F32)
    through, second = norm_backward(grad_tokens, normed, inverse, gain[...])
    grad_second[...] = second[None]
    total = grad[...].astype(F32) + through
    grad_after[...] = total
    whole[:rows, :] = total.astype(BF16)
    gather_quarters(copies, whole, rows)
    copies.finish()


def tokens_back(tensors, experts, *operands):
    rows, width = operands[-1].shape
    half = pltpu.VMEM((2 * rows, width), BF16)
    quarter = pltpu.VMEM((rows, width), BF16)
    small = pltpu.VMEM((experts, rows), F32)
    return pl.pallas_call(
        functools.partial(tokens_back_kernel, tensors),
        out_shape=[
            jax.ShapeDtypeStruct((4 * rows, width), BF16),
            jax.ShapeDtypeStruct((rows, width), F32),
            jax.ShapeDtypeStruct((experts, width), F32),
            jax.ShapeDtypeStruct((1, width), F32),
        ],
        in_specs=[vmem()] * len(operands),
        out_specs=[vmem()] * 4,
        scratch_shapes=[half, half]
        + [quarter] * 6
        + [pltpu.VMEM((experts, 2 * rows), F32), small, small, small, small]
        + [pltpu.SemaphoreType.DMA((16,)), pltpu.SemaphoreType.DMA((16,))],
        compiler_params=pltpu.CompilerParams(
            collective_id=2, has_side_effects=True, vmem_limit_bytes=48 * 2**20
        ),
        cost_estimate=pl.CostEstimate(flops=6 * 10**10, bytes_accessed=10**7, transcendentals=0),
    )(*operands)


def inputs_back_kernel(
    tensors,
    experts,
    grads,
    weight,
    stream,
    gain,
    grad_after,
    early,
    whole,
    sums,
    sent,
    got,
    crossing,
    crossed,
    running,
    arrived,
    send,
    recv,
):
    copies = Copies(tensors, send, recv)
    bits = [1 << k for k in range(experts.bit_length() - 1)]
    copies.greet([copies.core, copies.far] + [copies.across(bit) for bit in bits])
    rows = stream.shape[0]

    def part(place):
        return dot(grads[place * rows : (place + 1) * rows, :], weight[...], 1, 1)

    grad_in = sum_quarter(copies, part, sent, got, crossing, crossed)
    _, normed, inverse = rms_norm(stream[...].astype(F32), gain[...])
    through, first = norm_backward(grad_in, normed, inverse, gain[...])
    whole[:rows, :] = (grad_after[...] + through).astype(BF16)

    def fill():
        running[0] = early[...]
        running[0, experts + 1 : experts + 2, :] = first[None]
        steps = [copies.core] + [copies.across(bit) for bit in bits] + [copies.far]
        for step, device in enumerate(steps):
            copy = copies.start(running.at[step], arrived.at[step], device)
            copy.wait_recv()
            if step + 1 < len(steps):
                running[step + 1] = running[step] + arrived[step]
            else:
                sums[...] = running[step] + arrived[step]

    gather_quarters(copies, whole, rows, fill)
    copies.finish()


def inputs_back(tensors, experts, *operands):
    rows, width = operands[2].shape
    early = operands[-1].shape
    steps = 1 + experts.bit_length()
    return pl.pallas_call(
        functools.partial(inputs_back_kernel, tensors, experts),
        out_shape=[
            jax.ShapeDtypeStruct((4 * rows, width), BF16),
            jax.ShapeDtypeStruct(early, F32),
        ],
        in_specs=[vmem()] * len(operands),
        out_specs=[vmem()] * 2,
        scratch_shapes=[
            pltpu.VMEM((2 * rows, width), BF16),
            pltpu.VMEM((2 * rows, width), BF16),
            pltpu.VMEM((rows, width), BF16),
            pltpu.VMEM((rows, width), BF16),
            pltpu.VMEM((steps,) + early, F32),
            pltpu.VMEM((steps,) + early, F32),
            pltpu.SemaphoreType.DMA((6 + steps,)),
            pltpu.SemaphoreType.DMA((6 + steps,)),
        ],
        compiler_params=pltpu.CompilerParams(
            collective_id=3, has_side_effects=True, vmem_limit_bytes=48 * 2**20
        ),
        cost_estimate=pl.CostEstimate(flops=5 * 10**10, bytes_accessed=10**7, transcendentals=0),
    )(*operands)


def shards(
    experts,
    tensors,
    inputs,
    routes,
    cotangent,
    first_gain,
    second_gain,
    w_query,
    w_key,
    w_value,
    w_output,
    w_router,
    w_gate,
    w_up,
    w_down,
):
    links = Links(experts, tensors)
    line, place, side = links.line, links.place, links.side
    length, width = inputs.shape
    heads = w_query.shape[1] // HD
    hidden = w_gate.shape[2]
    group = HEADS // KV
    kv_head = links.tensor * heads // group
    scale = HD ** (-0.5)
    order = nearest_first(line)

    own_weights = jnp.concatenate([w_gate[0].T, w_up[0].T, w_down[0]], 0)
    short = line <= 4
    if short:
        arrived = {0: own_weights}
        for step in range(1, line):
            arrived[-step] = links.along(arrived[1 - step] if step > 1 else own_weights, 1)
            arrived[step] = links.along(arrived[step - 1] if step > 1 else own_weights, -1)
        weights = [own_weights]
        for slot in range(line - 1):
            takers = {}
            for p in range(line):
                takers.setdefault(order[p][slot], []).append(p)
            weights.append(pick(place, [(arrived[o], ps) for o, ps in takers.items()]))
    else:
        sides = [[2 * p + s for p in range(line)] for s in range(2)]
        weights = lax.all_gather(own_weights, "expert", axis_index_groups=sides)

    grad_rel = links.relative(cotangent)
    rows, half = length // 4, length // 2
    grad_half = links.over_pair(grad_rel[:half])
    grad_pair = jnp.concatenate([grad_half, links.over_tensor(grad_half, 1)], 0)
    routes_own = links.relative(routes).T
    routes_pair = links.over_pair(routes_own)

    cos_table, sin_table = rotary_tables(length, HD)
    residual = inputs.astype(F32)
    first_out, _, _ = rms_norm(residual, first_gain)
    attn_in = first_out.astype(BF16)
    key_weight = lax.dynamic_slice_in_dim(w_key, kv_head * HD, HD, 1)
    value_weight = lax.dynamic_slice_in_dim(w_value, kv_head * HD, HD, 1)
    query_rot = rotate(
        dot(attn_in, w_query, 1, 0).reshape(length, heads, HD), cos_table[:, None], sin_table[:, None]
    ).astype(BF16)
    key_rot = rotate(dot(attn_in, key_weight, 1, 0), cos_table, sin_table).astype(BF16)
    value_low = dot(attn_in, value_weight, 1, 0).astype(BF16)
    probs, contexts = [], []
    for head in range(heads):
        scores = causal(dot(query_rot[:, head], key_rot, 1, 1) * scale)
        peak = jnp.max(scores, axis=-1, keepdims=True)
        exponent = jnp.exp(scores - peak)
        prob = exponent / jnp.sum(exponent, axis=-1, keepdims=True)
        probs.append(prob)
        contexts.append(dot(prob.astype(BF16), value_low, 1, 0))
    context = jnp.concatenate(contexts, 1).astype(BF16)
    context_rel = links.relative(context)
    def own_quarter(values):
        return lax.dynamic_slice_in_dim(values, links.tensor * rows, rows, 0)

    stream = own_quarter(inputs)
    if short:
        early = [arrived[o] for o in (-1, 1) if o in arrived]
        context_rel, *early = lax.optimization_barrier([context_rel] + early)
    tokens_own, tokens_pair, after = attend_out(
        tensors, context_rel, w_output, stream, second_gain[None]
    )
    names = jnp.arange(experts, dtype=jnp.int32)[:, None, None]

    def gates_of(tokens, tokens_routes):
        logits = dot(router_rows, tokens, 1, 1)
        logit_exp = jnp.exp(logits - jnp.max(logits, axis=0, keepdims=True))
        probs = logit_exp / jnp.sum(logit_exp, axis=0, keepdims=True)
        named = jnp.any(tokens_routes[None] == names, axis=1).astype(F32)
        return probs, named, probs * named

    router_rows = w_router.T
    router_probs, named, gates_own = gates_of(tokens_own, routes_own)
    _, _, gates_pair = gates_of(tokens_pair, routes_pair)

    both_tokens, both_grads = (tokens_own, tokens_pair), (grad_rel, grad_pair)
    if short:
        offsets = jnp.asarray([[0] + order[p] for p in range(line)], jnp.int32)[place]
        slot_names = (place + offsets) * 2 + side
        last = line - 1
        first_own = expert_pass(tokens_own, grad_rel, gates_own, slot_names[:last], weights[:last])
        first_pair = expert_pass(tokens_pair, grad_pair, gates_pair, slot_names[:last], weights[:last])
        kept_pair, sent_pair, *last_pair = expert_pass(
            tokens_pair, grad_pair, gates_pair, slot_names[last:], weights[last:], first_pair[0], True
        )
        kept_own, sent_own, *last_own = expert_pass(
            tokens_own, grad_rel, gates_own, slot_names[last:], weights[last:], first_own[0], True
        )
        gate_own = jnp.concatenate([first_own[3], last_own[2]], 0)
        gate_pair = jnp.concatenate([first_pair[3], last_pair[2]], 0)
        gated_own = jnp.concatenate([first_own[1], last_own[0]], 0)
        gated_pair = jnp.concatenate([first_pair[1], last_pair[0]], 0)
        all_down = jnp.concatenate([w[2 * hidden :] for w in weights], 0)
    else:
        zeros = jnp.zeros((length, width), BF16)

        def step(totals, weight_at):
            weight, position = weight_at
            name = (position * 2 + side)[None]
            down = weight[2 * hidden :]
            own = expert_pass(tokens_own, grad_rel, gates_own, name, [weight], totals[0])
            pair = expert_pass(tokens_pair, grad_pair, gates_pair, name, [weight], totals[1])
            grads = weight_grad(
                0, hidden, (own[2], pair[2]), (own[1], pair[1]), both_tokens, both_grads, BF16
            )
            moe_own = totals[2] + dot(own[1], down, 0, 0)
            moe_pair = totals[3] + dot(pair[1], down, 0, 0)
            return (own[0], pair[0], moe_own, moe_pair), (own[3][0], pair[3][0], grads)

        (sum_own, sum_pair, moe_own, moe_pair), (gate_own, gate_pair, weight_grads) = lax.scan(
            step,
            (zeros, zeros, zeros.astype(F32), zeros.astype(F32)),
            (weights, jnp.arange(line, dtype=jnp.int32)),
        )
        kept_own, sent_own, kept_pair, sent_pair = sum_own[:half], sum_own[half:], sum_pair[:half], sum_pair[half:]

    slot_of = jnp.asarray(
        [
            [q if not short else 0 if q == p else 1 + order[p].index(q - p) for q in range(line)]
            for p in range(line)
        ],
        jnp.int32,
    )[place]
    numbers = jnp.arange(experts, dtype=jnp.int32)
    slot_at = slot_of[numbers // 2] + jnp.where(numbers % 2 == side, 0, line)
    slot_names_hot = (slot_at[:, None] == numbers[None, :]).astype(F32)
    gate_sums = jnp.concatenate([gate_own, gate_pair], 0)
    grad_after_low, grad_after, grad_router, grad_second = tokens_back(
        tensors,
        experts,
        kept_pair,
        sent_pair,
        kept_own,
        sent_own,
        gate_sums[:, :half],
        gate_sums[:, half:],
        slot_names_hot,
        router_probs[:, :rows],
        named[:, :rows],
        router_rows,
        after,
        second_gain[None],
        own_quarter(cotangent),
    )

    if short:
        moe_own = dot(gated_own, all_down, 0, 0).astype(BF16)
        moe_pair = dot(gated_pair, all_down, 0, 0).astype(BF16)
    moe = jnp.stack([moe_own, moe_pair])
    got = links.over_tensor(moe[:, half:].astype(BF16), 1).astype(F32)
    crossing = (moe[:, rows:half].astype(F32) + got[:, rows:]).astype(BF16)
    moe = moe[:, :rows].astype(F32) + got[:, :rows] + links.over_tensor(crossing, 2).astype(F32)
    moe = moe[0] + links.over_pair(moe[1].astype(BF16)).astype(F32)
    layer_out = links.absolute(links.gather((after + moe).astype(BF16)))

    def sum_rows(values):
        return lax.psum(values, "expert")

    def flow(step):
        got = None
        for reach in range(line - 1, 0, -1):
            takers = {}
            for p in range(line):
                if 0 <= p + step * reach < line:
                    takers.setdefault(1 + order[p].index(step * reach), []).append(p)
            total = pick(place, [(weight_grads[s], ps) for s, ps in takers.items()])
            if got is not None:
                total = total.astype(F32) + got.astype(F32)
            got = links.along(total.astype(BF16), step, reach)
        return got.astype(F32)

    if short:
        weight_grads = {}
        for slot in range(line - 1, -1, -1):
            if slot == last:
                columns, own, pair = 0, last_own, last_pair
            else:
                columns, own, pair = slot, first_own[1:], first_pair[1:]
            weight_grads[slot] = weight_grad(
                columns,
                hidden,
                (own[1], pair[1]),
                (own[0], pair[0]),
                both_tokens,
                both_grads,
                F32 if slot == 0 else BF16,
            )
        expert_grads = weight_grads[0]
        if line > 1:
            expert_grads = expert_grads + flow(1) + flow(-1)
    else:
        expert_grads = lax.psum_scatter(
            weight_grads, "expert", scatter_dimension=0, axis_index_groups=sides
        ).astype(F32)

    grad_output = dot(context_rel, grad_after_low, 0, 0).astype(BF16)
    grad_output = sum_rows(grad_output).astype(F32)
    grad_context = links.absolute(dot(grad_after_low, w_output, 1, 1).astype(BF16))
    grad_heads = grad_context.reshape(length, heads, HD)
    query_grads = []
    key_grad = jnp.zeros((length, HD), F32)
    value_grad = jnp.zeros((length, HD), F32)
    for head in range(heads):
        dprob = dot(grad_heads[:, head], value_low, 1, 1)
        delta = jnp.sum(probs[head] * dprob, axis=-1, keepdims=True)
        dscore = (probs[head] * (dprob - delta)).astype(BF16)
        query_grads.append(dot(dscore, key_rot, 1, 0) * scale)
        key_grad = key_grad + dot(dscore, query_rot[:, head], 0, 0) * scale
        value_grad = value_grad + dot(probs[head].astype(BF16), grad_heads[:, head], 0, 0)
    query_grad = jnp.concatenate(
        [unrotate(g, cos_table, sin_table).astype(BF16) for g in query_grads], 1
    )
    key_grad = unrotate(key_grad, cos_table, sin_table).astype(BF16)
    value_grad = value_grad.astype(BF16)
    attn_weights = jnp.concatenate([w_query, key_weight, value_weight], 1)
    attn_grads = jnp.concatenate([query_grad, key_grad, value_grad], 1)
    grads_rel = links.relative(attn_grads)
    early = jnp.zeros((-(-(experts + 2) // 8) * 8, width), F32)
    early = early.at[:experts].set(grad_router).at[experts : experts + 1].set(grad_second)
    grad_inputs, sums = inputs_back(
        tensors, experts, grads_rel, attn_weights, stream, first_gain[None], grad_after, early
    )
    grad_inputs = links.absolute(grad_inputs)
    grad_router, grad_second, grad_first = sums[:experts].T, sums[experts], sums[experts + 1]
    query_width = heads * HD
    attn_weight_grads = dot(attn_grads, attn_in, 0, 0)
    lead = links.tensor % 2
    kv_kept = lax.dynamic_slice_in_dim(attn_weight_grads, query_width + lead * HD, HD, 0)
    kv_sent = lax.dynamic_slice_in_dim(attn_weight_grads, query_width + (1 - lead) * HD, HD, 0)
    kv_kept = kv_kept + links.over_tensor(kv_sent.astype(BF16), 1).astype(F32)
    summed = sum_rows(
        jnp.concatenate([attn_weight_grads[:query_width].astype(BF16), kv_kept.astype(BF16)], 0)
    )
    grad_query = summed[:query_width].T.astype(F32)
    kv_mine = summed[query_width:]
    kv_theirs = links.over_tensor(kv_mine, 2)
    first_head = kv_head == 0
    kv_both = jnp.concatenate(
        [jnp.where(first_head, kv_mine, kv_theirs), jnp.where(first_head, kv_theirs, kv_mine)], 0
    )
    kv_other = links.over_tensor(kv_both, 1)
    grad_key = jnp.where(lead == 0, kv_both, kv_other).T.astype(F32)
    grad_value = jnp.where(lead == 0, kv_other, kv_both).T.astype(F32)

    return (
        layer_out,
        grad_inputs,
        grad_first,
        grad_second,
        grad_query,
        grad_key,
        grad_value,
        grad_output,
        grad_router,
        expert_grads[:hidden].T[None],
        expert_grads[hidden : 2 * hidden].T[None],
        expert_grads[2 * hidden :][None],
    )


def solution(mesh):
    experts, tensors = mesh.shape["expert"], mesh.shape["tensor"]
    in_specs = (
        P("expert", None),
        P("expert", None),
        P("expert", None),
        P(),
        P(),
        P(None, "tensor"),
        P(),
        P(),
        P("tensor", None),
        P(),
        P("expert", None, "tensor"),
        P("expert", None, "tensor"),
        P("expert", "tensor", None),
    )
    out_specs = (
        P("expert", None),
        P("expert", None),
        P(),
        P(),
        P(None, "tensor"),
        P(),
        P(),
        P("tensor", None),
        P(),
        P("expert", None, "tensor"),
        P("expert", None, "tensor"),
        P("expert", "tensor", None),
    )

    def run(*arrays):
        return shards(experts, tensors, *arrays)

    return jax.shard_map(run, mesh=mesh, in_specs=in_specs, out_specs=out_specs, check_vma=False)
```

```python
import functools

import jax
import jax.numpy as jnp
import numpy as np
from jax import lax
from jax.experimental import pallas as pl
from jax.experimental.pallas import tpu as pltpu
from jax.sharding import PartitionSpec as P

HEADS = 12
KV = 2
HD = 128
EPSILON = 1e-06
ROPE_BASE = 10000.0
NEGATIVE = -1e30
F32 = jnp.float32
BF16 = jnp.bfloat16


def dot(left, right, left_dim, right_dim):
    return lax.dot_general(
        left, right, (((left_dim,), (right_dim,)), ((), ())), preferred_element_type=F32
    )


def rms_norm(values, gain):
    inverse = lax.rsqrt(jnp.mean(values * values, axis=-1, keepdims=True) + EPSILON)
    normed = values * inverse
    return normed * gain, normed, inverse


def norm_backward(upstream, normed, inverse, gain):
    scaled = upstream * gain
    through = inverse * (scaled - normed * jnp.mean(scaled * normed, axis=-1, keepdims=True))
    return through, jnp.sum(upstream * normed, axis=0)


def rotary_tables(length):
    frequency = np.float32(ROPE_BASE) ** (-np.arange(HD // 2, dtype=np.float32) * np.float32(2.0 / HD))
    angles = np.arange(length, dtype=np.float32)[:, None] * frequency.astype(np.float32)[None]
    cos, sin = np.cos(angles), np.sin(angles)
    return np.concatenate([cos, cos], 1), np.concatenate([-sin, sin], 1)


def turned(values, cos, sin, back=False):
    other = pltpu.roll(values, HD // 2, 1) * sin
    return values * cos - other if back else values * cos + other


class Links:
    def __init__(self, experts, tensors):
        self.experts, self.tensors = experts, tensors
        self.line = experts // 2
        self.tensor = lax.axis_index("tensor")
        expert = lax.axis_index("expert")
        self.place, self.side = expert // 2, expert % 2

    def over_tensor(self, values, bit):
        return lax.ppermute(values, "tensor", [(i, i ^ bit) for i in range(self.tensors)])

    def over_expert(self, values, bit):
        return lax.ppermute(values, "expert", [(i, i ^ bit) for i in range(self.experts)])

    def over_pair(self, values):
        return self.over_expert(values, 1)

    def relative(self, values):
        rows = values.shape[0] // 4
        return jnp.concatenate(
            [
                lax.dynamic_slice_in_dim(values, (self.tensor ^ r) * rows, rows, 0)
                for r in (0, 2, 1, 3)
            ],
            0,
        )

    def absolute(self, values):
        rows = values.shape[0] // 4
        place = jnp.asarray([0, 2, 1, 3], jnp.int32)
        return jnp.concatenate(
            [
                lax.dynamic_slice_in_dim(values, place[self.tensor ^ q] * rows, rows, 0)
                for q in range(4)
            ],
            0,
        )

    def gather(self, quarter):
        both = jnp.concatenate([quarter, self.over_tensor(quarter, 2)], 0)
        return jnp.concatenate([both, self.over_tensor(both, 1)], 0)


def nearest_first(line):
    tables = []
    for place in range(line):
        offsets = [p - place for p in range(line) if p != place]
        tables.append(sorted(offsets, key=lambda o: (abs(o), -o)))
    return tables


def expert_kernel(count, hidden, split, prior, *refs):
    names, tokens, grads, gates = refs[:4]
    weights, refs = refs[4 : 4 + count], refs[4 + count :]
    if prior:
        before, refs = refs[0], refs[1:]
    outs, (gated_out, grad_pre_out, rows_out) = refs[: 2 if split else 1], refs[2 if split else 1 :]
    tile, grad_tile = tokens[...], grads[...]
    total = before[...].astype(F32) if prior else None
    for slot in range(count):
        weight = weights[slot]
        pre = dot(weight[: 2 * hidden, :], tile, 1, 1)
        back = dot(weight[2 * hidden :, :], grad_tile, 1, 1)
        gate = gates[pl.ds(names[slot], 1), :]
        gate_pre, up_pre = pre[:hidden], pre[hidden:]
        sigmoid = jax.nn.sigmoid(gate_pre)
        activated = gate_pre * sigmoid
        hid = (activated * up_pre).astype(BF16).astype(F32)
        rows_out[slot : slot + 1, :] = jnp.sum(hid * back, axis=0, keepdims=True)
        gated_out[slot * hidden : (slot + 1) * hidden, :] = (hid * gate).astype(BF16)
        grad_hidden = back * gate
        grad_pre = jnp.concatenate(
            [
                (grad_hidden * up_pre * (sigmoid * (1.0 + gate_pre * (1.0 - sigmoid)))).astype(BF16),
                (grad_hidden * activated).astype(BF16),
            ],
            0,
        )
        grad_pre_out[2 * slot * hidden : 2 * (slot + 1) * hidden, :] = grad_pre
        part = dot(grad_pre, weight[: 2 * hidden, :], 0, 0)
        total = part if total is None else total + part
    if split:
        for step in range(2):

            @pl.when(pl.program_id(0) == step)
            def _(step=step):
                outs[step][...] = total.astype(BF16)
    else:
        outs[0][...] = total.astype(BF16)


def expert_pass(tokens, grads, gates, names, weights, before=None, split=False):
    count, length, width = len(weights), tokens.shape[0], tokens.shape[1]
    hidden = weights[0].shape[0] // 3
    tile = length // 2
    token_spec = pl.BlockSpec((tile, width), lambda i, *_: (i, 0))
    half_spec = pl.BlockSpec((tile, width), lambda i, *_: (0, 0))

    def column_spec(rows):
        return pl.BlockSpec((rows, tile), lambda i, *_: (0, i))

    weight_spec = pl.BlockSpec((3 * hidden, width), lambda i, *_: (0, 0))
    token_shape = jax.ShapeDtypeStruct((length, width), BF16)
    half_shape = jax.ShapeDtypeStruct((tile, width), BF16)
    columns = [(count * hidden, BF16), (2 * count * hidden, BF16), (count, F32)]
    return pl.pallas_call(
        functools.partial(expert_kernel, count, hidden, split, before is not None),
        grid_spec=pltpu.PrefetchScalarGridSpec(
            num_scalar_prefetch=1,
            grid=(2,),
            in_specs=[token_spec, token_spec, column_spec(gates.shape[0])]
            + [weight_spec] * count
            + [token_spec] * (before is not None),
            out_specs=([half_spec] * 2 if split else [token_spec]) + [column_spec(r) for r, _ in columns],
        ),
        out_shape=([half_shape] * 2 if split else [token_shape])
        + [jax.ShapeDtypeStruct((r, length), t) for r, t in columns],
        compiler_params=pltpu.CompilerParams(vmem_limit_bytes=48 * 2**20),
        cost_estimate=pl.CostEstimate(
            flops=2 * count * length * width * hidden * 5,
            bytes_accessed=(4 * length + 3 * hidden * count) * width * 2,
            transcendentals=0,
        ),
    )(names, tokens, grads, gates, *weights, *([before] if before is not None else []))


def weight_grad_kernel(grad_pre_own, grad_pre_pair, gated_own, gated_pair, own, pair, grad_own, grad_pair, out):
    rows = grad_pre_own.shape[0]
    out[:rows, :] = (
        dot(grad_pre_own[...], own[...], 1, 0) + dot(grad_pre_pair[...], pair[...], 1, 0)
    ).astype(out.dtype)
    out[rows:, :] = (
        dot(gated_own[...], grad_own[...], 1, 0) + dot(gated_pair[...], grad_pair[...], 1, 0)
    ).astype(out.dtype)


def weight_grad(slot, hidden, grad_pre, gated, tokens, grads, kept_as):
    length, width = tokens[0].shape
    tile = width // 3
    pre_spec = pl.BlockSpec((2 * hidden, length), lambda i: (slot, 0))
    gated_spec = pl.BlockSpec((hidden, length), lambda i: (slot, 0))
    token_spec = pl.BlockSpec((length, tile), lambda i: (0, i))
    return pl.pallas_call(
        weight_grad_kernel,
        grid=(3,),
        in_specs=[pre_spec] * 2 + [gated_spec] * 2 + [token_spec] * 4,
        out_specs=pl.BlockSpec((3 * hidden, tile), lambda i: (0, i)),
        out_shape=jax.ShapeDtypeStruct((3 * hidden, width), kept_as),
        compiler_params=pltpu.CompilerParams(vmem_limit_bytes=32 * 2**20),
        cost_estimate=pl.CostEstimate(
            flops=2 * 2 * length * width * hidden * 3,
            bytes_accessed=(4 * length + 6 * hidden) * width * 2,
            transcendentals=0,
        ),
    )(*grad_pre, *gated, *tokens, *grads)


MESH = pl.DeviceIdType.MESH


class Copies:
    def __init__(self, tensors, send, recv):
        self.send, self.recv, self.started = send, recv, []
        expert, tensor = lax.axis_index("expert"), lax.axis_index("tensor")
        self.core = (expert, tensor + 1 - 2 * (tensor % 2))
        self.far = (expert, (tensor + tensors // 2) % tensors)
        self.mate = (expert + 1 - 2 * (expert % 2), tensor)

    def across(self, bit):
        expert, tensor = lax.axis_index("expert"), lax.axis_index("tensor")
        return (expert + bit - 2 * bit * (expert // bit % 2), tensor)

    def greet(self, partners, line=0):
        barrier = pltpu.get_barrier_semaphore()
        for partner in partners:
            pl.semaphore_signal(barrier, inc=1, device_id=partner, device_id_type=MESH)
        count = len(partners)
        if line:
            expert, tensor = lax.axis_index("expert"), lax.axis_index("tensor")
            position = expert // 2
            for step, there in ((2, position < line - 1), (-2, position > 0)):

                @pl.when(there)
                def _(step=step):
                    device = (expert + step, tensor)
                    pl.semaphore_signal(barrier, inc=1, device_id=device, device_id_type=MESH)

            count = count + 1 - (position + 1) // line + (position + line - 1) // line
        pl.semaphore_wait(barrier, count)

    def start(self, source, target, device):
        place = len(self.started)
        copy = pltpu.make_async_remote_copy(
            src_ref=source,
            dst_ref=target,
            send_sem=self.send.at[place],
            recv_sem=self.recv.at[place],
            device_id=device,
            device_id_type=MESH,
        )
        copy.start()
        self.started.append(copy)
        return copy

    def along(self, source, target, step, sends, receives):
        device = (lax.axis_index("expert") + 2 * step, lax.axis_index("tensor"))
        return self.over_when(source, target, device, sends, receives)

    def over_when(self, source, target, device, sends, receives=None):
        place = len(self.started)
        copy = pltpu.make_async_remote_copy(
            src_ref=source,
            dst_ref=target,
            send_sem=self.send.at[place],
            recv_sem=self.recv.at[place],
            device_id=device,
            device_id_type=MESH,
        )
        pl.when(sends)(lambda: copy.start())
        self.started.append(When(copy, sends, sends if receives is None else receives))
        return self.started[-1]

    def finish(self):
        for copy in self.started:
            copy.wait_send()


class When:
    def __init__(self, copy, sends, receives):
        self.copy, self.sends, self.receives = copy, sends, receives

    def wait_send(self):
        pl.when(self.sends)(lambda: self.copy.wait_send())

    def wait_recv(self):
        pl.when(self.receives)(lambda: self.copy.wait_recv())


def sum_quarter(copies, part, sent, got, crossing, crossed, beside=None):
    rows = crossing.shape[0]
    sent[rows:, :] = part(3).astype(BF16)
    last = copies.start(sent.at[pl.ds(rows, rows)], got.at[pl.ds(rows, rows)], copies.core)
    sent[:rows, :] = part(2).astype(BF16)
    first = copies.start(sent.at[pl.ds(0, rows)], got.at[pl.ds(0, rows)], copies.core)
    other = part(1)
    last.wait_recv()
    crossing[...] = (other + got[rows:, :].astype(F32)).astype(BF16)
    far = copies.start(crossing, crossed, copies.far)
    if beside is not None:
        beside()
    mine = part(0)
    first.wait_recv()
    mine = mine + got[:rows, :].astype(F32)
    far.wait_recv()
    return mine + crossed[...].astype(F32)


def gather_quarters(copies, whole, rows, fill=None):
    far = copies.start(whole.at[pl.ds(0, rows)], whole.at[pl.ds(rows, rows)], copies.far)
    first = copies.start(whole.at[pl.ds(0, rows)], whole.at[pl.ds(2 * rows, rows)], copies.core)
    if fill is not None:
        fill()
    far.wait_recv()
    last = copies.start(whole.at[pl.ds(rows, rows)], whole.at[pl.ds(3 * rows, rows)], copies.core)
    first.wait_recv()
    last.wait_recv()


def quarter_at(place):
    tensor = lax.axis_index("tensor")
    return (tensor % 2 + place // 2) % 2 + 2 * ((tensor // 2 + place % 2) % 2)


def place_of(quarter):
    tensor = lax.axis_index("tensor")
    return 2 * ((tensor % 2 + quarter % 2) % 2) + (tensor // 2 + quarter // 2) % 2


def masked_scores(query, keys, start, scale):
    scores = dot(query, keys, 1, 1) * scale
    rows = lax.broadcasted_iota(jnp.int32, scores.shape, 0) + start
    cols = lax.broadcasted_iota(jnp.int32, scores.shape, 1)
    return jnp.where(cols <= rows, scores, NEGATIVE)


def attend_kernel(tensors, line, heads, *refs):
    refs = list(refs)
    stream, gain, weight, cos, sin, grad, routes = [refs.pop(0) for _ in range(7)]
    own_weights = refs.pop(0) if line else None
    attn_in, query, key, value, context, logsum = [refs.pop(0) for _ in range(6)]
    grad_rel, grad_pair, routes_pair = [refs.pop(0) for _ in range(3)]
    arrived = refs.pop(0) if line else None
    send, recv = refs
    copies = Copies(tensors, send, recv)
    expert = lax.axis_index("expert")
    position = expert // 2
    copies.greet([copies.core, copies.mate], line)
    length = stream.shape[0]
    rows = length // 4
    if line:
        up = copies.along(
            own_weights, arrived.at[1 - (position + 2) // line], 1, position < line - 1, position > 0
        )
        down = copies.along(own_weights, arrived.at[0], -1, position > 0, position < line - 1)
    mates = []
    for place in range(4):
        at = pl.ds(place * rows, rows)
        grad_rel[at, :] = grad[pl.ds(pl.multiple_of(quarter_at(place) * rows, rows), rows), :]
        if place < 2:
            mates.append(copies.start(grad_rel.at[at], grad_pair.at[at], copies.mate))
    routes_copy = copies.start(routes, routes_pair, copies.mate)
    for tile in range(4):
        at = slice(tile * rows, (tile + 1) * rows)
        normed = rms_norm(stream[at, :].astype(F32), gain[...])[0].astype(BF16)
        attn_in[at, :] = normed
        proj = dot(normed, weight[...], 1, 0)
        for head in range(heads + 1):
            part = proj[:, head * HD : (head + 1) * HD]
            part = turned(part, cos[at, :], sin[at, :]).astype(BF16)
            if head < heads:
                query[at, head * HD : (head + 1) * HD] = part
            else:
                key[at, :] = part
        value[at, :] = proj[:, (heads + 1) * HD :].astype(BF16)
    for tile in range(4):
        at, seen = slice(tile * rows, (tile + 1) * rows), (tile + 1) * rows
        to = pl.ds(pl.multiple_of(place_of(tile) * rows, rows), rows)
        for head in range(heads):
            columns = slice(head * HD, (head + 1) * HD)
            scores = masked_scores(query[at, columns], key[:seen, :], tile * rows, HD**-0.5)
            peak = jnp.max(scores, axis=-1, keepdims=True)
            exponent = jnp.exp(scores - peak)
            total = jnp.sum(exponent, axis=-1, keepdims=True)
            prob = (exponent / total).astype(BF16)
            context[to, columns] = dot(prob, value[:seen, :], 1, 0).astype(BF16)
            logsum[at, head : head + 1] = peak + jnp.log(total)
    cores = []
    for place in range(2):
        mates[place].wait_recv()
        source = grad_pair.at[pl.ds(place * rows, rows)]
        cores.append(copies.start(source, grad_pair.at[pl.ds((2 + place) * rows, rows)], copies.core))
    routes_copy.wait_recv()
    for copy in cores + ([up, down] if line else []):
        copy.wait_recv()
    copies.finish()


def anywhere():
    return pl.BlockSpec(memory_space=pl.ANY)


def attend(tensors, line, stream, gain, weight, cos, sin, grad, routes, own_weights):
    length, width = stream.shape
    heads = weight.shape[1] // HD - 2
    shape = jax.ShapeDtypeStruct
    return pl.pallas_call(
        functools.partial(attend_kernel, tensors, line, heads),
        out_shape=[
            shape((length, width), BF16),
            shape((length, heads * HD), BF16),
            shape((length, HD), BF16),
            shape((length, HD), BF16),
            shape((length, heads * HD), BF16),
            shape((length, HD), F32),
            shape((length, width), BF16),
            shape((length, width), BF16),
            shape(routes.shape, routes.dtype),
        ]
        + ([shape((2,) + own_weights.shape, BF16)] if line else []),
        in_specs=[vmem()] * 7 + [anywhere()] * bool(line),
        out_specs=[vmem()] * 9 + [anywhere()] * bool(line),
        scratch_shapes=[
            pltpu.SemaphoreType.DMA((8,)),
            pltpu.SemaphoreType.DMA((8,)),
        ],
        compiler_params=pltpu.CompilerParams(
            collective_id=4, has_side_effects=True, vmem_limit_bytes=48 * 2**20
        ),
        cost_estimate=pl.CostEstimate(flops=4 * 10**10, bytes_accessed=10**7, transcendentals=0),
    )(stream, gain, weight, cos, sin, grad, routes, *([own_weights] if line else []))


def attend_back(heads, grad, weight, query, key, value, logsum, cos, sin, grads, grads_rel, key_grad, value_grad):
    length = query.shape[0]
    rows = length // 4
    scale = HD**-0.5
    for tile in range(3, -1, -1):
        at, seen = slice(tile * rows, (tile + 1) * rows), (tile + 1) * rows
        to = pl.ds(pl.multiple_of(place_of(tile) * rows, rows), rows)
        grad_context = dot(grad[to, :], weight[...], 1, 1).astype(BF16)
        for head in range(heads):
            columns = slice(head * HD, (head + 1) * HD)
            head_query = query[at, columns]
            scores = masked_scores(head_query, key[:seen, :], tile * rows, scale)
            prob = jnp.exp(scores - logsum[at, head : head + 1])
            head_grad = grad_context[:, columns]
            dprob = dot(head_grad, value[:seen, :], 1, 1)
            delta = jnp.sum(prob * dprob, axis=-1, keepdims=True)
            dscore = (prob * (dprob - delta)).astype(BF16)
            dquery = dot(dscore, key[:seen, :], 1, 0) * scale
            dquery = turned(dquery, cos[at, :], sin[at, :], True).astype(BF16)
            grads[at, columns] = dquery
            grads_rel[to, columns] = dquery
            dkey = dot(dscore, head_query, 0, 0)
            dvalue = dot(prob.astype(BF16), head_grad, 0, 0)
            if tile == 3 and head == 0:
                key_grad[...] = dkey
                value_grad[...] = dvalue
            else:
                key_grad[:seen, :] += dkey
                value_grad[:seen, :] += dvalue
    for tile in range(4):
        at = slice(tile * rows, (tile + 1) * rows)
        to = pl.ds(pl.multiple_of(place_of(tile) * rows, rows), rows)
        dkey = turned(key_grad[at, :] * scale, cos[at, :], sin[at, :], True).astype(BF16)
        both = jnp.concatenate([dkey, value_grad[at, :].astype(BF16)], 1)
        grads[at, heads * HD :] = both
        grads_rel[to, heads * HD :] = both


def attend_out_kernel(tensors, line, *refs):
    refs = list(refs)
    context, weight, stream, gain = [refs.pop(0) for _ in range(4)]
    arrived = refs.pop(0) if line else None
    own, pair, after = [refs.pop(0) for _ in range(3)]
    second = refs.pop(0) if line else None
    sent, got, crossing, crossed, send, recv = refs
    copies = Copies(tensors, send, recv)
    position = lax.axis_index("expert") // 2
    copies.greet([copies.core, copies.far, copies.mate], line)
    if line:
        inner = (position > 0) & (position < line - 1)
        up = copies.along(arrived.at[1], second, 1, inner, position >= line // 2)
        down = copies.along(arrived.at[0], second, -1, inner, position < line // 2)
    rows = stream.shape[0]

    def part(place):
        return dot(context[place * rows : (place + 1) * rows, :], weight[...], 1, 0)

    total = stream[...].astype(F32) + sum_quarter(copies, part, sent, got, crossing, crossed)
    after[...] = total
    own[:rows, :] = rms_norm(total, gain[...])[0].astype(BF16)
    mate = copies.start(own.at[pl.ds(0, rows)], pair.at[pl.ds(0, rows)], copies.mate)
    gather_quarters(copies, own, rows)
    mate.wait_recv()
    gather_quarters(copies, pair, rows)
    if line:
        up.wait_recv()
        down.wait_recv()
    copies.finish()


def vmem():
    return pl.BlockSpec(memory_space=pltpu.VMEM)


def attend_out(tensors, line, context, weight, stream, gain, arrived):
    rows, width = stream.shape
    return pl.pallas_call(
        functools.partial(attend_out_kernel, tensors, line),
        out_shape=[
            jax.ShapeDtypeStruct((4 * rows, width), BF16),
            jax.ShapeDtypeStruct((4 * rows, width), BF16),
            jax.ShapeDtypeStruct((rows, width), F32),
        ]
        + ([jax.ShapeDtypeStruct(arrived.shape[1:], BF16)] if line else []),
        in_specs=[vmem()] * 4 + [anywhere()] * bool(line),
        out_specs=[vmem()] * 3 + [anywhere()] * bool(line),
        scratch_shapes=[
            pltpu.VMEM((2 * rows, width), BF16),
            pltpu.VMEM((2 * rows, width), BF16),
            pltpu.VMEM((rows, width), BF16),
            pltpu.VMEM((rows, width), BF16),
            pltpu.SemaphoreType.DMA((12,)),
            pltpu.SemaphoreType.DMA((12,)),
        ],
        compiler_params=pltpu.CompilerParams(
            collective_id=1, has_side_effects=True, vmem_limit_bytes=40 * 2**20
        ),
        cost_estimate=pl.CostEstimate(flops=6 * 10**10, bytes_accessed=10**7, transcendentals=0),
    )(context, weight, stream, gain, *([arrived] if line else []))


def tokens_back_kernel(tensors, line, hidden, heads, *refs):
    refs = list(refs)
    kept_pair, kept_own, rows_kept, rows_sent = [refs.pop(0) for _ in range(4)]
    names, probs, named, router, after, gain, grad = [refs.pop(0) for _ in range(7)]
    attention = [refs.pop(0) for _ in range(7)]
    sent_pair, sent_own, moe_own, moe_pair = [refs.pop(0) for _ in range(4)]
    factors = [refs.pop(0) for _ in range(12 if line else 0)]
    whole, grad_after, grad_router, grad_second = [refs.pop(0) for _ in range(4)]
    attention += [refs.pop(0) for _ in range(2)]
    moe_out, mate_moe = refs.pop(0), refs.pop(0)
    moe_got = refs.pop(0)
    weight_grads = [refs.pop(0) for _ in range(line)]
    going, turning = (refs.pop(0), refs.pop(0)) if line else (None, None)
    attention += [refs.pop(0) for _ in range(2)]
    moe_crossing, moe_crossed, block, local = [refs.pop(0) for _ in range(4)]
    if line:
        first_in, first_out, up_in, down_in = [refs.pop(0) for _ in range(4)]
    got_pair, got_own, crossing_pair, crossed_pair, crossing_own, crossed_own = [refs.pop(0) for _ in range(6)]
    mate_out, mate_in, rows_got, rows_crossing, rows_crossed, rows_mine, rows_mate, send, recv = refs
    copies = Copies(tensors, send, recv)
    position = lax.axis_index("expert") // 2
    copies.greet([copies.core, copies.far, copies.mate], line)
    rows = grad.shape[0]

    def weight_grad(slot):
        if not line:
            return
        last = slot == line - 1
        column = 0 if last else slot
        pre_own, pre_pair, gated_own, gated_pair = factors[4:8] if last else factors[:4]
        length, width = factors[8].shape
        tile = width // 6
        pre_spec = pl.BlockSpec((2 * hidden, length), lambda i: (column, 0))
        gated_spec = pl.BlockSpec((hidden, length), lambda i: (column, 0))
        token_spec = pl.BlockSpec((length, tile), lambda i: (0, i))
        pltpu.emit_pipeline(
            weight_grad_kernel,
            grid=(6,),
            in_specs=[pre_spec] * 2 + [gated_spec] * 2 + [token_spec] * 4,
            out_specs=[pl.BlockSpec((3 * hidden, tile), lambda i: (0, i))],
        )(pre_own, pre_pair, gated_own, gated_pair, *factors[8:], weight_grads[slot])

    low, high = pl.ds(0, rows), pl.ds(rows, rows)
    pair_last = copies.start(sent_pair.at[high], got_pair.at[high], copies.core)
    pair_first = copies.start(sent_pair.at[low], got_pair.at[low], copies.core)
    rows_core = copies.start(rows_sent, rows_got, copies.core)
    own_last = copies.start(sent_own.at[high], got_own.at[high], copies.core)
    own_first = copies.start(sent_own.at[low], got_own.at[low], copies.core)
    moe_core = [
        copies.start(source.at[pl.ds(2 * rows, 2 * rows)], moe_got.at[side], copies.core)
        for side, source in enumerate((moe_own, moe_pair))
    ]
    if line:
        weight_grad(line - 1)
        up = copies.along(weight_grads[-1], first_in, 1, position == 0, position == 1)
        down = copies.along(weight_grads[-1], first_in, -1, position == line - 1, position == line - 2)
        inner = (position > 0) & (position < line - 1)
    pair_last.wait_recv()
    crossing_pair[...] = (kept_pair[rows:, :].astype(F32) + got_pair[rows:, :].astype(F32)).astype(BF16)
    pair_far = copies.start(crossing_pair, crossed_pair, copies.far)
    rows_core.wait_recv()
    rows_crossing[...] = rows_kept[:, rows:] + rows_got[:, rows:]
    rows_far = copies.start(rows_crossing, rows_crossed, copies.far)
    pair_first.wait_recv()
    mine_pair = kept_pair[:rows, :].astype(F32) + got_pair[:rows, :].astype(F32)
    own_last.wait_recv()
    crossing_own[...] = (kept_own[rows:, :].astype(F32) + got_own[rows:, :].astype(F32)).astype(BF16)
    own_first.wait_recv()
    grad_tokens = kept_own[:rows, :].astype(F32) + got_own[:rows, :].astype(F32)
    for slot in range(line - 2, 0, -1):
        weight_grad(slot)
    pair_far.wait_recv()
    own_far = copies.start(crossing_own, crossed_own, copies.far)
    mate_out[...] = (mine_pair + crossed_pair[...].astype(F32)).astype(BF16)
    mate = copies.start(mate_out, mate_in, copies.mate)
    rows_far.wait_recv()
    rows_mine[...] = rows_kept[:, :rows] + rows_got[:, :rows] + rows_crossed[...]
    rows_over = copies.start(rows_mine, rows_mate, copies.mate)
    weight_grad(0)
    rows_over.wait_recv()
    count = rows_mine.shape[0] // 2
    slots = jnp.concatenate([rows_mine[:count, :], rows_mate[count:, :]], 0)
    dprobs = jnp.zeros(probs.shape, F32)
    for slot in range(2 * count):
        dprobs = dprobs + names[:, slot : slot + 1] * slots[slot : slot + 1, :]
    dprobs = dprobs * named[...]
    dlogits = (
        probs[...] * (dprobs - jnp.sum(probs[...] * dprobs, axis=0, keepdims=True))
    ).astype(BF16)
    second_out, normed, inverse = rms_norm(after[...], gain[...])
    grad_router[...] = dot(dlogits, second_out.astype(BF16), 1, 0)
    grad_tokens = grad_tokens + dot(dlogits, router[...], 0, 0)
    own_far.wait_recv()
    grad_tokens = grad_tokens + crossed_own[...].astype(F32)
    mate.wait_recv()
    grad_tokens = grad_tokens + mate_in[...].astype(F32)
    through, second = norm_backward(grad_tokens, normed, inverse, gain[...])
    grad_second[...] = second[None]
    total = grad[...].astype(F32) + through
    grad_after[...] = total
    whole[:rows, :] = total.astype(BF16)
    second = []

    def move(source, target, place):
        copy = pltpu.make_async_copy(source, target, local.at[place])
        copy.start()
        copy.wait()

    def moe_part(side, at):
        move((moe_own, moe_pair)[side].at[at], block.at[0], 0)
        move(moe_got.at[side, at], block.at[1], 0)
        return block[0].astype(F32) + block[1].astype(F32)

    def second_round():
        up.wait_recv()
        down.wait_recv()

        @pl.when(inner)
        def _():
            move(weight_grads[line - 1], first_out, 0)
            first_out[...] = (first_out[...].astype(F32) + first_in[...].astype(F32)).astype(BF16)

        @pl.when(jnp.logical_not(inner))
        def _():
            move(weight_grads[line - 2], first_out, 0)

        second.append(copies.along(first_out, up_in, 1, position < line // 2, inner))
        second.append(copies.along(first_out, down_in, -1, position >= line // 2, inner))

    gather_quarters(copies, whole, rows, second_round if line else None)
    moe_far = []
    for side in range(2):
        moe_core[side].wait_recv()
        moe_crossing[side] = moe_part(side, pl.ds(rows, rows)).astype(BF16)
        moe_far.append(copies.start(moe_crossing.at[side], moe_crossed.at[side], copies.far))
    attend_back(heads, whole, *attention)
    for side, target in enumerate((moe_out, mate_moe)):
        moe_far[side].wait_recv()
        total = moe_part(side, pl.ds(0, rows)) + moe_crossed[side].astype(F32)
        target[...] = (after[...] + total).astype(target.dtype) if side == 0 else total.astype(target.dtype)
    if line:
        move(weight_grads[1], going, 0)
        move(weight_grads[2], turning, 0)
        for copy in second:
            copy.wait_recv()

        @pl.when(inner)
        def _():
            going[...] = (going[...].astype(F32) + up_in[...].astype(F32)).astype(BF16)
            turning[...] = (turning[...].astype(F32) + down_in[...].astype(F32)).astype(BF16)

    copies.finish()


def tokens_back(tensors, experts, line, hidden, *operands):
    rows, width = operands[10].shape
    heads = operands[11].shape[0] // HD
    half = pltpu.VMEM((2 * rows, width), BF16)
    quarter = pltpu.VMEM((rows, width), BF16)
    two_quarters = pltpu.VMEM((2, rows, width), BF16)
    small = pltpu.VMEM((experts, rows), F32)
    shape = jax.ShapeDtypeStruct
    shard = shape((3 * hidden, width), BF16)
    outs = [
        shape((4 * rows, width), BF16),
        shape((rows, width), F32),
        shape((experts, width), F32),
        shape((1, width), F32),
        shape((4 * rows, (heads + 2) * HD), BF16),
        shape((4 * rows, (heads + 2) * HD), BF16),
        shape((rows, width), F32),
        shape((rows, width), BF16),
        shape((2, 2 * rows, width), BF16),
    ]
    grads = [shape(shard.shape, F32)] + [shard] * (line - 1) if line else []
    moving = [pltpu.VMEM(shard.shape, BF16)] * 4 if line else []
    return pl.pallas_call(
        functools.partial(tokens_back_kernel, tensors, line, hidden, heads),
        out_shape=outs + grads + [shard] * (2 if line else 0),
        in_specs=[vmem()] * 18 + [anywhere()] * (len(operands) - 18),
        out_specs=[vmem()] * 8 + [anywhere()] * (1 + line) + [vmem()] * (2 if line else 0),
        scratch_shapes=[pltpu.VMEM((4 * rows, HD), F32)] * 2
        + [two_quarters] * 3
        + [pltpu.SemaphoreType.DMA((1,))]
        + moving
        + [half, half]
        + [quarter] * 6
        + [pltpu.VMEM((experts, 2 * rows), F32), small, small, small, small]
        + [pltpu.SemaphoreType.DMA((24,)), pltpu.SemaphoreType.DMA((24,))],
        compiler_params=pltpu.CompilerParams(
            collective_id=2, has_side_effects=True, vmem_limit_bytes=60 * 2**20
        ),
        cost_estimate=pl.CostEstimate(flops=10**11, bytes_accessed=10**7, transcendentals=0),
    )(*operands)


def line_sum(copies, line, partial, whole, got, running, up_in, down_in):
    position, side = lax.axis_index("expert") // 2, lax.axis_index("expert") % 2
    count = partial.shape[0] // 2
    chunk = count // line
    order = [3 * (1 - position // 2), 2 - position // 2, position + 1 - 2 * (position % 2), position]
    over = []

    def rows_at(half, place):
        return pl.ds(pl.multiple_of(half * count + place * chunk, 16), chunk)

    def send_pair():
        for place in order:
            over.append(
                copies.start(partial.at[rows_at(1 - side, place)], got.at[rows_at(0, place)], copies.mate)
            )

    def part(place):
        mine = partial[rows_at(side, place), :].astype(F32)
        return mine + got[rows_at(0, place), :].astype(F32)

    flows = {1: {}, -1: {}}

    def reach_step(reach):
        over[line - 1 - reach].wait_recv()
        for way, (step, landed) in enumerate(((1, up_in), (-1, down_in))):
            target = position + step * reach
            sends = (target >= 0) & (target < line)
            origin = position - step
            receives = (origin >= 0) & (origin < line) & (origin + step * reach >= 0) & (origin + step * reach < line)
            slot = 3 * way + reach - 1
            if reach < line - 1:
                flows[step][reach + 1].wait_recv()

            @pl.when(sends)
            def _(slot=slot, target=target, landed=landed, step=step):
                running[slot] = part(target).astype(BF16)
                if reach < line - 1:

                    @pl.when((position - step >= 0) & (position - step < line))
                    def _():
                        total = part(target) + landed[reach].astype(F32)
                        running[slot] = total.astype(BF16)

            flows[step][reach] = copies.along(running.at[slot], landed.at[reach - 1], step, sends, receives)

    spread = []

    def settle():
        over[line - 1].wait_recv()
        flows[1][1].wait_recv()
        flows[-1][1].wait_recv()
        total = part(position)
        total = total + jnp.where(position > 0, up_in[0].astype(F32), 0.0)
        total = total + jnp.where(position < line - 1, down_in[0].astype(F32), 0.0)
        here = rows_at(side, position)
        whole[here, :] = total.astype(BF16)
        spread.append(copies.start(whole.at[here], whole.at[here], copies.mate))

    mates = []

    def spread_step(hop):
        for step in (1, -1):
            place = position - step * (hop - 1)
            sends = (place >= 0) & (place < line) & (position + step >= 0) & (position + step < line)
            origin = position - step * hop
            receives = (origin >= 0) & (origin < line)
            at = rows_at(side, jnp.clip(place, 0, line - 1))
            spread.append(copies.along(whole.at[at], whole.at[at], step, sends, receives))

    def spread_mate(hop):
        for step, copy in ((1, spread[2 * hop - 1]), (-1, spread[2 * hop])):
            copy.wait_recv()
            origin = position - step * hop
            there = (origin >= 0) & (origin < line)
            at = rows_at(side, jnp.clip(origin, 0, line - 1))
            mates.append(copies.over_when(whole.at[at], whole.at[at], copies.mate, there))

    def end():
        spread[0].wait_recv()
        for copy in mates:
            copy.wait_recv()

    return send_pair, reach_step, settle, spread_step, spread_mate, end


def inputs_back_kernel(tensors, experts, line, *refs):
    refs = list(refs)
    grads_rel, weight, stream, gain, grad_after, early = [refs.pop(0) for _ in range(6)]
    attn_in, grads, context, grad_low, layer_part, mate_out = [refs.pop(0) for _ in range(6)]
    going, turning = (refs.pop(0), refs.pop(0)) if line else (None, None)
    whole, layer, sums, summed, kv_out = [refs.pop(0) for _ in range(5)]
    final = refs.pop(0) if line else None
    partial, kv_sent, kv_got, mate_in = [refs.pop(0) for _ in range(4)]
    buffers = [refs.pop(0) for _ in range(4)] if line else []
    sent, got, crossing, crossed, running, arrived, send, recv = refs
    copies = Copies(tensors, send, recv)
    bits = [1 << k for k in range(experts.bit_length() - 1)]
    position = lax.axis_index("expert") // 2
    copies.greet([copies.core, copies.far] + [copies.across(bit) for bit in bits], line)
    rows = stream.shape[0]
    lines = []
    if line:
        end, inner = position == line - 1, (position > 0) & (position < line - 1)
        lines = [
            copies.along(going, final.at[0], 1, position < line - 1, position > 0),
            copies.along(going, final.at[1], -1, end, position == line - 2),
            copies.along(turning, final.at[1], -1, inner, position < line - 2),
        ]
    mate = copies.start(mate_out, mate_in, copies.mate)

    def part(place):
        return dot(grads_rel[place * rows : (place + 1) * rows, :], weight[...], 1, 1)

    if line:
        send_pair, reach_step, settle, spread_step, spread_mate, finish_sum = line_sum(
            copies, line, partial, summed, *buffers
        )

    def projections():
        lead = lax.axis_index("tensor") % 2
        query_width = context.shape[1]
        kept_at = pl.ds(pl.multiple_of(query_width + lead * HD, HD), HD)
        sent_at = pl.ds(pl.multiple_of(query_width + (1 - lead) * HD, HD), HD)
        kv_sent[...] = dot(grads[:, sent_at], attn_in[...], 0, 0).astype(BF16)
        kv = copies.start(kv_sent, kv_got, copies.core)
        partial[:query_width, :] = dot(grads[:, :query_width], attn_in[...], 0, 0).astype(BF16)
        partial[query_width + HD :, :] = dot(context[...], grad_low[...], 0, 0).astype(BF16)
        kept = dot(grads[:, kept_at], attn_in[...], 0, 0)
        kv.wait_recv()
        partial[query_width : query_width + HD, :] = (kept + kv_got[...].astype(F32)).astype(BF16)
        if line:
            send_pair()

    grad_in = sum_quarter(copies, part, sent, got, crossing, crossed, projections)
    _, normed, inverse = rms_norm(stream[...].astype(F32), gain[...])
    through, first = norm_backward(grad_in, normed, inverse, gain[...])
    whole[:rows, :] = (grad_after[...] + through).astype(BF16)

    def small_sums():
        running[0] = early[...]
        running[0, experts + 1 : experts + 2, :] = first[None]
        steps = [copies.core] + [copies.across(bit) for bit in bits] + [copies.far]
        for step, device in enumerate(steps):
            copy = copies.start(running.at[step], arrived.at[step], device)
            copy.wait_recv()
            if step + 1 < len(steps):
                running[step + 1] = running[step] + arrived[step]
            else:
                sums[...] = running[step] + arrived[step]

    def beside_inputs():
        mate.wait_recv()
        layer[:rows, :] = (layer_part[...] + mate_in[...].astype(F32)).astype(BF16)
        if line:
            for reach in range(line - 1, 0, -1):
                reach_step(reach)

    def beside_layer():
        if line:
            settle()
            spread_step(1)
        small_sums()
        if line:
            for hop in range(1, line):
                spread_mate(hop)
                if hop < line - 1:
                    spread_step(hop + 1)
            finish_sum()
            query_width = context.shape[1]
            mine = summed.at[pl.ds(query_width, HD)]
            far = copies.start(mine, kv_out.at[0], copies.far)
            first_kv = copies.start(mine, kv_out.at[1], copies.core)
            far.wait_recv()
            last_kv = copies.start(kv_out.at[0], kv_out.at[2], copies.core)
            first_kv.wait_recv()
            last_kv.wait_recv()

    gather_quarters(copies, whole, rows, beside_inputs)
    gather_quarters(copies, layer, rows, beside_layer)
    if not line:
        summed[...] = partial[...]
        kv_out[...] = jnp.zeros(kv_out.shape, BF16)
    for copy in lines:
        copy.wait_recv()
    copies.finish()


def inputs_back(tensors, experts, line, *operands):
    rows, width = operands[2].shape
    early = operands[5].shape
    steps = 1 + experts.bit_length()
    shape = jax.ShapeDtypeStruct
    query_width = operands[8].shape[1]
    projected = 2 * query_width + HD
    quarter = pltpu.VMEM((rows, width), BF16)
    half = pltpu.VMEM((2 * rows, width), BF16)
    buffers = []
    if line:
        chunk = projected // 2 // line
        buffers = [
            pltpu.VMEM((projected // 2, width), BF16),
            pltpu.VMEM((6, chunk, width), BF16),
            pltpu.VMEM((3, chunk, width), BF16),
            pltpu.VMEM((3, chunk, width), BF16),
        ]
    return pl.pallas_call(
        functools.partial(inputs_back_kernel, tensors, experts, line),
        out_shape=[
            shape((4 * rows, width), BF16),
            shape((4 * rows, width), BF16),
            shape(early, F32),
            shape((projected, width), BF16),
            shape((3, HD, width), BF16),
        ]
        + ([shape((2,) + operands[12].shape, BF16)] if line else []),
        in_specs=[vmem()] * 12 + [anywhere()] * (len(operands) - 12),
        out_specs=[vmem()] * 5 + [anywhere()] * bool(line),
        scratch_shapes=[
            pltpu.VMEM((projected, width), BF16),
            pltpu.VMEM((HD, width), BF16),
            pltpu.VMEM((HD, width), BF16),
            quarter,
        ]
        + buffers
        + [
            half,
            half,
            quarter,
            quarter,
            pltpu.VMEM((steps,) + early, F32),
            pltpu.VMEM((steps,) + early, F32),
            pltpu.SemaphoreType.DMA((50 + steps,)),
            pltpu.SemaphoreType.DMA((50 + steps,)),
        ],
        compiler_params=pltpu.CompilerParams(
            collective_id=3, has_side_effects=True, vmem_limit_bytes=60 * 2**20
        ),
        cost_estimate=pl.CostEstimate(flops=10**11, bytes_accessed=10**7, transcendentals=0),
    )(*operands)


def shards(
    experts,
    tensors,
    inputs,
    routes,
    cotangent,
    first_gain,
    second_gain,
    w_query,
    w_key,
    w_value,
    w_output,
    w_router,
    w_gate,
    w_up,
    w_down,
):
    links = Links(experts, tensors)
    line, place, side = links.line, links.place, links.side
    length, width = inputs.shape
    heads = w_query.shape[1] // HD
    hidden = w_gate.shape[2]
    group = HEADS // KV
    kv_head = links.tensor * heads // group
    scale = HD ** (-0.5)
    order = nearest_first(line)

    own_weights = jnp.concatenate([w_gate[0].T, w_up[0].T, w_down[0]], 0)
    short = line if line == 4 else 0
    if not short:
        sides = [[2 * p + s for p in range(line)] for s in range(2)]
        weights = lax.all_gather(own_weights, "expert", axis_index_groups=sides)

    rows, half = length // 4, length // 2
    cos, sin = rotary_tables(length)
    key_weight = lax.dynamic_slice_in_dim(w_key, kv_head * HD, HD, 1)
    value_weight = lax.dynamic_slice_in_dim(w_value, kv_head * HD, HD, 1)
    attn_weights = jnp.concatenate([w_query, key_weight, value_weight], 1)
    routes_own = links.relative(routes).T
    routes_own = jnp.concatenate([routes_own, routes_own], 0)
    attn_in, query, key, value, context_rel, logsum, grad_rel, grad_pair, routes_pair, *arrived = attend(
        tensors, short, inputs, first_gain[None], attn_weights, cos, sin, cotangent, routes_own, own_weights
    )

    def own_quarter(values):
        return lax.dynamic_slice_in_dim(values, links.tensor * rows, rows, 0)

    stream = own_quarter(inputs)
    tokens_own, tokens_pair, after, *second = attend_out(
        tensors, short, context_rel, w_output, stream, second_gain[None], *(arrived or [None])
    )
    if short:
        arrived, second = arrived[0], second[0]
        inner = jnp.logical_and(place > 0, place < line - 1)
        third = lax.ppermute(second, "expert", [(2 + s, s) for s in range(2)] + [(4 + s, 6 + s) for s in range(2)])
        weights = [
            own_weights,
            arrived[0],
            jnp.where(inner, arrived[1], second),
            jnp.where(inner, second, third),
        ]
    names = jnp.arange(experts, dtype=jnp.int32)[:, None, None]

    def gates_of(tokens, tokens_routes):
        logits = dot(router_rows, tokens, 1, 1)
        logit_exp = jnp.exp(logits - jnp.max(logits, axis=0, keepdims=True))
        probs = logit_exp / jnp.sum(logit_exp, axis=0, keepdims=True)
        named = jnp.any(tokens_routes[None] == names, axis=1).astype(F32)
        return probs, named, probs * named

    router_rows = w_router.T
    router_probs, named, gates_own = gates_of(tokens_own, routes_own[:4])
    _, _, gates_pair = gates_of(tokens_pair, routes_pair[:4])

    both_tokens, both_grads = (tokens_own, tokens_pair), (grad_rel, grad_pair)
    if short:
        offsets = jnp.asarray([[0] + order[p] for p in range(line)], jnp.int32)[place]
        slot_names = (place + offsets) * 2 + side
        last = line - 1
        first_own = expert_pass(tokens_own, grad_rel, gates_own, slot_names[:last], weights[:last])
        first_pair = expert_pass(tokens_pair, grad_pair, gates_pair, slot_names[:last], weights[:last])
        kept_pair, sent_pair, *last_pair = expert_pass(
            tokens_pair, grad_pair, gates_pair, slot_names[last:], weights[last:], first_pair[0], True
        )
        kept_own, sent_own, *last_own = expert_pass(
            tokens_own, grad_rel, gates_own, slot_names[last:], weights[last:], first_own[0], True
        )
        gate_own = jnp.concatenate([first_own[3], last_own[2]], 0)
        gate_pair = jnp.concatenate([first_pair[3], last_pair[2]], 0)
        gated_own = jnp.concatenate([first_own[1], last_own[0]], 0)
        gated_pair = jnp.concatenate([first_pair[1], last_pair[0]], 0)
        all_down = jnp.concatenate([w[2 * hidden :] for w in weights], 0)
    else:
        zeros = jnp.zeros((length, width), BF16)

        def step(totals, weight_at):
            weight, position = weight_at
            name = (position * 2 + side)[None]
            down = weight[2 * hidden :]
            own = expert_pass(tokens_own, grad_rel, gates_own, name, [weight], totals[0])
            pair = expert_pass(tokens_pair, grad_pair, gates_pair, name, [weight], totals[1])
            grads = weight_grad(
                0, hidden, (own[2], pair[2]), (own[1], pair[1]), both_tokens, both_grads, BF16
            )
            moe_own = totals[2] + dot(own[1], down, 0, 0)
            moe_pair = totals[3] + dot(pair[1], down, 0, 0)
            return (own[0], pair[0], moe_own, moe_pair), (own[3][0], pair[3][0], grads)

        (sum_own, sum_pair, moe_own, moe_pair), (gate_own, gate_pair, weight_grads) = lax.scan(
            step,
            (zeros, zeros, zeros.astype(F32), zeros.astype(F32)),
            (weights, jnp.arange(line, dtype=jnp.int32)),
        )
        kept_own, sent_own, kept_pair, sent_pair = sum_own[:half], sum_own[half:], sum_pair[:half], sum_pair[half:]

    slot_of = jnp.asarray(
        [
            [q if not short else 0 if q == p else 1 + order[p].index(q - p) for q in range(line)]
            for p in range(line)
        ],
        jnp.int32,
    )[place]
    numbers = jnp.arange(experts, dtype=jnp.int32)
    slot_at = slot_of[numbers // 2] + jnp.where(numbers % 2 == side, 0, line)
    slot_names_hot = (slot_at[:, None] == numbers[None, :]).astype(F32)
    gate_sums = jnp.concatenate([gate_own, gate_pair], 0)
    factors = []
    if short:
        factors = [first_own[2], first_pair[2], first_own[1], first_pair[1]]
        factors += [last_own[1], last_pair[1], last_own[0], last_pair[0], *both_tokens, *both_grads]
    if short:
        moe_own = dot(gated_own, all_down, 0, 0).astype(BF16)
        moe_pair = dot(gated_pair, all_down, 0, 0).astype(BF16)
    else:
        moe_own, moe_pair = moe_own.astype(BF16), moe_pair.astype(BF16)
    (
        grad_after_low,
        grad_after,
        grad_router,
        grad_second,
        attn_grads,
        grads_rel,
        layer_part,
        mate_moe,
        _,
        *weight_sums,
    ) = tokens_back(
        tensors,
        experts,
        short,
        hidden,
        kept_pair,
        kept_own,
        gate_sums[:, :half],
        gate_sums[:, half:],
        slot_names_hot,
        router_probs[:, :rows],
        named[:, :rows],
        router_rows,
        after,
        second_gain[None],
        own_quarter(cotangent),
        w_output,
        query,
        key,
        value,
        logsum,
        cos,
        sin,
        sent_pair,
        sent_own,
        moe_own,
        moe_pair,
        *factors,
    )

    line_sums = []
    if short:
        own_sum, line_sums = weight_sums[0], weight_sums[-2:]
    else:
        expert_grads = lax.psum_scatter(
            weight_grads, "expert", scatter_dimension=0, axis_index_groups=sides
        ).astype(F32)

    early = jnp.zeros((-(-(experts + 2) // 8) * 8, width), F32)
    early = early.at[:experts].set(grad_router).at[experts : experts + 1].set(grad_second)
    grad_inputs, layer_out, sums, summed, kv_rest, *got = inputs_back(
        tensors,
        experts,
        short,
        grads_rel,
        attn_weights,
        stream,
        first_gain[None],
        grad_after,
        early,
        attn_in,
        attn_grads,
        context_rel,
        grad_after_low,
        layer_part,
        mate_moe,
        *line_sums,
    )
    query_width = heads * HD
    if short:
        got = got[0].astype(F32)
        expert_grads = own_sum + jnp.where(place > 0, got[0], 0.0) + jnp.where(place < line - 1, got[1], 0.0)
        kv_mine, (kv_far, kv_core, kv_across) = summed[query_width : query_width + HD], kv_rest
    else:
        summed = lax.psum(summed, "expert")
        kv_mine = summed[query_width : query_width + HD]
        kv_far = links.over_tensor(kv_mine, 2)
        kv_core, kv_across = links.over_tensor(kv_mine, 1), links.over_tensor(kv_far, 1)
    grad_query = summed[:query_width].T.astype(F32)
    grad_output = summed[query_width + HD :].astype(F32)
    lead, low_head = links.tensor % 2 == 0, kv_head == 0
    keys = jnp.where(lead, kv_mine, kv_core), jnp.where(lead, kv_far, kv_across)
    values = jnp.where(lead, kv_core, kv_mine), jnp.where(lead, kv_across, kv_far)
    grad_key, grad_value = [
        jnp.concatenate([jnp.where(low_head, near, far), jnp.where(low_head, far, near)], 0).T.astype(F32)
        for near, far in (keys, values)
    ]
    grad_inputs, layer_out = links.absolute(grad_inputs), links.absolute(layer_out)
    grad_router, grad_second, grad_first = sums[:experts].T, sums[experts], sums[experts + 1]
    return (
        layer_out,
        grad_inputs,
        grad_first,
        grad_second,
        grad_query,
        grad_key,
        grad_value,
        grad_output,
        grad_router,
        expert_grads[:hidden].T[None],
        expert_grads[hidden : 2 * hidden].T[None],
        expert_grads[2 * hidden :][None],
    )


def solution(mesh):
    experts, tensors = mesh.shape["expert"], mesh.shape["tensor"]
    in_specs = (
        P("expert", None),
        P("expert", None),
        P("expert", None),
        P(),
        P(),
        P(None, "tensor"),
        P(),
        P(),
        P("tensor", None),
        P(),
        P("expert", None, "tensor"),
        P("expert", None, "tensor"),
        P("expert", "tensor", None),
    )
    out_specs = (
        P("expert", None),
        P("expert", None),
        P(),
        P(),
        P(None, "tensor"),
        P(),
        P(),
        P("tensor", None),
        P(),
        P("expert", None, "tensor"),
        P("expert", None, "tensor"),
        P("expert", "tensor", None),
    )

    def run(*arrays):
        return shards(experts, tensors, *arrays)

    return jax.shard_map(run, mesh=mesh, in_specs=in_specs, out_specs=out_specs, check_vma=False)
```

```python
import functools

import jax
import jax.numpy as jnp
import numpy as np
from jax import lax
from jax.experimental import pallas as pl
from jax.experimental.pallas import tpu as pltpu
from jax.sharding import PartitionSpec as P

HEADS = 12
KV = 2
HD = 128
EPSILON = 1e-06
ROPE_BASE = 10000.0
NEGATIVE = -1e30
F32 = jnp.float32
BF16 = jnp.bfloat16


def dot(left, right, left_dim, right_dim):
    return lax.dot_general(
        left, right, (((left_dim,), (right_dim,)), ((), ())), preferred_element_type=F32
    )


def rms_norm(values, gain):
    inverse = lax.rsqrt(jnp.mean(values * values, axis=-1, keepdims=True) + EPSILON)
    normed = values * inverse
    return normed * gain, normed, inverse


def norm_backward(upstream, normed, inverse, gain):
    scaled = upstream * gain
    through = inverse * (scaled - normed * jnp.mean(scaled * normed, axis=-1, keepdims=True))
    return through, jnp.sum(upstream * normed, axis=0)


def rotary_tables(length):
    frequency = np.float32(ROPE_BASE) ** (-np.arange(HD // 2, dtype=np.float32) * np.float32(2.0 / HD))
    angles = np.arange(length, dtype=np.float32)[:, None] * frequency.astype(np.float32)[None]
    cos, sin = np.cos(angles), np.sin(angles)
    return np.concatenate([cos, cos], 1), np.concatenate([-sin, sin], 1)


def turned(values, cos, sin, back=False):
    other = pltpu.roll(values, HD // 2, 1) * sin
    return values * cos - other if back else values * cos + other


class Links:
    def __init__(self, experts, tensors):
        self.experts, self.tensors = experts, tensors
        self.line = experts // 2
        self.tensor = lax.axis_index("tensor")
        expert = lax.axis_index("expert")
        self.place, self.side = expert // 2, expert % 2

    def over_tensor(self, values, bit):
        return lax.ppermute(values, "tensor", [(i, i ^ bit) for i in range(self.tensors)])

    def over_expert(self, values, bit):
        return lax.ppermute(values, "expert", [(i, i ^ bit) for i in range(self.experts)])

    def over_pair(self, values):
        return self.over_expert(values, 1)

    def relative(self, values):
        rows = values.shape[0] // 4
        return jnp.concatenate(
            [
                lax.dynamic_slice_in_dim(values, (self.tensor ^ r) * rows, rows, 0)
                for r in (0, 2, 1, 3)
            ],
            0,
        )

    def absolute(self, values):
        rows = values.shape[0] // 4
        place = jnp.asarray([0, 2, 1, 3], jnp.int32)
        return jnp.concatenate(
            [
                lax.dynamic_slice_in_dim(values, place[self.tensor ^ q] * rows, rows, 0)
                for q in range(4)
            ],
            0,
        )

    def gather(self, quarter):
        both = jnp.concatenate([quarter, self.over_tensor(quarter, 2)], 0)
        return jnp.concatenate([both, self.over_tensor(both, 1)], 0)


def nearest_first(line):
    tables = []
    for place in range(line):
        offsets = [p - place for p in range(line) if p != place]
        tables.append(sorted(offsets, key=lambda o: (abs(o), -o)))
    return tables


def expert_kernel(count, hidden, split, prior, *refs):
    names, tokens, grads, gates = refs[:4]
    weights, refs = refs[4 : 4 + count], refs[4 + count :]
    if prior:
        before, refs = refs[0], refs[1:]
    outs, (gated_out, grad_pre_out, rows_out) = refs[: 2 if split else 1], refs[2 if split else 1 :]
    tile, grad_tile = tokens[...], grads[...]
    total = before[...].astype(F32) if prior else None
    for slot in range(count):
        weight = weights[slot]
        pre = dot(weight[: 2 * hidden, :], tile, 1, 1)
        back = dot(weight[2 * hidden :, :], grad_tile, 1, 1)
        gate = gates[pl.ds(names[slot], 1), :]
        gate_pre, up_pre = pre[:hidden], pre[hidden:]
        sigmoid = jax.nn.sigmoid(gate_pre)
        activated = gate_pre * sigmoid
        hid = (activated * up_pre).astype(BF16).astype(F32)
        rows_out[slot : slot + 1, :] = jnp.sum(hid * back, axis=0, keepdims=True)
        gated_out[slot * hidden : (slot + 1) * hidden, :] = (hid * gate).astype(BF16)
        grad_hidden = back * gate
        grad_pre = jnp.concatenate(
            [
                (grad_hidden * up_pre * (sigmoid * (1.0 + gate_pre * (1.0 - sigmoid)))).astype(BF16),
                (grad_hidden * activated).astype(BF16),
            ],
            0,
        )
        grad_pre_out[2 * slot * hidden : 2 * (slot + 1) * hidden, :] = grad_pre
        part = dot(grad_pre, weight[: 2 * hidden, :], 0, 0)
        total = part if total is None else total + part
    if split:
        for step in range(2):

            @pl.when(pl.program_id(0) == step)
            def _(step=step):
                outs[step][...] = total.astype(BF16)
    else:
        outs[0][...] = total.astype(BF16)


def expert_pass(tokens, grads, gates, names, weights, before=None, split=False):
    count, length, width = len(weights), tokens.shape[0], tokens.shape[1]
    hidden = weights[0].shape[0] // 3
    tile = length // 2
    token_spec = pl.BlockSpec((tile, width), lambda i, *_: (i, 0))
    half_spec = pl.BlockSpec((tile, width), lambda i, *_: (0, 0))

    def column_spec(rows):
        return pl.BlockSpec((rows, tile), lambda i, *_: (0, i))

    weight_spec = pl.BlockSpec((3 * hidden, width), lambda i, *_: (0, 0))
    token_shape = in_hbm((length, width), BF16)
    half_shape = in_hbm((tile, width), BF16)
    columns = [(count * hidden, BF16), (2 * count * hidden, BF16), (count, F32)]
    return pl.pallas_call(
        functools.partial(expert_kernel, count, hidden, split, before is not None),
        grid_spec=pltpu.PrefetchScalarGridSpec(
            num_scalar_prefetch=1,
            grid=(2,),
            in_specs=[token_spec, token_spec, column_spec(gates.shape[0])]
            + [weight_spec] * count
            + [token_spec] * (before is not None),
            out_specs=([half_spec] * 2 if split else [token_spec]) + [column_spec(r) for r, _ in columns],
        ),
        out_shape=([half_shape] * 2 if split else [token_shape])
        + [in_hbm((r, length), t) for r, t in columns],
        compiler_params=pltpu.CompilerParams(vmem_limit_bytes=48 * 2**20),
        cost_estimate=pl.CostEstimate(
            flops=2 * count * length * width * hidden * 5,
            bytes_accessed=(4 * length + 3 * hidden * count) * width * 2,
            transcendentals=0,
        ),
    )(names, tokens, grads, gates, *weights, *([before] if before is not None else []))


def weight_grad_kernel(grad_pre_own, grad_pre_pair, gated_own, gated_pair, own, pair, grad_own, grad_pair, out):
    rows = grad_pre_own.shape[0]
    out[:rows, :] = (
        dot(grad_pre_own[...], own[...], 1, 0) + dot(grad_pre_pair[...], pair[...], 1, 0)
    ).astype(out.dtype)
    out[rows:, :] = (
        dot(gated_own[...], grad_own[...], 1, 0) + dot(gated_pair[...], grad_pair[...], 1, 0)
    ).astype(out.dtype)


def weight_grad(slot, hidden, grad_pre, gated, tokens, grads, kept_as):
    length, width = tokens[0].shape
    tile = width // 3
    pre_spec = pl.BlockSpec((2 * hidden, length), lambda i: (slot, 0))
    gated_spec = pl.BlockSpec((hidden, length), lambda i: (slot, 0))
    token_spec = pl.BlockSpec((length, tile), lambda i: (0, i))
    return pl.pallas_call(
        weight_grad_kernel,
        grid=(3,),
        in_specs=[pre_spec] * 2 + [gated_spec] * 2 + [token_spec] * 4,
        out_specs=pl.BlockSpec((3 * hidden, tile), lambda i: (0, i)),
        out_shape=jax.ShapeDtypeStruct((3 * hidden, width), kept_as),
        compiler_params=pltpu.CompilerParams(vmem_limit_bytes=32 * 2**20),
        cost_estimate=pl.CostEstimate(
            flops=2 * 2 * length * width * hidden * 3,
            bytes_accessed=(4 * length + 6 * hidden) * width * 2,
            transcendentals=0,
        ),
    )(*grad_pre, *gated, *tokens, *grads)


MESH = pl.DeviceIdType.MESH


class Copies:
    def __init__(self, tensors, send, recv):
        self.send, self.recv, self.started = send, recv, []
        expert, tensor = lax.axis_index("expert"), lax.axis_index("tensor")
        self.core = (expert, tensor + 1 - 2 * (tensor % 2))
        self.far = (expert, (tensor + tensors // 2) % tensors)
        self.mate = (expert + 1 - 2 * (expert % 2), tensor)

    def across(self, bit):
        expert, tensor = lax.axis_index("expert"), lax.axis_index("tensor")
        return (expert + bit - 2 * bit * (expert // bit % 2), tensor)

    def greet(self, partners, line=0):
        barrier = pltpu.get_barrier_semaphore()
        for partner in partners:
            pl.semaphore_signal(barrier, inc=1, device_id=partner, device_id_type=MESH)
        count = len(partners)
        if line:
            expert, tensor = lax.axis_index("expert"), lax.axis_index("tensor")
            position = expert // 2
            for step, there in ((2, position < line - 1), (-2, position > 0)):

                @pl.when(there)
                def _(step=step):
                    device = (expert + step, tensor)
                    pl.semaphore_signal(barrier, inc=1, device_id=device, device_id_type=MESH)

            count = count + 1 - (position + 1) // line + (position + line - 1) // line
        pl.semaphore_wait(barrier, count)

    def start(self, source, target, device):
        place = len(self.started)
        copy = pltpu.make_async_remote_copy(
            src_ref=source,
            dst_ref=target,
            send_sem=self.send.at[place],
            recv_sem=self.recv.at[place],
            device_id=device,
            device_id_type=MESH,
        )
        copy.start()
        self.started.append(copy)
        return copy

    def along(self, source, target, step, sends, receives):
        device = (lax.axis_index("expert") + 2 * step, lax.axis_index("tensor"))
        return self.over_when(source, target, device, sends, receives)

    def over_when(self, source, target, device, sends, receives=None):
        place = len(self.started)
        copy = pltpu.make_async_remote_copy(
            src_ref=source,
            dst_ref=target,
            send_sem=self.send.at[place],
            recv_sem=self.recv.at[place],
            device_id=device,
            device_id_type=MESH,
        )
        pl.when(sends)(lambda: copy.start())
        self.started.append(When(copy, sends, sends if receives is None else receives))
        return self.started[-1]

    def finish(self):
        for copy in self.started:
            copy.wait_send()


class When:
    def __init__(self, copy, sends, receives):
        self.copy, self.sends, self.receives = copy, sends, receives

    def wait_send(self):
        pl.when(self.sends)(lambda: self.copy.wait_send())

    def wait_recv(self):
        pl.when(self.receives)(lambda: self.copy.wait_recv())


def sum_quarter(copies, part, sent, got, crossing, crossed, beside=None):
    rows = crossing.shape[0]
    sent[rows:, :] = part(3).astype(BF16)
    last = copies.start(sent.at[pl.ds(rows, rows)], got.at[pl.ds(rows, rows)], copies.core)
    sent[:rows, :] = part(2).astype(BF16)
    first = copies.start(sent.at[pl.ds(0, rows)], got.at[pl.ds(0, rows)], copies.core)
    other = part(1)
    last.wait_recv()
    crossing[...] = (other + got[rows:, :].astype(F32)).astype(BF16)
    far = copies.start(crossing, crossed, copies.far)
    if beside is not None:
        beside()
    mine = part(0)
    first.wait_recv()
    mine = mine + got[:rows, :].astype(F32)
    far.wait_recv()
    return mine + crossed[...].astype(F32)


def gather_quarters(copies, whole, rows, fill=None):
    far = copies.start(whole.at[pl.ds(0, rows)], whole.at[pl.ds(rows, rows)], copies.far)
    first = copies.start(whole.at[pl.ds(0, rows)], whole.at[pl.ds(2 * rows, rows)], copies.core)
    if fill is not None:
        fill()
    far.wait_recv()
    last = copies.start(whole.at[pl.ds(rows, rows)], whole.at[pl.ds(3 * rows, rows)], copies.core)
    first.wait_recv()
    last.wait_recv()


def quarter_at(place):
    tensor = lax.axis_index("tensor")
    return (tensor % 2 + place // 2) % 2 + 2 * ((tensor // 2 + place % 2) % 2)


def place_of(quarter):
    tensor = lax.axis_index("tensor")
    return 2 * ((tensor % 2 + quarter % 2) % 2) + (tensor // 2 + quarter // 2) % 2


def masked_scores(query, keys, start, scale):
    scores = dot(query, keys, 1, 1) * scale
    rows = lax.broadcasted_iota(jnp.int32, scores.shape, 0) + start
    cols = lax.broadcasted_iota(jnp.int32, scores.shape, 1)
    return jnp.where(cols <= rows, scores, NEGATIVE)


def kv_columns(heads):
    head = lax.axis_index("tensor") * heads // (HEADS // KV)
    return pl.ds(pl.multiple_of(head * HD, HD), HD)


def attend_kernel(tensors, line, heads, *refs):
    refs = list(refs)
    stream, gain, w_query, w_key, w_value, cos, sin, grad, routes = [refs.pop(0) for _ in range(9)]
    own_weights = refs.pop(0) if line else None
    attn_in, query, key, value, context, logsum = [refs.pop(0) for _ in range(6)]
    grad_rel, grad_pair, routes_own, routes_pair = [refs.pop(0) for _ in range(4)]
    arrived = refs.pop(0) if line else None
    send, recv = refs
    copies = Copies(tensors, send, recv)
    expert = lax.axis_index("expert")
    position = expert // 2
    copies.greet([copies.core, copies.mate], line)
    length = stream.shape[0]
    rows = length // 4
    if line:
        up = copies.along(
            own_weights, arrived.at[1 - (position + 2) // line], 1, position < line - 1, position > 0
        )
        down = copies.along(own_weights, arrived.at[0], -1, position > 0, position < line - 1)
    mates = []
    for place in range(4):
        at = pl.ds(place * rows, rows)
        grad_rel[at, :] = grad[pl.ds(pl.multiple_of(quarter_at(place) * rows, rows), rows), :]
        if place < 2:
            mates.append(copies.start(grad_rel.at[at], grad_pair.at[at], copies.mate))
    routes_own[...] = jnp.zeros(routes_own.shape, jnp.int32)
    for place in range(4):
        source = pl.ds(pl.multiple_of(quarter_at(place) * rows, rows), rows)
        routes_own[: routes.shape[0], place * rows : (place + 1) * rows] = routes[:, source]
    routes_copy = copies.start(routes_own, routes_pair, copies.mate)
    kv_at = kv_columns(heads)
    for tile in range(4):
        at = slice(tile * rows, (tile + 1) * rows)
        normed = rms_norm(stream[at, :].astype(F32), gain[...])[0].astype(BF16)
        attn_in[at, :] = normed
        proj = dot(normed, w_query[...], 1, 0)
        for head in range(heads):
            columns = slice(head * HD, (head + 1) * HD)
            query[at, columns] = turned(proj[:, columns], cos[at, :], sin[at, :]).astype(BF16)
        key[at, :] = turned(dot(normed, w_key[:, kv_at], 1, 0), cos[at, :], sin[at, :]).astype(BF16)
        value[at, :] = dot(normed, w_value[:, kv_at], 1, 0).astype(BF16)
    for tile in range(4):
        at, seen = slice(tile * rows, (tile + 1) * rows), (tile + 1) * rows
        to = pl.ds(pl.multiple_of(place_of(tile) * rows, rows), rows)
        for head in range(heads):
            columns = slice(head * HD, (head + 1) * HD)
            scores = masked_scores(query[at, columns], key[:seen, :], tile * rows, HD**-0.5)
            peak = jnp.max(scores, axis=-1, keepdims=True)
            exponent = jnp.exp(scores - peak)
            total = jnp.sum(exponent, axis=-1, keepdims=True)
            prob = (exponent / total).astype(BF16)
            context[to, columns] = dot(prob, value[:seen, :], 1, 0).astype(BF16)
            logsum[at, head : head + 1] = peak + jnp.log(total)
    cores = []
    for place in range(2):
        mates[place].wait_recv()
        source = grad_pair.at[pl.ds(place * rows, rows)]
        cores.append(copies.start(source, grad_pair.at[pl.ds((2 + place) * rows, rows)], copies.core))
    routes_copy.wait_recv()
    for copy in cores + ([up, down] if line else []):
        copy.wait_recv()
    copies.finish()


def anywhere():
    return pl.BlockSpec(memory_space=pl.ANY)


def attend(tensors, line, stream, gain, w_query, w_key, w_value, cos, sin, grad, routes, own_weights):
    length, width = stream.shape
    heads = w_query.shape[1] // HD
    shape = in_hbm
    return pl.pallas_call(
        functools.partial(attend_kernel, tensors, line, heads),
        out_shape=[
            shape((length, width), BF16),
            shape((length, heads * HD), BF16),
            shape((length, HD), BF16),
            shape((length, HD), BF16),
            shape((length, heads * HD), BF16),
            shape((length, HD), F32),
            shape((length, width), BF16),
            shape((length, width), BF16),
            shape((8, length), routes.dtype),
            shape((8, length), routes.dtype),
        ]
        + ([shape((2,) + own_weights.shape, BF16)] if line else []),
        in_specs=[vmem()] * 9 + [anywhere()] * bool(line),
        out_specs=[vmem()] * 10 + [anywhere()] * bool(line),
        scratch_shapes=[
            pltpu.SemaphoreType.DMA((8,)),
            pltpu.SemaphoreType.DMA((8,)),
        ],
        compiler_params=pltpu.CompilerParams(
            collective_id=4, has_side_effects=True, vmem_limit_bytes=48 * 2**20
        ),
        cost_estimate=pl.CostEstimate(flops=4 * 10**10, bytes_accessed=10**7, transcendentals=0),
    )(stream, gain, w_query, w_key, w_value, cos, sin, grad, routes, *([own_weights] if line else []))


def attend_back(heads, grad, weight, query, key, value, logsum, cos, sin, grads, grads_rel, key_grad, value_grad):
    length = query.shape[0]
    rows = length // 4
    scale = HD**-0.5
    for tile in range(3, -1, -1):
        at, seen = slice(tile * rows, (tile + 1) * rows), (tile + 1) * rows
        to = pl.ds(pl.multiple_of(place_of(tile) * rows, rows), rows)
        grad_context = dot(grad[to, :], weight[...], 1, 1).astype(BF16)
        for head in range(heads):
            columns = slice(head * HD, (head + 1) * HD)
            head_query = query[at, columns]
            scores = masked_scores(head_query, key[:seen, :], tile * rows, scale)
            prob = jnp.exp(scores - logsum[at, head : head + 1])
            head_grad = grad_context[:, columns]
            dprob = dot(head_grad, value[:seen, :], 1, 1)
            delta = jnp.sum(prob * dprob, axis=-1, keepdims=True)
            dscore = (prob * (dprob - delta)).astype(BF16)
            dquery = dot(dscore, key[:seen, :], 1, 0) * scale
            dquery = turned(dquery, cos[at, :], sin[at, :], True).astype(BF16)
            grads[at, columns] = dquery
            grads_rel[to, columns] = dquery
            dkey = dot(dscore, head_query, 0, 0)
            dvalue = dot(prob.astype(BF16), head_grad, 0, 0)
            if tile == 3 and head == 0:
                key_grad[...] = dkey
                value_grad[...] = dvalue
            else:
                key_grad[:seen, :] += dkey
                value_grad[:seen, :] += dvalue
    for tile in range(4):
        at = slice(tile * rows, (tile + 1) * rows)
        to = pl.ds(pl.multiple_of(place_of(tile) * rows, rows), rows)
        dkey = turned(key_grad[at, :] * scale, cos[at, :], sin[at, :], True).astype(BF16)
        both = jnp.concatenate([dkey, value_grad[at, :].astype(BF16)], 1)
        grads[at, heads * HD :] = both
        grads_rel[to, heads * HD :] = both


def attend_out_kernel(tensors, line, *refs):
    refs = list(refs)
    context, weight, gain, stream = [refs.pop(0) for _ in range(4)]
    arrived = refs.pop(0) if line else None
    own, pair, after = [refs.pop(0) for _ in range(3)]
    second = refs.pop(0) if line else None
    sent, got, crossing, crossed, stream_in, local, send, recv = refs
    copies = Copies(tensors, send, recv)
    position = lax.axis_index("expert") // 2
    copies.greet([copies.core, copies.far, copies.mate], line)
    rows = after.shape[0]
    quarter = pl.ds(pl.multiple_of(lax.axis_index("tensor") * rows, rows), rows)
    load = pltpu.make_async_copy(stream.at[quarter], stream_in, local.at[0])
    load.start()
    if line:
        inner = (position > 0) & (position < line - 1)
        up = copies.along(arrived.at[1], second, 1, inner, position >= line // 2)
        down = copies.along(arrived.at[0], second, -1, inner, position < line // 2)

    def part(place):
        return dot(context[place * rows : (place + 1) * rows, :], weight[...], 1, 0)

    total = sum_quarter(copies, part, sent, got, crossing, crossed)
    load.wait()
    total = stream_in[...].astype(F32) + total
    after[...] = total
    own[:rows, :] = rms_norm(total, gain[...])[0].astype(BF16)
    mate = copies.start(own.at[pl.ds(0, rows)], pair.at[pl.ds(0, rows)], copies.mate)
    gather_quarters(copies, own, rows)
    mate.wait_recv()
    if line:
        up.wait_recv()
        down.wait_recv()
    else:
        gather_quarters(copies, pair, rows)
    copies.finish()


def in_hbm(dims, dtype):
    return pltpu.HBM(dims, dtype)


def vmem():
    return pl.BlockSpec(memory_space=pltpu.VMEM)


def attend_out(tensors, line, context, weight, gain, stream, arrived):
    length, width = stream.shape
    rows = length // 4
    return pl.pallas_call(
        functools.partial(attend_out_kernel, tensors, line),
        out_shape=[
            in_hbm((4 * rows, width), BF16),
            in_hbm((rows if line else 4 * rows, width), BF16),
            in_hbm((rows, width), F32),
        ]
        + ([in_hbm(arrived.shape[1:], BF16)] if line else []),
        in_specs=[vmem()] * 3 + [anywhere()] * (1 + bool(line)),
        out_specs=[vmem()] * 3 + [anywhere()] * bool(line),
        scratch_shapes=[
            pltpu.VMEM((2 * rows, width), BF16),
            pltpu.VMEM((2 * rows, width), BF16),
            pltpu.VMEM((rows, width), BF16),
            pltpu.VMEM((rows, width), BF16),
            pltpu.VMEM((rows, width), BF16),
            pltpu.SemaphoreType.DMA((1,)),
            pltpu.SemaphoreType.DMA((12,)),
            pltpu.SemaphoreType.DMA((12,)),
        ],
        compiler_params=pltpu.CompilerParams(
            collective_id=1, has_side_effects=True, vmem_limit_bytes=40 * 2**20
        ),
        cost_estimate=pl.CostEstimate(flops=6 * 10**10, bytes_accessed=10**7, transcendentals=0),
    )(context, weight, gain, stream, *([arrived] if line else []))


def hidden_units(weight, tile, grad_tile, gate, hidden):
    pre = dot(weight[: 2 * hidden, :], tile, 1, 1)
    back = dot(weight[2 * hidden :, :], grad_tile, 1, 1)
    gate_pre, up_pre = pre[:hidden], pre[hidden:]
    sigmoid = jax.nn.sigmoid(gate_pre)
    activated = gate_pre * sigmoid
    hid = (activated * up_pre).astype(BF16).astype(F32)
    row = jnp.sum(hid * back, axis=0, keepdims=True)
    grad_hidden = back * gate
    grad_pre = jnp.concatenate(
        [
            (grad_hidden * up_pre * (sigmoid * (1.0 + gate_pre * (1.0 - sigmoid)))).astype(BF16),
            (grad_hidden * activated).astype(BF16),
        ],
        0,
    )
    return row, (hid * gate).astype(BF16), grad_pre


def slot_offset(slot, position, line):
    if slot == 0:
        return 0
    table = [row[slot - 1] for row in nearest_first(line)]
    offset = table[0]
    for place in range(1, line):
        offset = offset + (table[place] - table[place - 1]) * (position // place > 0)
    return offset


def first_pass_kernel(tensors, experts, line, hidden, *refs):
    refs = list(refs)
    router, routes_own, routes_pair = [refs.pop(0) for _ in range(3)]
    own_there, quarter, grad_own_there, grad_pair_there, own_weights, arrived, second = [
        refs.pop(0) for _ in range(7)
    ]
    pair = refs.pop(0)
    outs = [[refs.pop(0) for _ in range(7)] for _ in range(2)]
    last_weight, all_down = refs.pop(0), refs.pop(0)
    own, grad_own, grad_pair, weights, local, send, recv = refs
    copies = Copies(tensors, send, recv)
    expert = lax.axis_index("expert")
    position, side = expert // 2, expert % 2
    copies.greet([copies.core, copies.far], line)
    rows = quarter.shape[0]
    inner = (position > 0) & (position < line - 1)
    outer = jnp.logical_not(inner)
    down = copies.along(second, weights.at[3], -1, position == 1, position == 0)
    up = copies.along(second, weights.at[3], 1, position == line - 2, position == line - 1)
    far = copies.start(quarter, pair.at[pl.ds(rows, rows)], copies.far)
    first = copies.start(quarter, pair.at[pl.ds(2 * rows, rows)], copies.core)

    def load(source, target, place):
        return pltpu.make_async_copy(source, target, local.at[place])

    loads = [
        load(own_weights, weights.at[0], 0),
        load(own_there, own, 1),
        load(grad_own_there, grad_own, 2),
        load(arrived.at[0], weights.at[1], 3),
    ]
    for copy in loads:
        copy.start()
    pl.when(inner)(lambda: load(arrived.at[1], weights.at[2], 4).start())
    pl.when(outer)(lambda: load(second, weights.at[2], 4).start())
    later = [load(quarter, pair.at[pl.ds(0, rows)], 5), load(grad_pair_there, grad_pair, 6)]
    for copy in later:
        copy.start()
    spare = load(second, weights.at[3], 7)
    pl.when(inner)(lambda: spare.start())
    names = [(position + slot_offset(slot, position, line)) * 2 + side for slot in range(line)]
    tile = 2 * rows

    def run(tokens, grads, routes, out, which):
        total_out, gated_out, grad_pre_out, rows_out, last_gate_out, probs_out, named_out = out
        at = pl.ds(which * tile, tile)
        tokens_tile, grad_tile = tokens[at, :], grads[at, :]
        logits = dot(router[...], tokens_tile, 1, 1)[:experts]
        logit_exp = jnp.exp(logits - jnp.max(logits, axis=0, keepdims=True))
        probs = logit_exp / jnp.sum(logit_exp, axis=0, keepdims=True)
        number = lax.broadcasted_iota(jnp.int32, probs.shape, 0)
        named = jnp.zeros(probs.shape, F32)
        for choice in range(routes.shape[0] // 2):
            named = jnp.where(routes[choice : choice + 1, at] == number, 1.0, named)
        gates = probs * named
        probs_out[:, at] = probs
        named_out[:, at] = named

        def gate_of(slot):
            return jnp.sum(jnp.where(number == names[slot], gates, 0.0), axis=0, keepdims=True)

        last_gate_out[0:1, at] = gate_of(line - 1)
        total = None
        for slot in range(line - 1):
            row, gated, grad_pre = hidden_units(
                weights.at[slot], tokens_tile, grad_tile, gate_of(slot), hidden
            )
            rows_out[slot : slot + 1, at] = row
            gated_out[slot * hidden : (slot + 1) * hidden, at] = gated
            grad_pre_out[2 * slot * hidden : 2 * (slot + 1) * hidden, at] = grad_pre
            part = dot(grad_pre, weights[slot, : 2 * hidden, :], 0, 0)
            total = part if total is None else total + part
        total_out[at, :] = total.astype(BF16)

    for copy in loads:
        copy.wait()
    load(second, weights.at[2], 4).wait()
    for which in range(2):
        run(own, grad_own, routes_own, outs[0], which)
    for slot in range(line - 1):
        all_down[slot * hidden : (slot + 1) * hidden, :] = weights[slot, 2 * hidden :, :]
    far.wait_recv()
    last = copies.start(pair.at[pl.ds(rows, rows)], pair.at[pl.ds(3 * rows, rows)], copies.core)
    for copy in later:
        copy.wait()
    run(pair, grad_pair, routes_pair, outs[1], 0)
    first.wait_recv()
    last.wait_recv()
    run(pair, grad_pair, routes_pair, outs[1], 1)
    pl.when(inner)(lambda: spare.wait())
    up.wait_recv()
    down.wait_recv()
    last_weight[...] = weights[line - 1]
    all_down[(line - 1) * hidden :, :] = weights[line - 1, 2 * hidden :, :]
    copies.finish()


def first_pass(tensors, experts, line, hidden, *operands):
    length, width = operands[3].shape
    shape = in_hbm
    count = line - 1
    out = [
        shape((length, width), BF16),
        shape((count * hidden, length), BF16),
        shape((2 * count * hidden, length), BF16),
        shape((8, length), F32),
        shape((8, length), F32),
        shape((experts, length), F32),
        shape((experts, length), F32),
    ]
    tokens = pltpu.VMEM((length, width), BF16)
    return pl.pallas_call(
        functools.partial(first_pass_kernel, tensors, experts, line, hidden),
        out_shape=[shape((length, width), BF16)]
        + out * 2
        + [shape((3 * hidden, width), BF16), shape((line * hidden, width), BF16)],
        in_specs=[vmem()] * 3 + [anywhere()] * 7,
        out_specs=[vmem()] * 17,
        scratch_shapes=[
            tokens,
            tokens,
            tokens,
            pltpu.VMEM((line, 3 * hidden, width), BF16),
            pltpu.SemaphoreType.DMA((8,)),
            pltpu.SemaphoreType.DMA((5,)),
            pltpu.SemaphoreType.DMA((5,)),
        ],
        compiler_params=pltpu.CompilerParams(
            collective_id=5, has_side_effects=True, vmem_limit_bytes=63 * 2**20
        ),
        cost_estimate=pl.CostEstimate(flops=5 * 10**10, bytes_accessed=10**7, transcendentals=0),
    )(*operands)


def tokens_back_kernel(tensors, line, hidden, heads, *refs):
    refs = list(refs)
    kept_pair, kept_own, rows_kept, rows_sent = [refs.pop(0) for _ in range(4)]
    probs, named, router, after, gain = [refs.pop(0) for _ in range(5)]
    attention = [refs.pop(0) for _ in range(7)]
    grad_there, sent_pair, sent_own = [refs.pop(0) for _ in range(3)]
    factors = [refs.pop(0) for _ in range(12 if line else 0)]
    all_down = refs.pop(0) if line else None
    moe_own, moe_pair = (refs.pop(0), refs.pop(0)) if not line else (None, None)
    whole, grad_after, grad_router, grad_second = [refs.pop(0) for _ in range(4)]
    attention += [refs.pop(0) for _ in range(2)]
    moe_out, moe_cross, mate_moe = [refs.pop(0) for _ in range(3)]
    moe_got = refs.pop(0)
    if line:
        moe_own, moe_pair = refs.pop(0), refs.pop(0)
    weight_grads = [refs.pop(0) for _ in range(line)]
    going, turning = (refs.pop(0), refs.pop(0)) if line else (None, None)
    attention += [refs.pop(0) for _ in range(2)]
    moe_crossing, moe_crossed, grad, block, local = [refs.pop(0) for _ in range(5)]
    if line:
        first_in, first_out, up_in, down_in, down_in_place = [refs.pop(0) for _ in range(5)]
    got_pair, got_own, crossing_pair, crossed_pair, crossing_own, crossed_own = [refs.pop(0) for _ in range(6)]
    mate_out, mate_in, rows_got, rows_crossing, rows_crossed, rows_mine, rows_mate, send, recv = refs
    copies = Copies(tensors, send, recv)
    position = lax.axis_index("expert") // 2
    copies.greet([copies.core, copies.far, copies.mate], line)
    rows = grad.shape[0]
    loads = [pltpu.make_async_copy(grad_there.at[pl.ds(0, rows)], grad, local.at[1])]
    if line:
        loads.append(pltpu.make_async_copy(all_down, down_in_place, local.at[2]))
    for copy in loads:
        copy.start()
    moe_core = []

    def experts_out():
        if line:
            first_rows = (line - 1) * hidden

            def body(first, last, out):
                total = dot(first[...], down_in_place[:first_rows, :], 0, 0)
                out[...] = (total + dot(last[...], down_in_place[first_rows:, :], 0, 0)).astype(BF16)

            for gated, last, out in ((factors[2], factors[6], moe_own), (factors[3], factors[7], moe_pair)):
                pltpu.emit_pipeline(
                    body,
                    grid=(4,),
                    in_specs=[
                        pl.BlockSpec((first_rows, rows), lambda i: (0, i)),
                        pl.BlockSpec((hidden, rows), lambda i: (0, i)),
                    ],
                    out_specs=[pl.BlockSpec((rows, moe_own.shape[1]), lambda i: (i, 0))],
                )(gated, last, out)
        for side, source in enumerate((moe_own, moe_pair)):
            moe_core.append(
                copies.start(source.at[pl.ds(2 * rows, 2 * rows)], moe_got.at[side], copies.core)
            )

    def weight_grad(slot):
        if not line:
            return
        last = slot == line - 1
        column = 0 if last else slot
        pre_own, pre_pair, gated_own, gated_pair = factors[4:8] if last else factors[:4]
        length, width = factors[8].shape
        tile = width // 6
        pre_spec = pl.BlockSpec((2 * hidden, length), lambda i: (column, 0))
        gated_spec = pl.BlockSpec((hidden, length), lambda i: (column, 0))
        token_spec = pl.BlockSpec((length, tile), lambda i: (0, i))
        pltpu.emit_pipeline(
            weight_grad_kernel,
            grid=(6,),
            in_specs=[pre_spec] * 2 + [gated_spec] * 2 + [token_spec] * 4,
            out_specs=[pl.BlockSpec((3 * hidden, tile), lambda i: (0, i))],
        )(pre_own, pre_pair, gated_own, gated_pair, *factors[8:], weight_grads[slot])

    low, high = pl.ds(0, rows), pl.ds(rows, rows)
    pair_last = copies.start(sent_pair.at[high], got_pair.at[high], copies.core)
    pair_first = copies.start(sent_pair.at[low], got_pair.at[low], copies.core)
    rows_core = copies.start(rows_sent, rows_got, copies.core)
    own_last = copies.start(sent_own.at[high], got_own.at[high], copies.core)
    own_first = copies.start(sent_own.at[low], got_own.at[low], copies.core)
    if line:
        weight_grad(line - 1)
        up = copies.along(weight_grads[-1], first_in, 1, position == 0, position == 1)
        down = copies.along(weight_grads[-1], first_in, -1, position == line - 1, position == line - 2)
        inner = (position > 0) & (position < line - 1)
    pair_last.wait_recv()
    crossing_pair[...] = (kept_pair[rows:, :].astype(F32) + got_pair[rows:, :].astype(F32)).astype(BF16)
    pair_far = copies.start(crossing_pair, crossed_pair, copies.far)
    rows_core.wait_recv()
    rows_crossing[...] = rows_kept[:, rows:] + rows_got[:, rows:]
    rows_far = copies.start(rows_crossing, rows_crossed, copies.far)
    pair_first.wait_recv()
    mine_pair = kept_pair[:rows, :].astype(F32) + got_pair[:rows, :].astype(F32)
    own_last.wait_recv()
    crossing_own[...] = (kept_own[rows:, :].astype(F32) + got_own[rows:, :].astype(F32)).astype(BF16)
    own_first.wait_recv()
    grad_tokens = kept_own[:rows, :].astype(F32) + got_own[:rows, :].astype(F32)
    for slot in range(line - 2, 0, -1):
        weight_grad(slot)
    for copy in loads:
        copy.wait()
    pair_far.wait_recv()
    own_far = copies.start(crossing_own, crossed_own, copies.far)
    mate_out[...] = (mine_pair + crossed_pair[...].astype(F32)).astype(BF16)
    mate = copies.start(mate_out, mate_in, copies.mate)
    rows_far.wait_recv()
    rows_mine[...] = rows_kept[:, :rows] + rows_got[:, :rows] + rows_crossed[...]
    rows_over = copies.start(rows_mine, rows_mate, copies.mate)
    experts_out()
    rows_over.wait_recv()
    count = rows_mine.shape[0] // 2
    slots = jnp.concatenate([rows_mine[:count, :], rows_mate[count:, :]], 0)
    dprobs = jnp.zeros(probs.shape, F32)
    number = lax.broadcasted_iota(jnp.int32, probs.shape, 0)
    chip_side = lax.axis_index("expert") % 2
    for slot in range(count):
        at = position + slot_offset(slot, position, line) if line else slot
        for half in range(2):
            name = at * 2 + chip_side + half - 2 * half * chip_side
            row = slots[half * count + slot : half * count + slot + 1, :]
            dprobs = jnp.where(number == name, row, dprobs)
    dprobs = dprobs * named[...]
    dlogits = (
        probs[...] * (dprobs - jnp.sum(probs[...] * dprobs, axis=0, keepdims=True))
    ).astype(BF16)
    second_out, normed, inverse = rms_norm(after[...], gain[...])
    grad_router[...] = dot(dlogits, second_out.astype(BF16), 1, 0)
    grad_tokens = grad_tokens + dot(dlogits, router[...], 0, 0)
    own_far.wait_recv()
    grad_tokens = grad_tokens + crossed_own[...].astype(F32)
    mate.wait_recv()
    grad_tokens = grad_tokens + mate_in[...].astype(F32)
    through, second = norm_backward(grad_tokens, normed, inverse, gain[...])
    grad_second[...] = second[None]
    total = grad[...].astype(F32) + through
    grad_after[...] = total
    whole[:rows, :] = total.astype(BF16)
    second = []

    def move(source, target, place):
        copy = pltpu.make_async_copy(source, target, local.at[place])
        copy.start()
        copy.wait()

    def moe_part(side, at):
        move((moe_own, moe_pair)[side].at[at], block.at[0], 0)
        move(moe_got.at[side, at], block.at[1], 0)
        return block[0].astype(F32) + block[1].astype(F32)

    def second_round():
        up.wait_recv()
        down.wait_recv()

        @pl.when(inner)
        def _():
            move(weight_grads[line - 1], first_out, 0)
            first_out[...] = (first_out[...].astype(F32) + first_in[...].astype(F32)).astype(BF16)

        @pl.when(jnp.logical_not(inner))
        def _():
            move(weight_grads[line - 2], first_out, 0)

        second.append(copies.along(first_out, up_in, 1, position < line // 2, inner))
        second.append(copies.along(first_out, down_in, -1, position >= line // 2, inner))

    def beside():
        if line:
            second_round()
            weight_grad(0)

    gather_quarters(copies, whole, rows, beside)
    for copy in moe_core:
        copy.wait_recv()
    moe_crossing[...] = moe_part(1, pl.ds(rows, rows)).astype(BF16)
    moe_far = copies.start(moe_crossing, moe_crossed, copies.far)
    moe_cross[...] = moe_part(0, pl.ds(rows, rows)).astype(BF16)
    moe_out[...] = after[...] + moe_part(0, pl.ds(0, rows))
    attend_back(heads, whole, *attention)
    moe_far.wait_recv()
    mate_moe[...] = (moe_part(1, pl.ds(0, rows)) + moe_crossed[...].astype(F32)).astype(BF16)
    if line:
        move(weight_grads[1], going, 0)
        move(weight_grads[2], turning, 0)
        for copy in second:
            copy.wait_recv()

        @pl.when(inner)
        def _():
            going[...] = (going[...].astype(F32) + up_in[...].astype(F32)).astype(BF16)
            turning[...] = (turning[...].astype(F32) + down_in[...].astype(F32)).astype(BF16)

    copies.finish()


def tokens_back(tensors, experts, line, hidden, *operands):
    rows, width = operands[7].shape
    heads = operands[9].shape[0] // HD
    half = pltpu.VMEM((2 * rows, width), BF16)
    quarter = pltpu.VMEM((rows, width), BF16)
    two_quarters = pltpu.VMEM((2, rows, width), BF16)
    small = pltpu.VMEM((experts, rows), F32)
    shape = in_hbm
    shard = shape((3 * hidden, width), BF16)
    outs = [
        shape((4 * rows, width), BF16),
        shape((rows, width), F32),
        shape((experts, width), F32),
        shape((1, width), F32),
        shape((4 * rows, (heads + 2) * HD), BF16),
        shape((4 * rows, (heads + 2) * HD), BF16),
        shape((rows, width), F32),
        shape((rows, width), BF16),
        shape((rows, width), BF16),
        shape((2, 2 * rows, width), BF16),
    ]
    grads = [shape((3 * hidden, width), F32)] + [shard] * (line - 1) if line else []
    moving = [pltpu.VMEM((3 * hidden, width), BF16)] * 4 + [pltpu.VMEM((line * hidden, width), BF16)] if line else []
    moe = [shape((4 * rows, width), BF16)] * 2 if line else []
    return pl.pallas_call(
        functools.partial(tokens_back_kernel, tensors, line, hidden, heads),
        out_shape=outs + moe + grads + [shard] * (2 if line else 0),
        in_specs=[vmem()] * 16 + [anywhere()] * (len(operands) - 16),
        out_specs=[vmem()] * 9 + [anywhere()] * (1 + len(moe) + line) + [vmem()] * (2 if line else 0),
        scratch_shapes=[pltpu.VMEM((4 * rows, HD), F32)] * 2
        + [quarter, quarter, quarter, two_quarters]
        + [pltpu.SemaphoreType.DMA((3,))]
        + moving
        + [half, half]
        + [quarter] * 6
        + [pltpu.VMEM((experts, 2 * rows), F32), small, small, small, small]
        + [pltpu.SemaphoreType.DMA((24,)), pltpu.SemaphoreType.DMA((24,))],
        compiler_params=pltpu.CompilerParams(
            collective_id=2, has_side_effects=True, vmem_limit_bytes=63 * 2**20
        ),
        cost_estimate=pl.CostEstimate(flops=10**11, bytes_accessed=10**7, transcendentals=0),
    )(*operands)


def line_sum(copies, line, partial, whole, got, running, up_in, down_in):
    position, side = lax.axis_index("expert") // 2, lax.axis_index("expert") % 2
    count = partial.shape[0] // 2
    chunk = count // line
    order = [3 * (1 - position // 2), 2 - position // 2, position + 1 - 2 * (position % 2), position]
    over = []

    def rows_at(half, place):
        return pl.ds(pl.multiple_of(half * count + place * chunk, 16), chunk)

    def send_pair():
        for place in order:
            over.append(
                copies.start(partial.at[rows_at(1 - side, place)], got.at[rows_at(0, place)], copies.mate)
            )

    def part(place):
        mine = partial[rows_at(side, place), :].astype(F32)
        return mine + got[rows_at(0, place), :].astype(F32)

    flows = {1: {}, -1: {}}

    def reach_step(reach):
        over[line - 1 - reach].wait_recv()
        for way, (step, landed) in enumerate(((1, up_in), (-1, down_in))):
            target = position + step * reach
            sends = (target >= 0) & (target < line)
            origin = position - step
            receives = (origin >= 0) & (origin < line) & (origin + step * reach >= 0) & (origin + step * reach < line)
            slot = 3 * way + reach - 1
            if reach < line - 1:
                flows[step][reach + 1].wait_recv()

            @pl.when(sends)
            def _(slot=slot, target=target, landed=landed, step=step):
                running[slot] = part(target).astype(BF16)
                if reach < line - 1:

                    @pl.when((position - step >= 0) & (position - step < line))
                    def _():
                        total = part(target) + landed[reach].astype(F32)
                        running[slot] = total.astype(BF16)

            flows[step][reach] = copies.along(running.at[slot], landed.at[reach - 1], step, sends, receives)

    spread, mates = {}, {}

    def settle():
        over[line - 1].wait_recv()
        flows[1][1].wait_recv()
        flows[-1][1].wait_recv()
        total = part(position)
        total = total + jnp.where(position > 0, up_in[0].astype(F32), 0.0)
        total = total + jnp.where(position < line - 1, down_in[0].astype(F32), 0.0)
        here = rows_at(side, position)
        whole[here, :] = total.astype(BF16)
        mates[0] = [copies.start(whole.at[here], whole.at[here], copies.mate)]

    def spread_start(hop):
        spread[hop] = []
        for step in (1, -1):
            place = position - step * (hop - 1)
            sends = (place >= 0) & (place < line) & (position + step >= 0) & (position + step < line)
            origin = position - step * hop
            receives = (origin >= 0) & (origin < line)
            at = rows_at(side, jnp.clip(place, 0, line - 1))
            spread[hop].append(copies.along(whole.at[at], whole.at[at], step, sends, receives))

    def spread_end(hop):
        mates[hop] = []
        for step, copy in zip((1, -1), spread[hop]):
            copy.wait_recv()
            origin = position - step * hop
            there = (origin >= 0) & (origin < line)
            at = rows_at(side, jnp.clip(origin, 0, line - 1))
            mates[hop].append(copies.over_when(whole.at[at], whole.at[at], copies.mate, there))

    def mates_end(hop):
        for copy in mates[hop]:
            copy.wait_recv()

    return send_pair, reach_step, settle, spread_start, spread_end, mates_end


class SmallSum:
    def __init__(self, copies, devices, running, arrived, sums):
        self.copies, self.devices, self.running, self.arrived, self.sums = copies, devices, running, arrived, sums
        self.at, self.copy = 0, None

    def step(self):
        if self.copy is not None:
            self.copy.wait_recv()
            total = self.running[self.at] + self.arrived[self.at]
            self.at += 1
            self.copy = None
            if self.at == len(self.devices):
                self.sums[...] = total
            else:
                self.running[self.at] = total
        if self.at < len(self.devices):
            self.copy = self.copies.start(
                self.running.at[self.at], self.arrived.at[self.at], self.devices[self.at]
            )

    def end(self):
        while self.copy is not None:
            self.step()


class Gather:
    def __init__(self, copies, tensors, whole, rows):
        self.copies, self.whole, self.rows = copies, whole, rows
        tensor = lax.axis_index("tensor")
        self.mine = pl.ds(pl.multiple_of(tensor * rows, rows), rows)
        self.there = pl.ds(pl.multiple_of((tensor + tensors // 2) % tensors * rows, rows), rows)

    def start(self):
        self.far = self.copies.start(self.whole.at[self.mine], self.whole.at[self.mine], self.copies.far)
        self.first = self.copies.start(self.whole.at[self.mine], self.whole.at[self.mine], self.copies.core)

    def forward(self):
        self.far.wait_recv()
        self.last = self.copies.start(self.whole.at[self.there], self.whole.at[self.there], self.copies.core)

    def end(self):
        self.first.wait_recv()
        self.last.wait_recv()


def inputs_back_kernel(tensors, experts, line, hidden, *refs):
    refs = list(refs)
    grads_rel, w_query, w_key, w_value, gain, grad_after = [refs.pop(0) for _ in range(6)]
    grad_router, grad_second = refs.pop(0), refs.pop(0)
    attn_in, grads, context, grad_low, layer_part, moe_cross, mate_out = [refs.pop(0) for _ in range(7)]
    stream = refs.pop(0)
    own_sum, going, turning = [refs.pop(0) for _ in range(3)] if line else [None] * 3
    whole, layer, sums, summed, kv_out = [refs.pop(0) for _ in range(5)]
    weight_outs = [refs.pop(0) for _ in range(3 if line else 0)]
    partial, kv_sent, kv_got, mate_in, moe_crossed, stream_in, local = [refs.pop(0) for _ in range(7)]
    buffers = [refs.pop(0) for _ in range(4)] if line else []
    final, block = (refs.pop(0), refs.pop(0)) if line else (None, None)
    sent, got, crossing, crossed, running, arrived, send, recv = refs
    copies = Copies(tensors, send, recv)
    bits = [1 << k for k in range(experts.bit_length() - 1)]
    position = lax.axis_index("expert") // 2
    copies.greet([copies.core, copies.far] + [copies.across(bit) for bit in bits], line)
    rows = grad_after.shape[0]
    quarter = pl.ds(pl.multiple_of(lax.axis_index("tensor") * rows, rows), rows)
    load = pltpu.make_async_copy(stream.at[quarter], stream_in, local.at[0])
    load.start()
    lines = []
    if line:
        end, inner = position == line - 1, (position > 0) & (position < line - 1)
        lines = [
            copies.along(going, final.at[0], 1, position < line - 1, position > 0),
            copies.along(going, final.at[1], -1, end, position == line - 2),
            copies.along(turning, final.at[1], -1, inner, position < line - 2),
        ]
        send_pair, reach_step, settle, spread_start, spread_end, mates_end = line_sum(
            copies, line, partial, summed, *buffers
        )

    lead = lax.axis_index("tensor") % 2
    query_width = context.shape[1]
    first_rows = partial.shape[0] // 8
    kv_rows = pl.ds(first_rows, HD)
    kept_at = pl.ds(pl.multiple_of(query_width + lead * HD, HD), HD)
    sent_at = pl.ds(pl.multiple_of(query_width + (1 - lead) * HD, HD), HD)
    width = attn_in.shape[1]
    sent_grads, kept_grads, query_grads = grads[:, sent_at], grads[:, kept_at], grads[:, :query_width]
    for block_at in range(0, width, HD):
        columns = slice(block_at, block_at + HD)
        kv_sent[:, columns] = dot(attn_in[:, columns], sent_grads, 0, 0).astype(BF16)
    kv = copies.start(kv_sent, kv_got, copies.core)
    for block_at in range(0, width, query_width):
        columns = slice(block_at, block_at + query_width)
        query_block = dot(attn_in[:, columns], query_grads, 0, 0).astype(BF16)
        partial[:first_rows, columns] = query_block[:first_rows]
        partial[first_rows + HD : query_width + HD, columns] = query_block[first_rows:]
    partial[query_width + HD :, :] = dot(context[...], grad_low[...], 0, 0).astype(BF16)
    kv.wait_recv()
    for block_at in range(0, width, HD):
        columns = slice(block_at, block_at + HD)
        kept = dot(attn_in[:, columns], kept_grads, 0, 0)
        partial[kv_rows, columns] = (kept + kv_got[:, columns].astype(F32)).astype(BF16)
    if line:
        send_pair()
    mate = copies.start(mate_out, mate_in, copies.mate)

    heads = query_width // HD
    kv_at = kv_columns(heads)

    def part(place):
        at = slice(place * rows, (place + 1) * rows)
        total = dot(grads_rel[at, :query_width], w_query[...], 1, 1)
        total = total + dot(grads_rel[at, query_width : query_width + HD], w_key[:, kv_at], 1, 1)
        return total + dot(grads_rel[at, query_width + HD :], w_value[:, kv_at], 1, 1)

    def beside():
        if line:
            reach_step(line - 1)

    grad_in = sum_quarter(copies, part, sent, got, crossing, crossed, beside)
    load.wait()
    _, normed, inverse = rms_norm(stream_in[...].astype(F32), gain[...])
    through, first = norm_backward(grad_in, normed, inverse, gain[...])
    whole[quarter, :] = (grad_after[...] + through).astype(BF16)
    inputs_gather = Gather(copies, tensors, whole, rows)
    inputs_gather.start()
    running[0] = jnp.zeros(sums.shape, F32)
    running[0, :experts, :] = grad_router[...]
    running[0, experts : experts + 1, :] = grad_second[...]
    running[0, experts + 1 : experts + 2, :] = first[None]
    small = SmallSum(
        copies, [copies.core] + [copies.across(bit) for bit in bits] + [copies.far], running, arrived, sums
    )
    small.step()
    if line:
        for reach in range(line - 2, 0, -1):
            reach_step(reach)
            small.step()
    inputs_gather.forward()
    moe_far = copies.start(moe_cross, moe_crossed, copies.far)
    if line:
        settle()
        spread_start(1)
        small.step()
        spread_end(1)
        spread_start(2)
        small.step()
    mate.wait_recv()
    moe_far.wait_recv()
    layer[quarter, :] = (
        layer_part[...] + moe_crossed[...].astype(F32) + mate_in[...].astype(F32)
    ).astype(BF16)
    layer_gather = Gather(copies, tensors, layer, rows)
    layer_gather.start()
    if line:
        spread_end(2)
        spread_start(3)
        small.step()
        for copy in lines:
            copy.wait_recv()
        for index, out in enumerate(weight_outs):
            at = pl.ds(index * hidden, hidden)
            move = pltpu.make_async_copy(own_sum.at[at], block, local.at[0])
            move.start()
            move.wait()
            total = block[...] + jnp.where(position > 0, final[0, at, :].astype(F32), 0.0)
            total = total + jnp.where(position < line - 1, final[1, at, :].astype(F32), 0.0)
            out[...] = total
        for hop in range(3):
            mates_end(hop)
        far = copies.start(summed.at[kv_rows], kv_out.at[0], copies.far)
        near = copies.start(summed.at[kv_rows], kv_out.at[1], copies.core)
        spread_end(3)
        layer_gather.forward()
        far.wait_recv()
        across = copies.start(kv_out.at[0], kv_out.at[2], copies.core)
        mates_end(3)
        near.wait_recv()
        across.wait_recv()
    else:
        layer_gather.forward()
        summed[...] = partial[...]
        kv_out[...] = jnp.zeros(kv_out.shape, BF16)
    small.end()
    inputs_gather.end()
    layer_gather.end()
    copies.finish()


def inputs_back(tensors, experts, line, hidden, *operands):
    rows, width = operands[5].shape
    early = (-(-(experts + 2) // 8) * 8, width)
    steps = 1 + experts.bit_length()
    shape = jax.ShapeDtypeStruct
    query_width = operands[10].shape[1]
    projected = 2 * query_width + HD
    quarter = pltpu.VMEM((rows, width), BF16)
    half = pltpu.VMEM((2 * rows, width), BF16)
    buffers, outs = [], []
    if line:
        chunk = projected // 2 // line
        buffers = [
            pltpu.VMEM((projected // 2, width), BF16),
            pltpu.VMEM((6, chunk, width), BF16),
            pltpu.VMEM((3, chunk, width), BF16),
            pltpu.VMEM((3, chunk, width), BF16),
            pltpu.VMEM((2, 3 * hidden, width), BF16),
            pltpu.VMEM((hidden, width), F32),
        ]
        outs = [in_hbm((hidden, width), F32)] * 3
    return pl.pallas_call(
        functools.partial(inputs_back_kernel, tensors, experts, line, hidden),
        out_shape=[
            in_hbm((4 * rows, width), BF16),
            in_hbm((4 * rows, width), BF16),
            shape(early, F32),
            shape((projected, width), BF16),
            shape((3, HD, width), BF16),
        ]
        + outs,
        in_specs=[vmem()] * 15 + [anywhere()] * (len(operands) - 15),
        out_specs=[vmem()] * (5 + len(outs)),
        scratch_shapes=[
            pltpu.VMEM((projected, width), BF16),
            pltpu.VMEM((HD, width), BF16),
            pltpu.VMEM((HD, width), BF16),
            quarter,
            quarter,
            quarter,
            pltpu.SemaphoreType.DMA((1,)),
        ]
        + buffers
        + [
            half,
            half,
            quarter,
            quarter,
            pltpu.VMEM((steps,) + early, F32),
            pltpu.VMEM((steps,) + early, F32),
            pltpu.SemaphoreType.DMA((50 + steps,)),
            pltpu.SemaphoreType.DMA((50 + steps,)),
        ],
        compiler_params=pltpu.CompilerParams(
            collective_id=3, has_side_effects=True, vmem_limit_bytes=63 * 2**20
        ),
        cost_estimate=pl.CostEstimate(flops=10**11, bytes_accessed=10**7, transcendentals=0),
    )(*operands)


def shards(
    experts,
    tensors,
    inputs,
    routes,
    cotangent,
    first_gain,
    second_gain,
    w_query,
    w_key,
    w_value,
    w_output,
    w_router,
    w_gate,
    w_up,
    w_down,
):
    links = Links(experts, tensors)
    line, place, side = links.line, links.place, links.side
    length, width = inputs.shape
    heads = w_query.shape[1] // HD
    hidden = w_gate.shape[2]
    group = HEADS // KV
    kv_head = links.tensor * heads // group
    scale = HD ** (-0.5)
    order = nearest_first(line)

    own_weights = jnp.concatenate([w_gate[0].T, w_up[0].T, w_down[0]], 0)
    short = line if line == 4 else 0
    if not short:
        sides = [[2 * p + s for p in range(line)] for s in range(2)]
        weights = lax.all_gather(own_weights, "expert", axis_index_groups=sides)

    rows, half = length // 4, length // 2
    cos, sin = rotary_tables(length)
    attn_in, query, key, value, context_rel, logsum, grad_rel, grad_pair, routes_own, routes_pair, *arrived = attend(
        tensors,
        short,
        inputs,
        first_gain[None],
        w_query,
        w_key,
        w_value,
        cos,
        sin,
        cotangent,
        routes.T,
        own_weights,
    )

    tokens_own, tokens_pair, after, *second = attend_out(
        tensors, short, context_rel, w_output, second_gain[None], inputs, *(arrived or [None])
    )
    router_rows = w_router.T
    if short:
        router_padded = jnp.concatenate([router_rows, router_rows], 0)
        tokens_pair, *outs, last_weight, all_down = first_pass(
            tensors,
            experts,
            line,
            hidden,
            router_padded,
            routes_own,
            routes_pair,
            tokens_own,
            tokens_pair,
            grad_rel,
            grad_pair,
            own_weights,
            arrived[0],
            second[0],
        )
        *first_own, last_gate_own, router_probs, named = outs[:7]
        *first_pair, last_gate_pair, _, _ = outs[7:]
    else:
        names = jnp.arange(experts, dtype=jnp.int32)[:, None, None]

        def gates_of(tokens, tokens_routes):
            logits = dot(router_rows, tokens, 1, 1)
            logit_exp = jnp.exp(logits - jnp.max(logits, axis=0, keepdims=True))
            probs = logit_exp / jnp.sum(logit_exp, axis=0, keepdims=True)
            named = jnp.any(tokens_routes[None] == names, axis=1).astype(F32)
            return probs, named, probs * named

        router_probs, named, gates_own = gates_of(tokens_own, routes_own[:4])
        _, _, gates_pair = gates_of(tokens_pair, routes_pair[:4])
    both_tokens, both_grads = (tokens_own, tokens_pair), (grad_rel, grad_pair)
    if short:
        last = line - 1
        only = jnp.zeros((1,), jnp.int32)
        kept_pair, sent_pair, *last_pair = expert_pass(
            tokens_pair, grad_pair, last_gate_pair, only, [last_weight], first_pair[0], True
        )
        kept_own, sent_own, *last_own = expert_pass(
            tokens_own, grad_rel, last_gate_own, only, [last_weight], first_own[0], True
        )
        gate_own = jnp.concatenate([first_own[3][:last], last_own[2]], 0)
        gate_pair = jnp.concatenate([first_pair[3][:last], last_pair[2]], 0)
    else:
        zeros = jnp.zeros((length, width), BF16)

        def step(totals, weight_at):
            weight, position = weight_at
            name = (position * 2 + side)[None]
            down = weight[2 * hidden :]
            own = expert_pass(tokens_own, grad_rel, gates_own, name, [weight], totals[0])
            pair = expert_pass(tokens_pair, grad_pair, gates_pair, name, [weight], totals[1])
            grads = weight_grad(
                0, hidden, (own[2], pair[2]), (own[1], pair[1]), both_tokens, both_grads, BF16
            )
            moe_own = totals[2] + dot(own[1], down, 0, 0)
            moe_pair = totals[3] + dot(pair[1], down, 0, 0)
            return (own[0], pair[0], moe_own, moe_pair), (own[3][0], pair[3][0], grads)

        (sum_own, sum_pair, moe_own, moe_pair), (gate_own, gate_pair, weight_grads) = lax.scan(
            step,
            (zeros, zeros, zeros.astype(F32), zeros.astype(F32)),
            (weights, jnp.arange(line, dtype=jnp.int32)),
        )
        kept_own, sent_own, kept_pair, sent_pair = sum_own[:half], sum_own[half:], sum_pair[:half], sum_pair[half:]

    gate_sums = jnp.concatenate([gate_own, gate_pair], 0)
    factors = []
    if short:
        factors = [first_own[2], first_pair[2], first_own[1], first_pair[1]]
        factors += [last_own[1], last_pair[1], last_own[0], last_pair[0], *both_tokens, *both_grads, all_down]
    if not short:
        factors = [moe_own.astype(BF16), moe_pair.astype(BF16)]
    (
        grad_after_low,
        grad_after,
        grad_router,
        grad_second,
        attn_grads,
        grads_rel,
        layer_part,
        moe_cross,
        mate_moe,
        _,
        *weight_sums,
    ) = tokens_back(
        tensors,
        experts,
        short,
        hidden,
        kept_pair,
        kept_own,
        gate_sums[:, :half],
        gate_sums[:, half:],
        router_probs[:, :rows],
        named[:, :rows],
        router_rows,
        after,
        second_gain[None],
        w_output,
        query,
        key,
        value,
        logsum,
        cos,
        sin,
        grad_rel,
        sent_pair,
        sent_own,
        *factors,
    )

    line_sums = []
    if short:
        line_sums = [weight_sums[2], *weight_sums[-2:]]
    else:
        expert_grads = lax.psum_scatter(
            weight_grads, "expert", scatter_dimension=0, axis_index_groups=sides
        ).astype(F32)

    grad_inputs, layer_out, sums, summed, kv_rest, *weight_grads_out = inputs_back(
        tensors,
        experts,
        short,
        hidden,
        grads_rel,
        w_query,
        w_key,
        w_value,
        first_gain[None],
        grad_after,
        grad_router,
        grad_second,
        attn_in,
        attn_grads,
        context_rel,
        grad_after_low,
        layer_part,
        moe_cross,
        mate_moe,
        inputs,
        *line_sums,
    )
    query_width = heads * HD
    first_rows = summed.shape[0] // 8
    kv_at = slice(first_rows, first_rows + HD)
    if short:
        kv_mine, (kv_far, kv_core, kv_across) = summed[kv_at], kv_rest
    else:
        summed = lax.psum(summed, "expert")
        kv_mine = summed[kv_at]
        kv_far = links.over_tensor(kv_mine, 2)
        kv_core, kv_across = links.over_tensor(kv_mine, 1), links.over_tensor(kv_far, 1)
    grad_query = jnp.concatenate([summed[:first_rows], summed[first_rows + HD : query_width + HD]], 0)

    def unfold(values):
        count, blocks = values.shape[0], values.shape[1] // values.shape[0]
        parts = [values[:, b * count : (b + 1) * count] for b in range(blocks)]
        return jnp.concatenate(parts, 0).astype(F32)

    grad_query = unfold(grad_query)
    grad_output = summed[query_width + HD :].astype(F32)
    lead, low_head = links.tensor % 2 == 0, kv_head == 0
    keys = jnp.where(lead, kv_mine, kv_core), jnp.where(lead, kv_far, kv_across)
    values = jnp.where(lead, kv_core, kv_mine), jnp.where(lead, kv_across, kv_far)
    grad_key, grad_value = [
        jnp.concatenate([unfold(jnp.where(low_head, near, far)), unfold(jnp.where(low_head, far, near))], 1)
        for near, far in (keys, values)
    ]
    if not short:
        weight_grads_out = [expert_grads[i * hidden : (i + 1) * hidden] for i in range(3)]
    grad_router, grad_second, grad_first = sums[:experts].T, sums[experts], sums[experts + 1]
    return (
        layer_out,
        grad_inputs,
        grad_first,
        grad_second,
        grad_query,
        grad_key,
        grad_value,
        grad_output,
        grad_router,
        weight_grads_out[0].T[None],
        weight_grads_out[1].T[None],
        weight_grads_out[2][None],
    )


def solution(mesh):
    experts, tensors = mesh.shape["expert"], mesh.shape["tensor"]
    in_specs = (
        P("expert", None),
        P("expert", None),
        P("expert", None),
        P(),
        P(),
        P(None, "tensor"),
        P(),
        P(),
        P("tensor", None),
        P(),
        P("expert", None, "tensor"),
        P("expert", None, "tensor"),
        P("expert", "tensor", None),
    )
    out_specs = (
        P("expert", None),
        P("expert", None),
        P(),
        P(),
        P(None, "tensor"),
        P(),
        P(),
        P("tensor", None),
        P(),
        P("expert", None, "tensor"),
        P("expert", None, "tensor"),
        P("expert", "tensor", None),
    )

    def run(*arrays):
        return shards(experts, tensors, *arrays)

    return jax.shard_map(run, mesh=mesh, in_specs=in_specs, out_specs=out_specs, check_vma=False)
```

```python
import functools

import jax
import jax.numpy as jnp
import numpy as np
from jax import lax
from jax.experimental import pallas as pl
from jax.experimental.pallas import tpu as pltpu
from jax.sharding import PartitionSpec as P

HEADS = 12
KV = 2
HD = 128
EPSILON = 1e-06
ROPE_BASE = 10000.0
NEGATIVE = -1e30
F32 = jnp.float32
BF16 = jnp.bfloat16


def dot(left, right, left_dim, right_dim):
    return lax.dot_general(
        left, right, (((left_dim,), (right_dim,)), ((), ())), preferred_element_type=F32
    )


def rms_norm(values, gain):
    inverse = lax.rsqrt(jnp.mean(values * values, axis=-1, keepdims=True) + EPSILON)
    normed = values * inverse
    return normed * gain, normed, inverse


def norm_backward(upstream, normed, inverse, gain):
    scaled = upstream * gain
    through = inverse * (scaled - normed * jnp.mean(scaled * normed, axis=-1, keepdims=True))
    return through, jnp.sum(upstream * normed, axis=0)


def rotary_tables(length):
    frequency = np.float32(ROPE_BASE) ** (-np.arange(HD // 2, dtype=np.float32) * np.float32(2.0 / HD))
    angles = np.arange(length, dtype=np.float32)[:, None] * frequency.astype(np.float32)[None]
    cos, sin = np.cos(angles), np.sin(angles)
    return np.concatenate([cos, cos], 1), np.concatenate([-sin, sin], 1)


def turned(values, cos, sin, back=False):
    other = pltpu.roll(values, HD // 2, 1) * sin
    return values * cos - other if back else values * cos + other


class Links:
    def __init__(self, experts, tensors):
        self.experts, self.tensors = experts, tensors
        self.line = experts // 2
        self.tensor = lax.axis_index("tensor")
        expert = lax.axis_index("expert")
        self.place, self.side = expert // 2, expert % 2

    def over_tensor(self, values, bit):
        return lax.ppermute(values, "tensor", [(i, i ^ bit) for i in range(self.tensors)])

    def over_expert(self, values, bit):
        return lax.ppermute(values, "expert", [(i, i ^ bit) for i in range(self.experts)])

    def over_pair(self, values):
        return self.over_expert(values, 1)

    def relative(self, values):
        rows = values.shape[0] // 4
        return jnp.concatenate(
            [
                lax.dynamic_slice_in_dim(values, (self.tensor ^ r) * rows, rows, 0)
                for r in (0, 2, 1, 3)
            ],
            0,
        )

    def absolute(self, values):
        rows = values.shape[0] // 4
        place = jnp.asarray([0, 2, 1, 3], jnp.int32)
        return jnp.concatenate(
            [
                lax.dynamic_slice_in_dim(values, place[self.tensor ^ q] * rows, rows, 0)
                for q in range(4)
            ],
            0,
        )

    def gather(self, quarter):
        both = jnp.concatenate([quarter, self.over_tensor(quarter, 2)], 0)
        return jnp.concatenate([both, self.over_tensor(both, 1)], 0)


def nearest_first(line):
    tables = []
    for place in range(line):
        offsets = [p - place for p in range(line) if p != place]
        tables.append(sorted(offsets, key=lambda o: (abs(o), -o)))
    return tables


def expert_kernel(count, hidden, split, prior, *refs):
    names, tokens, grads, gates = refs[:4]
    weights, refs = refs[4 : 4 + count], refs[4 + count :]
    if prior:
        before, refs = refs[0], refs[1:]
    outs, (gated_out, grad_pre_out, rows_out) = refs[: 2 if split else 1], refs[2 if split else 1 :]
    tile, grad_tile = tokens[...], grads[...]
    total = before[...].astype(F32) if prior else None
    for slot in range(count):
        weight = weights[slot]
        pre = dot(weight[: 2 * hidden, :], tile, 1, 1)
        back = dot(weight[2 * hidden :, :], grad_tile, 1, 1)
        gate = gates[pl.ds(names[slot], 1), :]
        gate_pre, up_pre = pre[:hidden], pre[hidden:]
        sigmoid = jax.nn.sigmoid(gate_pre)
        activated = gate_pre * sigmoid
        hid = (activated * up_pre).astype(BF16).astype(F32)
        rows_out[slot : slot + 1, :] = jnp.sum(hid * back, axis=0, keepdims=True)
        gated_out[slot * hidden : (slot + 1) * hidden, :] = (hid * gate).astype(BF16)
        grad_hidden = back * gate
        grad_pre = jnp.concatenate(
            [
                (grad_hidden * up_pre * (sigmoid * (1.0 + gate_pre * (1.0 - sigmoid)))).astype(BF16),
                (grad_hidden * activated).astype(BF16),
            ],
            0,
        )
        grad_pre_out[2 * slot * hidden : 2 * (slot + 1) * hidden, :] = grad_pre
        part = dot(grad_pre, weight[: 2 * hidden, :], 0, 0)
        total = part if total is None else total + part
    if split:
        for step in range(2):

            @pl.when(pl.program_id(0) == step)
            def _(step=step):
                outs[step][...] = total.astype(BF16)
    else:
        outs[0][...] = total.astype(BF16)


def expert_pass(tokens, grads, gates, names, weights, before=None, split=False):
    count, length, width = len(weights), tokens.shape[0], tokens.shape[1]
    hidden = weights[0].shape[0] // 3
    tile = length // 2
    token_spec = pl.BlockSpec((tile, width), lambda i, *_: (i, 0))
    half_spec = pl.BlockSpec((tile, width), lambda i, *_: (0, 0))

    def column_spec(rows):
        return pl.BlockSpec((rows, tile), lambda i, *_: (0, i))

    weight_spec = pl.BlockSpec((3 * hidden, width), lambda i, *_: (0, 0))
    token_shape = in_hbm((length, width), BF16)
    half_shape = in_hbm((tile, width), BF16)
    columns = [(count * hidden, BF16), (2 * count * hidden, BF16), (count, F32)]
    return pl.pallas_call(
        functools.partial(expert_kernel, count, hidden, split, before is not None),
        grid_spec=pltpu.PrefetchScalarGridSpec(
            num_scalar_prefetch=1,
            grid=(2,),
            in_specs=[token_spec, token_spec, column_spec(gates.shape[0])]
            + [weight_spec] * count
            + [token_spec] * (before is not None),
            out_specs=([half_spec] * 2 if split else [token_spec]) + [column_spec(r) for r, _ in columns],
        ),
        out_shape=([half_shape] * 2 if split else [token_shape])
        + [in_hbm((r, length), t) for r, t in columns],
        compiler_params=pltpu.CompilerParams(vmem_limit_bytes=48 * 2**20),
        cost_estimate=pl.CostEstimate(
            flops=2 * count * length * width * hidden * 5,
            bytes_accessed=(4 * length + 3 * hidden * count) * width * 2,
            transcendentals=0,
        ),
    )(names, *in_place([tokens, grads, gates, *weights] + ([before] if before is not None else [])))


def weight_grad_kernel(grad_pre_own, grad_pre_pair, gated_own, gated_pair, own, pair, grad_own, grad_pair, out):
    rows = grad_pre_own.shape[0]
    out[:rows, :] = (
        dot(grad_pre_own[...], own[...], 1, 0) + dot(grad_pre_pair[...], pair[...], 1, 0)
    ).astype(out.dtype)
    out[rows:, :] = (
        dot(gated_own[...], grad_own[...], 1, 0) + dot(gated_pair[...], grad_pair[...], 1, 0)
    ).astype(out.dtype)


def weight_grad(slot, hidden, grad_pre, gated, tokens, grads, kept_as):
    length, width = tokens[0].shape
    tile = width // 3
    pre_spec = pl.BlockSpec((2 * hidden, length), lambda i: (slot, 0))
    gated_spec = pl.BlockSpec((hidden, length), lambda i: (slot, 0))
    token_spec = pl.BlockSpec((length, tile), lambda i: (0, i))
    return pl.pallas_call(
        weight_grad_kernel,
        grid=(3,),
        in_specs=[pre_spec] * 2 + [gated_spec] * 2 + [token_spec] * 4,
        out_specs=pl.BlockSpec((3 * hidden, tile), lambda i: (0, i)),
        out_shape=jax.ShapeDtypeStruct((3 * hidden, width), kept_as),
        compiler_params=pltpu.CompilerParams(vmem_limit_bytes=32 * 2**20),
        cost_estimate=pl.CostEstimate(
            flops=2 * 2 * length * width * hidden * 3,
            bytes_accessed=(4 * length + 6 * hidden) * width * 2,
            transcendentals=0,
        ),
    )(*grad_pre, *gated, *tokens, *grads)


MESH = pl.DeviceIdType.MESH


class Copies:
    def __init__(self, tensors, send, recv):
        self.send, self.recv, self.started = send, recv, []
        expert, tensor = lax.axis_index("expert"), lax.axis_index("tensor")
        self.core = (expert, tensor + 1 - 2 * (tensor % 2))
        self.far = (expert, (tensor + tensors // 2) % tensors)
        self.mate = (expert + 1 - 2 * (expert % 2), tensor)

    def across(self, bit):
        expert, tensor = lax.axis_index("expert"), lax.axis_index("tensor")
        return (expert + bit - 2 * bit * (expert // bit % 2), tensor)

    def greet(self, partners, line=0):
        barrier = pltpu.get_barrier_semaphore()
        for partner in partners:
            pl.semaphore_signal(barrier, inc=1, device_id=partner, device_id_type=MESH)
        count = len(partners)
        if line:
            expert, tensor = lax.axis_index("expert"), lax.axis_index("tensor")
            position = expert // 2
            for step, there in ((2, position < line - 1), (-2, position > 0)):

                @pl.when(there)
                def _(step=step):
                    device = (expert + step, tensor)
                    pl.semaphore_signal(barrier, inc=1, device_id=device, device_id_type=MESH)

            count = count + 1 - (position + 1) // line + (position + line - 1) // line
        pl.semaphore_wait(barrier, count)

    def start(self, source, target, device):
        place = len(self.started)
        copy = pltpu.make_async_remote_copy(
            src_ref=source,
            dst_ref=target,
            send_sem=self.send.at[place],
            recv_sem=self.recv.at[place],
            device_id=device,
            device_id_type=MESH,
        )
        copy.start()
        self.started.append(copy)
        return copy

    def along(self, source, target, step, sends, receives):
        device = (lax.axis_index("expert") + 2 * step, lax.axis_index("tensor"))
        return self.over_when(source, target, device, sends, receives)

    def over_when(self, source, target, device, sends, receives=None):
        place = len(self.started)
        copy = pltpu.make_async_remote_copy(
            src_ref=source,
            dst_ref=target,
            send_sem=self.send.at[place],
            recv_sem=self.recv.at[place],
            device_id=device,
            device_id_type=MESH,
        )
        pl.when(sends)(lambda: copy.start())
        self.started.append(When(copy, sends, sends if receives is None else receives))
        return self.started[-1]

    def finish(self):
        for copy in self.started:
            copy.wait_send()


class Moves:
    def __init__(self, semaphores):
        self.semaphores, self.count, self.open = semaphores, 0, []

    def start(self, *pairs):
        for source, target in pairs:
            copy = pltpu.make_async_copy(source, target, self.semaphores.at[self.count])
            copy.start()
            self.count += 1
            self.open.append(copy)

    def wait(self):
        for copy in self.open:
            copy.wait()
        self.open = []


def buffers_of(arrays):
    return [pltpu.VMEM(a.shape, a.dtype) for a in arrays]


class When:
    def __init__(self, copy, sends, receives):
        self.copy, self.sends, self.receives = copy, sends, receives

    def wait_send(self):
        pl.when(self.sends)(lambda: self.copy.wait_send())

    def wait_recv(self):
        pl.when(self.receives)(lambda: self.copy.wait_recv())


def sum_quarter(copies, part, sent, got, crossing, crossed, beside=None):
    rows = crossing.shape[0]
    sent[rows:, :] = part(3).astype(BF16)
    last = copies.start(sent.at[pl.ds(rows, rows)], got.at[pl.ds(rows, rows)], copies.core)
    sent[:rows, :] = part(2).astype(BF16)
    first = copies.start(sent.at[pl.ds(0, rows)], got.at[pl.ds(0, rows)], copies.core)
    other = part(1)
    last.wait_recv()
    crossing[...] = (other + got[rows:, :].astype(F32)).astype(BF16)
    far = copies.start(crossing, crossed, copies.far)
    if beside is not None:
        beside()
    mine = part(0)
    first.wait_recv()
    mine = mine + got[:rows, :].astype(F32)
    far.wait_recv()
    return mine + crossed[...].astype(F32)


def gather_quarters(copies, whole, rows, fill=None):
    far = copies.start(whole.at[pl.ds(0, rows)], whole.at[pl.ds(rows, rows)], copies.far)
    first = copies.start(whole.at[pl.ds(0, rows)], whole.at[pl.ds(2 * rows, rows)], copies.core)
    if fill is not None:
        fill()
    far.wait_recv()
    last = copies.start(whole.at[pl.ds(rows, rows)], whole.at[pl.ds(3 * rows, rows)], copies.core)
    first.wait_recv()
    last.wait_recv()


def quarter_at(place):
    tensor = lax.axis_index("tensor")
    return (tensor % 2 + place // 2) % 2 + 2 * ((tensor // 2 + place % 2) % 2)


def place_of(quarter):
    tensor = lax.axis_index("tensor")
    return 2 * ((tensor % 2 + quarter % 2) % 2) + (tensor // 2 + quarter // 2) % 2


def masked_scores(query, keys, start, scale):
    scores = dot(query, keys, 1, 1) * scale
    rows = lax.broadcasted_iota(jnp.int32, scores.shape, 0) + start
    cols = lax.broadcasted_iota(jnp.int32, scores.shape, 1)
    return jnp.where(cols <= rows, scores, NEGATIVE)


def kv_columns(heads):
    head = lax.axis_index("tensor") * heads // (HEADS // KV)
    return pl.ds(pl.multiple_of(head * HD, HD), HD)


def attend_kernel(tensors, line, heads, *refs):
    refs = list(refs)
    ins_there = [refs.pop(0) for _ in range(9)]
    own_weights = refs.pop(0) if line else None
    outs_there = [refs.pop(0) for _ in range(10)]
    arrived = refs.pop(0) if line else None
    ins, outs = [refs.pop(0) for _ in range(9)], [refs.pop(0) for _ in range(10)]
    stream, gain, w_query, w_key, w_value, cos, sin, grad, routes = ins
    attn_in, query, key, value, context, logsum, grad_rel, grad_pair, routes_own, routes_pair = outs
    local, send, recv = refs
    moves = Moves(local)
    moves.start(*zip(ins_there, ins))
    copies = Copies(tensors, send, recv)
    expert = lax.axis_index("expert")
    position = expert // 2
    copies.greet([copies.core, copies.mate], line)
    length = stream.shape[0]
    rows = length // 4
    if line:
        up = copies.along(
            own_weights, arrived.at[1 - (position + 2) // line], 1, position < line - 1, position > 0
        )
        down = copies.along(own_weights, arrived.at[0], -1, position > 0, position < line - 1)
    moves.wait()
    mates = []
    for place in range(4):
        at = pl.ds(place * rows, rows)
        grad_rel[at, :] = grad[pl.ds(pl.multiple_of(quarter_at(place) * rows, rows), rows), :]
        if place < 2:
            mates.append(copies.start(grad_rel.at[at], grad_pair.at[at], copies.mate))
    routes_own[...] = jnp.zeros(routes_own.shape, jnp.int32)
    for place in range(4):
        source = pl.ds(pl.multiple_of(quarter_at(place) * rows, rows), rows)
        routes_own[: routes.shape[0], place * rows : (place + 1) * rows] = routes[:, source]
    routes_copy = copies.start(routes_own, routes_pair, copies.mate)
    kv_at = kv_columns(heads)
    for tile in range(4):
        at = slice(tile * rows, (tile + 1) * rows)
        normed = rms_norm(stream[at, :].astype(F32), gain[...])[0].astype(BF16)
        attn_in[at, :] = normed
        proj = dot(normed, w_query[...], 1, 0)
        for head in range(heads):
            columns = slice(head * HD, (head + 1) * HD)
            query[at, columns] = turned(proj[:, columns], cos[at, :], sin[at, :]).astype(BF16)
        key[at, :] = turned(dot(normed, w_key[:, kv_at], 1, 0), cos[at, :], sin[at, :]).astype(BF16)
        value[at, :] = dot(normed, w_value[:, kv_at], 1, 0).astype(BF16)
    for tile in range(4):
        at, seen = slice(tile * rows, (tile + 1) * rows), (tile + 1) * rows
        to = pl.ds(pl.multiple_of(place_of(tile) * rows, rows), rows)
        for head in range(heads):
            columns = slice(head * HD, (head + 1) * HD)
            scores = masked_scores(query[at, columns], key[:seen, :], tile * rows, HD**-0.5)
            peak = jnp.max(scores, axis=-1, keepdims=True)
            exponent = jnp.exp(scores - peak)
            total = jnp.sum(exponent, axis=-1, keepdims=True)
            prob = (exponent / total).astype(BF16)
            context[to, columns] = dot(prob, value[:seen, :], 1, 0).astype(BF16)
            logsum[at, head : head + 1] = peak + jnp.log(total)
    pair_outs = (grad_pair, routes_pair)
    moves.start(*[pair for pair in zip(outs, outs_there) if all(pair[0] is not out for out in pair_outs)])
    cores = []
    for place in range(2):
        mates[place].wait_recv()
        source = grad_pair.at[pl.ds(place * rows, rows)]
        cores.append(copies.start(source, grad_pair.at[pl.ds((2 + place) * rows, rows)], copies.core))
    routes_copy.wait_recv()
    for copy in cores:
        copy.wait_recv()
    moves.start((grad_pair, outs_there[7]), (routes_pair, outs_there[9]))
    if line:
        up.wait_recv()
        down.wait_recv()
    moves.wait()
    copies.finish()


def anywhere():
    return pl.BlockSpec(memory_space=pl.ANY)


def attend(tensors, line, stream, gain, w_query, w_key, w_value, cos, sin, grad, routes, own_weights):
    length, width = stream.shape
    heads = w_query.shape[1] // HD
    outs = [
        ((length, width), BF16),
        ((length, heads * HD), BF16),
        ((length, HD), BF16),
        ((length, HD), BF16),
        ((length, heads * HD), BF16),
        ((length, HD), F32),
        ((length, width), BF16),
        ((length, width), BF16),
        ((8, length), routes.dtype),
        ((8, length), routes.dtype),
    ]
    operands = in_place([stream, gain, w_query, w_key, w_value, cos, sin, grad, routes])
    return pl.pallas_call(
        functools.partial(attend_kernel, tensors, line, heads),
        out_shape=[in_hbm(*out) for out in outs]
        + ([in_hbm((2,) + own_weights.shape, BF16)] if line else []),
        in_specs=[anywhere()] * (9 + bool(line)),
        out_specs=[anywhere()] * (10 + bool(line)),
        scratch_shapes=buffers_of(operands)
        + [pltpu.VMEM(*out) for out in outs]
        + [
            pltpu.SemaphoreType.DMA((19,)),
            pltpu.SemaphoreType.DMA((8,)),
            pltpu.SemaphoreType.DMA((8,)),
        ],
        compiler_params=pltpu.CompilerParams(
            collective_id=4, has_side_effects=True, vmem_limit_bytes=48 * 2**20
        ),
        cost_estimate=pl.CostEstimate(flops=4 * 10**10, bytes_accessed=10**7, transcendentals=0),
    )(*operands, *([own_weights] if line else []))


def attend_back(heads, grad, weight, query, key, value, logsum, cos, sin, grads, grads_rel, key_grad, value_grad):
    length = query.shape[0]
    rows = length // 4
    scale = HD**-0.5
    for tile in range(3, -1, -1):
        at, seen = slice(tile * rows, (tile + 1) * rows), (tile + 1) * rows
        to = pl.ds(pl.multiple_of(place_of(tile) * rows, rows), rows)
        grad_context = dot(grad[to, :], weight[...], 1, 1).astype(BF16)
        for head in range(heads):
            columns = slice(head * HD, (head + 1) * HD)
            head_query = query[at, columns]
            scores = masked_scores(head_query, key[:seen, :], tile * rows, scale)
            prob = jnp.exp(scores - logsum[at, head : head + 1])
            head_grad = grad_context[:, columns]
            dprob = dot(head_grad, value[:seen, :], 1, 1)
            delta = jnp.sum(prob * dprob, axis=-1, keepdims=True)
            dscore = (prob * (dprob - delta)).astype(BF16)
            dquery = dot(dscore, key[:seen, :], 1, 0) * scale
            dquery = turned(dquery, cos[at, :], sin[at, :], True).astype(BF16)
            grads[at, columns] = dquery
            grads_rel[to, columns] = dquery
            dkey = dot(dscore, head_query, 0, 0)
            dvalue = dot(prob.astype(BF16), head_grad, 0, 0)
            if tile == 3 and head == 0:
                key_grad[...] = dkey
                value_grad[...] = dvalue
            else:
                key_grad[:seen, :] += dkey
                value_grad[:seen, :] += dvalue
    for tile in range(4):
        at = slice(tile * rows, (tile + 1) * rows)
        to = pl.ds(pl.multiple_of(place_of(tile) * rows, rows), rows)
        dkey = turned(key_grad[at, :] * scale, cos[at, :], sin[at, :], True).astype(BF16)
        both = jnp.concatenate([dkey, value_grad[at, :].astype(BF16)], 1)
        grads[at, heads * HD :] = both
        grads_rel[to, heads * HD :] = both


def attend_out_kernel(tensors, line, *refs):
    refs = list(refs)
    ins_there, stream = [refs.pop(0) for _ in range(3)], refs.pop(0)
    arrived = refs.pop(0) if line else None
    outs_there = [refs.pop(0) for _ in range(3)]
    second = refs.pop(0) if line else None
    context, weight, gain = ins = [refs.pop(0) for _ in range(3)]
    own, pair, after = [refs.pop(0) for _ in range(3)]
    sent, got, crossing, crossed, stream_in, local, send, recv = refs
    copies = Copies(tensors, send, recv)
    moves = Moves(local)
    moves.start(*zip(ins_there, ins))
    position = lax.axis_index("expert") // 2
    copies.greet([copies.core, copies.far, copies.mate], line)
    rows = after.shape[0]
    quarter = pl.ds(pl.multiple_of(lax.axis_index("tensor") * rows, rows), rows)
    moves.start((stream.at[quarter], stream_in))
    if line:
        inner = (position > 0) & (position < line - 1)
        up = copies.along(arrived.at[1], second, 1, inner, position >= line // 2)
        down = copies.along(arrived.at[0], second, -1, inner, position < line // 2)

    def part(place):
        return dot(context[place * rows : (place + 1) * rows, :], weight[...], 1, 0)

    moves.wait()
    total = sum_quarter(copies, part, sent, got, crossing, crossed)
    total = stream_in[...].astype(F32) + total
    after[...] = total
    own[:rows, :] = rms_norm(total, gain[...])[0].astype(BF16)
    mate = copies.start(own.at[pl.ds(0, rows)], pair.at[pl.ds(0, rows)], copies.mate)
    moves.start((after, outs_there[2]))
    gather_quarters(copies, own, rows)
    mate.wait_recv()
    moves.start((own, outs_there[0]))
    if line:
        moves.start((pair, outs_there[1]))
        up.wait_recv()
        down.wait_recv()
    else:
        gather_quarters(copies, pair, rows)
        moves.start((pair, outs_there[1]))
    moves.wait()
    copies.finish()


def in_hbm(dims, dtype):
    return pltpu.HBM(dims, dtype)


def in_place(operands):
    return [pltpu.with_memory_space_constraint(o, pltpu.HBM) if o.size > 2**17 else o for o in operands]


def vmem():
    return pl.BlockSpec(memory_space=pltpu.VMEM)


def attend_out(tensors, line, context, weight, gain, stream, arrived):
    length, width = stream.shape
    rows = length // 4
    outs = [((length, width), BF16), ((rows if line else length, width), BF16), ((rows, width), F32)]
    operands = in_place([context, weight, gain])
    stream, *arrived = in_place([stream] + ([arrived] if line else []))
    return pl.pallas_call(
        functools.partial(attend_out_kernel, tensors, line),
        out_shape=[in_hbm(*out) for out in outs]
        + ([in_hbm(arrived[0].shape[1:], BF16)] if line else []),
        in_specs=[anywhere()] * (4 + bool(line)),
        out_specs=[anywhere()] * (3 + bool(line)),
        scratch_shapes=buffers_of(operands)
        + [pltpu.VMEM(*out) for out in outs]
        + [
            pltpu.VMEM((2 * rows, width), BF16),
            pltpu.VMEM((2 * rows, width), BF16),
            pltpu.VMEM((rows, width), BF16),
            pltpu.VMEM((rows, width), BF16),
            pltpu.VMEM((rows, width), BF16),
            pltpu.SemaphoreType.DMA((7,)),
            pltpu.SemaphoreType.DMA((12,)),
            pltpu.SemaphoreType.DMA((12,)),
        ],
        compiler_params=pltpu.CompilerParams(
            collective_id=1, has_side_effects=True, vmem_limit_bytes=40 * 2**20
        ),
        cost_estimate=pl.CostEstimate(flops=6 * 10**10, bytes_accessed=10**7, transcendentals=0),
    )(*operands, stream, *arrived)


def hidden_units(weight, tile, grad_tile, gate, hidden):
    pre = dot(weight[: 2 * hidden, :], tile, 1, 1)
    back = dot(weight[2 * hidden :, :], grad_tile, 1, 1)
    gate_pre, up_pre = pre[:hidden], pre[hidden:]
    sigmoid = jax.nn.sigmoid(gate_pre)
    activated = gate_pre * sigmoid
    hid = (activated * up_pre).astype(BF16).astype(F32)
    row = jnp.sum(hid * back, axis=0, keepdims=True)
    grad_hidden = back * gate
    grad_pre = jnp.concatenate(
        [
            (grad_hidden * up_pre * (sigmoid * (1.0 + gate_pre * (1.0 - sigmoid)))).astype(BF16),
            (grad_hidden * activated).astype(BF16),
        ],
        0,
    )
    return row, (hid * gate).astype(BF16), grad_pre


def slot_offset(slot, position, line):
    if slot == 0:
        return 0
    table = [row[slot - 1] for row in nearest_first(line)]
    offset = table[0]
    for place in range(1, line):
        offset = offset + (table[place] - table[place - 1]) * (position // place > 0)
    return offset


def first_pass_kernel(tensors, experts, line, hidden, *refs):
    refs = list(refs)
    router, routes_own, routes_pair = [refs.pop(0) for _ in range(3)]
    own_there, quarter, grad_own_there, grad_pair_there, own_weights, arrived, second = [
        refs.pop(0) for _ in range(7)
    ]
    pair_there = refs.pop(0)
    outs_there = [[refs.pop(0) for _ in range(7)] for _ in range(2)]
    last_weight, all_down = refs.pop(0), refs.pop(0)
    pair = refs.pop(0)
    outs = [[refs.pop(0) for _ in range(7)] for _ in range(2)]
    own, grad_own, grad_pair, weights, local, stores, send, recv = refs
    copies = Copies(tensors, send, recv)
    moves = Moves(stores)
    expert = lax.axis_index("expert")
    position, side = expert // 2, expert % 2
    copies.greet([copies.core, copies.far], line)
    rows = quarter.shape[0]
    inner = (position > 0) & (position < line - 1)
    outer = jnp.logical_not(inner)
    down = copies.along(second, weights.at[3], -1, position == 1, position == 0)
    up = copies.along(second, weights.at[3], 1, position == line - 2, position == line - 1)
    far = copies.start(quarter, pair.at[pl.ds(rows, rows)], copies.far)
    first = copies.start(quarter, pair.at[pl.ds(2 * rows, rows)], copies.core)

    def load(source, target, place):
        return pltpu.make_async_copy(source, target, local.at[place])

    loads = [
        load(own_weights, weights.at[0], 0),
        load(own_there, own, 1),
        load(grad_own_there, grad_own, 2),
        load(arrived.at[0], weights.at[1], 3),
    ]
    for copy in loads:
        copy.start()
    pl.when(inner)(lambda: load(arrived.at[1], weights.at[2], 4).start())
    pl.when(outer)(lambda: load(second, weights.at[2], 4).start())
    later = [load(quarter, pair.at[pl.ds(0, rows)], 5), load(grad_pair_there, grad_pair, 6)]
    for copy in later:
        copy.start()
    spare = load(second, weights.at[3], 7)
    pl.when(inner)(lambda: spare.start())
    names = [(position + slot_offset(slot, position, line)) * 2 + side for slot in range(line)]
    tile = 2 * rows

    def run(tokens, grads, routes, out, which):
        total_out, gated_out, grad_pre_out, rows_out, last_gate_out, probs_out, named_out = out
        at = pl.ds(which * tile, tile)
        tokens_tile, grad_tile = tokens[at, :], grads[at, :]
        logits = dot(router[...], tokens_tile, 1, 1)[:experts]
        logit_exp = jnp.exp(logits - jnp.max(logits, axis=0, keepdims=True))
        probs = logit_exp / jnp.sum(logit_exp, axis=0, keepdims=True)
        number = lax.broadcasted_iota(jnp.int32, probs.shape, 0)
        named = jnp.zeros(probs.shape, F32)
        for choice in range(routes.shape[0] // 2):
            named = jnp.where(routes[choice : choice + 1, at] == number, 1.0, named)
        gates = probs * named
        probs_out[:, at] = probs
        named_out[:, at] = named

        def gate_of(slot):
            return jnp.sum(jnp.where(number == names[slot], gates, 0.0), axis=0, keepdims=True)

        last_gate_out[0:1, at] = gate_of(line - 1)
        total = None
        for slot in range(line - 1):
            row, gated, grad_pre = hidden_units(
                weights.at[slot], tokens_tile, grad_tile, gate_of(slot), hidden
            )
            rows_out[slot : slot + 1, at] = row
            gated_out[slot * hidden : (slot + 1) * hidden, at] = gated
            grad_pre_out[2 * slot * hidden : 2 * (slot + 1) * hidden, at] = grad_pre
            part = dot(grad_pre, weights[slot, : 2 * hidden, :], 0, 0)
            total = part if total is None else total + part
        total_out[at, :] = total.astype(BF16)

    for copy in loads:
        copy.wait()
    load(second, weights.at[2], 4).wait()
    for which in range(2):
        run(own, grad_own, routes_own, outs[0], which)
    moves.start(*zip(outs[0], outs_there[0]))
    for slot in range(line - 1):
        moves.start((weights.at[slot, pl.ds(2 * hidden, hidden)], all_down.at[pl.ds(slot * hidden, hidden)]))
    far.wait_recv()
    last = copies.start(pair.at[pl.ds(rows, rows)], pair.at[pl.ds(3 * rows, rows)], copies.core)
    for copy in later:
        copy.wait()
    run(pair, grad_pair, routes_pair, outs[1], 0)
    first.wait_recv()
    last.wait_recv()
    run(pair, grad_pair, routes_pair, outs[1], 1)
    moves.start((pair, pair_there), *zip(outs[1], outs_there[1]))
    pl.when(inner)(lambda: spare.wait())
    up.wait_recv()
    down.wait_recv()
    slot = line - 1
    moves.start((weights.at[slot, pl.ds(2 * hidden, hidden)], all_down.at[pl.ds(slot * hidden, hidden)]))
    moves.start((weights.at[slot], last_weight))
    moves.wait()
    copies.finish()


def first_pass(tensors, experts, line, hidden, *operands):
    length, width = operands[3].shape
    operands = in_place(operands)
    count = line - 1
    out = [
        ((length, width), BF16),
        ((count * hidden, length), BF16),
        ((2 * count * hidden, length), BF16),
        ((8, length), F32),
        ((8, length), F32),
        ((experts, length), F32),
        ((experts, length), F32),
    ]
    tokens = pltpu.VMEM((length, width), BF16)
    whole = [((length, width), BF16)] + out * 2
    return pl.pallas_call(
        functools.partial(first_pass_kernel, tensors, experts, line, hidden),
        out_shape=[in_hbm(*o) for o in whole]
        + [in_hbm((3 * hidden, width), BF16), in_hbm((line * hidden, width), BF16)],
        in_specs=[vmem()] * 3 + [anywhere()] * 7,
        out_specs=[anywhere()] * 17,
        scratch_shapes=[pltpu.VMEM(*o) for o in whole]
        + [
            tokens,
            tokens,
            tokens,
            pltpu.VMEM((line, 3 * hidden, width), BF16),
            pltpu.SemaphoreType.DMA((8,)),
            pltpu.SemaphoreType.DMA((20,)),
            pltpu.SemaphoreType.DMA((5,)),
            pltpu.SemaphoreType.DMA((5,)),
        ],
        compiler_params=pltpu.CompilerParams(
            collective_id=5, has_side_effects=True, vmem_limit_bytes=63 * 2**20
        ),
        cost_estimate=pl.CostEstimate(flops=5 * 10**10, bytes_accessed=10**7, transcendentals=0),
    )(*operands)


def tokens_back_kernel(tensors, line, hidden, heads, *refs):
    refs = list(refs)
    gate_rows = [refs.pop(0) for _ in range(4 if line else 1)]
    probs_all, named_all, router, gain = [refs.pop(0) for _ in range(4)]
    ins_there = [refs.pop(0) for _ in range(11)]
    attn_in, grad_there, sent_pair, sent_own = [refs.pop(0) for _ in range(4)]
    factors = [refs.pop(0) for _ in range(12 if line else 0)]
    all_down = refs.pop(0) if line else None
    moe_own, moe_pair = (refs.pop(0), refs.pop(0)) if not line else (None, None)
    outs_there = [refs.pop(0) for _ in range(7)]
    partial_there, moe_got = refs.pop(0), refs.pop(0)
    if line:
        moe_own, moe_pair = refs.pop(0), refs.pop(0)
    weight_grads = [refs.pop(0) for _ in range(line)]
    lines_there = [refs.pop(0) for _ in range(2 if line else 0)]
    ins, outs = [refs.pop(0) for _ in range(11)], [refs.pop(0) for _ in range(7)]
    kept_pair, kept_own, after, w_output, query, key, value, logsum, cos, sin, context = ins
    grad_after, grad_router, grad_second, grads_rel, moe_out, moe_cross, mate_moe = outs
    whole, attn_grads, key_grad, value_grad, kv_sent, kv_got = [refs.pop(0) for _ in range(6)]
    moe_crossing, moe_crossed, grad, block, local, stores = [refs.pop(0) for _ in range(6)]
    if line:
        first_in, first_out, up_in, down_in, turning, down_in_place = [refs.pop(0) for _ in range(6)]
        going = first_in
    got_pair, got_own, crossing_pair, crossed_pair, crossing_own, crossed_own = [refs.pop(0) for _ in range(6)]
    mate_out, mate_in, rows_kept, rows_sent, rows_got = [refs.pop(0) for _ in range(5)]
    rows_crossing, rows_crossed, rows_mine, rows_mate, send, recv = refs
    copies = Copies(tensors, send, recv)
    moves = Moves(stores)
    rows = grad.shape[0]
    moves.start(*zip(ins_there, ins), (grad_there.at[pl.ds(0, rows)], grad))
    if line:
        moves.start((all_down, down_in_place))
    position = lax.axis_index("expert") // 2
    copies.greet([copies.core, copies.far, copies.mate], line)
    if line:
        for index, (first, last) in enumerate(zip(gate_rows[::2], gate_rows[1::2])):
            top, low = slice(index * line, (index + 1) * line - 1), slice((index + 1) * line - 1, (index + 1) * line)
            for half, out in enumerate((rows_kept, rows_sent)):
                columns = slice(2 * half * rows, 2 * (half + 1) * rows)
                out[top, :] = first[: line - 1, columns]
                out[low, :] = last[:, columns]
    else:
        rows_kept[...] = gate_rows[0][:, : 2 * rows]
        rows_sent[...] = gate_rows[0][:, 2 * rows :]
    probs, named = probs_all[:, :rows], named_all[:, :rows]
    moe_core = []

    def experts_out():
        if line:
            first_rows = (line - 1) * hidden

            def body(first, last, out):
                total = dot(first[...], down_in_place[:first_rows, :], 0, 0)
                out[...] = (total + dot(last[...], down_in_place[first_rows:, :], 0, 0)).astype(BF16)

            for gated, last, out in ((factors[2], factors[6], moe_own), (factors[3], factors[7], moe_pair)):
                pltpu.emit_pipeline(
                    body,
                    grid=(4,),
                    in_specs=[
                        pl.BlockSpec((first_rows, rows), lambda i: (0, i)),
                        pl.BlockSpec((hidden, rows), lambda i: (0, i)),
                    ],
                    out_specs=[pl.BlockSpec((rows, moe_own.shape[1]), lambda i: (i, 0))],
                )(gated, last, out)
        for side, source in enumerate((moe_own, moe_pair)):
            moe_core.append(
                copies.start(source.at[pl.ds(2 * rows, 2 * rows)], moe_got.at[side], copies.core)
            )

    def make_weight_grads(slots, factors, tokens):
        count = len(slots)
        length, width = tokens[0].shape
        tile = width // 6
        once = pl.Buffered(buffer_count=1)
        pre_spec = pl.BlockSpec((2 * hidden * count, length), lambda i: (0, 0), pipeline_mode=once)
        gated_spec = pl.BlockSpec((hidden * count, length), lambda i: (0, 0), pipeline_mode=once)
        token_spec = pl.BlockSpec((length, tile), lambda i: (0, i))

        def body(pre_own, pre_pair, gated_own, gated_pair, own, pair, grad_own, grad_pair, *outs):
            for index, out in enumerate(outs):
                pre = slice(2 * hidden * index, 2 * hidden * (index + 1))
                gated = slice(hidden * index, hidden * (index + 1))
                total = dot(pre_own[pre, :], own[...], 1, 0) + dot(pre_pair[pre, :], pair[...], 1, 0)
                out[: 2 * hidden, :] = total.astype(out.dtype)
                total = dot(gated_own[gated, :], grad_own[...], 1, 0)
                total = total + dot(gated_pair[gated, :], grad_pair[...], 1, 0)
                out[2 * hidden :, :] = total.astype(out.dtype)

        pltpu.emit_pipeline(
            body,
            grid=(6,),
            in_specs=[pre_spec] * 2 + [gated_spec] * 2 + [token_spec] * 4,
            out_specs=[pl.BlockSpec((3 * hidden, tile), lambda i: (0, i))] * count,
        )(*factors, *tokens, *[weight_grads[slot] for slot in slots])

    low, high = pl.ds(0, rows), pl.ds(rows, rows)
    pair_last = copies.start(sent_pair.at[high], got_pair.at[high], copies.core)
    pair_first = copies.start(sent_pair.at[low], got_pair.at[low], copies.core)
    rows_core = copies.start(rows_sent, rows_got, copies.core)
    own_last = copies.start(sent_own.at[high], got_own.at[high], copies.core)
    own_first = copies.start(sent_own.at[low], got_own.at[low], copies.core)
    if line:
        make_weight_grads([line - 1], factors[4:8], factors[8:])
        up = copies.along(weight_grads[-1], first_in, 1, position == 0, position == 1)
        down = copies.along(weight_grads[-1], first_in, -1, position == line - 1, position == line - 2)
        inner = (position > 0) & (position < line - 1)
    moves.wait()
    pair_last.wait_recv()
    crossing_pair[...] = (kept_pair[rows:, :].astype(F32) + got_pair[rows:, :].astype(F32)).astype(BF16)
    pair_far = copies.start(crossing_pair, crossed_pair, copies.far)
    rows_core.wait_recv()
    rows_crossing[...] = rows_kept[:, rows:] + rows_got[:, rows:]
    rows_far = copies.start(rows_crossing, rows_crossed, copies.far)
    pair_first.wait_recv()
    mine_pair = kept_pair[:rows, :].astype(F32) + got_pair[:rows, :].astype(F32)
    own_last.wait_recv()
    crossing_own[...] = (kept_own[rows:, :].astype(F32) + got_own[rows:, :].astype(F32)).astype(BF16)
    own_first.wait_recv()
    grad_tokens = kept_own[:rows, :].astype(F32) + got_own[:rows, :].astype(F32)
    if line:
        make_weight_grads(list(range(line - 1)), factors[:4], factors[8:])
    pair_far.wait_recv()
    own_far = copies.start(crossing_own, crossed_own, copies.far)
    mate_out[...] = (mine_pair + crossed_pair[...].astype(F32)).astype(BF16)
    mate = copies.start(mate_out, mate_in, copies.mate)
    rows_far.wait_recv()
    rows_mine[...] = rows_kept[:, :rows] + rows_got[:, :rows] + rows_crossed[...]
    rows_over = copies.start(rows_mine, rows_mate, copies.mate)
    experts_out()
    rows_over.wait_recv()
    count = rows_mine.shape[0] // 2
    slots = jnp.concatenate([rows_mine[:count, :], rows_mate[count:, :]], 0)
    dprobs = jnp.zeros(probs.shape, F32)
    number = lax.broadcasted_iota(jnp.int32, probs.shape, 0)
    chip_side = lax.axis_index("expert") % 2
    for slot in range(count):
        at = position + slot_offset(slot, position, line) if line else slot
        for half in range(2):
            name = at * 2 + chip_side + half - 2 * half * chip_side
            row = slots[half * count + slot : half * count + slot + 1, :]
            dprobs = jnp.where(number == name, row, dprobs)
    dprobs = dprobs * named
    dlogits = (
        probs * (dprobs - jnp.sum(probs * dprobs, axis=0, keepdims=True))
    ).astype(BF16)
    second_out, normed, inverse = rms_norm(after[...], gain[...])
    grad_router[...] = dot(dlogits, second_out.astype(BF16), 1, 0)
    grad_tokens = grad_tokens + dot(dlogits, router[...], 0, 0)
    own_far.wait_recv()
    grad_tokens = grad_tokens + crossed_own[...].astype(F32)
    mate.wait_recv()
    grad_tokens = grad_tokens + mate_in[...].astype(F32)
    through, second = norm_backward(grad_tokens, normed, inverse, gain[...])
    grad_second[...] = second[None]
    total = grad[...].astype(F32) + through
    grad_after[...] = total
    whole[:rows, :] = total.astype(BF16)
    moves.start(*zip(outs[:3], outs_there[:3]))
    moves.start((attn_in.at[pl.ds(0, 2 * rows)], got_pair), (attn_in.at[pl.ds(2 * rows, 2 * rows)], got_own))
    second = []

    def move(source, target, place):
        copy = pltpu.make_async_copy(source, target, local.at[place])
        copy.start()
        copy.wait()

    def moe_part(side, at):
        move((moe_own, moe_pair)[side].at[at], block.at[0], 0)
        move(moe_got.at[side, at], block.at[1], 0)
        return block[0].astype(F32) + block[1].astype(F32)

    def second_round():
        up.wait_recv()
        down.wait_recv()

        @pl.when(inner)
        def _():
            move(weight_grads[line - 1], first_out, 0)
            first_out[...] = (first_out[...].astype(F32) + first_in[...].astype(F32)).astype(BF16)

        @pl.when(jnp.logical_not(inner))
        def _():
            move(weight_grads[line - 2], first_out, 0)

        second.append(copies.along(first_out, up_in, 1, position < line // 2, inner))
        second.append(copies.along(first_out, down_in, -1, position >= line // 2, inner))

    def beside():
        if line:
            second_round()
        for copy in moe_core:
            copy.wait_recv()
        moe_crossing[...] = moe_part(1, pl.ds(rows, rows)).astype(BF16)
        moe_cross[...] = moe_part(0, pl.ds(rows, rows)).astype(BF16)
        moe_out[...] = after[...] + moe_part(0, pl.ds(0, rows))
        mate_moe[...] = moe_part(1, pl.ds(0, rows)).astype(BF16)

    gather_quarters(copies, whole, rows, beside)
    moe_far = copies.start(moe_crossing, moe_crossed, copies.far)
    attend_back(
        heads, whole, w_output, query, key, value, logsum, cos, sin, attn_grads, grads_rel, key_grad, value_grad
    )
    moves.start(*zip(outs[3:6], outs_there[3:6]))

    lead = lax.axis_index("tensor") % 2
    query_width = heads * HD
    first_rows = partial_there.shape[0] // 8
    kept_at = pl.ds(pl.multiple_of(query_width + lead * HD, HD), HD)
    sent_at = pl.ds(pl.multiple_of(query_width + (1 - lead) * HD, HD), HD)
    width = whole.shape[1]
    moves.wait()

    def by_columns(columns, grads_at):
        total = dot(got_pair[:, columns], attn_grads[: 2 * rows, grads_at], 0, 0)
        return total + dot(got_own[:, columns], attn_grads[2 * rows :, grads_at], 0, 0)

    for block_at in range(0, width, HD):
        columns = slice(block_at, block_at + HD)
        kv_sent[:, columns] = by_columns(columns, sent_at).astype(BF16)
    kv = copies.start(kv_sent, kv_got, copies.core)
    for block_at in range(0, width, query_width):
        columns = slice(block_at, block_at + query_width)
        query_block = by_columns(columns, slice(0, query_width)).astype(BF16)
        kept_pair[:first_rows, columns] = query_block[:first_rows]
        kept_pair[first_rows + HD : query_width + HD, columns] = query_block[first_rows:]
    kept_own[:query_width, :] = dot(context[...], whole[...], 0, 0).astype(BF16)
    kv.wait_recv()
    for block_at in range(0, width, HD):
        columns = slice(block_at, block_at + HD)
        kept = by_columns(columns, kept_at)
        kept_pair[first_rows : first_rows + HD, columns] = (kept + kv_got[:, columns].astype(F32)).astype(BF16)
    top = query_width + HD
    moves.start(
        (kept_pair.at[pl.ds(0, top)], partial_there.at[pl.ds(0, top)]),
        (kept_own.at[pl.ds(0, query_width)], partial_there.at[pl.ds(top, query_width)]),
    )
    moe_far.wait_recv()
    mate_moe[...] = (mate_moe[...].astype(F32) + moe_crossed[...].astype(F32)).astype(BF16)
    moves.start((mate_moe, outs_there[6]))
    if line:
        move(weight_grads[1], going, 0)
        move(weight_grads[2], turning, 0)
        for copy in second:
            copy.wait_recv()

        @pl.when(inner)
        def _():
            going[...] = (going[...].astype(F32) + up_in[...].astype(F32)).astype(BF16)
            turning[...] = (turning[...].astype(F32) + down_in[...].astype(F32)).astype(BF16)

        moves.start((going, lines_there[0]), (turning, lines_there[1]))
    moves.wait()
    copies.finish()


def tokens_back(tensors, experts, line, hidden, heads, length, width, *operands):
    rows = length // 4
    half = ((2 * rows, width), BF16)
    quarter = ((rows, width), BF16)
    shard = ((3 * hidden, width), BF16)
    small = ((experts, rows), F32)
    both = ((experts, 2 * rows), F32)
    outs = [
        ((rows, width), F32),
        ((experts, width), F32),
        ((1, width), F32),
        ((length, (heads + 2) * HD), BF16),
        ((rows, width), F32),
        quarter,
        quarter,
    ]
    there = [((2 * heads * HD + HD, width), BF16), ((2, 2 * rows, width), BF16)]
    if line:
        there += [((length, width), BF16)] * 2 + [((3 * hidden, width), F32)] + [shard] * (line - 1) + [shard] * 2
    first = 8 if line else 5
    scratch = outs + [
        ((length, width), BF16),
        ((length, (heads + 2) * HD), BF16),
        ((length, HD), F32),
        ((length, HD), F32),
        ((HD, width), BF16),
        ((HD, width), BF16),
        quarter,
        quarter,
        quarter,
        ((2, rows, width), BF16),
    ]
    later = [half, half] + [quarter] * 6 + [both, both, both] + [small] * 4
    if line:
        later = [shard] * 5 + [((line * hidden, width), BF16)] + later
    operands = in_place(operands)
    return pl.pallas_call(
        functools.partial(tokens_back_kernel, tensors, line, hidden, heads),
        out_shape=[in_hbm(*o) for o in outs + there],
        in_specs=[vmem()] * first + [anywhere()] * (len(operands) - first),
        out_specs=[anywhere()] * len(outs + there),
        scratch_shapes=buffers_of(operands[first : first + 11])
        + [pltpu.VMEM(*o) for o in scratch]
        + [pltpu.SemaphoreType.DMA((1,)), pltpu.SemaphoreType.DMA((32,))]
        + [pltpu.VMEM(*o) for o in later]
        + [pltpu.SemaphoreType.DMA((24,)), pltpu.SemaphoreType.DMA((24,))],
        compiler_params=pltpu.CompilerParams(
            collective_id=2, has_side_effects=True, vmem_limit_bytes=63 * 2**20
        ),
        cost_estimate=pl.CostEstimate(flops=10**11, bytes_accessed=10**7, transcendentals=0),
    )(*operands)


def line_sum(copies, line, partial_there, partial, whole, got, running, up_in, down_in):
    position, side = lax.axis_index("expert") // 2, lax.axis_index("expert") % 2
    count = partial.shape[0] // 2
    chunk = count // line
    order = [3 * (1 - position // 2), 2 - position // 2, position + 1 - 2 * (position % 2), position]
    over = []

    def rows_at(half, place):
        return pl.ds(pl.multiple_of(half * count + place * chunk, 16), chunk)

    def send_pair():
        for place in order:
            over.append(
                copies.start(partial_there.at[rows_at(1 - side, place)], got.at[rows_at(0, place)], copies.mate)
            )

    def part(place):
        mine = partial[rows_at(side, place), :].astype(F32)
        return mine + got[rows_at(0, place), :].astype(F32)

    flows = {1: {}, -1: {}}

    def reach_step(reach):
        over[line - 1 - reach].wait_recv()
        for way, (step, landed) in enumerate(((1, up_in), (-1, down_in))):
            target = position + step * reach
            sends = (target >= 0) & (target < line)
            origin = position - step
            receives = (origin >= 0) & (origin < line) & (origin + step * reach >= 0) & (origin + step * reach < line)
            slot = 3 * way + reach - 1
            if reach < line - 1:
                flows[step][reach + 1].wait_recv()

            @pl.when(sends)
            def _(slot=slot, target=target, landed=landed, step=step):
                running[slot] = part(target).astype(BF16)
                if reach < line - 1:

                    @pl.when((position - step >= 0) & (position - step < line))
                    def _():
                        total = part(target) + landed[reach].astype(F32)
                        running[slot] = total.astype(BF16)

            flows[step][reach] = copies.along(running.at[slot], landed.at[reach - 1], step, sends, receives)

    spread, mates = {}, {}

    def settle():
        over[line - 1].wait_recv()
        flows[1][1].wait_recv()
        flows[-1][1].wait_recv()
        total = part(position)
        total = total + jnp.where(position > 0, up_in[0].astype(F32), 0.0)
        total = total + jnp.where(position < line - 1, down_in[0].astype(F32), 0.0)
        here = rows_at(side, position)
        whole[here, :] = total.astype(BF16)
        mates[0] = [copies.start(whole.at[here], whole.at[here], copies.mate)]

    def spread_start(hop):
        spread[hop] = []
        for step in (1, -1):
            place = position - step * (hop - 1)
            sends = (place >= 0) & (place < line) & (position + step >= 0) & (position + step < line)
            origin = position - step * hop
            receives = (origin >= 0) & (origin < line)
            at = rows_at(side, jnp.clip(place, 0, line - 1))
            spread[hop].append(copies.along(whole.at[at], whole.at[at], step, sends, receives))

    def spread_end(hop):
        mates[hop] = []
        for step, copy in zip((1, -1), spread[hop]):
            copy.wait_recv()
            origin = position - step * hop
            there = (origin >= 0) & (origin < line)
            at = rows_at(side, jnp.clip(origin, 0, line - 1))
            mates[hop].append(copies.over_when(whole.at[at], whole.at[at], copies.mate, there))

    def mates_end(hop):
        for copy in mates[hop]:
            copy.wait_recv()

    return send_pair, reach_step, settle, spread_start, spread_end, mates_end


class SmallSum:
    def __init__(self, copies, devices, running, arrived, sums):
        self.copies, self.devices, self.running, self.arrived, self.sums = copies, devices, running, arrived, sums
        self.at, self.copy = 0, None

    def step(self):
        if self.copy is not None:
            self.copy.wait_recv()
            total = self.running[self.at] + self.arrived[self.at]
            self.at += 1
            self.copy = None
            if self.at == len(self.devices):
                self.sums[...] = total
            else:
                self.running[self.at] = total
        if self.at < len(self.devices):
            self.copy = self.copies.start(
                self.running.at[self.at], self.arrived.at[self.at], self.devices[self.at]
            )

    def end(self):
        while self.copy is not None:
            self.step()


class Gather:
    def __init__(self, copies, tensors, whole, rows):
        self.copies, self.whole, self.rows = copies, whole, rows
        tensor = lax.axis_index("tensor")
        self.mine = pl.ds(pl.multiple_of(tensor * rows, rows), rows)
        self.there = pl.ds(pl.multiple_of((tensor + tensors // 2) % tensors * rows, rows), rows)

    def start(self):
        self.far = self.copies.start(self.whole.at[self.mine], self.whole.at[self.mine], self.copies.far)
        self.first = self.copies.start(self.whole.at[self.mine], self.whole.at[self.mine], self.copies.core)

    def forward(self):
        self.far.wait_recv()
        self.last = self.copies.start(self.whole.at[self.there], self.whole.at[self.there], self.copies.core)

    def end(self):
        self.first.wait_recv()
        self.last.wait_recv()


def inputs_back_kernel(tensors, experts, line, hidden, *refs):
    refs = list(refs)
    gain, grad_router, grad_second = [refs.pop(0) for _ in range(3)]
    ins_there = [refs.pop(0) for _ in range(7)]
    moe_cross, mate_out, stream = [refs.pop(0) for _ in range(3)]
    own_sum, going, turning = [refs.pop(0) for _ in range(3)] if line else [None] * 3
    outs_there = [refs.pop(0) for _ in range(8 if line else 5)]
    ins, outs = [refs.pop(0) for _ in range(7)], [refs.pop(0) for _ in range(8 if line else 5)]
    grads_rel, w_query, w_key, w_value, grad_after, layer_part, partial = ins
    (whole, layer, sums, summed, kv_out), weight_outs = outs[:5], outs[5:]
    mate_in, moe_crossed, stream_in, local, stores = [refs.pop(0) for _ in range(5)]
    buffers = [refs.pop(0) for _ in range(4)] if line else []
    final, block = (refs.pop(0), refs.pop(0)) if line else (None, None)
    sent, got, crossing, crossed, running, arrived, send, recv = refs
    copies = Copies(tensors, send, recv)
    moves = Moves(stores)
    rows = grad_after.shape[0]
    quarter = pl.ds(pl.multiple_of(lax.axis_index("tensor") * rows, rows), rows)
    moves.start(*zip(ins_there, ins), (stream.at[quarter], stream_in))
    bits = [1 << k for k in range(experts.bit_length() - 1)]
    position = lax.axis_index("expert") // 2
    copies.greet([copies.core, copies.far] + [copies.across(bit) for bit in bits], line)
    lines = []
    moe_far = copies.start(moe_cross, moe_crossed, copies.far)
    if line:
        send_pair, reach_step, settle, spread_start, spread_end, mates_end = line_sum(
            copies, line, ins_there[6], partial, summed, *buffers
        )
        send_pair()
        end, inner = position == line - 1, (position > 0) & (position < line - 1)
        lines = [
            copies.along(going, final.at[0], 1, position < line - 1, position > 0),
            copies.along(going, final.at[1], -1, end, position == line - 2),
            copies.along(turning, final.at[1], -1, inner, position < line - 2),
        ]
    mate = copies.start(mate_out, mate_in, copies.mate)
    heads = w_query.shape[1] // HD
    query_width = heads * HD
    kv_rows = pl.ds(partial.shape[0] // 8, HD)
    kv_at = kv_columns(heads)
    moves.wait()

    def part(place):
        at = slice(place * rows, (place + 1) * rows)
        total = dot(grads_rel[at, :query_width], w_query[...], 1, 1)
        total = total + dot(grads_rel[at, query_width : query_width + HD], w_key[:, kv_at], 1, 1)
        return total + dot(grads_rel[at, query_width + HD :], w_value[:, kv_at], 1, 1)

    def beside():
        if line:
            reach_step(line - 1)

    grad_in = sum_quarter(copies, part, sent, got, crossing, crossed, beside)
    _, normed, inverse = rms_norm(stream_in[...].astype(F32), gain[...])
    through, first = norm_backward(grad_in, normed, inverse, gain[...])
    whole[quarter, :] = (grad_after[...] + through).astype(BF16)
    inputs_gather = Gather(copies, tensors, whole, rows)
    inputs_gather.start()
    running[0] = jnp.zeros(sums.shape, F32)
    running[0, :experts, :] = grad_router[...]
    running[0, experts : experts + 1, :] = grad_second[...]
    running[0, experts + 1 : experts + 2, :] = first[None]
    small = SmallSum(
        copies, [copies.core] + [copies.across(bit) for bit in bits] + [copies.far], running, arrived, sums
    )
    small.step()
    if line:
        for reach in range(line - 2, 0, -1):
            reach_step(reach)
            small.step()
    mate.wait_recv()
    moe_far.wait_recv()
    layer[quarter, :] = (
        layer_part[...] + moe_crossed[...].astype(F32) + mate_in[...].astype(F32)
    ).astype(BF16)
    layer_gather = Gather(copies, tensors, layer, rows)
    layer_gather.start()
    inputs_gather.forward()
    if line:
        settle()
        spread_start(1)
        small.step()
        spread_end(1)
        spread_start(2)
        small.step()
        spread_end(2)
        spread_start(3)
        small.step()
        for copy in lines:
            copy.wait_recv()
        for index, out in enumerate(weight_outs):
            at = pl.ds(index * hidden, hidden)
            move = pltpu.make_async_copy(own_sum.at[at], block, local.at[0])
            move.start()
            move.wait()
            total = block[...] + jnp.where(position > 0, final[0, at, :].astype(F32), 0.0)
            total = total + jnp.where(position < line - 1, final[1, at, :].astype(F32), 0.0)
            out[...] = total
            moves.start((out, outs_there[5 + index]))
        for hop in range(3):
            mates_end(hop)
        far = copies.start(summed.at[kv_rows], kv_out.at[0], copies.far)
        near = copies.start(summed.at[kv_rows], kv_out.at[1], copies.core)
        spread_end(3)
        layer_gather.forward()
        far.wait_recv()
        across = copies.start(kv_out.at[0], kv_out.at[2], copies.core)
        mates_end(3)
        near.wait_recv()
        across.wait_recv()
    else:
        layer_gather.forward()
        summed[...] = partial[...]
        kv_out[...] = jnp.zeros(kv_out.shape, BF16)
    small.end()
    moves.start((sums, outs_there[2]), (summed, outs_there[3]), (kv_out, outs_there[4]))
    inputs_gather.end()
    layer_gather.end()
    moves.start((whole, outs_there[0]), (layer, outs_there[1]))
    moves.wait()
    copies.finish()


def inputs_back(tensors, experts, line, hidden, heads, length, width, *operands):
    rows = length // 4
    early = (-(-(experts + 2) // 8) * 8, width)
    steps = 1 + experts.bit_length()
    projected = 2 * heads * HD + HD
    quarter, half = ((rows, width), BF16), ((2 * rows, width), BF16)
    outs = [
        ((length, width), BF16),
        ((length, width), BF16),
        (early, F32),
        ((projected, width), BF16),
        ((3, HD, width), BF16),
    ]
    buffers = []
    if line:
        chunk = projected // 2 // line
        buffers = [
            ((projected // 2, width), BF16),
            ((6, chunk, width), BF16),
            ((3, chunk, width), BF16),
            ((3, chunk, width), BF16),
            ((2, 3 * hidden, width), BF16),
            ((hidden, width), F32),
        ]
        outs = outs + [((hidden, width), F32)] * 3
    buffers += [half, half, quarter, quarter, ((steps,) + early, F32), ((steps,) + early, F32)]
    operands = in_place(operands)
    return pl.pallas_call(
        functools.partial(inputs_back_kernel, tensors, experts, line, hidden),
        out_shape=[in_hbm(*o) for o in outs],
        in_specs=[vmem()] * 3 + [anywhere()] * (len(operands) - 3),
        out_specs=[anywhere()] * len(outs),
        scratch_shapes=buffers_of(operands[3:10])
        + [pltpu.VMEM(*o) for o in outs + [quarter] * 3]
        + [pltpu.SemaphoreType.DMA((1,)), pltpu.SemaphoreType.DMA((16,))]
        + [pltpu.VMEM(*o) for o in buffers]
        + [pltpu.SemaphoreType.DMA((50 + steps,)), pltpu.SemaphoreType.DMA((50 + steps,))],
        compiler_params=pltpu.CompilerParams(
            collective_id=3, has_side_effects=True, vmem_limit_bytes=63 * 2**20
        ),
        cost_estimate=pl.CostEstimate(flops=10**11, bytes_accessed=10**7, transcendentals=0),
    )(*operands)


def shards(
    experts,
    tensors,
    inputs,
    routes,
    cotangent,
    first_gain,
    second_gain,
    w_query,
    w_key,
    w_value,
    w_output,
    w_router,
    w_gate,
    w_up,
    w_down,
):
    links = Links(experts, tensors)
    line, place, side = links.line, links.place, links.side
    length, width = inputs.shape
    heads = w_query.shape[1] // HD
    hidden = w_gate.shape[2]
    group = HEADS // KV
    kv_head = links.tensor * heads // group
    scale = HD ** (-0.5)
    order = nearest_first(line)

    own_weights = jnp.concatenate([w_gate[0].T, w_up[0].T, w_down[0]], 0)
    short = line if line == 4 else 0
    if not short:
        sides = [[2 * p + s for p in range(line)] for s in range(2)]
        weights = lax.all_gather(own_weights, "expert", axis_index_groups=sides)

    rows, half = length // 4, length // 2
    cos, sin = [jnp.asarray(table) for table in rotary_tables(length)]
    attn_in, query, key, value, context_rel, logsum, grad_rel, grad_pair, routes_own, routes_pair, *arrived = attend(
        tensors,
        short,
        inputs,
        first_gain[None],
        w_query,
        w_key,
        w_value,
        cos,
        sin,
        cotangent,
        routes.T,
        own_weights,
    )

    tokens_own, tokens_pair, after, *second = attend_out(
        tensors, short, context_rel, w_output, second_gain[None], inputs, *(arrived or [None])
    )
    router_rows = w_router.T
    if short:
        router_padded = jnp.concatenate([router_rows, router_rows], 0)
        tokens_pair, *outs, last_weight, all_down = first_pass(
            tensors,
            experts,
            line,
            hidden,
            router_padded,
            routes_own,
            routes_pair,
            tokens_own,
            tokens_pair,
            grad_rel,
            grad_pair,
            own_weights,
            arrived[0],
            second[0],
        )
        *first_own, last_gate_own, router_probs, named = outs[:7]
        *first_pair, last_gate_pair, _, _ = outs[7:]
    else:
        names = jnp.arange(experts, dtype=jnp.int32)[:, None, None]

        def gates_of(tokens, tokens_routes):
            logits = dot(router_rows, tokens, 1, 1)
            logit_exp = jnp.exp(logits - jnp.max(logits, axis=0, keepdims=True))
            probs = logit_exp / jnp.sum(logit_exp, axis=0, keepdims=True)
            named = jnp.any(tokens_routes[None] == names, axis=1).astype(F32)
            return probs, named, probs * named

        router_probs, named, gates_own = gates_of(tokens_own, routes_own[:4])
        _, _, gates_pair = gates_of(tokens_pair, routes_pair[:4])
    both_tokens, both_grads = (tokens_own, tokens_pair), (grad_rel, grad_pair)
    if short:
        last = line - 1
        only = jnp.zeros((1,), jnp.int32)
        kept_pair, sent_pair, *last_pair = expert_pass(
            tokens_pair, grad_pair, last_gate_pair, only, [last_weight], first_pair[0], True
        )
        kept_own, sent_own, *last_own = expert_pass(
            tokens_own, grad_rel, last_gate_own, only, [last_weight], first_own[0], True
        )
        gate_rows = [first_own[3], last_own[2], first_pair[3], last_pair[2]]
    else:
        zeros = jnp.zeros((length, width), BF16)

        def step(totals, weight_at):
            weight, position = weight_at
            name = (position * 2 + side)[None]
            down = weight[2 * hidden :]
            own = expert_pass(tokens_own, grad_rel, gates_own, name, [weight], totals[0])
            pair = expert_pass(tokens_pair, grad_pair, gates_pair, name, [weight], totals[1])
            grads = weight_grad(
                0, hidden, (own[2], pair[2]), (own[1], pair[1]), both_tokens, both_grads, BF16
            )
            moe_own = totals[2] + dot(own[1], down, 0, 0)
            moe_pair = totals[3] + dot(pair[1], down, 0, 0)
            return (own[0], pair[0], moe_own, moe_pair), (own[3][0], pair[3][0], grads)

        (sum_own, sum_pair, moe_own, moe_pair), (gate_own, gate_pair, weight_grads) = lax.scan(
            step,
            (zeros, zeros, zeros.astype(F32), zeros.astype(F32)),
            (weights, jnp.arange(line, dtype=jnp.int32)),
        )
        kept_own, sent_own, kept_pair, sent_pair = sum_own[:half], sum_own[half:], sum_pair[:half], sum_pair[half:]

    if short:
        factors = [first_own[2], first_pair[2], first_own[1], first_pair[1]]
        factors += [last_own[1], last_pair[1], last_own[0], last_pair[0], *both_tokens, *both_grads, all_down]
    else:
        gate_rows = [jnp.concatenate([gate_own, gate_pair], 0)]
        factors = [moe_own.astype(BF16), moe_pair.astype(BF16)]
    (
        grad_after,
        grad_router,
        grad_second,
        grads_rel,
        layer_part,
        moe_cross,
        mate_moe,
        partial,
        _,
        *weight_sums,
    ) = tokens_back(
        tensors,
        experts,
        short,
        hidden,
        heads,
        length,
        width,
        *gate_rows,
        router_probs,
        named,
        router_rows,
        second_gain[None],
        kept_pair,
        kept_own,
        after,
        w_output,
        query,
        key,
        value,
        logsum,
        cos,
        sin,
        context_rel,
        attn_in,
        grad_rel,
        sent_pair,
        sent_own,
        *factors,
    )

    line_sums = []
    if short:
        line_sums = [weight_sums[2], *weight_sums[-2:]]
    else:
        expert_grads = lax.psum_scatter(
            weight_grads, "expert", scatter_dimension=0, axis_index_groups=sides
        ).astype(F32)

    grad_inputs, layer_out, sums, summed, kv_rest, *weight_grads_out = inputs_back(
        tensors,
        experts,
        short,
        hidden,
        heads,
        length,
        width,
        first_gain[None],
        grad_router,
        grad_second,
        grads_rel,
        w_query,
        w_key,
        w_value,
        grad_after,
        layer_part,
        partial,
        moe_cross,
        mate_moe,
        inputs,
        *line_sums,
    )
    query_width = heads * HD
    first_rows = summed.shape[0] // 8
    kv_at = slice(first_rows, first_rows + HD)
    if short:
        kv_mine, (kv_far, kv_core, kv_across) = summed[kv_at], kv_rest
    else:
        summed = lax.psum(summed, "expert")
        kv_mine = summed[kv_at]
        kv_far = links.over_tensor(kv_mine, 2)
        kv_core, kv_across = links.over_tensor(kv_mine, 1), links.over_tensor(kv_far, 1)
    grad_query = jnp.concatenate([summed[:first_rows], summed[first_rows + HD : query_width + HD]], 0)

    def unfold(values):
        count, blocks = values.shape[0], values.shape[1] // values.shape[0]
        parts = [values[:, b * count : (b + 1) * count] for b in range(blocks)]
        return jnp.concatenate(parts, 0).astype(F32)

    grad_query = unfold(grad_query)
    grad_output = summed[query_width + HD :].astype(F32)
    lead, low_head = links.tensor % 2 == 0, kv_head == 0
    keys = jnp.where(lead, kv_mine, kv_core), jnp.where(lead, kv_far, kv_across)
    values = jnp.where(lead, kv_core, kv_mine), jnp.where(lead, kv_across, kv_far)
    grad_key, grad_value = [
        jnp.concatenate([unfold(jnp.where(low_head, near, far)), unfold(jnp.where(low_head, far, near))], 1)
        for near, far in (keys, values)
    ]
    if not short:
        weight_grads_out = [expert_grads[i * hidden : (i + 1) * hidden] for i in range(3)]
    grad_router, grad_second, grad_first = sums[:experts].T, sums[experts], sums[experts + 1]
    return (
        layer_out,
        grad_inputs,
        grad_first,
        grad_second,
        grad_query,
        grad_key,
        grad_value,
        grad_output,
        grad_router,
        weight_grads_out[0].T[None],
        weight_grads_out[1].T[None],
        weight_grads_out[2][None],
    )


def solution(mesh):
    experts, tensors = mesh.shape["expert"], mesh.shape["tensor"]
    in_specs = (
        P("expert", None),
        P("expert", None),
        P("expert", None),
        P(),
        P(),
        P(None, "tensor"),
        P(),
        P(),
        P("tensor", None),
        P(),
        P("expert", None, "tensor"),
        P("expert", None, "tensor"),
        P("expert", "tensor", None),
    )
    out_specs = (
        P("expert", None),
        P("expert", None),
        P(),
        P(),
        P(None, "tensor"),
        P(),
        P(),
        P("tensor", None),
        P(),
        P("expert", None, "tensor"),
        P("expert", None, "tensor"),
        P("expert", "tensor", None),
    )

    def run(*arrays):
        return shards(experts, tensors, *arrays)

    return jax.shard_map(run, mesh=mesh, in_specs=in_specs, out_specs=out_specs, check_vma=False)
```

```python
import functools

import jax
import jax.numpy as jnp
import numpy as np
from jax import lax
from jax.experimental import pallas as pl
from jax.experimental.pallas import tpu as pltpu
from jax.sharding import PartitionSpec as P

HEADS = 12
KV = 2
HD = 128
EPSILON = 1e-06
ROPE_BASE = 10000.0
NEGATIVE = -1e30
F32 = jnp.float32
BF16 = jnp.bfloat16


def dot(left, right, left_dim, right_dim):
    return lax.dot_general(
        left, right, (((left_dim,), (right_dim,)), ((), ())), preferred_element_type=F32
    )


def rms_norm(values, gain):
    inverse = lax.rsqrt(jnp.mean(values * values, axis=-1, keepdims=True) + EPSILON)
    normed = values * inverse
    return normed * gain, normed, inverse


def norm_backward(upstream, normed, inverse, gain):
    scaled = upstream * gain
    through = inverse * (scaled - normed * jnp.mean(scaled * normed, axis=-1, keepdims=True))
    return through, jnp.sum(upstream * normed, axis=0)


def rotary_tables(length):
    frequency = np.float32(ROPE_BASE) ** (-np.arange(HD // 2, dtype=np.float32) * np.float32(2.0 / HD))
    angles = np.arange(length, dtype=np.float32)[:, None] * frequency.astype(np.float32)[None]
    cos, sin = np.cos(angles), np.sin(angles)
    return np.concatenate([cos, cos], 1), np.concatenate([-sin, sin], 1)


def turned(values, cos, sin, back=False):
    other = pltpu.roll(values, HD // 2, 1) * sin
    return values * cos - other if back else values * cos + other


class Links:
    def __init__(self, experts, tensors):
        self.experts, self.tensors = experts, tensors
        self.line = experts // 2
        self.tensor = lax.axis_index("tensor")
        expert = lax.axis_index("expert")
        self.place, self.side = expert // 2, expert % 2

    def over_tensor(self, values, bit):
        return lax.ppermute(values, "tensor", [(i, i ^ bit) for i in range(self.tensors)])

    def over_expert(self, values, bit):
        return lax.ppermute(values, "expert", [(i, i ^ bit) for i in range(self.experts)])

    def over_pair(self, values):
        return self.over_expert(values, 1)

    def relative(self, values):
        rows = values.shape[0] // 4
        return jnp.concatenate(
            [
                lax.dynamic_slice_in_dim(values, (self.tensor ^ r) * rows, rows, 0)
                for r in (0, 2, 1, 3)
            ],
            0,
        )

    def absolute(self, values):
        rows = values.shape[0] // 4
        place = jnp.asarray([0, 2, 1, 3], jnp.int32)
        return jnp.concatenate(
            [
                lax.dynamic_slice_in_dim(values, place[self.tensor ^ q] * rows, rows, 0)
                for q in range(4)
            ],
            0,
        )

    def gather(self, quarter):
        both = jnp.concatenate([quarter, self.over_tensor(quarter, 2)], 0)
        return jnp.concatenate([both, self.over_tensor(both, 1)], 0)


def nearest_first(line):
    tables = []
    for place in range(line):
        offsets = [p - place for p in range(line) if p != place]
        tables.append(sorted(offsets, key=lambda o: (abs(o), -o)))
    return tables


def expert_kernel(count, hidden, split, prior, *refs):
    names, tokens, grads, gates = refs[:4]
    weights, refs = refs[4 : 4 + count], refs[4 + count :]
    if prior:
        before, refs = refs[0], refs[1:]
    outs, (gated_out, grad_pre_out, rows_out) = refs[: 2 if split else 1], refs[2 if split else 1 :]
    tile, grad_tile = tokens[...], grads[...]
    total = before[...].astype(F32) if prior else None
    for slot in range(count):
        weight = weights[slot]
        pre = dot(weight[: 2 * hidden, :], tile, 1, 1)
        back = dot(weight[2 * hidden :, :], grad_tile, 1, 1)
        gate = gates[pl.ds(names[slot], 1), :]
        gate_pre, up_pre = pre[:hidden], pre[hidden:]
        sigmoid = jax.nn.sigmoid(gate_pre)
        activated = gate_pre * sigmoid
        hid = (activated * up_pre).astype(BF16).astype(F32)
        rows_out[slot : slot + 1, :] = jnp.sum(hid * back, axis=0, keepdims=True)
        gated_out[slot * hidden : (slot + 1) * hidden, :] = (hid * gate).astype(BF16)
        grad_hidden = back * gate
        grad_pre = jnp.concatenate(
            [
                (grad_hidden * up_pre * (sigmoid * (1.0 + gate_pre * (1.0 - sigmoid)))).astype(BF16),
                (grad_hidden * activated).astype(BF16),
            ],
            0,
        )
        grad_pre_out[2 * slot * hidden : 2 * (slot + 1) * hidden, :] = grad_pre
        part = dot(grad_pre, weight[: 2 * hidden, :], 0, 0)
        total = part if total is None else total + part
    if split:
        for step in range(2):

            @pl.when(pl.program_id(0) == step)
            def _(step=step):
                outs[step][...] = total.astype(BF16)
    else:
        outs[0][...] = total.astype(BF16)


def expert_pass(tokens, grads, gates, names, weights, before=None, split=False):
    count, length, width = len(weights), tokens.shape[0], tokens.shape[1]
    hidden = weights[0].shape[0] // 3
    tile = length // 2
    token_spec = pl.BlockSpec((tile, width), lambda i, *_: (i, 0))
    half_spec = pl.BlockSpec((tile, width), lambda i, *_: (0, 0))

    def column_spec(rows):
        return pl.BlockSpec((rows, tile), lambda i, *_: (0, i))

    weight_spec = pl.BlockSpec((3 * hidden, width), lambda i, *_: (0, 0))
    token_shape = in_hbm((length, width), BF16)
    half_shape = in_hbm((tile, width), BF16)
    columns = [(count * hidden, BF16), (2 * count * hidden, BF16), (count, F32)]
    return pl.pallas_call(
        functools.partial(expert_kernel, count, hidden, split, before is not None),
        grid_spec=pltpu.PrefetchScalarGridSpec(
            num_scalar_prefetch=1,
            grid=(2,),
            in_specs=[token_spec, token_spec, column_spec(gates.shape[0])]
            + [weight_spec] * count
            + [token_spec] * (before is not None),
            out_specs=([half_spec] * 2 if split else [token_spec]) + [column_spec(r) for r, _ in columns],
        ),
        out_shape=([half_shape] * 2 if split else [token_shape])
        + [in_hbm((r, length), t) for r, t in columns],
        compiler_params=pltpu.CompilerParams(vmem_limit_bytes=48 * 2**20),
        cost_estimate=pl.CostEstimate(
            flops=2 * count * length * width * hidden * 5,
            bytes_accessed=(4 * length + 3 * hidden * count) * width * 2,
            transcendentals=0,
        ),
    )(names, *in_place([tokens, grads, gates, *weights] + ([before] if before is not None else [])))


def last_expert_kernel(hidden, weight, *refs):
    step = pl.program_id(0)
    weight_grad, total_grad = refs[-2:]

    @pl.when(step == 0)
    def _():
        total_grad[...] = jnp.zeros(total_grad.shape, F32)

    for side in range(2):
        tokens, grads, gate, before = refs[4 * side : 4 * side + 4]
        kept, sent, gated_out, row_out = refs[8 + 4 * side : 12 + 4 * side]

        @pl.when(step // 2 == side)
        def _(tokens=tokens, grads=grads, gate=gate, before=before, kept=kept, sent=sent, side=side,
              gated_out=gated_out, row_out=row_out):
            row, gated, grad_pre = hidden_units(weight, tokens[...], grads[...], gate[0:1, :], hidden)
            row_out[...] = row
            gated_out[...] = gated
            total_grad[: 2 * hidden, :] += dot(grad_pre, tokens[...], 1, 0)
            total_grad[2 * hidden :, :] += dot(gated, grads[...], 1, 0)
            total = (before[...].astype(F32) + dot(grad_pre, weight[: 2 * hidden, :], 0, 0)).astype(BF16)

            @pl.when(step % 2 == 0)
            def _():
                kept[...] = total

            @pl.when(step % 2 == 1)
            def _():
                sent[...] = total

    @pl.when(step == 3)
    def _():
        weight_grad[...] = total_grad[...].astype(BF16)


def last_expert(hidden, weight, pair, own):
    length, width = pair[0].shape
    tile = length // 2

    def specs(at):
        token = pl.BlockSpec((tile, width), lambda i: (at(i), 0))
        half = pl.BlockSpec((tile, width), lambda i: (0, 0))

        def column(rows):
            return pl.BlockSpec((rows, tile), lambda i: (0, at(i)))

        return [token, token, column(8), token], [half, half, column(hidden), column(1)]

    pair_ins, pair_outs = specs(lambda i: jnp.minimum(i, 1))
    own_ins, own_outs = specs(lambda i: jnp.maximum(i - 2, 0))
    shapes = [
        in_hbm((tile, width), BF16),
        in_hbm((tile, width), BF16),
        in_hbm((hidden, length), BF16),
        in_hbm((1, length), F32),
    ]
    whole = pl.BlockSpec((3 * hidden, width), lambda i: (0, 0))
    outs = pl.pallas_call(
        functools.partial(last_expert_kernel, hidden),
        grid=(4,),
        in_specs=[whole] + pair_ins + own_ins,
        out_specs=pair_outs + own_outs + [whole],
        out_shape=shapes * 2 + [in_hbm((3 * hidden, width), BF16)],
        scratch_shapes=[pltpu.VMEM((3 * hidden, width), F32)],
        compiler_params=pltpu.CompilerParams(vmem_limit_bytes=60 * 2**20),
        cost_estimate=pl.CostEstimate(
            flops=4 * length * width * hidden * 8,
            bytes_accessed=(8 * length + 3 * hidden) * width * 2,
            transcendentals=0,
        ),
    )(*in_place([weight, *pair, *own]))
    return outs[:4], outs[4:8], outs[8]


def weight_grad_kernel(grad_pre_own, grad_pre_pair, gated_own, gated_pair, own, pair, grad_own, grad_pair, out):
    rows = grad_pre_own.shape[0]
    out[:rows, :] = (
        dot(grad_pre_own[...], own[...], 1, 0) + dot(grad_pre_pair[...], pair[...], 1, 0)
    ).astype(out.dtype)
    out[rows:, :] = (
        dot(gated_own[...], grad_own[...], 1, 0) + dot(gated_pair[...], grad_pair[...], 1, 0)
    ).astype(out.dtype)


def weight_grad(slot, hidden, grad_pre, gated, tokens, grads, kept_as):
    length, width = tokens[0].shape
    tile = width // 3
    pre_spec = pl.BlockSpec((2 * hidden, length), lambda i: (slot, 0))
    gated_spec = pl.BlockSpec((hidden, length), lambda i: (slot, 0))
    token_spec = pl.BlockSpec((length, tile), lambda i: (0, i))
    return pl.pallas_call(
        weight_grad_kernel,
        grid=(3,),
        in_specs=[pre_spec] * 2 + [gated_spec] * 2 + [token_spec] * 4,
        out_specs=pl.BlockSpec((3 * hidden, tile), lambda i: (0, i)),
        out_shape=jax.ShapeDtypeStruct((3 * hidden, width), kept_as),
        compiler_params=pltpu.CompilerParams(vmem_limit_bytes=32 * 2**20),
        cost_estimate=pl.CostEstimate(
            flops=2 * 2 * length * width * hidden * 3,
            bytes_accessed=(4 * length + 6 * hidden) * width * 2,
            transcendentals=0,
        ),
    )(*grad_pre, *gated, *tokens, *grads)


MESH = pl.DeviceIdType.MESH


class Copies:
    def __init__(self, tensors, send, recv):
        self.send, self.recv, self.started, self.drained = send, recv, [], []
        expert, tensor = lax.axis_index("expert"), lax.axis_index("tensor")
        self.core = (expert, tensor + 1 - 2 * (tensor % 2))
        self.far = (expert, (tensor + tensors // 2) % tensors)
        self.mate = (expert + 1 - 2 * (expert % 2), tensor)

    def across(self, bit):
        expert, tensor = lax.axis_index("expert"), lax.axis_index("tensor")
        return (expert + bit - 2 * bit * (expert // bit % 2), tensor)

    def greet(self, partners, line=0):
        barrier = pltpu.get_barrier_semaphore()
        for partner in partners:
            pl.semaphore_signal(barrier, inc=1, device_id=partner, device_id_type=MESH)
        count = len(partners)
        if line:
            expert, tensor = lax.axis_index("expert"), lax.axis_index("tensor")
            position = expert // 2
            for step, there in ((2, position < line - 1), (-2, position > 0)):

                @pl.when(there)
                def _(step=step):
                    device = (expert + step, tensor)
                    pl.semaphore_signal(barrier, inc=1, device_id=device, device_id_type=MESH)

            count = count + 1 - (position + 1) // line + (position + line - 1) // line
        pl.semaphore_wait(barrier, count)

    def start(self, source, target, device):
        place = len(self.started)
        copy = pltpu.make_async_remote_copy(
            src_ref=source,
            dst_ref=target,
            send_sem=self.send.at[place],
            recv_sem=self.recv.at[place],
            device_id=device,
            device_id_type=MESH,
        )
        copy.start()
        self.started.append(copy)
        return copy

    def along(self, source, target, step, sends, receives):
        device = (lax.axis_index("expert") + 2 * step, lax.axis_index("tensor"))
        return self.over_when(source, target, device, sends, receives)

    def over_when(self, source, target, device, sends, receives=None):
        place = len(self.started)
        copy = pltpu.make_async_remote_copy(
            src_ref=source,
            dst_ref=target,
            send_sem=self.send.at[place],
            recv_sem=self.recv.at[place],
            device_id=device,
            device_id_type=MESH,
        )
        pl.when(sends)(lambda: copy.start())
        self.started.append(When(copy, sends, sends if receives is None else receives))
        return self.started[-1]

    def drain(self, copy):
        copy.wait_send()
        self.drained.append(copy)

    def finish(self):
        for copy in self.started:
            if all(copy is not done for done in self.drained):
                copy.wait_send()


class Moves:
    def __init__(self, semaphores):
        self.semaphores, self.count, self.open = semaphores, 0, []

    def start(self, *pairs):
        for source, target in pairs:
            copy = pltpu.make_async_copy(source, target, self.semaphores.at[self.count])
            copy.start()
            self.count += 1
            self.open.append(copy)

    def wait(self):
        for copy in self.open:
            copy.wait()
        self.open = []


def buffers_of(arrays):
    return [pltpu.VMEM(a.shape, a.dtype) for a in arrays]


class When:
    def __init__(self, copy, sends, receives):
        self.copy, self.sends, self.receives = copy, sends, receives

    def wait_send(self):
        pl.when(self.sends)(lambda: self.copy.wait_send())

    def wait_recv(self):
        pl.when(self.receives)(lambda: self.copy.wait_recv())


def sum_quarter(copies, part, sent, got, crossing, crossed, beside=None):
    rows = crossing.shape[0]
    sent[rows:, :] = part(3).astype(BF16)
    last = copies.start(sent.at[pl.ds(rows, rows)], got.at[pl.ds(rows, rows)], copies.core)
    sent[:rows, :] = part(2).astype(BF16)
    first = copies.start(sent.at[pl.ds(0, rows)], got.at[pl.ds(0, rows)], copies.core)
    other = part(1)
    last.wait_recv()
    crossing[...] = (other + got[rows:, :].astype(F32)).astype(BF16)
    far = copies.start(crossing, crossed, copies.far)
    if beside is not None:
        beside()
    mine = part(0)
    first.wait_recv()
    mine = mine + got[:rows, :].astype(F32)
    far.wait_recv()
    return mine + crossed[...].astype(F32)


def gather_quarters(copies, whole, rows, fill=None):
    far = copies.start(whole.at[pl.ds(0, rows)], whole.at[pl.ds(rows, rows)], copies.far)
    first = copies.start(whole.at[pl.ds(0, rows)], whole.at[pl.ds(2 * rows, rows)], copies.core)
    if fill is not None:
        fill()
    far.wait_recv()
    last = copies.start(whole.at[pl.ds(rows, rows)], whole.at[pl.ds(3 * rows, rows)], copies.core)
    first.wait_recv()
    last.wait_recv()


def quarter_at(place):
    tensor = lax.axis_index("tensor")
    return (tensor % 2 + place // 2) % 2 + 2 * ((tensor // 2 + place % 2) % 2)


def place_of(quarter):
    tensor = lax.axis_index("tensor")
    return 2 * ((tensor % 2 + quarter % 2) % 2) + (tensor // 2 + quarter // 2) % 2


def masked_scores(query, keys, start, scale):
    scores = dot(query, keys, 1, 1) * scale
    rows = lax.broadcasted_iota(jnp.int32, scores.shape, 0) + start
    cols = lax.broadcasted_iota(jnp.int32, scores.shape, 1)
    return jnp.where(cols <= rows, scores, NEGATIVE)


def kv_columns(heads):
    head = lax.axis_index("tensor") * heads // (HEADS // KV)
    return pl.ds(pl.multiple_of(head * HD, HD), HD)


def attend_kernel(tensors, line, heads, *refs):
    refs = list(refs)
    ins_there = [refs.pop(0) for _ in range(9)]
    own_weights = [refs.pop(0) for _ in range(3 if line else 0)]
    outs_there = [refs.pop(0) for _ in range(10)]
    arrived = refs.pop(0) if line else None
    ins, outs = [refs.pop(0) for _ in range(9)], [refs.pop(0) for _ in range(10)]
    stream, gain, w_query, w_key, w_value, cos, sin, grad, routes = ins
    attn_in, query, key, value, context, logsum, grad_rel, grad_pair, routes_own, routes_pair = outs
    local, send, recv = refs
    moves = Moves(local)
    moves.start(*zip(ins_there, ins))
    copies = Copies(tensors, send, recv)
    expert = lax.axis_index("expert")
    position = expert // 2
    copies.greet([copies.core, copies.mate], line)
    length = stream.shape[0]
    rows = length // 4
    if line:
        lines = []
        for index, weight in enumerate(own_weights):
            at = pl.ds(index * weight.shape[0], weight.shape[0])
            there = arrived.at[1 - (position + 2) // line, at]
            lines.append(copies.along(weight, there, 1, position < line - 1, position > 0))
            lines.append(copies.along(weight, arrived.at[0, at], -1, position > 0, position < line - 1))
    moves.wait()
    mates = []
    for place in range(4):
        at = pl.ds(place * rows, rows)
        grad_rel[at, :] = grad[pl.ds(pl.multiple_of(quarter_at(place) * rows, rows), rows), :]
        if place < 2:
            mates.append(copies.start(grad_rel.at[at], grad_pair.at[at], copies.mate))
    routes_own[...] = jnp.zeros(routes_own.shape, jnp.int32)
    for place in range(4):
        source = pl.ds(pl.multiple_of(quarter_at(place) * rows, rows), rows)
        routes_own[: routes.shape[0], place * rows : (place + 1) * rows] = routes[:, source]
    routes_copy = copies.start(routes_own, routes_pair, copies.mate)
    kv_at = kv_columns(heads)
    for tile in range(4):
        at = slice(tile * rows, (tile + 1) * rows)
        normed = rms_norm(stream[at, :].astype(F32), gain[...])[0].astype(BF16)
        attn_in[at, :] = normed
        proj = dot(normed, w_query[...], 1, 0)
        for head in range(heads):
            columns = slice(head * HD, (head + 1) * HD)
            query[at, columns] = turned(proj[:, columns], cos[at, :], sin[at, :]).astype(BF16)
        key[at, :] = turned(dot(normed, w_key[:, kv_at], 1, 0), cos[at, :], sin[at, :]).astype(BF16)
        value[at, :] = dot(normed, w_value[:, kv_at], 1, 0).astype(BF16)
    for tile in range(4):
        at, seen = slice(tile * rows, (tile + 1) * rows), (tile + 1) * rows
        to = pl.ds(pl.multiple_of(place_of(tile) * rows, rows), rows)
        for head in range(heads):
            columns = slice(head * HD, (head + 1) * HD)
            scores = masked_scores(query[at, columns], key[:seen, :], tile * rows, HD**-0.5)
            peak = jnp.max(scores, axis=-1, keepdims=True)
            exponent = jnp.exp(scores - peak)
            total = jnp.sum(exponent, axis=-1, keepdims=True)
            prob = (exponent / total).astype(BF16)
            context[to, columns] = dot(prob, value[:seen, :], 1, 0).astype(BF16)
            logsum[at, head : head + 1] = peak + jnp.log(total)
    pair_outs = (grad_pair, routes_pair)
    moves.start(*[pair for pair in zip(outs, outs_there) if all(pair[0] is not out for out in pair_outs)])
    cores = []
    for place in range(2):
        mates[place].wait_recv()
        source = grad_pair.at[pl.ds(place * rows, rows)]
        cores.append(copies.start(source, grad_pair.at[pl.ds((2 + place) * rows, rows)], copies.core))
    routes_copy.wait_recv()
    for copy in cores:
        copy.wait_recv()
    moves.start((grad_pair, outs_there[7]), (routes_pair, outs_there[9]))
    if line:
        for copy in lines:
            copy.wait_recv()
    moves.wait()
    copies.finish()


def anywhere():
    return pl.BlockSpec(memory_space=pl.ANY)


def attend(tensors, line, stream, gain, w_query, w_key, w_value, cos, sin, grad, routes, own_weights):
    length, width = stream.shape
    heads = w_query.shape[1] // HD
    outs = [
        ((length, width), BF16),
        ((length, heads * HD), BF16),
        ((length, HD), BF16),
        ((length, HD), BF16),
        ((length, heads * HD), BF16),
        ((length, HD), F32),
        ((length, width), BF16),
        ((length, width), BF16),
        ((8, length), routes.dtype),
        ((8, length), routes.dtype),
    ]
    operands = in_place([stream, gain, w_query, w_key, w_value, cos, sin, grad, routes])
    return pl.pallas_call(
        functools.partial(attend_kernel, tensors, line, heads),
        out_shape=[in_hbm(*out) for out in outs]
        + ([in_hbm((2, sum(w.shape[0] for w in own_weights), width), BF16)] if line else []),
        in_specs=[anywhere()] * (12 if line else 9),
        out_specs=[anywhere()] * (10 + bool(line)),
        scratch_shapes=buffers_of(operands)
        + [pltpu.VMEM(*out) for out in outs]
        + [
            pltpu.SemaphoreType.DMA((19,)),
            pltpu.SemaphoreType.DMA((12,)),
            pltpu.SemaphoreType.DMA((12,)),
        ],
        compiler_params=pltpu.CompilerParams(
            collective_id=4, has_side_effects=True, vmem_limit_bytes=48 * 2**20
        ),
        cost_estimate=pl.CostEstimate(flops=4 * 10**10, bytes_accessed=10**7, transcendentals=0),
    )(*operands, *(in_place(own_weights) if line else []))


def attend_back(
    tiles, heads, grad, weight, query, key, value, logsum, cos, sin, grads, grads_rel, key_grad, value_grad
):
    length = query.shape[0]
    rows = length // 4
    scale = HD**-0.5
    for tile in tiles:
        at, seen = slice(tile * rows, (tile + 1) * rows), (tile + 1) * rows
        to = pl.ds(pl.multiple_of(place_of(tile) * rows, rows), rows)
        grad_context = dot(grad[to, :], weight[...], 1, 1).astype(BF16)
        for head in range(heads):
            columns = slice(head * HD, (head + 1) * HD)
            head_query = query[at, columns]
            scores = masked_scores(head_query, key[:seen, :], tile * rows, scale)
            prob = jnp.exp(scores - logsum[at, head : head + 1])
            head_grad = grad_context[:, columns]
            dprob = dot(head_grad, value[:seen, :], 1, 1)
            delta = jnp.sum(prob * dprob, axis=-1, keepdims=True)
            dscore = (prob * (dprob - delta)).astype(BF16)
            dquery = dot(dscore, key[:seen, :], 1, 0) * scale
            dquery = turned(dquery, cos[at, :], sin[at, :], True).astype(BF16)
            grads[at, columns] = dquery
            grads_rel[to, columns] = dquery
            dkey = dot(dscore, head_query, 0, 0)
            dvalue = dot(prob.astype(BF16), head_grad, 0, 0)
            key_grad[:seen, :] += dkey
            value_grad[:seen, :] += dvalue


def attend_back_end(heads, cos, sin, grads, grads_rel, key_grad, value_grad):
    rows = grads.shape[0] // 4
    scale = HD**-0.5
    for tile in range(4):
        at = slice(tile * rows, (tile + 1) * rows)
        to = pl.ds(pl.multiple_of(place_of(tile) * rows, rows), rows)
        dkey = turned(key_grad[at, :] * scale, cos[at, :], sin[at, :], True).astype(BF16)
        both = jnp.concatenate([dkey, value_grad[at, :].astype(BF16)], 1)
        grads[at, heads * HD :] = both
        grads_rel[to, heads * HD :] = both


def attend_out_kernel(tensors, line, *refs):
    refs = list(refs)
    ins_there, stream = [refs.pop(0) for _ in range(3)], refs.pop(0)
    arrived = refs.pop(0) if line else None
    outs_there = [refs.pop(0) for _ in range(3)]
    second = refs.pop(0) if line else None
    context, weight, gain = ins = [refs.pop(0) for _ in range(3)]
    own, pair, after = [refs.pop(0) for _ in range(3)]
    sent, got, crossing, crossed, stream_in, local, send, recv = refs
    copies = Copies(tensors, send, recv)
    moves = Moves(local)
    moves.start(*zip(ins_there, ins))
    position = lax.axis_index("expert") // 2
    copies.greet([copies.core, copies.far, copies.mate], line)
    rows = after.shape[0]
    quarter = pl.ds(pl.multiple_of(lax.axis_index("tensor") * rows, rows), rows)
    moves.start((stream.at[quarter], stream_in))
    if line:
        inner = (position > 0) & (position < line - 1)
        up = copies.along(arrived.at[1], second, 1, inner, position >= line // 2)
        down = copies.along(arrived.at[0], second, -1, inner, position < line // 2)

    def part(place):
        return dot(context[place * rows : (place + 1) * rows, :], weight[...], 1, 0)

    moves.wait()
    total = sum_quarter(copies, part, sent, got, crossing, crossed)
    total = stream_in[...].astype(F32) + total
    after[...] = total
    own[:rows, :] = rms_norm(total, gain[...])[0].astype(BF16)
    mate = copies.start(own.at[pl.ds(0, rows)], pair.at[pl.ds(0, rows)], copies.mate)
    moves.start((after, outs_there[2]))
    gather_quarters(copies, own, rows)
    mate.wait_recv()
    moves.start((own, outs_there[0]))
    if line:
        moves.start((pair, outs_there[1]))
        up.wait_recv()
        down.wait_recv()
    else:
        gather_quarters(copies, pair, rows)
        moves.start((pair, outs_there[1]))
    moves.wait()
    copies.finish()


def in_hbm(dims, dtype):
    return pltpu.HBM(dims, dtype)


def in_place(operands):
    return [pltpu.with_memory_space_constraint(o, pltpu.HBM) if o.size >= 2**16 else o for o in operands]


def vmem():
    return pl.BlockSpec(memory_space=pltpu.VMEM)


def attend_out(tensors, line, context, weight, gain, stream, arrived):
    length, width = stream.shape
    rows = length // 4
    outs = [((length, width), BF16), ((rows if line else length, width), BF16), ((rows, width), F32)]
    operands = in_place([context, weight, gain])
    stream, *arrived = in_place([stream] + ([arrived] if line else []))
    return pl.pallas_call(
        functools.partial(attend_out_kernel, tensors, line),
        out_shape=[in_hbm(*out) for out in outs]
        + ([in_hbm(arrived[0].shape[1:], BF16)] if line else []),
        in_specs=[anywhere()] * (4 + bool(line)),
        out_specs=[anywhere()] * (3 + bool(line)),
        scratch_shapes=buffers_of(operands)
        + [pltpu.VMEM(*out) for out in outs]
        + [
            pltpu.VMEM((2 * rows, width), BF16),
            pltpu.VMEM((2 * rows, width), BF16),
            pltpu.VMEM((rows, width), BF16),
            pltpu.VMEM((rows, width), BF16),
            pltpu.VMEM((rows, width), BF16),
            pltpu.SemaphoreType.DMA((7,)),
            pltpu.SemaphoreType.DMA((12,)),
            pltpu.SemaphoreType.DMA((12,)),
        ],
        compiler_params=pltpu.CompilerParams(
            collective_id=1, has_side_effects=True, vmem_limit_bytes=40 * 2**20
        ),
        cost_estimate=pl.CostEstimate(flops=6 * 10**10, bytes_accessed=10**7, transcendentals=0),
    )(*operands, stream, *arrived)


def hidden_units(weight, tile, grad_tile, gate, hidden):
    pre = dot(weight[: 2 * hidden, :], tile, 1, 1)
    back = dot(weight[2 * hidden :, :], grad_tile, 1, 1)
    gate_pre, up_pre = pre[:hidden], pre[hidden:]
    sigmoid = jax.nn.sigmoid(gate_pre)
    activated = gate_pre * sigmoid
    hid = (activated * up_pre).astype(BF16).astype(F32)
    row = jnp.sum(hid * back, axis=0, keepdims=True)
    grad_hidden = back * gate
    grad_pre = jnp.concatenate(
        [
            (grad_hidden * up_pre * (sigmoid * (1.0 + gate_pre * (1.0 - sigmoid)))).astype(BF16),
            (grad_hidden * activated).astype(BF16),
        ],
        0,
    )
    return row, (hid * gate).astype(BF16), grad_pre


def slot_offset(slot, position, line):
    if slot == 0:
        return 0
    table = [row[slot - 1] for row in nearest_first(line)]
    offset = table[0]
    for place in range(1, line):
        offset = offset + (table[place] - table[place - 1]) * (position // place > 0)
    return offset


def first_pass_kernel(tensors, experts, line, hidden, *refs):
    refs = list(refs)
    router, routes_own, routes_pair = [refs.pop(0) for _ in range(3)]
    own_there, quarter, grad_own_there, grad_pair_there, arrived, second = [refs.pop(0) for _ in range(6)]
    own_weights = [refs.pop(0) for _ in range(3)]
    pair_there = refs.pop(0)
    outs_there = [[refs.pop(0) for _ in range(7)] for _ in range(2)]
    last_weight, all_down = refs.pop(0), refs.pop(0)
    pair = refs.pop(0)
    outs = [[refs.pop(0) for _ in range(7)] for _ in range(2)]
    own, grad_own, grad_pair, weights, local, stores, send, recv = refs
    copies = Copies(tensors, send, recv)
    moves = Moves(stores)
    expert = lax.axis_index("expert")
    position, side = expert // 2, expert % 2
    copies.greet([copies.core, copies.far], line)
    rows = quarter.shape[0]
    inner = (position > 0) & (position < line - 1)
    outer = jnp.logical_not(inner)
    down = copies.along(second, weights.at[3], -1, position == 1, position == 0)
    up = copies.along(second, weights.at[3], 1, position == line - 2, position == line - 1)
    far = copies.start(quarter, pair.at[pl.ds(rows, rows)], copies.far)
    first = copies.start(quarter, pair.at[pl.ds(2 * rows, rows)], copies.core)

    def load(source, target, place):
        return pltpu.make_async_copy(source, target, local.at[place])

    loads = [
        *[
            load(weight, weights.at[0, pl.ds(index * hidden, hidden)], (0, 8, 9)[index])
            for index, weight in enumerate(own_weights)
        ],
        load(own_there, own, 1),
        load(grad_own_there, grad_own, 2),
        load(arrived.at[0], weights.at[1], 3),
    ]
    for copy in loads:
        copy.start()
    pl.when(inner)(lambda: load(arrived.at[1], weights.at[2], 4).start())
    pl.when(outer)(lambda: load(second, weights.at[2], 4).start())
    later = [load(quarter, pair.at[pl.ds(0, rows)], 5), load(grad_pair_there, grad_pair, 6)]
    for copy in later:
        copy.start()
    spare = load(second, weights.at[3], 7)
    pl.when(inner)(lambda: spare.start())
    names = [(position + slot_offset(slot, position, line)) * 2 + side for slot in range(line)]
    tile = 2 * rows

    def run(tokens, grads, routes, out, which):
        total_out, gated_out, grad_pre_out, rows_out, last_gate_out, probs_out, named_out = out
        at = pl.ds(which * tile, tile)
        tokens_tile, grad_tile = tokens[at, :], grads[at, :]
        logits = dot(router[...], tokens_tile, 1, 1)[:experts]
        logit_exp = jnp.exp(logits - jnp.max(logits, axis=0, keepdims=True))
        probs = logit_exp / jnp.sum(logit_exp, axis=0, keepdims=True)
        number = lax.broadcasted_iota(jnp.int32, probs.shape, 0)
        named = jnp.zeros(probs.shape, F32)
        for choice in range(routes.shape[0] // 2):
            named = jnp.where(routes[choice : choice + 1, at] == number, 1.0, named)
        gates = probs * named
        probs_out[:, at] = probs
        named_out[:, at] = named

        def gate_of(slot):
            return jnp.sum(jnp.where(number == names[slot], gates, 0.0), axis=0, keepdims=True)

        last_gate_out[0:1, at] = gate_of(line - 1)
        total = None
        for slot in range(line - 1):
            row, gated, grad_pre = hidden_units(
                weights.at[slot], tokens_tile, grad_tile, gate_of(slot), hidden
            )
            rows_out[slot : slot + 1, at] = row
            gated_out[slot * hidden : (slot + 1) * hidden, at] = gated
            grad_pre_out[2 * slot * hidden : 2 * (slot + 1) * hidden, at] = grad_pre
            part = dot(grad_pre, weights[slot, : 2 * hidden, :], 0, 0)
            total = part if total is None else total + part
        total_out[at, :] = total.astype(BF16)

    for copy in loads:
        copy.wait()
    load(second, weights.at[2], 4).wait()
    for which in range(2):
        run(own, grad_own, routes_own, outs[0], which)
    moves.start(*zip(outs[0], outs_there[0]))
    for slot in range(line - 1):
        moves.start((weights.at[slot, pl.ds(2 * hidden, hidden)], all_down.at[pl.ds(slot * hidden, hidden)]))
    far.wait_recv()
    last = copies.start(pair.at[pl.ds(rows, rows)], pair.at[pl.ds(3 * rows, rows)], copies.core)
    for copy in later:
        copy.wait()
    run(pair, grad_pair, routes_pair, outs[1], 0)
    first.wait_recv()
    last.wait_recv()
    run(pair, grad_pair, routes_pair, outs[1], 1)
    moves.start((pair, pair_there), *zip(outs[1], outs_there[1]))
    pl.when(inner)(lambda: spare.wait())
    up.wait_recv()
    down.wait_recv()
    slot = line - 1
    moves.start((weights.at[slot, pl.ds(2 * hidden, hidden)], all_down.at[pl.ds(slot * hidden, hidden)]))
    moves.start((weights.at[slot], last_weight))
    moves.wait()
    copies.finish()


def first_pass(tensors, experts, line, hidden, *operands):
    length, width = operands[3].shape
    operands = in_place(operands)
    count = line - 1
    out = [
        ((length, width), BF16),
        ((count * hidden, length), BF16),
        ((2 * count * hidden, length), BF16),
        ((8, length), F32),
        ((8, length), F32),
        ((experts, length), F32),
        ((experts, length), F32),
    ]
    tokens = pltpu.VMEM((length, width), BF16)
    whole = [((length, width), BF16)] + out * 2
    return pl.pallas_call(
        functools.partial(first_pass_kernel, tensors, experts, line, hidden),
        out_shape=[in_hbm(*o) for o in whole]
        + [in_hbm((3 * hidden, width), BF16), in_hbm((line * hidden, width), BF16)],
        in_specs=[vmem()] * 3 + [anywhere()] * 9,
        out_specs=[anywhere()] * 17,
        scratch_shapes=[pltpu.VMEM(*o) for o in whole]
        + [
            tokens,
            tokens,
            tokens,
            pltpu.VMEM((line, 3 * hidden, width), BF16),
            pltpu.SemaphoreType.DMA((10,)),
            pltpu.SemaphoreType.DMA((20,)),
            pltpu.SemaphoreType.DMA((5,)),
            pltpu.SemaphoreType.DMA((5,)),
        ],
        compiler_params=pltpu.CompilerParams(
            collective_id=5, has_side_effects=True, vmem_limit_bytes=63 * 2**20
        ),
        cost_estimate=pl.CostEstimate(flops=5 * 10**10, bytes_accessed=10**7, transcendentals=0),
    )(*operands)


def tokens_back_kernel(tensors, line, hidden, heads, *refs):
    refs = list(refs)
    gate_rows = [refs.pop(0) for _ in range(4 if line else 1)]
    probs_all, named_all, router, gain = [refs.pop(0) for _ in range(4)]
    ins_there = [refs.pop(0) for _ in range(11)]
    attn_in, grad_there, sent_pair, sent_own = [refs.pop(0) for _ in range(4)]
    factors = [refs.pop(0) for _ in range(10 if line else 0)]
    all_down, last_grad = (refs.pop(0), refs.pop(0)) if line else (None, None)
    moe_own, moe_pair = (refs.pop(0), refs.pop(0)) if not line else (None, None)
    outs_there = [refs.pop(0) for _ in range(6)]
    partial_there, moe_got = refs.pop(0), refs.pop(0)
    if line:
        moe_own, moe_pair = refs.pop(0), refs.pop(0)
    weight_grads = [refs.pop(0) for _ in range(line - 1 if line else 0)]
    lines_there = [refs.pop(0) for _ in range(2 if line else 0)]
    ins, outs = [refs.pop(0) for _ in range(11)], [refs.pop(0) for _ in range(6)]
    kept_pair, kept_own, after, w_output, query, key, value, logsum, cos, sin, context = ins
    grad_after, grad_router, grad_second, grads_rel, moe_out, moe_cross = outs
    whole, attn_grads, key_grad, value_grad, kv_got = [refs.pop(0) for _ in range(5)]
    moe_half, moe_mate, grad, block, local, stores = [refs.pop(0) for _ in range(6)]
    if line:
        first_in, first_out, up_in, down_in, turning, down_in_place = [refs.pop(0) for _ in range(6)]
        going = first_in
    got_pair, got_own, crossing_pair, crossed_pair, crossing_own, crossed_own = [refs.pop(0) for _ in range(6)]
    mate_out, mate_in, rows_kept, rows_sent, rows_got = [refs.pop(0) for _ in range(5)]
    rows_crossing, rows_crossed, rows_mine, rows_mate, send, recv = refs
    copies = Copies(tensors, send, recv)
    moves = Moves(stores)
    rows = grad.shape[0]
    moves.start(*zip(ins_there, ins), (grad_there.at[pl.ds(0, rows)], grad))
    if line:
        moves.start((all_down, down_in_place))
    position = lax.axis_index("expert") // 2
    copies.greet([copies.core, copies.far, copies.mate], line)
    if line:
        for index, (first, last) in enumerate(zip(gate_rows[::2], gate_rows[1::2])):
            top, low = slice(index * line, (index + 1) * line - 1), slice((index + 1) * line - 1, (index + 1) * line)
            for half, out in enumerate((rows_kept, rows_sent)):
                columns = slice(2 * half * rows, 2 * (half + 1) * rows)
                out[top, :] = first[: line - 1, columns]
                out[low, :] = last[:, columns]
    else:
        rows_kept[...] = gate_rows[0][:, : 2 * rows]
        rows_sent[...] = gate_rows[0][:, 2 * rows :]
    probs, named = probs_all[:, :rows], named_all[:, :rows]
    moe_core = []

    def experts_out():
        if line:
            first_rows = (line - 1) * hidden

            def body(first, last, out):
                total = dot(first[...], down_in_place[:first_rows, :], 0, 0)
                out[...] = (total + dot(last[...], down_in_place[first_rows:, :], 0, 0)).astype(BF16)

            for gated, last, out in ((factors[2], factors[4], moe_own), (factors[3], factors[5], moe_pair)):
                pltpu.emit_pipeline(
                    body,
                    grid=(4,),
                    in_specs=[
                        pl.BlockSpec((first_rows, rows), lambda i: (0, i)),
                        pl.BlockSpec((hidden, rows), lambda i: (0, i)),
                    ],
                    out_specs=[pl.BlockSpec((rows, moe_own.shape[1]), lambda i: (i, 0))],
                )(gated, last, out)
        for side, source in enumerate((moe_own, moe_pair)):
            moe_core.append(
                copies.start(source.at[pl.ds(2 * rows, 2 * rows)], moe_got.at[side], copies.core)
            )

    def make_weight_grads(slots, factors, tokens):
        count = len(slots)
        length, width = tokens[0].shape
        tile = width // 6
        once = pl.Buffered(buffer_count=1)
        pre_spec = pl.BlockSpec((2 * hidden * count, length), lambda i: (0, 0), pipeline_mode=once)
        gated_spec = pl.BlockSpec((hidden * count, length), lambda i: (0, 0), pipeline_mode=once)
        token_spec = pl.BlockSpec((length, tile), lambda i: (0, i))

        def body(pre_own, pre_pair, gated_own, gated_pair, own, pair, grad_own, grad_pair, *outs):
            for index, out in enumerate(outs):
                pre = slice(2 * hidden * index, 2 * hidden * (index + 1))
                gated = slice(hidden * index, hidden * (index + 1))
                total = dot(pre_own[pre, :], own[...], 1, 0) + dot(pre_pair[pre, :], pair[...], 1, 0)
                out[: 2 * hidden, :] = total.astype(out.dtype)
                total = dot(gated_own[gated, :], grad_own[...], 1, 0)
                total = total + dot(gated_pair[gated, :], grad_pair[...], 1, 0)
                out[2 * hidden :, :] = total.astype(out.dtype)

        pltpu.emit_pipeline(
            body,
            grid=(6,),
            in_specs=[pre_spec] * 2 + [gated_spec] * 2 + [token_spec] * 4,
            out_specs=[pl.BlockSpec((3 * hidden, tile), lambda i: (0, i))] * count,
        )(*factors, *tokens, *[weight_grads[slot] for slot in slots])

    low, high = pl.ds(0, rows), pl.ds(rows, rows)
    pair_last = copies.start(sent_pair.at[high], got_pair.at[high], copies.core)
    pair_first = copies.start(sent_pair.at[low], got_pair.at[low], copies.core)
    rows_core = copies.start(rows_sent, rows_got, copies.core)
    own_last = copies.start(sent_own.at[high], got_own.at[high], copies.core)
    own_first = copies.start(sent_own.at[low], got_own.at[low], copies.core)
    if line:
        up = copies.along(last_grad, first_in, 1, position == 0, position == 1)
        down = copies.along(last_grad, first_in, -1, position == line - 1, position == line - 2)
        inner = (position > 0) & (position < line - 1)
    moves.wait()
    pair_last.wait_recv()
    crossing_pair[...] = (kept_pair[rows:, :].astype(F32) + got_pair[rows:, :].astype(F32)).astype(BF16)
    pair_far = copies.start(crossing_pair, crossed_pair, copies.far)
    rows_core.wait_recv()
    rows_crossing[...] = rows_kept[:, rows:] + rows_got[:, rows:]
    rows_far = copies.start(rows_crossing, rows_crossed, copies.far)
    pair_first.wait_recv()
    mine_pair = kept_pair[:rows, :].astype(F32) + got_pair[:rows, :].astype(F32)
    own_last.wait_recv()
    crossing_own[...] = (kept_own[rows:, :].astype(F32) + got_own[rows:, :].astype(F32)).astype(BF16)
    own_first.wait_recv()
    grad_tokens = kept_own[:rows, :].astype(F32) + got_own[:rows, :].astype(F32)
    if line:
        make_weight_grads(list(range(line - 1)), factors[:4], factors[6:])
    pair_far.wait_recv()
    own_far = copies.start(crossing_own, crossed_own, copies.far)
    mate_out[...] = (mine_pair + crossed_pair[...].astype(F32)).astype(BF16)
    mate = copies.start(mate_out, mate_in, copies.mate)
    rows_far.wait_recv()
    rows_mine[...] = rows_kept[:, :rows] + rows_got[:, :rows] + rows_crossed[...]
    rows_over = copies.start(rows_mine, rows_mate, copies.mate)
    def move(source, target, place):
        copy = pltpu.make_async_copy(source, target, local.at[place])
        copy.start()
        copy.wait()

    def moe_part(side, at):
        move((moe_own, moe_pair)[side].at[at], block.at[0], 0)
        move(moe_got.at[side, at], block.at[1], 0)
        return block[0].astype(F32) + block[1].astype(F32)

    experts_out()
    for copy in moe_core:
        copy.wait_recv()
    for place in range(2):
        moe_half[place] = moe_part(1, pl.ds(place * rows, rows)).astype(BF16)
    rows_over.wait_recv()
    count = rows_mine.shape[0] // 2
    slots = jnp.concatenate([rows_mine[:count, :], rows_mate[count:, :]], 0)
    dprobs = jnp.zeros(probs.shape, F32)
    number = lax.broadcasted_iota(jnp.int32, probs.shape, 0)
    chip_side = lax.axis_index("expert") % 2
    for slot in range(count):
        at = position + slot_offset(slot, position, line) if line else slot
        for half in range(2):
            name = at * 2 + chip_side + half - 2 * half * chip_side
            row = slots[half * count + slot : half * count + slot + 1, :]
            dprobs = jnp.where(number == name, row, dprobs)
    dprobs = dprobs * named
    dlogits = (
        probs * (dprobs - jnp.sum(probs * dprobs, axis=0, keepdims=True))
    ).astype(BF16)
    second_out, normed, inverse = rms_norm(after[...], gain[...])
    grad_router[...] = dot(dlogits, second_out.astype(BF16), 1, 0)
    grad_tokens = grad_tokens + dot(dlogits, router[...], 0, 0)
    own_far.wait_recv()
    grad_tokens = grad_tokens + crossed_own[...].astype(F32)
    mate.wait_recv()
    moe_over = copies.start(moe_half, moe_mate, copies.mate)
    grad_tokens = grad_tokens + mate_in[...].astype(F32)
    through, second = norm_backward(grad_tokens, normed, inverse, gain[...])
    grad_second[...] = second[None]
    total = grad[...].astype(F32) + through
    grad_after[...] = total
    whole[:rows, :] = total.astype(BF16)
    moves.start(*zip(outs[:3], outs_there[:3]))
    moves.start((attn_in.at[pl.ds(0, 2 * rows)], got_pair), (attn_in.at[pl.ds(2 * rows, 2 * rows)], got_own))
    second = []

    def second_round():
        up.wait_recv()
        down.wait_recv()

        @pl.when(inner)
        def _():
            move(last_grad, first_out, 0)
            first_out[...] = (first_out[...].astype(F32) + first_in[...].astype(F32)).astype(BF16)

        @pl.when(jnp.logical_not(inner))
        def _():
            move(weight_grads[line - 2], first_out, 0)

        second.append(copies.along(first_out, up_in, 1, position < line // 2, inner))
        second.append(copies.along(first_out, down_in, -1, position >= line // 2, inner))

    def beside():
        if line:
            second_round()
        moe_cross[...] = moe_part(0, pl.ds(rows, rows)).astype(BF16)
        moe_out[...] = after[...] + moe_part(0, pl.ds(0, rows))

    far = copies.start(whole.at[pl.ds(0, rows)], whole.at[pl.ds(rows, rows)], copies.far)
    first = copies.start(whole.at[pl.ds(0, rows)], whole.at[pl.ds(2 * rows, rows)], copies.core)
    beside()
    key_grad[...] = jnp.zeros(key_grad.shape, F32)
    value_grad[...] = jnp.zeros(value_grad.shape, F32)
    attention = [w_output, query, key, value, logsum, cos, sin, attn_grads, grads_rel, key_grad, value_grad]
    low_half = lax.axis_index("tensor") // 2 == 0
    high_half = lax.axis_index("tensor") // 2 > 0
    first.wait_recv()
    pl.when(low_half)(lambda: attend_back((1, 0), heads, whole, *attention))
    pl.when(high_half)(lambda: attend_back((3, 2), heads, whole, *attention))
    far.wait_recv()
    last = copies.start(whole.at[pl.ds(rows, rows)], whole.at[pl.ds(3 * rows, rows)], copies.core)
    last.wait_recv()
    pl.when(low_half)(lambda: attend_back((3, 2), heads, whole, *attention))
    pl.when(high_half)(lambda: attend_back((1, 0), heads, whole, *attention))
    attend_back_end(heads, cos, sin, attn_grads, grads_rel, key_grad, value_grad)
    moves.start((grads_rel, outs_there[3]))

    lead = lax.axis_index("tensor") % 2
    query_width = heads * HD
    first_rows = partial_there.shape[0] // 8
    kept_at = pl.ds(pl.multiple_of(query_width + lead * HD, HD), HD)
    sent_at = pl.ds(pl.multiple_of(query_width + (1 - lead) * HD, HD), HD)
    width = whole.shape[1]
    moves.wait()

    def by_columns(columns, grads_at):
        total = dot(got_pair[:, columns], attn_grads[: 2 * rows, grads_at], 0, 0)
        return total + dot(got_own[:, columns], attn_grads[2 * rows :, grads_at], 0, 0)

    copies.drain(pair_far)
    for block_at in range(0, width, HD):
        columns = slice(block_at, block_at + HD)
        crossing_pair[:HD, columns] = by_columns(columns, sent_at).astype(BF16)
    kv = copies.start(crossing_pair.at[pl.ds(0, HD)], kv_got, copies.core)
    for block_at in range(0, width, query_width):
        columns = slice(block_at, block_at + query_width)
        query_block = by_columns(columns, slice(0, query_width)).astype(BF16)
        kept_pair[:first_rows, columns] = query_block[:first_rows]
        kept_pair[first_rows + HD : query_width + HD, columns] = query_block[first_rows:]
    kept_own[:query_width, :] = dot(context[...], whole[...], 0, 0).astype(BF16)
    kv.wait_recv()
    for block_at in range(0, width, HD):
        columns = slice(block_at, block_at + HD)
        kept = by_columns(columns, kept_at)
        kept_pair[first_rows : first_rows + HD, columns] = (kept + kv_got[:, columns].astype(F32)).astype(BF16)
    top = query_width + HD
    moves.start(
        (kept_pair.at[pl.ds(0, top)], partial_there.at[pl.ds(0, top)]),
        (kept_own.at[pl.ds(0, query_width)], partial_there.at[pl.ds(top, query_width)]),
    )
    moe_over.wait_recv()
    moe_out[...] += moe_mate[0].astype(F32)
    moe_cross[...] = (moe_cross[...].astype(F32) + moe_mate[1].astype(F32)).astype(BF16)
    moves.start(*zip(outs[4:], outs_there[4:]))
    if line:
        move(weight_grads[1], going, 0)
        move(weight_grads[2], turning, 0)
        for copy in second:
            copy.wait_recv()

        @pl.when(inner)
        def _():
            going[...] = (going[...].astype(F32) + up_in[...].astype(F32)).astype(BF16)
            turning[...] = (turning[...].astype(F32) + down_in[...].astype(F32)).astype(BF16)

        moves.start((going, lines_there[0]), (turning, lines_there[1]))
    moves.wait()
    copies.finish()


def tokens_back(tensors, experts, line, hidden, heads, length, width, *operands):
    rows = length // 4
    half = ((2 * rows, width), BF16)
    quarter = ((rows, width), BF16)
    shard = ((3 * hidden, width), BF16)
    small = ((experts, rows), F32)
    both = ((experts, 2 * rows), F32)
    outs = [
        ((rows, width), F32),
        ((experts, width), F32),
        ((1, width), F32),
        ((length, (heads + 2) * HD), BF16),
        ((rows, width), F32),
        quarter,
    ]
    there = [((2 * heads * HD + HD, width), BF16), ((2, 2 * rows, width), BF16)]
    if line:
        there += [((length, width), BF16)] * 2 + [((3 * hidden, width), F32)] + [shard] * (line - 2) + [shard] * 2
    first = 8 if line else 5
    scratch = outs + [
        ((length, width), BF16),
        ((length, (heads + 2) * HD), BF16),
        ((length, HD), F32),
        ((length, HD), F32),
        ((HD, width), BF16),
        ((2, rows, width), BF16),
        ((2, rows, width), BF16),
        quarter,
        ((2, rows, width), BF16),
    ]
    later = [half, half] + [quarter] * 6 + [both, both, both] + [small] * 4
    if line:
        later = [shard] * 5 + [((line * hidden, width), BF16)] + later
    operands = in_place(operands)
    return pl.pallas_call(
        functools.partial(tokens_back_kernel, tensors, line, hidden, heads),
        out_shape=[in_hbm(*o) for o in outs + there],
        in_specs=[vmem()] * first + [anywhere()] * (len(operands) - first),
        out_specs=[anywhere()] * len(outs + there),
        scratch_shapes=buffers_of(operands[first : first + 11])
        + [pltpu.VMEM(*o) for o in scratch]
        + [pltpu.SemaphoreType.DMA((1,)), pltpu.SemaphoreType.DMA((32,))]
        + [pltpu.VMEM(*o) for o in later]
        + [pltpu.SemaphoreType.DMA((24,)), pltpu.SemaphoreType.DMA((24,))],
        compiler_params=pltpu.CompilerParams(
            collective_id=2, has_side_effects=True, vmem_limit_bytes=63 * 2**20
        ),
        cost_estimate=pl.CostEstimate(flops=10**11, bytes_accessed=10**7, transcendentals=0),
    )(*operands)


def line_sum(copies, line, partial_there, partial, whole, got, running, up_in, down_in):
    position, side = lax.axis_index("expert") // 2, lax.axis_index("expert") % 2
    count = partial.shape[0] // 2
    chunk = count // line
    order = [3 * (1 - position // 2), 2 - position // 2, position + 1 - 2 * (position % 2), position]
    over = []

    def rows_at(half, place):
        return pl.ds(pl.multiple_of(half * count + place * chunk, 16), chunk)

    def send_pair():
        for place in order:
            over.append(
                copies.start(partial_there.at[rows_at(1 - side, place)], got.at[rows_at(0, place)], copies.mate)
            )

    def part(place):
        mine = partial[rows_at(side, place), :].astype(F32)
        return mine + got[rows_at(0, place), :].astype(F32)

    flows = {1: {}, -1: {}}

    def reach_step(reach):
        over[line - 1 - reach].wait_recv()
        for way, (step, landed) in enumerate(((1, up_in), (-1, down_in))):
            target = position + step * reach
            sends = (target >= 0) & (target < line)
            origin = position - step
            receives = (origin >= 0) & (origin < line) & (origin + step * reach >= 0) & (origin + step * reach < line)
            slot = 3 * way + reach - 1
            if reach < line - 1:
                flows[step][reach + 1].wait_recv()

            @pl.when(sends)
            def _(slot=slot, target=target, landed=landed, step=step):
                running[slot] = part(target).astype(BF16)
                if reach < line - 1:

                    @pl.when((position - step >= 0) & (position - step < line))
                    def _():
                        total = part(target) + landed[reach].astype(F32)
                        running[slot] = total.astype(BF16)

            flows[step][reach] = copies.along(running.at[slot], landed.at[reach - 1], step, sends, receives)

    spread, mates = {}, {}

    def settle():
        over[line - 1].wait_recv()
        flows[1][1].wait_recv()
        flows[-1][1].wait_recv()
        total = part(position)
        total = total + jnp.where(position > 0, up_in[0].astype(F32), 0.0)
        total = total + jnp.where(position < line - 1, down_in[0].astype(F32), 0.0)
        here = rows_at(side, position)
        whole[here, :] = total.astype(BF16)
        mates[0] = [copies.start(whole.at[here], whole.at[here], copies.mate)]

    def spread_start(hop):
        spread[hop] = []
        for step in (1, -1):
            place = position - step * (hop - 1)
            sends = (place >= 0) & (place < line) & (position + step >= 0) & (position + step < line)
            origin = position - step * hop
            receives = (origin >= 0) & (origin < line)
            at = rows_at(side, jnp.clip(place, 0, line - 1))
            spread[hop].append(copies.along(whole.at[at], whole.at[at], step, sends, receives))

    def spread_end(hop):
        mates[hop] = []
        for step, copy in zip((1, -1), spread[hop]):
            copy.wait_recv()
            origin = position - step * hop
            there = (origin >= 0) & (origin < line)
            at = rows_at(side, jnp.clip(origin, 0, line - 1))
            mates[hop].append(copies.over_when(whole.at[at], whole.at[at], copies.mate, there))

    def mates_end(hop):
        for copy in mates[hop]:
            copy.wait_recv()

    return send_pair, reach_step, settle, spread_start, spread_end, mates_end


class SmallSum:
    def __init__(self, copies, devices, running, arrived, sums):
        self.copies, self.devices, self.running, self.arrived, self.sums = copies, devices, running, arrived, sums
        self.at, self.copy = 0, None

    def step(self):
        if self.copy is not None:
            self.copy.wait_recv()
            total = self.running[self.at] + self.arrived[self.at]
            self.at += 1
            self.copy = None
            if self.at == len(self.devices):
                self.sums[...] = total
            else:
                self.running[self.at] = total
        if self.at < len(self.devices):
            self.copy = self.copies.start(
                self.running.at[self.at], self.arrived.at[self.at], self.devices[self.at]
            )

    def end(self):
        while self.copy is not None:
            self.step()


class Gather:
    def __init__(self, copies, tensors, whole, rows):
        self.copies, self.whole, self.rows = copies, whole, rows
        tensor = lax.axis_index("tensor")
        self.mine = pl.ds(pl.multiple_of(tensor * rows, rows), rows)
        self.there = pl.ds(pl.multiple_of((tensor + tensors // 2) % tensors * rows, rows), rows)

    def start(self):
        self.far = self.copies.start(self.whole.at[self.mine], self.whole.at[self.mine], self.copies.far)
        self.first = self.copies.start(self.whole.at[self.mine], self.whole.at[self.mine], self.copies.core)

    def forward(self):
        self.far.wait_recv()
        self.last = self.copies.start(self.whole.at[self.there], self.whole.at[self.there], self.copies.core)

    def end(self):
        self.first.wait_recv()
        self.last.wait_recv()


def inputs_back_kernel(tensors, experts, line, hidden, *refs):
    refs = list(refs)
    gain, grad_router, grad_second = [refs.pop(0) for _ in range(3)]
    ins_there = [refs.pop(0) for _ in range(7)]
    moe_cross, stream = [refs.pop(0) for _ in range(2)]
    own_sum, going, turning = [refs.pop(0) for _ in range(3)] if line else [None] * 3
    outs_there = [refs.pop(0) for _ in range(8 if line else 5)]
    ins, outs = [refs.pop(0) for _ in range(7)], [refs.pop(0) for _ in range(8 if line else 5)]
    grads_rel, w_query, w_key, w_value, grad_after, layer_part, partial = ins
    (whole, layer, sums, summed, kv_out), weight_outs = outs[:5], outs[5:]
    moe_crossed, stream_in, local, stores = [refs.pop(0) for _ in range(4)]
    buffers = [refs.pop(0) for _ in range(4)] if line else []
    final, block = (refs.pop(0), refs.pop(0)) if line else (None, None)
    sent, got, crossing, crossed, running, arrived, send, recv = refs
    copies = Copies(tensors, send, recv)
    moves = Moves(stores)
    rows = grad_after.shape[0]
    quarter = pl.ds(pl.multiple_of(lax.axis_index("tensor") * rows, rows), rows)
    moves.start(*zip(ins_there, ins), (stream.at[quarter], stream_in))
    bits = [1 << k for k in range(experts.bit_length() - 1)]
    position = lax.axis_index("expert") // 2
    copies.greet([copies.core, copies.far] + [copies.across(bit) for bit in bits], line)
    lines = []
    moe_far = copies.start(moe_cross, moe_crossed, copies.far)
    if line:
        send_pair, reach_step, settle, spread_start, spread_end, mates_end = line_sum(
            copies, line, ins_there[6], partial, summed, *buffers
        )
        send_pair()
        end, inner = position == line - 1, (position > 0) & (position < line - 1)
        lines = [
            copies.along(going, final.at[0], 1, position < line - 1, position > 0),
            copies.along(going, final.at[1], -1, end, position == line - 2),
            copies.along(turning, final.at[1], -1, inner, position < line - 2),
        ]
    heads = w_query.shape[1] // HD
    query_width = heads * HD
    kv_rows = pl.ds(partial.shape[0] // 8, HD)
    kv_at = kv_columns(heads)
    moves.wait()

    def part(place):
        at = slice(place * rows, (place + 1) * rows)
        total = dot(grads_rel[at, :query_width], w_query[...], 1, 1)
        total = total + dot(grads_rel[at, query_width : query_width + HD], w_key[:, kv_at], 1, 1)
        return total + dot(grads_rel[at, query_width + HD :], w_value[:, kv_at], 1, 1)

    def beside():
        if line:
            reach_step(line - 1)
            reach_step(line - 2)

    grad_in = sum_quarter(copies, part, sent, got, crossing, crossed, beside)
    _, normed, inverse = rms_norm(stream_in[...].astype(F32), gain[...])
    through, first = norm_backward(grad_in, normed, inverse, gain[...])
    whole[quarter, :] = (grad_after[...] + through).astype(BF16)
    inputs_gather = Gather(copies, tensors, whole, rows)
    inputs_gather.start()
    running[0] = jnp.zeros(sums.shape, F32)
    running[0, :experts, :] = grad_router[...]
    running[0, experts : experts + 1, :] = grad_second[...]
    running[0, experts + 1 : experts + 2, :] = first[None]
    small = SmallSum(
        copies, [copies.core] + [copies.across(bit) for bit in bits] + [copies.far], running, arrived, sums
    )
    small.step()
    if line:
        for reach in range(line - 3, 0, -1):
            reach_step(reach)
    small.step()
    moe_far.wait_recv()
    layer[quarter, :] = (layer_part[...] + moe_crossed[...].astype(F32)).astype(BF16)
    layer_gather = Gather(copies, tensors, layer, rows)
    layer_gather.start()
    if line:
        settle()
        spread_start(1)
        small.step()
        spread_end(1)
        spread_start(2)
        small.step()
    inputs_gather.forward()
    if line:
        spread_end(2)
        spread_start(3)
        small.step()
        for copy in lines:
            copy.wait_recv()
        for index, out in enumerate(weight_outs):
            at = pl.ds(index * hidden, hidden)
            move = pltpu.make_async_copy(own_sum.at[at], block, local.at[0])
            move.start()
            move.wait()
            total = block[...] + jnp.where(position > 0, final[0, at, :].astype(F32), 0.0)
            total = total + jnp.where(position < line - 1, final[1, at, :].astype(F32), 0.0)
            out[...] = total
            moves.start((out, outs_there[5 + index]))
        for hop in range(3):
            mates_end(hop)
        far = copies.start(summed.at[kv_rows], kv_out.at[0], copies.far)
        near = copies.start(summed.at[kv_rows], kv_out.at[1], copies.core)
        spread_end(3)
        layer_gather.forward()
        far.wait_recv()
        across = copies.start(kv_out.at[0], kv_out.at[2], copies.core)
        mates_end(3)
        near.wait_recv()
        across.wait_recv()
    else:
        layer_gather.forward()
        summed[...] = partial[...]
        kv_out[...] = jnp.zeros(kv_out.shape, BF16)
    small.end()
    moves.start((sums, outs_there[2]), (summed, outs_there[3]), (kv_out, outs_there[4]))
    inputs_gather.end()
    layer_gather.end()
    moves.start((whole, outs_there[0]), (layer, outs_there[1]))
    moves.wait()
    copies.finish()


def inputs_back(tensors, experts, line, hidden, heads, length, width, *operands):
    rows = length // 4
    early = (-(-(experts + 2) // 8) * 8, width)
    steps = 1 + experts.bit_length()
    projected = 2 * heads * HD + HD
    quarter, half = ((rows, width), BF16), ((2 * rows, width), BF16)
    outs = [
        ((length, width), BF16),
        ((length, width), BF16),
        (early, F32),
        ((projected, width), BF16),
        ((3, HD, width), BF16),
    ]
    buffers = []
    if line:
        chunk = projected // 2 // line
        buffers = [
            ((projected // 2, width), BF16),
            ((6, chunk, width), BF16),
            ((3, chunk, width), BF16),
            ((3, chunk, width), BF16),
            ((2, 3 * hidden, width), BF16),
            ((hidden, width), F32),
        ]
        outs = outs + [((hidden, width), F32)] * 3
    buffers += [half, half, quarter, quarter, ((steps,) + early, F32), ((steps,) + early, F32)]
    operands = in_place(operands)
    return pl.pallas_call(
        functools.partial(inputs_back_kernel, tensors, experts, line, hidden),
        out_shape=[in_hbm(*o) for o in outs],
        in_specs=[vmem()] * 3 + [anywhere()] * (len(operands) - 3),
        out_specs=[anywhere()] * len(outs),
        scratch_shapes=buffers_of(operands[3:10])
        + [pltpu.VMEM(*o) for o in outs + [quarter] * 2]
        + [pltpu.SemaphoreType.DMA((1,)), pltpu.SemaphoreType.DMA((16,))]
        + [pltpu.VMEM(*o) for o in buffers]
        + [pltpu.SemaphoreType.DMA((50 + steps,)), pltpu.SemaphoreType.DMA((50 + steps,))],
        compiler_params=pltpu.CompilerParams(
            collective_id=3, has_side_effects=True, vmem_limit_bytes=63 * 2**20
        ),
        cost_estimate=pl.CostEstimate(flops=10**11, bytes_accessed=10**7, transcendentals=0),
    )(*operands)


def results_kernel(query_width, layer, inputs, gate, up, down, summed, kv_rest, *outs):
    layer_out, inputs_out, gate_out, up_out, down_out, query_out, output_out, key_out, value_out = outs
    step = pl.program_id(0)
    for source, out in ((layer, layer_out), (inputs, inputs_out), (gate, gate_out), (up, up_out), (down, down_out)):
        out[...] = source[...]
    first_rows, top = summed.shape[0] // 8, query_width + HD
    columns = pl.ds(pl.multiple_of(step * query_width, HD), query_width)
    query_out[:first_rows, :] = summed[:first_rows, columns].astype(F32)
    query_out[first_rows:, :] = summed[first_rows + HD : top, columns].astype(F32)
    part = query_width // 4
    output_out[...] = summed[pl.ds(pl.multiple_of(top + step * part, 16), part), :].astype(F32)
    tensor = lax.axis_index("tensor")
    lead, low_head = tensor % 2 == 0, tensor * (query_width // HD) // (HEADS // KV) == 0
    for block in range(query_width // HD):
        at = pl.ds(pl.multiple_of(step * query_width + block * HD, HD), HD)
        mine = summed[first_rows : first_rows + HD, at].astype(F32)
        far, core, across = [kv_rest[k, :, at].astype(F32) for k in range(3)]
        rows = slice(block * HD, (block + 1) * HD)
        for out, near, other in (
            (key_out, jnp.where(lead, mine, core), jnp.where(lead, far, across)),
            (value_out, jnp.where(lead, core, mine), jnp.where(lead, across, far)),
        ):
            out[rows, :HD] = jnp.where(low_head, near, other)
            out[rows, HD:] = jnp.where(low_head, other, near)


def results(query_width, *operands):
    (length, width), (hidden, _) = operands[0].shape, operands[2].shape
    shape = jax.ShapeDtypeStruct

    def rows(count):
        return pl.BlockSpec((count // 4, width), lambda i: (i, 0))

    def whole(dims):
        return pl.BlockSpec(dims, lambda i: (0,) * len(dims))

    def columns(count):
        return pl.BlockSpec((width // 4, count), lambda i: (i, 0))

    same = [rows(length), rows(length)] + [rows(hidden)] * 3
    return pl.pallas_call(
        functools.partial(results_kernel, query_width),
        grid=(4,),
        in_specs=same + [whole(operands[5].shape), whole(operands[6].shape)],
        out_specs=same + [columns(query_width), rows(query_width), columns(2 * HD), columns(2 * HD)],
        out_shape=[shape((length, width), BF16)] * 2
        + [shape((hidden, width), F32)] * 3
        + [shape((width, query_width), F32), shape((query_width, width), F32)]
        + [shape((width, 2 * HD), F32)] * 2,
        compiler_params=pltpu.CompilerParams(vmem_limit_bytes=40 * 2**20),
        cost_estimate=pl.CostEstimate(flops=0, bytes_accessed=3 * 10**7, transcendentals=0),
    )(*in_place(operands))


def shards(
    experts,
    tensors,
    inputs,
    routes,
    cotangent,
    first_gain,
    second_gain,
    w_query,
    w_key,
    w_value,
    w_output,
    w_router,
    w_gate,
    w_up,
    w_down,
):
    links = Links(experts, tensors)
    line, place, side = links.line, links.place, links.side
    length, width = inputs.shape
    heads = w_query.shape[1] // HD
    hidden = w_gate.shape[2]
    group = HEADS // KV
    kv_head = links.tensor * heads // group
    scale = HD ** (-0.5)
    order = nearest_first(line)

    own_weights = [w_gate[0].T, w_up[0].T, w_down[0]]
    short = line if line == 4 else 0
    if not short:
        sides = [[2 * p + s for p in range(line)] for s in range(2)]
        weights = lax.all_gather(jnp.concatenate(own_weights, 0), "expert", axis_index_groups=sides)

    rows, half = length // 4, length // 2
    cos, sin = [jnp.asarray(table) for table in rotary_tables(length)]
    attn_in, query, key, value, context_rel, logsum, grad_rel, grad_pair, routes_own, routes_pair, *arrived = attend(
        tensors,
        short,
        inputs,
        first_gain[None],
        w_query,
        w_key,
        w_value,
        cos,
        sin,
        cotangent,
        routes.T,
        own_weights,
    )

    tokens_own, tokens_pair, after, *second = attend_out(
        tensors, short, context_rel, w_output, second_gain[None], inputs, *(arrived or [None])
    )
    router_rows = w_router.T
    if short:
        router_padded = jnp.concatenate([router_rows, router_rows], 0)
        tokens_pair, *outs, last_weight, all_down = first_pass(
            tensors,
            experts,
            line,
            hidden,
            router_padded,
            routes_own,
            routes_pair,
            tokens_own,
            tokens_pair,
            grad_rel,
            grad_pair,
            arrived[0],
            second[0],
            *own_weights,
        )
        *first_own, last_gate_own, router_probs, named = outs[:7]
        *first_pair, last_gate_pair, _, _ = outs[7:]
    else:
        names = jnp.arange(experts, dtype=jnp.int32)[:, None, None]

        def gates_of(tokens, tokens_routes):
            logits = dot(router_rows, tokens, 1, 1)
            logit_exp = jnp.exp(logits - jnp.max(logits, axis=0, keepdims=True))
            probs = logit_exp / jnp.sum(logit_exp, axis=0, keepdims=True)
            named = jnp.any(tokens_routes[None] == names, axis=1).astype(F32)
            return probs, named, probs * named

        router_probs, named, gates_own = gates_of(tokens_own, routes_own[:4])
        _, _, gates_pair = gates_of(tokens_pair, routes_pair[:4])
    both_tokens, both_grads = (tokens_own, tokens_pair), (grad_rel, grad_pair)
    if short:
        (kept_pair, sent_pair, *last_pair), (kept_own, sent_own, *last_own), last_grad = last_expert(
            hidden,
            last_weight,
            (tokens_pair, grad_pair, last_gate_pair, first_pair[0]),
            (tokens_own, grad_rel, last_gate_own, first_own[0]),
        )
        gate_rows = [first_own[3], last_own[1], first_pair[3], last_pair[1]]
    else:
        zeros = jnp.zeros((length, width), BF16)

        def step(totals, weight_at):
            weight, position = weight_at
            name = (position * 2 + side)[None]
            down = weight[2 * hidden :]
            own = expert_pass(tokens_own, grad_rel, gates_own, name, [weight], totals[0])
            pair = expert_pass(tokens_pair, grad_pair, gates_pair, name, [weight], totals[1])
            grads = weight_grad(
                0, hidden, (own[2], pair[2]), (own[1], pair[1]), both_tokens, both_grads, BF16
            )
            moe_own = totals[2] + dot(own[1], down, 0, 0)
            moe_pair = totals[3] + dot(pair[1], down, 0, 0)
            return (own[0], pair[0], moe_own, moe_pair), (own[3][0], pair[3][0], grads)

        (sum_own, sum_pair, moe_own, moe_pair), (gate_own, gate_pair, weight_grads) = lax.scan(
            step,
            (zeros, zeros, zeros.astype(F32), zeros.astype(F32)),
            (weights, jnp.arange(line, dtype=jnp.int32)),
        )
        kept_own, sent_own, kept_pair, sent_pair = sum_own[:half], sum_own[half:], sum_pair[:half], sum_pair[half:]

    if short:
        factors = [first_own[2], first_pair[2], first_own[1], first_pair[1]]
        factors += [last_own[0], last_pair[0], *both_tokens, *both_grads, all_down, last_grad]
    else:
        gate_rows = [jnp.concatenate([gate_own, gate_pair], 0)]
        factors = [moe_own.astype(BF16), moe_pair.astype(BF16)]
    (
        grad_after,
        grad_router,
        grad_second,
        grads_rel,
        layer_part,
        moe_cross,
        partial,
        _,
        *weight_sums,
    ) = tokens_back(
        tensors,
        experts,
        short,
        hidden,
        heads,
        length,
        width,
        *gate_rows,
        router_probs,
        named,
        router_rows,
        second_gain[None],
        kept_pair,
        kept_own,
        after,
        w_output,
        query,
        key,
        value,
        logsum,
        cos,
        sin,
        context_rel,
        attn_in,
        grad_rel,
        sent_pair,
        sent_own,
        *factors,
    )

    line_sums = []
    if short:
        line_sums = [weight_sums[2], *weight_sums[-2:]]
    else:
        expert_grads = lax.psum_scatter(
            weight_grads, "expert", scatter_dimension=0, axis_index_groups=sides
        ).astype(F32)

    grad_inputs, layer_out, sums, summed, kv_rest, *weight_grads_out = inputs_back(
        tensors,
        experts,
        short,
        hidden,
        heads,
        length,
        width,
        first_gain[None],
        grad_router,
        grad_second,
        grads_rel,
        w_query,
        w_key,
        w_value,
        grad_after,
        layer_part,
        partial,
        moe_cross,
        inputs,
        *line_sums,
    )
    query_width = heads * HD
    if not short:
        summed = lax.psum(summed, "expert")
        first_rows = summed.shape[0] // 8
        kv_far = links.over_tensor(summed[first_rows : first_rows + HD], 2)
        both = jnp.concatenate([summed[first_rows : first_rows + HD], kv_far], 0)
        kv_core = links.over_tensor(both, 1)
        kv_rest = jnp.stack([kv_far, kv_core[:HD], kv_core[HD:]])
        weight_grads_out = [expert_grads[i * hidden : (i + 1) * hidden] for i in range(3)]
    (
        layer_out,
        grad_inputs,
        grad_gate,
        grad_up,
        grad_down,
        grad_query,
        grad_output,
        grad_key,
        grad_value,
    ) = results(query_width, layer_out, grad_inputs, *weight_grads_out, summed, kv_rest)
    grad_router, grad_second, grad_first = sums[:experts].T, sums[experts], sums[experts + 1]
    return (
        layer_out,
        grad_inputs,
        grad_first,
        grad_second,
        grad_query,
        grad_key,
        grad_value,
        grad_output,
        grad_router,
        grad_gate.T[None],
        grad_up.T[None],
        grad_down[None],
    )


def solution(mesh):
    experts, tensors = mesh.shape["expert"], mesh.shape["tensor"]
    in_specs = (
        P("expert", None),
        P("expert", None),
        P("expert", None),
        P(),
        P(),
        P(None, "tensor"),
        P(),
        P(),
        P("tensor", None),
        P(),
        P("expert", None, "tensor"),
        P("expert", None, "tensor"),
        P("expert", "tensor", None),
    )
    out_specs = (
        P("expert", None),
        P("expert", None),
        P(),
        P(),
        P(None, "tensor"),
        P(),
        P(),
        P("tensor", None),
        P(),
        P("expert", None, "tensor"),
        P("expert", None, "tensor"),
        P("expert", "tensor", None),
    )

    def run(*arrays):
        return shards(experts, tensors, *arrays)

    return jax.shard_map(run, mesh=mesh, in_specs=in_specs, out_specs=out_specs, check_vma=False)
```

```python
import functools

import jax
import jax.numpy as jnp
import numpy as np
from jax import lax
from jax.experimental import pallas as pl
from jax.experimental.pallas import tpu as pltpu
from jax.sharding import PartitionSpec as P

HEADS = 12
KV = 2
HD = 128
EPSILON = 1e-06
ROPE_BASE = 10000.0
NEGATIVE = -1e30
F32 = jnp.float32
BF16 = jnp.bfloat16


def dot(left, right, left_dim, right_dim):
    return lax.dot_general(
        left, right, (((left_dim,), (right_dim,)), ((), ())), preferred_element_type=F32
    )


def rms_norm(values, gain):
    inverse = lax.rsqrt(jnp.mean(values * values, axis=-1, keepdims=True) + EPSILON)
    normed = values * inverse
    return normed * gain, normed, inverse


def norm_backward(upstream, normed, inverse, gain):
    scaled = upstream * gain
    through = inverse * (scaled - normed * jnp.mean(scaled * normed, axis=-1, keepdims=True))
    return through, jnp.sum(upstream * normed, axis=0)


def rotary_tables(length):
    frequency = np.float32(ROPE_BASE) ** (-np.arange(HD // 2, dtype=np.float32) * np.float32(2.0 / HD))
    angles = np.arange(length, dtype=np.float32)[:, None] * frequency.astype(np.float32)[None]
    cos, sin = np.cos(angles), np.sin(angles)
    return np.concatenate([cos, cos], 1), np.concatenate([-sin, sin], 1)


def turned(values, cos, sin, back=False):
    other = pltpu.roll(values, HD // 2, 1) * sin
    return values * cos - other if back else values * cos + other


class Links:
    def __init__(self, experts, tensors):
        self.experts, self.tensors = experts, tensors
        self.line = experts // 2
        self.tensor = lax.axis_index("tensor")
        expert = lax.axis_index("expert")
        self.place, self.side = expert // 2, expert % 2

    def over_tensor(self, values, bit):
        return lax.ppermute(values, "tensor", [(i, i ^ bit) for i in range(self.tensors)])

    def over_expert(self, values, bit):
        return lax.ppermute(values, "expert", [(i, i ^ bit) for i in range(self.experts)])

    def over_pair(self, values):
        return self.over_expert(values, 1)

    def relative(self, values):
        rows = values.shape[0] // 4
        return jnp.concatenate(
            [
                lax.dynamic_slice_in_dim(values, (self.tensor ^ r) * rows, rows, 0)
                for r in (0, 2, 1, 3)
            ],
            0,
        )

    def absolute(self, values):
        rows = values.shape[0] // 4
        place = jnp.asarray([0, 2, 1, 3], jnp.int32)
        return jnp.concatenate(
            [
                lax.dynamic_slice_in_dim(values, place[self.tensor ^ q] * rows, rows, 0)
                for q in range(4)
            ],
            0,
        )

    def gather(self, quarter):
        both = jnp.concatenate([quarter, self.over_tensor(quarter, 2)], 0)
        return jnp.concatenate([both, self.over_tensor(both, 1)], 0)


def nearest_first(line):
    tables = []
    for place in range(line):
        offsets = [p - place for p in range(line) if p != place]
        tables.append(sorted(offsets, key=lambda o: (abs(o), -o)))
    return tables


def expert_kernel(count, hidden, split, prior, *refs):
    names, tokens, grads, gates = refs[:4]
    weights, refs = refs[4 : 4 + count], refs[4 + count :]
    if prior:
        before, refs = refs[0], refs[1:]
    outs, (gated_out, grad_pre_out, rows_out) = refs[: 2 if split else 1], refs[2 if split else 1 :]
    tile, grad_tile = tokens[...], grads[...]
    total = before[...].astype(F32) if prior else None
    for slot in range(count):
        weight = weights[slot]
        pre = dot(weight[: 2 * hidden, :], tile, 1, 1)
        back = dot(weight[2 * hidden :, :], grad_tile, 1, 1)
        gate = gates[pl.ds(names[slot], 1), :]
        gate_pre, up_pre = pre[:hidden], pre[hidden:]
        sigmoid = jax.nn.sigmoid(gate_pre)
        activated = gate_pre * sigmoid
        hid = (activated * up_pre).astype(BF16).astype(F32)
        rows_out[slot : slot + 1, :] = jnp.sum(hid * back, axis=0, keepdims=True)
        gated_out[slot * hidden : (slot + 1) * hidden, :] = (hid * gate).astype(BF16)
        grad_hidden = back * gate
        grad_pre = jnp.concatenate(
            [
                (grad_hidden * up_pre * (sigmoid * (1.0 + gate_pre * (1.0 - sigmoid)))).astype(BF16),
                (grad_hidden * activated).astype(BF16),
            ],
            0,
        )
        grad_pre_out[2 * slot * hidden : 2 * (slot + 1) * hidden, :] = grad_pre
        part = dot(grad_pre, weight[: 2 * hidden, :], 0, 0)
        total = part if total is None else total + part
    if split:
        for step in range(2):

            @pl.when(pl.program_id(0) == step)
            def _(step=step):
                outs[step][...] = total.astype(BF16)
    else:
        outs[0][...] = total.astype(BF16)


def expert_pass(tokens, grads, gates, names, weights, before=None, split=False):
    count, length, width = len(weights), tokens.shape[0], tokens.shape[1]
    hidden = weights[0].shape[0] // 3
    tile = length // 2
    token_spec = pl.BlockSpec((tile, width), lambda i, *_: (i, 0))
    half_spec = pl.BlockSpec((tile, width), lambda i, *_: (0, 0))

    def column_spec(rows):
        return pl.BlockSpec((rows, tile), lambda i, *_: (0, i))

    weight_spec = pl.BlockSpec((3 * hidden, width), lambda i, *_: (0, 0))
    token_shape = in_hbm((length, width), BF16)
    half_shape = in_hbm((tile, width), BF16)
    columns = [(count * hidden, BF16), (2 * count * hidden, BF16), (count, F32)]
    return pl.pallas_call(
        functools.partial(expert_kernel, count, hidden, split, before is not None),
        grid_spec=pltpu.PrefetchScalarGridSpec(
            num_scalar_prefetch=1,
            grid=(2,),
            in_specs=[token_spec, token_spec, column_spec(gates.shape[0])]
            + [weight_spec] * count
            + [token_spec] * (before is not None),
            out_specs=([half_spec] * 2 if split else [token_spec]) + [column_spec(r) for r, _ in columns],
        ),
        out_shape=([half_shape] * 2 if split else [token_shape])
        + [in_hbm((r, length), t) for r, t in columns],
        compiler_params=pltpu.CompilerParams(vmem_limit_bytes=48 * 2**20),
        cost_estimate=pl.CostEstimate(
            flops=2 * count * length * width * hidden * 5,
            bytes_accessed=(4 * length + 3 * hidden * count) * width * 2,
            transcendentals=0,
        ),
    )(names, *in_place([tokens, grads, gates, *weights] + ([before] if before is not None else [])))


def last_expert_kernel(hidden, weight, *refs):
    step = pl.program_id(0)
    weight_grad, total_grad = refs[-2:]

    @pl.when(step == 0)
    def _():
        total_grad[...] = jnp.zeros(total_grad.shape, F32)

    for side in range(2):
        tokens, grads, gate, before = refs[4 * side : 4 * side + 4]
        kept, sent, gated_out, row_out = refs[8 + 4 * side : 12 + 4 * side]

        @pl.when(step // 2 == side)
        def _(tokens=tokens, grads=grads, gate=gate, before=before, kept=kept, sent=sent, side=side,
              gated_out=gated_out, row_out=row_out):
            row, gated, grad_pre = hidden_units(weight, tokens[...], grads[...], gate[0:1, :], hidden)
            row_out[...] = row
            gated_out[...] = gated
            total_grad[: 2 * hidden, :] += dot(grad_pre, tokens[...], 1, 0)
            total_grad[2 * hidden :, :] += dot(gated, grads[...], 1, 0)
            total = (before[...].astype(F32) + dot(grad_pre, weight[: 2 * hidden, :], 0, 0)).astype(BF16)

            @pl.when(step % 2 == 0)
            def _():
                kept[...] = total

            @pl.when(step % 2 == 1)
            def _():
                sent[...] = total

    @pl.when(step == 3)
    def _():
        weight_grad[...] = total_grad[...].astype(BF16)


def last_expert(hidden, weight, pair, own):
    length, width = pair[0].shape
    tile = length // 2

    def specs(at):
        token = pl.BlockSpec((tile, width), lambda i: (at(i), 0))
        half = pl.BlockSpec((tile, width), lambda i: (0, 0))

        def column(rows):
            return pl.BlockSpec((rows, tile), lambda i: (0, at(i)))

        return [token, token, column(8), token], [half, half, column(hidden), column(1)]

    pair_ins, pair_outs = specs(lambda i: jnp.minimum(i, 1))
    own_ins, own_outs = specs(lambda i: jnp.maximum(i - 2, 0))
    shapes = [
        in_hbm((tile, width), BF16),
        in_hbm((tile, width), BF16),
        in_hbm((hidden, length), BF16),
        in_hbm((1, length), F32),
    ]
    whole = pl.BlockSpec((3 * hidden, width), lambda i: (0, 0))
    outs = pl.pallas_call(
        functools.partial(last_expert_kernel, hidden),
        grid=(4,),
        in_specs=[whole] + pair_ins + own_ins,
        out_specs=pair_outs + own_outs + [whole],
        out_shape=shapes * 2 + [in_hbm((3 * hidden, width), BF16)],
        scratch_shapes=[pltpu.VMEM((3 * hidden, width), F32)],
        compiler_params=pltpu.CompilerParams(vmem_limit_bytes=60 * 2**20),
        cost_estimate=pl.CostEstimate(
            flops=4 * length * width * hidden * 8,
            bytes_accessed=(8 * length + 3 * hidden) * width * 2,
            transcendentals=0,
        ),
    )(*in_place([weight, *pair, *own]))
    return outs[:4], outs[4:8], outs[8]


def weight_grad_kernel(grad_pre_own, grad_pre_pair, gated_own, gated_pair, own, pair, grad_own, grad_pair, out):
    rows = grad_pre_own.shape[0]
    out[:rows, :] = (
        dot(grad_pre_own[...], own[...], 1, 0) + dot(grad_pre_pair[...], pair[...], 1, 0)
    ).astype(out.dtype)
    out[rows:, :] = (
        dot(gated_own[...], grad_own[...], 1, 0) + dot(gated_pair[...], grad_pair[...], 1, 0)
    ).astype(out.dtype)


def weight_grad(slot, hidden, grad_pre, gated, tokens, grads, kept_as):
    length, width = tokens[0].shape
    tile = width // 3
    pre_spec = pl.BlockSpec((2 * hidden, length), lambda i: (slot, 0))
    gated_spec = pl.BlockSpec((hidden, length), lambda i: (slot, 0))
    token_spec = pl.BlockSpec((length, tile), lambda i: (0, i))
    return pl.pallas_call(
        weight_grad_kernel,
        grid=(3,),
        in_specs=[pre_spec] * 2 + [gated_spec] * 2 + [token_spec] * 4,
        out_specs=pl.BlockSpec((3 * hidden, tile), lambda i: (0, i)),
        out_shape=jax.ShapeDtypeStruct((3 * hidden, width), kept_as),
        compiler_params=pltpu.CompilerParams(vmem_limit_bytes=32 * 2**20),
        cost_estimate=pl.CostEstimate(
            flops=2 * 2 * length * width * hidden * 3,
            bytes_accessed=(4 * length + 6 * hidden) * width * 2,
            transcendentals=0,
        ),
    )(*grad_pre, *gated, *tokens, *grads)


MESH = pl.DeviceIdType.MESH


class Copies:
    def __init__(self, tensors, send, recv):
        self.send, self.recv, self.started, self.drained = send, recv, [], []
        expert, tensor = lax.axis_index("expert"), lax.axis_index("tensor")
        self.core = (expert, tensor + 1 - 2 * (tensor % 2))
        self.far = (expert, (tensor + tensors // 2) % tensors)
        self.mate = (expert + 1 - 2 * (expert % 2), tensor)

    def across(self, bit):
        expert, tensor = lax.axis_index("expert"), lax.axis_index("tensor")
        return (expert + bit - 2 * bit * (expert // bit % 2), tensor)

    def greet(self, partners, line=0):
        barrier = pltpu.get_barrier_semaphore()
        for partner in partners:
            pl.semaphore_signal(barrier, inc=1, device_id=partner, device_id_type=MESH)
        count = len(partners)
        if line:
            expert, tensor = lax.axis_index("expert"), lax.axis_index("tensor")
            position = expert // 2
            for step, there in ((2, position < line - 1), (-2, position > 0)):

                @pl.when(there)
                def _(step=step):
                    device = (expert + step, tensor)
                    pl.semaphore_signal(barrier, inc=1, device_id=device, device_id_type=MESH)

            count = count + 1 - (position + 1) // line + (position + line - 1) // line
        pl.semaphore_wait(barrier, count)

    def start(self, source, target, device):
        place = len(self.started)
        copy = pltpu.make_async_remote_copy(
            src_ref=source,
            dst_ref=target,
            send_sem=self.send.at[place],
            recv_sem=self.recv.at[place],
            device_id=device,
            device_id_type=MESH,
        )
        copy.start()
        self.started.append(copy)
        return copy

    def along(self, source, target, step, sends, receives):
        device = (lax.axis_index("expert") + 2 * step, lax.axis_index("tensor"))
        return self.over_when(source, target, device, sends, receives)

    def over_when(self, source, target, device, sends, receives=None):
        place = len(self.started)
        copy = pltpu.make_async_remote_copy(
            src_ref=source,
            dst_ref=target,
            send_sem=self.send.at[place],
            recv_sem=self.recv.at[place],
            device_id=device,
            device_id_type=MESH,
        )
        pl.when(sends)(lambda: copy.start())
        self.started.append(When(copy, sends, sends if receives is None else receives))
        return self.started[-1]

    def drain(self, copy):
        copy.wait_send()
        self.drained.append(copy)

    def finish(self):
        for copy in self.started:
            if all(copy is not done for done in self.drained):
                copy.wait_send()


class Moves:
    def __init__(self, semaphores):
        self.semaphores, self.count, self.open = semaphores, 0, []

    def start(self, *pairs):
        for source, target in pairs:
            copy = pltpu.make_async_copy(source, target, self.semaphores.at[self.count])
            copy.start()
            self.count += 1
            self.open.append(copy)

    def wait(self):
        for copy in self.open:
            copy.wait()
        self.open = []


def buffers_of(arrays):
    return [pltpu.VMEM(a.shape, a.dtype) for a in arrays]


class When:
    def __init__(self, copy, sends, receives):
        self.copy, self.sends, self.receives = copy, sends, receives

    def wait_send(self):
        pl.when(self.sends)(lambda: self.copy.wait_send())

    def wait_recv(self):
        pl.when(self.receives)(lambda: self.copy.wait_recv())


def sum_quarter(copies, part, sent, got, crossing, crossed, beside=None):
    rows = crossing.shape[0]
    sent[rows:, :] = part(3).astype(BF16)
    last = copies.start(sent.at[pl.ds(rows, rows)], got.at[pl.ds(rows, rows)], copies.core)
    sent[:rows, :] = part(2).astype(BF16)
    first = copies.start(sent.at[pl.ds(0, rows)], got.at[pl.ds(0, rows)], copies.core)
    other = part(1)
    last.wait_recv()
    crossing[...] = (other + got[rows:, :].astype(F32)).astype(BF16)
    far = copies.start(crossing, crossed, copies.far)
    if beside is not None:
        beside()
    mine = part(0)
    first.wait_recv()
    mine = mine + got[:rows, :].astype(F32)
    far.wait_recv()
    return mine + crossed[...].astype(F32)


def gather_quarters(copies, whole, rows, fill=None):
    far = copies.start(whole.at[pl.ds(0, rows)], whole.at[pl.ds(rows, rows)], copies.far)
    first = copies.start(whole.at[pl.ds(0, rows)], whole.at[pl.ds(2 * rows, rows)], copies.core)
    if fill is not None:
        fill()
    far.wait_recv()
    last = copies.start(whole.at[pl.ds(rows, rows)], whole.at[pl.ds(3 * rows, rows)], copies.core)
    first.wait_recv()
    last.wait_recv()


def quarter_at(place):
    tensor = lax.axis_index("tensor")
    return (tensor % 2 + place // 2) % 2 + 2 * ((tensor // 2 + place % 2) % 2)


def place_of(quarter):
    tensor = lax.axis_index("tensor")
    return 2 * ((tensor % 2 + quarter % 2) % 2) + (tensor // 2 + quarter // 2) % 2


def masked_scores(query, keys, start, scale):
    scores = dot(query, keys, 1, 1) * scale
    rows = lax.broadcasted_iota(jnp.int32, scores.shape, 0) + start
    cols = lax.broadcasted_iota(jnp.int32, scores.shape, 1)
    return jnp.where(cols <= rows, scores, NEGATIVE)


def kv_columns(heads):
    head = lax.axis_index("tensor") * heads // (HEADS // KV)
    return pl.ds(pl.multiple_of(head * HD, HD), HD)


def attend_kernel(tensors, line, heads, *refs):
    refs = list(refs)
    ins_there = [refs.pop(0) for _ in range(9)]
    own_weights = [refs.pop(0) for _ in range(3 if line else 0)]
    outs_there = [refs.pop(0) for _ in range(10)]
    arrived = refs.pop(0) if line else None
    ins, outs = [refs.pop(0) for _ in range(9)], [refs.pop(0) for _ in range(10)]
    stream, gain, w_query, w_key, w_value, cos, sin, grad, routes = ins
    attn_in, query, key, value, context, logsum, grad_rel, grad_pair, routes_own, routes_pair = outs
    local, send, recv = refs
    moves = Moves(local)
    moves.start(*zip(ins_there, ins))
    copies = Copies(tensors, send, recv)
    expert = lax.axis_index("expert")
    position = expert // 2
    copies.greet([copies.core, copies.mate], line)
    length = stream.shape[0]
    rows = length // 4
    if line:
        lines = []
        for index, weight in enumerate(own_weights):
            at = pl.ds(index * weight.shape[0], weight.shape[0])
            there = arrived.at[1 - (position + 2) // line, at]
            lines.append(copies.along(weight, there, 1, position < line - 1, position > 0))
            lines.append(copies.along(weight, arrived.at[0, at], -1, position > 0, position < line - 1))
    moves.wait()
    mates = []
    for place in range(4):
        at = pl.ds(place * rows, rows)
        grad_rel[at, :] = grad[pl.ds(pl.multiple_of(quarter_at(place) * rows, rows), rows), :]
        if place < 2:
            mates.append(copies.start(grad_rel.at[at], grad_pair.at[at], copies.mate))
    routes_own[...] = jnp.zeros(routes_own.shape, jnp.int32)
    for place in range(4):
        source = pl.ds(pl.multiple_of(quarter_at(place) * rows, rows), rows)
        routes_own[: routes.shape[0], place * rows : (place + 1) * rows] = routes[:, source]
    routes_copy = copies.start(routes_own, routes_pair, copies.mate)
    kv_at = kv_columns(heads)
    for tile in range(4):
        at = slice(tile * rows, (tile + 1) * rows)
        normed = rms_norm(stream[at, :].astype(F32), gain[...])[0].astype(BF16)
        attn_in[at, :] = normed
        proj = dot(normed, w_query[...], 1, 0)
        for head in range(heads):
            columns = slice(head * HD, (head + 1) * HD)
            query[at, columns] = turned(proj[:, columns], cos[at, :], sin[at, :]).astype(BF16)
        key[at, :] = turned(dot(normed, w_key[:, kv_at], 1, 0), cos[at, :], sin[at, :]).astype(BF16)
        value[at, :] = dot(normed, w_value[:, kv_at], 1, 0).astype(BF16)
    for tile in range(4):
        at, seen = slice(tile * rows, (tile + 1) * rows), (tile + 1) * rows
        to = pl.ds(pl.multiple_of(place_of(tile) * rows, rows), rows)
        for head in range(heads):
            columns = slice(head * HD, (head + 1) * HD)
            scores = masked_scores(query[at, columns], key[:seen, :], tile * rows, HD**-0.5)
            peak = jnp.max(scores, axis=-1, keepdims=True)
            exponent = jnp.exp(scores - peak)
            total = jnp.sum(exponent, axis=-1, keepdims=True)
            prob = (exponent / total).astype(BF16)
            context[to, columns] = dot(prob, value[:seen, :], 1, 0).astype(BF16)
            logsum[at, head : head + 1] = peak + jnp.log(total)
    pair_outs = (grad_pair, routes_pair)
    moves.start(*[pair for pair in zip(outs, outs_there) if all(pair[0] is not out for out in pair_outs)])
    cores = []
    for place in range(2):
        mates[place].wait_recv()
        source = grad_pair.at[pl.ds(place * rows, rows)]
        cores.append(copies.start(source, grad_pair.at[pl.ds((2 + place) * rows, rows)], copies.core))
    routes_copy.wait_recv()
    for copy in cores:
        copy.wait_recv()
    moves.start((grad_pair, outs_there[7]), (routes_pair, outs_there[9]))
    if line:
        for copy in lines:
            copy.wait_recv()
    moves.wait()
    copies.finish()


def anywhere():
    return pl.BlockSpec(memory_space=pl.ANY)


def attend(tensors, line, stream, gain, w_query, w_key, w_value, cos, sin, grad, routes, own_weights):
    length, width = stream.shape
    heads = w_query.shape[1] // HD
    outs = [
        ((length, width), BF16),
        ((length, heads * HD), BF16),
        ((length, HD), BF16),
        ((length, HD), BF16),
        ((length, heads * HD), BF16),
        ((length, HD), F32),
        ((length, width), BF16),
        ((length, width), BF16),
        ((8, length), routes.dtype),
        ((8, length), routes.dtype),
    ]
    operands = in_place([stream, gain, w_query, w_key, w_value, cos, sin, grad, routes])
    return pl.pallas_call(
        functools.partial(attend_kernel, tensors, line, heads),
        out_shape=[in_hbm(*out) for out in outs]
        + ([in_hbm((2, sum(w.shape[0] for w in own_weights), width), BF16)] if line else []),
        in_specs=[anywhere()] * (12 if line else 9),
        out_specs=[anywhere()] * (10 + bool(line)),
        scratch_shapes=buffers_of(operands)
        + [pltpu.VMEM(*out) for out in outs]
        + [
            pltpu.SemaphoreType.DMA((19,)),
            pltpu.SemaphoreType.DMA((12,)),
            pltpu.SemaphoreType.DMA((12,)),
        ],
        compiler_params=pltpu.CompilerParams(
            collective_id=4, has_side_effects=True, vmem_limit_bytes=48 * 2**20
        ),
        cost_estimate=pl.CostEstimate(flops=4 * 10**10, bytes_accessed=10**7, transcendentals=0),
    )(*operands, *(in_place(own_weights) if line else []))


def attend_back(
    tiles, heads, grad, weight, query, key, value, logsum, cos, sin, grads, grads_rel, key_grad, value_grad
):
    length = query.shape[0]
    rows = length // 4
    scale = HD**-0.5
    for tile in tiles:
        at, seen = slice(tile * rows, (tile + 1) * rows), (tile + 1) * rows
        to = pl.ds(pl.multiple_of(place_of(tile) * rows, rows), rows)
        grad_context = dot(grad[to, :], weight[...], 1, 1).astype(BF16)
        for head in range(heads):
            columns = slice(head * HD, (head + 1) * HD)
            head_query = query[at, columns]
            scores = masked_scores(head_query, key[:seen, :], tile * rows, scale)
            prob = jnp.exp(scores - logsum[at, head : head + 1])
            head_grad = grad_context[:, columns]
            dprob = dot(head_grad, value[:seen, :], 1, 1)
            delta = jnp.sum(prob * dprob, axis=-1, keepdims=True)
            dscore = (prob * (dprob - delta)).astype(BF16)
            dquery = dot(dscore, key[:seen, :], 1, 0) * scale
            dquery = turned(dquery, cos[at, :], sin[at, :], True).astype(BF16)
            grads[at, columns] = dquery
            grads_rel[to, columns] = dquery
            dkey = dot(dscore, head_query, 0, 0)
            dvalue = dot(prob.astype(BF16), head_grad, 0, 0)
            key_grad[:seen, :] += dkey
            value_grad[:seen, :] += dvalue


def attend_back_end(heads, cos, sin, grads, grads_rel, key_grad, value_grad):
    rows = grads.shape[0] // 4
    scale = HD**-0.5
    for tile in range(4):
        at = slice(tile * rows, (tile + 1) * rows)
        to = pl.ds(pl.multiple_of(place_of(tile) * rows, rows), rows)
        dkey = turned(key_grad[at, :] * scale, cos[at, :], sin[at, :], True).astype(BF16)
        both = jnp.concatenate([dkey, value_grad[at, :].astype(BF16)], 1)
        grads[at, heads * HD :] = both
        grads_rel[to, heads * HD :] = both


def attend_out_kernel(tensors, line, *refs):
    refs = list(refs)
    ins_there, stream = [refs.pop(0) for _ in range(3)], refs.pop(0)
    arrived = refs.pop(0) if line else None
    outs_there = [refs.pop(0) for _ in range(3)]
    second = refs.pop(0) if line else None
    context, weight, gain = ins = [refs.pop(0) for _ in range(3)]
    own, pair, after = [refs.pop(0) for _ in range(3)]
    sent, got, crossing, crossed, stream_in, local, send, recv = refs
    copies = Copies(tensors, send, recv)
    moves = Moves(local)
    moves.start(*zip(ins_there, ins))
    position = lax.axis_index("expert") // 2
    copies.greet([copies.core, copies.far, copies.mate], line)
    rows = after.shape[0]
    quarter = pl.ds(pl.multiple_of(lax.axis_index("tensor") * rows, rows), rows)
    moves.start((stream.at[quarter], stream_in))
    if line:
        inner = (position > 0) & (position < line - 1)
        up = copies.along(arrived.at[1], second, 1, inner, position >= line // 2)
        down = copies.along(arrived.at[0], second, -1, inner, position < line // 2)

    def part(place):
        return dot(context[place * rows : (place + 1) * rows, :], weight[...], 1, 0)

    moves.wait()
    total = sum_quarter(copies, part, sent, got, crossing, crossed)
    total = stream_in[...].astype(F32) + total
    after[...] = total
    own[:rows, :] = rms_norm(total, gain[...])[0].astype(BF16)
    mate = copies.start(own.at[pl.ds(0, rows)], pair.at[pl.ds(0, rows)], copies.mate)
    moves.start((after, outs_there[2]))
    gather_quarters(copies, own, rows)
    mate.wait_recv()
    moves.start((own, outs_there[0]))
    if line:
        moves.start((pair, outs_there[1]))
        up.wait_recv()
        down.wait_recv()
    else:
        gather_quarters(copies, pair, rows)
        moves.start((pair, outs_there[1]))
    moves.wait()
    copies.finish()


def in_hbm(dims, dtype):
    return pltpu.HBM(dims, dtype)


def in_place(operands):
    return [pltpu.with_memory_space_constraint(o, pltpu.HBM) if o.size >= 2**16 else o for o in operands]


def vmem():
    return pl.BlockSpec(memory_space=pltpu.VMEM)


def attend_out(tensors, line, context, weight, gain, stream, arrived):
    length, width = stream.shape
    rows = length // 4
    outs = [((length, width), BF16), ((rows if line else length, width), BF16), ((rows, width), F32)]
    operands = in_place([context, weight, gain])
    stream, *arrived = in_place([stream] + ([arrived] if line else []))
    return pl.pallas_call(
        functools.partial(attend_out_kernel, tensors, line),
        out_shape=[in_hbm(*out) for out in outs]
        + ([in_hbm(arrived[0].shape[1:], BF16)] if line else []),
        in_specs=[anywhere()] * (4 + bool(line)),
        out_specs=[anywhere()] * (3 + bool(line)),
        scratch_shapes=buffers_of(operands)
        + [pltpu.VMEM(*out) for out in outs]
        + [
            pltpu.VMEM((2 * rows, width), BF16),
            pltpu.VMEM((2 * rows, width), BF16),
            pltpu.VMEM((rows, width), BF16),
            pltpu.VMEM((rows, width), BF16),
            pltpu.VMEM((rows, width), BF16),
            pltpu.SemaphoreType.DMA((7,)),
            pltpu.SemaphoreType.DMA((12,)),
            pltpu.SemaphoreType.DMA((12,)),
        ],
        compiler_params=pltpu.CompilerParams(
            collective_id=1, has_side_effects=True, vmem_limit_bytes=40 * 2**20
        ),
        cost_estimate=pl.CostEstimate(flops=6 * 10**10, bytes_accessed=10**7, transcendentals=0),
    )(*operands, stream, *arrived)


def hidden_units(weight, tile, grad_tile, gate, hidden):
    pre = dot(weight[: 2 * hidden, :], tile, 1, 1)
    back = dot(weight[2 * hidden :, :], grad_tile, 1, 1)
    gate_pre, up_pre = pre[:hidden], pre[hidden:]
    sigmoid = jax.nn.sigmoid(gate_pre)
    activated = gate_pre * sigmoid
    hid = (activated * up_pre).astype(BF16).astype(F32)
    row = jnp.sum(hid * back, axis=0, keepdims=True)
    grad_hidden = back * gate
    grad_pre = jnp.concatenate(
        [
            (grad_hidden * up_pre * (sigmoid * (1.0 + gate_pre * (1.0 - sigmoid)))).astype(BF16),
            (grad_hidden * activated).astype(BF16),
        ],
        0,
    )
    return row, (hid * gate).astype(BF16), grad_pre


def slot_offset(slot, position, line):
    if slot == 0:
        return 0
    table = [row[slot - 1] for row in nearest_first(line)]
    offset = table[0]
    for place in range(1, line):
        offset = offset + (table[place] - table[place - 1]) * (position // place > 0)
    return offset


def first_pass_kernel(tensors, experts, line, hidden, *refs):
    refs = list(refs)
    router, routes_own, routes_pair = [refs.pop(0) for _ in range(3)]
    own_there, quarter, grad_own_there, grad_pair_there, arrived, second = [refs.pop(0) for _ in range(6)]
    own_weights = [refs.pop(0) for _ in range(3)]
    pair_there = refs.pop(0)
    outs_there = [[refs.pop(0) for _ in range(7)] for _ in range(2)]
    last_weight, all_down = refs.pop(0), refs.pop(0)
    pair = refs.pop(0)
    outs = [[refs.pop(0) for _ in range(7)] for _ in range(2)]
    own, grad_own, grad_pair, weights, local, stores, send, recv = refs
    copies = Copies(tensors, send, recv)
    moves = Moves(stores)
    expert = lax.axis_index("expert")
    position, side = expert // 2, expert % 2
    copies.greet([copies.core, copies.far], line)
    rows = quarter.shape[0]
    inner = (position > 0) & (position < line - 1)
    outer = jnp.logical_not(inner)
    down = copies.along(second, weights.at[3], -1, position == 1, position == 0)
    up = copies.along(second, weights.at[3], 1, position == line - 2, position == line - 1)
    far = copies.start(quarter, pair.at[pl.ds(rows, rows)], copies.far)
    first = copies.start(quarter, pair.at[pl.ds(2 * rows, rows)], copies.core)

    def load(source, target, place):
        return pltpu.make_async_copy(source, target, local.at[place])

    loads = [
        *[
            load(weight, weights.at[0, pl.ds(index * hidden, hidden)], (0, 8, 9)[index])
            for index, weight in enumerate(own_weights)
        ],
        load(own_there, own, 1),
        load(grad_own_there, grad_own, 2),
        load(arrived.at[0], weights.at[1], 3),
    ]
    for copy in loads:
        copy.start()
    pl.when(inner)(lambda: load(arrived.at[1], weights.at[2], 4).start())
    pl.when(outer)(lambda: load(second, weights.at[2], 4).start())
    later = [load(quarter, pair.at[pl.ds(0, rows)], 5), load(grad_pair_there, grad_pair, 6)]
    for copy in later:
        copy.start()
    spare = load(second, weights.at[3], 7)
    pl.when(inner)(lambda: spare.start())
    names = [(position + slot_offset(slot, position, line)) * 2 + side for slot in range(line)]
    tile = 2 * rows

    def run(tokens, grads, routes, out, which):
        total_out, gated_out, grad_pre_out, rows_out, last_gate_out, probs_out, named_out = out
        at = pl.ds(which * tile, tile)
        tokens_tile, grad_tile = tokens[at, :], grads[at, :]
        logits = dot(router[...], tokens_tile, 1, 1)[:experts]
        logit_exp = jnp.exp(logits - jnp.max(logits, axis=0, keepdims=True))
        probs = logit_exp / jnp.sum(logit_exp, axis=0, keepdims=True)
        number = lax.broadcasted_iota(jnp.int32, probs.shape, 0)
        named = jnp.zeros(probs.shape, F32)
        for choice in range(routes.shape[0] // 2):
            named = jnp.where(routes[choice : choice + 1, at] == number, 1.0, named)
        gates = probs * named
        probs_out[:, at] = probs
        named_out[:, at] = named

        def gate_of(slot):
            return jnp.sum(jnp.where(number == names[slot], gates, 0.0), axis=0, keepdims=True)

        last_gate_out[0:1, at] = gate_of(line - 1)
        total = None
        for slot in range(line - 1):
            row, gated, grad_pre = hidden_units(
                weights.at[slot], tokens_tile, grad_tile, gate_of(slot), hidden
            )
            rows_out[slot : slot + 1, at] = row
            gated_out[slot * hidden : (slot + 1) * hidden, at] = gated
            grad_pre_out[2 * slot * hidden : 2 * (slot + 1) * hidden, at] = grad_pre
            part = dot(grad_pre, weights[slot, : 2 * hidden, :], 0, 0)
            total = part if total is None else total + part
        total_out[at, :] = total.astype(BF16)

    for copy in loads:
        copy.wait()
    load(second, weights.at[2], 4).wait()
    for which in range(2):
        run(own, grad_own, routes_own, outs[0], which)
    moves.start(*zip(outs[0], outs_there[0]))
    for slot in range(line - 1):
        moves.start((weights.at[slot, pl.ds(2 * hidden, hidden)], all_down.at[pl.ds(slot * hidden, hidden)]))
    far.wait_recv()
    last = copies.start(pair.at[pl.ds(rows, rows)], pair.at[pl.ds(3 * rows, rows)], copies.core)
    for copy in later:
        copy.wait()
    run(pair, grad_pair, routes_pair, outs[1], 0)
    first.wait_recv()
    last.wait_recv()
    run(pair, grad_pair, routes_pair, outs[1], 1)
    moves.start((pair, pair_there), *zip(outs[1], outs_there[1]))
    pl.when(inner)(lambda: spare.wait())
    up.wait_recv()
    down.wait_recv()
    slot = line - 1
    moves.start((weights.at[slot, pl.ds(2 * hidden, hidden)], all_down.at[pl.ds(slot * hidden, hidden)]))
    moves.start((weights.at[slot], last_weight))
    moves.wait()
    copies.finish()


def first_pass(tensors, experts, line, hidden, *operands):
    length, width = operands[3].shape
    operands = in_place(operands)
    count = line - 1
    out = [
        ((length, width), BF16),
        ((count * hidden, length), BF16),
        ((2 * count * hidden, length), BF16),
        ((8, length), F32),
        ((8, length), F32),
        ((experts, length), F32),
        ((experts, length), F32),
    ]
    tokens = pltpu.VMEM((length, width), BF16)
    whole = [((length, width), BF16)] + out * 2
    return pl.pallas_call(
        functools.partial(first_pass_kernel, tensors, experts, line, hidden),
        out_shape=[in_hbm(*o) for o in whole]
        + [in_hbm((3 * hidden, width), BF16), in_hbm((line * hidden, width), BF16)],
        in_specs=[vmem()] * 3 + [anywhere()] * 9,
        out_specs=[anywhere()] * 17,
        scratch_shapes=[pltpu.VMEM(*o) for o in whole]
        + [
            tokens,
            tokens,
            tokens,
            pltpu.VMEM((line, 3 * hidden, width), BF16),
            pltpu.SemaphoreType.DMA((10,)),
            pltpu.SemaphoreType.DMA((20,)),
            pltpu.SemaphoreType.DMA((5,)),
            pltpu.SemaphoreType.DMA((5,)),
        ],
        compiler_params=pltpu.CompilerParams(
            collective_id=5, has_side_effects=True, vmem_limit_bytes=63 * 2**20
        ),
        cost_estimate=pl.CostEstimate(flops=5 * 10**10, bytes_accessed=10**7, transcendentals=0),
    )(*operands)


def tokens_back_kernel(tensors, line, hidden, heads, *refs):
    refs = list(refs)
    gate_rows = [refs.pop(0) for _ in range(4 if line else 1)]
    probs_all, named_all, router, gain = [refs.pop(0) for _ in range(4)]
    ins_there = [refs.pop(0) for _ in range(11)]
    attn_in, grad_there, sent_pair, sent_own = [refs.pop(0) for _ in range(4)]
    factors = [refs.pop(0) for _ in range(10 if line else 0)]
    all_down, last_grad = (refs.pop(0), refs.pop(0)) if line else (None, None)
    moe_own, moe_pair = (refs.pop(0), refs.pop(0)) if not line else (None, None)
    outs_there = [refs.pop(0) for _ in range(6)]
    partial_there, moe_got = refs.pop(0), refs.pop(0)
    if line:
        moe_own, moe_pair = refs.pop(0), refs.pop(0)
    weight_grads = [refs.pop(0) for _ in range(line - 1 if line else 0)]
    lines_there = [refs.pop(0) for _ in range(2 if line else 0)]
    ins, outs = [refs.pop(0) for _ in range(11)], [refs.pop(0) for _ in range(6)]
    kept_pair, kept_own, after, w_output, query, key, value, logsum, cos, sin, context = ins
    grad_after, grad_router, grad_second, grads_rel, moe_out, moe_cross = outs
    whole, attn_grads, key_grad, value_grad, kv_got = [refs.pop(0) for _ in range(5)]
    moe_half, moe_mate, grad, block, local, stores = [refs.pop(0) for _ in range(6)]
    if line:
        first_in, first_out, up_in, down_in, turning, down_in_place = [refs.pop(0) for _ in range(6)]
        going = first_in
    got_pair, got_own, crossing_pair, crossed_pair, crossing_own, crossed_own = [refs.pop(0) for _ in range(6)]
    mate_out, mate_in, rows_kept, rows_sent, rows_got = [refs.pop(0) for _ in range(5)]
    rows_crossing, rows_crossed, rows_mine, rows_mate, send, recv = refs
    copies = Copies(tensors, send, recv)
    moves = Moves(stores)
    rows = grad.shape[0]
    moves.start(*zip(ins_there, ins), (grad_there.at[pl.ds(0, rows)], grad))
    if line:
        moves.start((all_down, down_in_place))
    position = lax.axis_index("expert") // 2
    copies.greet([copies.core, copies.far, copies.mate], line)
    if line:
        for index, (first, last) in enumerate(zip(gate_rows[::2], gate_rows[1::2])):
            top, low = slice(index * line, (index + 1) * line - 1), slice((index + 1) * line - 1, (index + 1) * line)
            for half, out in enumerate((rows_kept, rows_sent)):
                columns = slice(2 * half * rows, 2 * (half + 1) * rows)
                out[top, :] = first[: line - 1, columns]
                out[low, :] = last[:, columns]
    else:
        rows_kept[...] = gate_rows[0][:, : 2 * rows]
        rows_sent[...] = gate_rows[0][:, 2 * rows :]
    probs, named = probs_all[:, :rows], named_all[:, :rows]
    moe_core = []

    def experts_out():
        if line:
            first_rows = (line - 1) * hidden

            def body(first, last, out):
                total = dot(first[...], down_in_place[:first_rows, :], 0, 0)
                out[...] = (total + dot(last[...], down_in_place[first_rows:, :], 0, 0)).astype(BF16)

            for gated, last, out in ((factors[2], factors[4], moe_own), (factors[3], factors[5], moe_pair)):
                pltpu.emit_pipeline(
                    body,
                    grid=(4,),
                    in_specs=[
                        pl.BlockSpec((first_rows, rows), lambda i: (0, i)),
                        pl.BlockSpec((hidden, rows), lambda i: (0, i)),
                    ],
                    out_specs=[pl.BlockSpec((rows, moe_own.shape[1]), lambda i: (i, 0))],
                )(gated, last, out)
        for side, source in enumerate((moe_own, moe_pair)):
            moe_core.append(
                copies.start(source.at[pl.ds(2 * rows, 2 * rows)], moe_got.at[side], copies.core)
            )

    def make_weight_grads(slots, factors, tokens):
        count = len(slots)
        length, width = tokens[0].shape
        tile = width // 6
        once = pl.Buffered(buffer_count=1)
        pre_spec = pl.BlockSpec((2 * hidden * count, length), lambda i: (0, 0), pipeline_mode=once)
        gated_spec = pl.BlockSpec((hidden * count, length), lambda i: (0, 0), pipeline_mode=once)
        token_spec = pl.BlockSpec((length, tile), lambda i: (0, i))

        def body(pre_own, pre_pair, gated_own, gated_pair, own, pair, grad_own, grad_pair, *outs):
            for index, out in enumerate(outs):
                pre = slice(2 * hidden * index, 2 * hidden * (index + 1))
                gated = slice(hidden * index, hidden * (index + 1))
                total = dot(pre_own[pre, :], own[...], 1, 0) + dot(pre_pair[pre, :], pair[...], 1, 0)
                out[: 2 * hidden, :] = total.astype(out.dtype)
                total = dot(gated_own[gated, :], grad_own[...], 1, 0)
                total = total + dot(gated_pair[gated, :], grad_pair[...], 1, 0)
                out[2 * hidden :, :] = total.astype(out.dtype)

        pltpu.emit_pipeline(
            body,
            grid=(6,),
            in_specs=[pre_spec] * 2 + [gated_spec] * 2 + [token_spec] * 4,
            out_specs=[pl.BlockSpec((3 * hidden, tile), lambda i: (0, i))] * count,
        )(*factors, *tokens, *[weight_grads[slot] for slot in slots])

    low, high = pl.ds(0, rows), pl.ds(rows, rows)
    pair_last = copies.start(sent_pair.at[high], got_pair.at[high], copies.core)
    pair_first = copies.start(sent_pair.at[low], got_pair.at[low], copies.core)
    rows_core = copies.start(rows_sent, rows_got, copies.core)
    own_last = copies.start(sent_own.at[high], got_own.at[high], copies.core)
    own_first = copies.start(sent_own.at[low], got_own.at[low], copies.core)
    if line:
        up = copies.along(last_grad, first_in, 1, position == 0, position == 1)
        down = copies.along(last_grad, first_in, -1, position == line - 1, position == line - 2)
        inner = (position > 0) & (position < line - 1)
    moves.wait()
    pair_last.wait_recv()
    crossing_pair[...] = (kept_pair[rows:, :].astype(F32) + got_pair[rows:, :].astype(F32)).astype(BF16)
    pair_far = copies.start(crossing_pair, crossed_pair, copies.far)
    rows_core.wait_recv()
    rows_crossing[...] = rows_kept[:, rows:] + rows_got[:, rows:]
    rows_far = copies.start(rows_crossing, rows_crossed, copies.far)
    pair_first.wait_recv()
    mine_pair = kept_pair[:rows, :].astype(F32) + got_pair[:rows, :].astype(F32)
    own_last.wait_recv()
    crossing_own[...] = (kept_own[rows:, :].astype(F32) + got_own[rows:, :].astype(F32)).astype(BF16)
    own_first.wait_recv()
    grad_tokens = kept_own[:rows, :].astype(F32) + got_own[:rows, :].astype(F32)
    if line:
        make_weight_grads(list(range(line - 1)), factors[:4], factors[6:])
    pair_far.wait_recv()
    own_far = copies.start(crossing_own, crossed_own, copies.far)
    mate_out[...] = (mine_pair + crossed_pair[...].astype(F32)).astype(BF16)
    mate = copies.start(mate_out, mate_in, copies.mate)
    rows_far.wait_recv()
    rows_mine[...] = rows_kept[:, :rows] + rows_got[:, :rows] + rows_crossed[...]
    rows_over = copies.start(rows_mine, rows_mate, copies.mate)
    def move(source, target, place):
        copy = pltpu.make_async_copy(source, target, local.at[place])
        copy.start()
        copy.wait()

    def moe_part(side, at):
        move((moe_own, moe_pair)[side].at[at], block.at[0], 0)
        move(moe_got.at[side, at], block.at[1], 0)
        return block[0].astype(F32) + block[1].astype(F32)

    experts_out()
    for copy in moe_core:
        copy.wait_recv()
    for place in range(2):
        moe_half[place] = moe_part(1, pl.ds(place * rows, rows)).astype(BF16)
    rows_over.wait_recv()
    count = rows_mine.shape[0] // 2
    slots = jnp.concatenate([rows_mine[:count, :], rows_mate[count:, :]], 0)
    dprobs = jnp.zeros(probs.shape, F32)
    number = lax.broadcasted_iota(jnp.int32, probs.shape, 0)
    chip_side = lax.axis_index("expert") % 2
    for slot in range(count):
        at = position + slot_offset(slot, position, line) if line else slot
        for half in range(2):
            name = at * 2 + chip_side + half - 2 * half * chip_side
            row = slots[half * count + slot : half * count + slot + 1, :]
            dprobs = jnp.where(number == name, row, dprobs)
    dprobs = dprobs * named
    dlogits = (
        probs * (dprobs - jnp.sum(probs * dprobs, axis=0, keepdims=True))
    ).astype(BF16)
    second_out, normed, inverse = rms_norm(after[...], gain[...])
    grad_router[...] = dot(dlogits, second_out.astype(BF16), 1, 0)
    grad_tokens = grad_tokens + dot(dlogits, router[...], 0, 0)
    rounds = []

    def second_round():
        up.wait_recv()
        down.wait_recv()

        @pl.when(inner)
        def _():
            move(last_grad, first_out, 0)
            first_out[...] = (first_out[...].astype(F32) + first_in[...].astype(F32)).astype(BF16)

        @pl.when(jnp.logical_not(inner))
        def _():
            move(weight_grads[line - 2], first_out, 0)

        rounds.append(copies.along(first_out, up_in, 1, position < line // 2, inner))
        rounds.append(copies.along(first_out, down_in, -1, position >= line // 2, inner))

    if line:
        second_round()
    own_far.wait_recv()
    grad_tokens = grad_tokens + crossed_own[...].astype(F32)
    mate.wait_recv()
    moe_over = copies.start(moe_half, moe_mate, copies.mate)
    grad_tokens = grad_tokens + mate_in[...].astype(F32)
    through, second = norm_backward(grad_tokens, normed, inverse, gain[...])
    grad_second[...] = second[None]
    total = grad[...].astype(F32) + through
    grad_after[...] = total
    whole[:rows, :] = total.astype(BF16)
    moves.start(*zip(outs[:3], outs_there[:3]))
    moves.start((attn_in.at[pl.ds(0, 2 * rows)], got_pair), (attn_in.at[pl.ds(2 * rows, 2 * rows)], got_own))

    def beside():
        moe_cross[...] = moe_part(0, pl.ds(rows, rows)).astype(BF16)
        moe_out[...] = after[...] + moe_part(0, pl.ds(0, rows))

    far = copies.start(whole.at[pl.ds(0, rows)], whole.at[pl.ds(rows, rows)], copies.far)
    first = copies.start(whole.at[pl.ds(0, rows)], whole.at[pl.ds(2 * rows, rows)], copies.core)
    beside()
    key_grad[...] = jnp.zeros(key_grad.shape, F32)
    value_grad[...] = jnp.zeros(value_grad.shape, F32)
    attention = [w_output, query, key, value, logsum, cos, sin, attn_grads, grads_rel, key_grad, value_grad]
    low_half = lax.axis_index("tensor") // 2 == 0
    high_half = lax.axis_index("tensor") // 2 > 0
    first.wait_recv()
    pl.when(low_half)(lambda: attend_back((1, 0), heads, whole, *attention))
    pl.when(high_half)(lambda: attend_back((3, 2), heads, whole, *attention))
    far.wait_recv()
    last = copies.start(whole.at[pl.ds(rows, rows)], whole.at[pl.ds(3 * rows, rows)], copies.core)
    last.wait_recv()
    pl.when(low_half)(lambda: attend_back((3, 2), heads, whole, *attention))
    pl.when(high_half)(lambda: attend_back((1, 0), heads, whole, *attention))
    attend_back_end(heads, cos, sin, attn_grads, grads_rel, key_grad, value_grad)
    moves.start((grads_rel, outs_there[3]))

    lead = lax.axis_index("tensor") % 2
    query_width = heads * HD
    first_rows = partial_there.shape[0] // 8
    kept_at = pl.ds(pl.multiple_of(query_width + lead * HD, HD), HD)
    sent_at = pl.ds(pl.multiple_of(query_width + (1 - lead) * HD, HD), HD)
    width = whole.shape[1]
    moves.wait()

    def by_columns(columns, grads_at):
        total = dot(got_pair[:, columns], attn_grads[: 2 * rows, grads_at], 0, 0)
        return total + dot(got_own[:, columns], attn_grads[2 * rows :, grads_at], 0, 0)

    copies.drain(pair_far)
    for block_at in range(0, width, HD):
        columns = slice(block_at, block_at + HD)
        crossing_pair[:HD, columns] = by_columns(columns, sent_at).astype(BF16)
    kv = copies.start(crossing_pair.at[pl.ds(0, HD)], kv_got, copies.core)
    for block_at in range(0, width, query_width):
        columns = slice(block_at, block_at + query_width)
        query_block = by_columns(columns, slice(0, query_width)).astype(BF16)
        kept_pair[:first_rows, columns] = query_block[:first_rows]
        kept_pair[first_rows + HD : query_width + HD, columns] = query_block[first_rows:]
    kept_own[:query_width, :] = dot(context[...], whole[...], 0, 0).astype(BF16)
    kv.wait_recv()
    for block_at in range(0, width, HD):
        columns = slice(block_at, block_at + HD)
        kept = by_columns(columns, kept_at)
        kept_pair[first_rows : first_rows + HD, columns] = (kept + kv_got[:, columns].astype(F32)).astype(BF16)
    top = query_width + HD
    moves.start(
        (kept_pair.at[pl.ds(0, top)], partial_there.at[pl.ds(0, top)]),
        (kept_own.at[pl.ds(0, query_width)], partial_there.at[pl.ds(top, query_width)]),
    )
    moe_over.wait_recv()
    moe_out[...] += moe_mate[0].astype(F32)
    moe_cross[...] = (moe_cross[...].astype(F32) + moe_mate[1].astype(F32)).astype(BF16)
    moves.start(*zip(outs[4:], outs_there[4:]))
    if line:
        move(weight_grads[1], going, 0)
        move(weight_grads[2], turning, 0)
        for copy in rounds:
            copy.wait_recv()

        @pl.when(inner)
        def _():
            going[...] = (going[...].astype(F32) + up_in[...].astype(F32)).astype(BF16)
            turning[...] = (turning[...].astype(F32) + down_in[...].astype(F32)).astype(BF16)

        moves.start((going, lines_there[0]), (turning, lines_there[1]))
    moves.wait()
    copies.finish()


def tokens_back(tensors, experts, line, hidden, heads, length, width, *operands):
    rows = length // 4
    half = ((2 * rows, width), BF16)
    quarter = ((rows, width), BF16)
    shard = ((3 * hidden, width), BF16)
    small = ((experts, rows), F32)
    both = ((experts, 2 * rows), F32)
    outs = [
        ((rows, width), F32),
        ((experts, width), F32),
        ((1, width), F32),
        ((length, (heads + 2) * HD), BF16),
        ((rows, width), F32),
        quarter,
    ]
    there = [((2 * heads * HD + HD, width), BF16), ((2, 2 * rows, width), BF16)]
    if line:
        there += [((length, width), BF16)] * 2 + [((3 * hidden, width), F32)] + [shard] * (line - 2) + [shard] * 2
    first = 8 if line else 5
    scratch = outs + [
        ((length, width), BF16),
        ((length, (heads + 2) * HD), BF16),
        ((length, HD), F32),
        ((length, HD), F32),
        ((HD, width), BF16),
        ((2, rows, width), BF16),
        ((2, rows, width), BF16),
        quarter,
        ((2, rows, width), BF16),
    ]
    later = [half, half] + [quarter] * 6 + [both, both, both] + [small] * 4
    if line:
        later = [shard] * 5 + [((line * hidden, width), BF16)] + later
    operands = in_place(operands)
    return pl.pallas_call(
        functools.partial(tokens_back_kernel, tensors, line, hidden, heads),
        out_shape=[in_hbm(*o) for o in outs + there],
        in_specs=[vmem()] * first + [anywhere()] * (len(operands) - first),
        out_specs=[anywhere()] * len(outs + there),
        scratch_shapes=buffers_of(operands[first : first + 11])
        + [pltpu.VMEM(*o) for o in scratch]
        + [pltpu.SemaphoreType.DMA((1,)), pltpu.SemaphoreType.DMA((32,))]
        + [pltpu.VMEM(*o) for o in later]
        + [pltpu.SemaphoreType.DMA((24,)), pltpu.SemaphoreType.DMA((24,))],
        compiler_params=pltpu.CompilerParams(
            collective_id=2, has_side_effects=True, vmem_limit_bytes=63 * 2**20
        ),
        cost_estimate=pl.CostEstimate(flops=10**11, bytes_accessed=10**7, transcendentals=0),
    )(*operands)


def line_sum(copies, line, partial_there, partial, whole, got, running, up_in, down_in):
    position, side = lax.axis_index("expert") // 2, lax.axis_index("expert") % 2
    count = partial.shape[0] // 2
    chunk = count // line
    order = [3 * (1 - position // 2), 2 - position // 2, position + 1 - 2 * (position % 2), position]
    over = []

    def rows_at(half, place):
        return pl.ds(pl.multiple_of(half * count + place * chunk, 16), chunk)

    def send_pair():
        for place in order:
            over.append(
                copies.start(partial_there.at[rows_at(1 - side, place)], got.at[rows_at(0, place)], copies.mate)
            )

    def part(place):
        mine = partial[rows_at(side, place), :].astype(F32)
        return mine + got[rows_at(0, place), :].astype(F32)

    flows = {1: {}, -1: {}}

    def reach_step(reach):
        over[line - 1 - reach].wait_recv()
        for way, (step, landed) in enumerate(((1, up_in), (-1, down_in))):
            target = position + step * reach
            sends = (target >= 0) & (target < line)
            origin = position - step
            receives = (origin >= 0) & (origin < line) & (origin + step * reach >= 0) & (origin + step * reach < line)
            slot = 3 * way + reach - 1
            if reach < line - 1:
                flows[step][reach + 1].wait_recv()

            @pl.when(sends)
            def _(slot=slot, target=target, landed=landed, step=step):
                running[slot] = part(target).astype(BF16)
                if reach < line - 1:

                    @pl.when((position - step >= 0) & (position - step < line))
                    def _():
                        total = part(target) + landed[reach].astype(F32)
                        running[slot] = total.astype(BF16)

            flows[step][reach] = copies.along(running.at[slot], landed.at[reach - 1], step, sends, receives)

    spread, mates = {}, {}

    def settle():
        over[line - 1].wait_recv()
        flows[1][1].wait_recv()
        flows[-1][1].wait_recv()
        total = part(position)
        total = total + jnp.where(position > 0, up_in[0].astype(F32), 0.0)
        total = total + jnp.where(position < line - 1, down_in[0].astype(F32), 0.0)
        here = rows_at(side, position)
        whole[here, :] = total.astype(BF16)
        mates[0] = [copies.start(whole.at[here], whole.at[here], copies.mate)]

    def spread_start(hop):
        spread[hop] = []
        for step in (1, -1):
            place = position - step * (hop - 1)
            sends = (place >= 0) & (place < line) & (position + step >= 0) & (position + step < line)
            origin = position - step * hop
            receives = (origin >= 0) & (origin < line)
            at = rows_at(side, jnp.clip(place, 0, line - 1))
            spread[hop].append(copies.along(whole.at[at], whole.at[at], step, sends, receives))

    def spread_end(hop):
        mates[hop] = []
        for step, copy in zip((1, -1), spread[hop]):
            copy.wait_recv()
            origin = position - step * hop
            there = (origin >= 0) & (origin < line)
            at = rows_at(side, jnp.clip(origin, 0, line - 1))
            mates[hop].append(copies.over_when(whole.at[at], whole.at[at], copies.mate, there))

    def mates_end(hop):
        for copy in mates[hop]:
            copy.wait_recv()

    return send_pair, reach_step, settle, spread_start, spread_end, mates_end


class SmallSum:
    def __init__(self, copies, devices, running, arrived, sums):
        self.copies, self.devices, self.running, self.arrived, self.sums = copies, devices, running, arrived, sums
        self.at, self.copy = 0, None

    def step(self):
        if self.copy is not None:
            self.copy.wait_recv()
            total = self.running[self.at] + self.arrived[self.at]
            self.at += 1
            self.copy = None
            if self.at == len(self.devices):
                self.sums[...] = total
            else:
                self.running[self.at] = total
        if self.at < len(self.devices):
            self.copy = self.copies.start(
                self.running.at[self.at], self.arrived.at[self.at], self.devices[self.at]
            )

    def end(self):
        while self.copy is not None:
            self.step()


class Gather:
    def __init__(self, copies, tensors, whole, rows):
        self.copies, self.whole, self.rows = copies, whole, rows
        tensor = lax.axis_index("tensor")
        self.mine = pl.ds(pl.multiple_of(tensor * rows, rows), rows)
        self.there = pl.ds(pl.multiple_of((tensor + tensors // 2) % tensors * rows, rows), rows)

    def start(self):
        self.far = self.copies.start(self.whole.at[self.mine], self.whole.at[self.mine], self.copies.far)
        self.first = self.copies.start(self.whole.at[self.mine], self.whole.at[self.mine], self.copies.core)

    def forward(self):
        self.far.wait_recv()
        self.last = self.copies.start(self.whole.at[self.there], self.whole.at[self.there], self.copies.core)

    def end(self):
        self.first.wait_recv()
        self.last.wait_recv()


def inputs_back_kernel(tensors, experts, line, hidden, *refs):
    refs = list(refs)
    gain, grad_router, grad_second = [refs.pop(0) for _ in range(3)]
    ins_there = [refs.pop(0) for _ in range(7)]
    moe_cross, stream = [refs.pop(0) for _ in range(2)]
    own_sum, going, turning = [refs.pop(0) for _ in range(3)] if line else [None] * 3
    outs_there = [refs.pop(0) for _ in range(8 if line else 5)]
    ins, outs = [refs.pop(0) for _ in range(7)], [refs.pop(0) for _ in range(8 if line else 5)]
    grads_rel, w_query, w_key, w_value, grad_after, layer_part, partial = ins
    (whole, layer, sums, summed, kv_out), weight_outs = outs[:5], outs[5:]
    moe_crossed, stream_in, local, stores = [refs.pop(0) for _ in range(4)]
    buffers = [refs.pop(0) for _ in range(4)] if line else []
    final, block = (refs.pop(0), refs.pop(0)) if line else (None, None)
    sent, got, crossing, crossed, running, arrived, send, recv = refs
    copies = Copies(tensors, send, recv)
    moves = Moves(stores)
    rows = grad_after.shape[0]
    quarter = pl.ds(pl.multiple_of(lax.axis_index("tensor") * rows, rows), rows)
    moves.start(*zip(ins_there, ins), (stream.at[quarter], stream_in))
    bits = [1 << k for k in range(experts.bit_length() - 1)]
    position = lax.axis_index("expert") // 2
    copies.greet([copies.core, copies.far] + [copies.across(bit) for bit in bits], line)
    lines = []
    moe_far = copies.start(moe_cross, moe_crossed, copies.far)
    if line:
        send_pair, reach_step, settle, spread_start, spread_end, mates_end = line_sum(
            copies, line, ins_there[6], partial, summed, *buffers
        )
        send_pair()
        end, inner = position == line - 1, (position > 0) & (position < line - 1)
        lines = [
            copies.along(going, final.at[0], 1, position < line - 1, position > 0),
            copies.along(going, final.at[1], -1, end, position == line - 2),
            copies.along(turning, final.at[1], -1, inner, position < line - 2),
        ]
    heads = w_query.shape[1] // HD
    query_width = heads * HD
    kv_rows = pl.ds(partial.shape[0] // 8, HD)
    kv_at = kv_columns(heads)
    moves.wait()

    def part(place):
        at = slice(place * rows, (place + 1) * rows)
        total = dot(grads_rel[at, :query_width], w_query[...], 1, 1)
        total = total + dot(grads_rel[at, query_width : query_width + HD], w_key[:, kv_at], 1, 1)
        return total + dot(grads_rel[at, query_width + HD :], w_value[:, kv_at], 1, 1)

    def beside():
        if line:
            reach_step(line - 1)
            reach_step(line - 2)

    grad_in = sum_quarter(copies, part, sent, got, crossing, crossed, beside)
    _, normed, inverse = rms_norm(stream_in[...].astype(F32), gain[...])
    through, first = norm_backward(grad_in, normed, inverse, gain[...])
    whole[quarter, :] = (grad_after[...] + through).astype(BF16)
    inputs_gather = Gather(copies, tensors, whole, rows)
    inputs_gather.start()
    running[0] = jnp.zeros(sums.shape, F32)
    running[0, :experts, :] = grad_router[...]
    running[0, experts : experts + 1, :] = grad_second[...]
    running[0, experts + 1 : experts + 2, :] = first[None]
    small = SmallSum(
        copies, [copies.core] + [copies.across(bit) for bit in bits] + [copies.far], running, arrived, sums
    )
    small.step()
    if line:
        for reach in range(line - 3, 0, -1):
            reach_step(reach)
    small.step()
    moe_far.wait_recv()
    layer[quarter, :] = (layer_part[...] + moe_crossed[...].astype(F32)).astype(BF16)
    layer_gather = Gather(copies, tensors, layer, rows)
    layer_gather.start()
    if line:
        settle()
        spread_start(1)
        small.step()
        spread_end(1)
        spread_start(2)
        small.step()
    inputs_gather.forward()
    if line:
        spread_end(2)
        spread_start(3)
        small.step()
        for copy in lines:
            copy.wait_recv()
        for index, out in enumerate(weight_outs):
            at = pl.ds(index * hidden, hidden)
            move = pltpu.make_async_copy(own_sum.at[at], block, local.at[0])
            move.start()
            move.wait()
            total = block[...] + jnp.where(position > 0, final[0, at, :].astype(F32), 0.0)
            total = total + jnp.where(position < line - 1, final[1, at, :].astype(F32), 0.0)
            out[...] = total
            moves.start((out, outs_there[5 + index]))
        for hop in range(3):
            mates_end(hop)
        far = copies.start(summed.at[kv_rows], kv_out.at[0], copies.far)
        near = copies.start(summed.at[kv_rows], kv_out.at[1], copies.core)
        spread_end(3)
        layer_gather.forward()
        far.wait_recv()
        across = copies.start(kv_out.at[0], kv_out.at[2], copies.core)
        mates_end(3)
        near.wait_recv()
        across.wait_recv()
    else:
        layer_gather.forward()
        summed[...] = partial[...]
        kv_out[...] = jnp.zeros(kv_out.shape, BF16)
    small.end()
    moves.start((sums, outs_there[2]), (summed, outs_there[3]), (kv_out, outs_there[4]))
    inputs_gather.end()
    layer_gather.end()
    moves.start((whole, outs_there[0]), (layer, outs_there[1]))
    moves.wait()
    copies.finish()


def inputs_back(tensors, experts, line, hidden, heads, length, width, *operands):
    rows = length // 4
    early = (-(-(experts + 2) // 8) * 8, width)
    steps = 1 + experts.bit_length()
    projected = 2 * heads * HD + HD
    quarter, half = ((rows, width), BF16), ((2 * rows, width), BF16)
    outs = [
        ((length, width), BF16),
        ((length, width), BF16),
        (early, F32),
        ((projected, width), BF16),
        ((3, HD, width), BF16),
    ]
    buffers = []
    if line:
        chunk = projected // 2 // line
        buffers = [
            ((projected // 2, width), BF16),
            ((6, chunk, width), BF16),
            ((3, chunk, width), BF16),
            ((3, chunk, width), BF16),
            ((2, 3 * hidden, width), BF16),
            ((hidden, width), F32),
        ]
        outs = outs + [((hidden, width), F32)] * 3
    buffers += [half, half, quarter, quarter, ((steps,) + early, F32), ((steps,) + early, F32)]
    operands = in_place(operands)
    return pl.pallas_call(
        functools.partial(inputs_back_kernel, tensors, experts, line, hidden),
        out_shape=[in_hbm(*o) for o in outs],
        in_specs=[vmem()] * 3 + [anywhere()] * (len(operands) - 3),
        out_specs=[anywhere()] * len(outs),
        scratch_shapes=buffers_of(operands[3:10])
        + [pltpu.VMEM(*o) for o in outs + [quarter] * 2]
        + [pltpu.SemaphoreType.DMA((1,)), pltpu.SemaphoreType.DMA((16,))]
        + [pltpu.VMEM(*o) for o in buffers]
        + [pltpu.SemaphoreType.DMA((50 + steps,)), pltpu.SemaphoreType.DMA((50 + steps,))],
        compiler_params=pltpu.CompilerParams(
            collective_id=3, has_side_effects=True, vmem_limit_bytes=63 * 2**20
        ),
        cost_estimate=pl.CostEstimate(flops=10**11, bytes_accessed=10**7, transcendentals=0),
    )(*operands)


def results_kernel(query_width, layer, inputs, gate, up, down, summed, kv_rest, *outs):
    layer_out, inputs_out, gate_out, up_out, down_out, query_out, output_out, key_out, value_out = outs
    step = pl.program_id(0)
    for source, out in ((layer, layer_out), (inputs, inputs_out), (gate, gate_out), (up, up_out), (down, down_out)):
        out[...] = source[...]
    first_rows, top = summed.shape[0] // 8, query_width + HD
    columns = pl.ds(pl.multiple_of(step * query_width, HD), query_width)
    query_out[:first_rows, :] = summed[:first_rows, columns].astype(F32)
    query_out[first_rows:, :] = summed[first_rows + HD : top, columns].astype(F32)
    part = query_width // 4
    output_out[...] = summed[pl.ds(pl.multiple_of(top + step * part, 16), part), :].astype(F32)
    tensor = lax.axis_index("tensor")
    lead, low_head = tensor % 2 == 0, tensor * (query_width // HD) // (HEADS // KV) == 0
    for block in range(query_width // HD):
        at = pl.ds(pl.multiple_of(step * query_width + block * HD, HD), HD)
        mine = summed[first_rows : first_rows + HD, at].astype(F32)
        far, core, across = [kv_rest[k, :, at].astype(F32) for k in range(3)]
        rows = slice(block * HD, (block + 1) * HD)
        for out, near, other in (
            (key_out, jnp.where(lead, mine, core), jnp.where(lead, far, across)),
            (value_out, jnp.where(lead, core, mine), jnp.where(lead, across, far)),
        ):
            out[rows, :HD] = jnp.where(low_head, near, other)
            out[rows, HD:] = jnp.where(low_head, other, near)


def results(query_width, *operands):
    (length, width), (hidden, _) = operands[0].shape, operands[2].shape
    shape = jax.ShapeDtypeStruct

    def rows(count):
        return pl.BlockSpec((count // 4, width), lambda i: (i, 0))

    def whole(dims):
        return pl.BlockSpec(dims, lambda i: (0,) * len(dims))

    def columns(count):
        return pl.BlockSpec((width // 4, count), lambda i: (i, 0))

    same = [rows(length), rows(length)] + [rows(hidden)] * 3
    return pl.pallas_call(
        functools.partial(results_kernel, query_width),
        grid=(4,),
        in_specs=same + [whole(operands[5].shape), whole(operands[6].shape)],
        out_specs=same + [columns(query_width), rows(query_width), columns(2 * HD), columns(2 * HD)],
        out_shape=[shape((length, width), BF16)] * 2
        + [shape((hidden, width), F32)] * 3
        + [shape((width, query_width), F32), shape((query_width, width), F32)]
        + [shape((width, 2 * HD), F32)] * 2,
        compiler_params=pltpu.CompilerParams(vmem_limit_bytes=40 * 2**20),
        cost_estimate=pl.CostEstimate(flops=0, bytes_accessed=3 * 10**7, transcendentals=0),
    )(*in_place(operands))


def shards(
    experts,
    tensors,
    inputs,
    routes,
    cotangent,
    first_gain,
    second_gain,
    w_query,
    w_key,
    w_value,
    w_output,
    w_router,
    w_gate,
    w_up,
    w_down,
):
    links = Links(experts, tensors)
    line, place, side = links.line, links.place, links.side
    length, width = inputs.shape
    heads = w_query.shape[1] // HD
    hidden = w_gate.shape[2]
    group = HEADS // KV
    kv_head = links.tensor * heads // group
    scale = HD ** (-0.5)
    order = nearest_first(line)

    own_weights = [w_gate[0].T, w_up[0].T, w_down[0]]
    short = line if line == 4 else 0
    if not short:
        sides = [[2 * p + s for p in range(line)] for s in range(2)]
        weights = lax.all_gather(jnp.concatenate(own_weights, 0), "expert", axis_index_groups=sides)

    rows, half = length // 4, length // 2
    cos, sin = [jnp.asarray(table) for table in rotary_tables(length)]
    attn_in, query, key, value, context_rel, logsum, grad_rel, grad_pair, routes_own, routes_pair, *arrived = attend(
        tensors,
        short,
        inputs,
        first_gain[None],
        w_query,
        w_key,
        w_value,
        cos,
        sin,
        cotangent,
        routes.T,
        own_weights,
    )

    tokens_own, tokens_pair, after, *second = attend_out(
        tensors, short, context_rel, w_output, second_gain[None], inputs, *(arrived or [None])
    )
    router_rows = w_router.T
    if short:
        router_padded = jnp.concatenate([router_rows, router_rows], 0)
        tokens_pair, *outs, last_weight, all_down = first_pass(
            tensors,
            experts,
            line,
            hidden,
            router_padded,
            routes_own,
            routes_pair,
            tokens_own,
            tokens_pair,
            grad_rel,
            grad_pair,
            arrived[0],
            second[0],
            *own_weights,
        )
        *first_own, last_gate_own, router_probs, named = outs[:7]
        *first_pair, last_gate_pair, _, _ = outs[7:]
    else:
        names = jnp.arange(experts, dtype=jnp.int32)[:, None, None]

        def gates_of(tokens, tokens_routes):
            logits = dot(router_rows, tokens, 1, 1)
            logit_exp = jnp.exp(logits - jnp.max(logits, axis=0, keepdims=True))
            probs = logit_exp / jnp.sum(logit_exp, axis=0, keepdims=True)
            named = jnp.any(tokens_routes[None] == names, axis=1).astype(F32)
            return probs, named, probs * named

        router_probs, named, gates_own = gates_of(tokens_own, routes_own[:4])
        _, _, gates_pair = gates_of(tokens_pair, routes_pair[:4])
    both_tokens, both_grads = (tokens_own, tokens_pair), (grad_rel, grad_pair)
    if short:
        (kept_pair, sent_pair, *last_pair), (kept_own, sent_own, *last_own), last_grad = last_expert(
            hidden,
            last_weight,
            (tokens_pair, grad_pair, last_gate_pair, first_pair[0]),
            (tokens_own, grad_rel, last_gate_own, first_own[0]),
        )
        gate_rows = [first_own[3], last_own[1], first_pair[3], last_pair[1]]
    else:
        zeros = jnp.zeros((length, width), BF16)

        def step(totals, weight_at):
            weight, position = weight_at
            name = (position * 2 + side)[None]
            down = weight[2 * hidden :]
            own = expert_pass(tokens_own, grad_rel, gates_own, name, [weight], totals[0])
            pair = expert_pass(tokens_pair, grad_pair, gates_pair, name, [weight], totals[1])
            grads = weight_grad(
                0, hidden, (own[2], pair[2]), (own[1], pair[1]), both_tokens, both_grads, BF16
            )
            moe_own = totals[2] + dot(own[1], down, 0, 0)
            moe_pair = totals[3] + dot(pair[1], down, 0, 0)
            return (own[0], pair[0], moe_own, moe_pair), (own[3][0], pair[3][0], grads)

        (sum_own, sum_pair, moe_own, moe_pair), (gate_own, gate_pair, weight_grads) = lax.scan(
            step,
            (zeros, zeros, zeros.astype(F32), zeros.astype(F32)),
            (weights, jnp.arange(line, dtype=jnp.int32)),
        )
        kept_own, sent_own, kept_pair, sent_pair = sum_own[:half], sum_own[half:], sum_pair[:half], sum_pair[half:]

    if short:
        factors = [first_own[2], first_pair[2], first_own[1], first_pair[1]]
        factors += [last_own[0], last_pair[0], *both_tokens, *both_grads, all_down, last_grad]
    else:
        gate_rows = [jnp.concatenate([gate_own, gate_pair], 0)]
        factors = [moe_own.astype(BF16), moe_pair.astype(BF16)]
    (
        grad_after,
        grad_router,
        grad_second,
        grads_rel,
        layer_part,
        moe_cross,
        partial,
        _,
        *weight_sums,
    ) = tokens_back(
        tensors,
        experts,
        short,
        hidden,
        heads,
        length,
        width,
        *gate_rows,
        router_probs,
        named,
        router_rows,
        second_gain[None],
        kept_pair,
        kept_own,
        after,
        w_output,
        query,
        key,
        value,
        logsum,
        cos,
        sin,
        context_rel,
        attn_in,
        grad_rel,
        sent_pair,
        sent_own,
        *factors,
    )

    line_sums = []
    if short:
        line_sums = [weight_sums[2], *weight_sums[-2:]]
    else:
        expert_grads = lax.psum_scatter(
            weight_grads, "expert", scatter_dimension=0, axis_index_groups=sides
        ).astype(F32)

    grad_inputs, layer_out, sums, summed, kv_rest, *weight_grads_out = inputs_back(
        tensors,
        experts,
        short,
        hidden,
        heads,
        length,
        width,
        first_gain[None],
        grad_router,
        grad_second,
        grads_rel,
        w_query,
        w_key,
        w_value,
        grad_after,
        layer_part,
        partial,
        moe_cross,
        inputs,
        *line_sums,
    )
    query_width = heads * HD
    if not short:
        summed = lax.psum(summed, "expert")
        first_rows = summed.shape[0] // 8
        kv_far = links.over_tensor(summed[first_rows : first_rows + HD], 2)
        both = jnp.concatenate([summed[first_rows : first_rows + HD], kv_far], 0)
        kv_core = links.over_tensor(both, 1)
        kv_rest = jnp.stack([kv_far, kv_core[:HD], kv_core[HD:]])
        weight_grads_out = [expert_grads[i * hidden : (i + 1) * hidden] for i in range(3)]
    (
        layer_out,
        grad_inputs,
        grad_gate,
        grad_up,
        grad_down,
        grad_query,
        grad_output,
        grad_key,
        grad_value,
    ) = results(query_width, layer_out, grad_inputs, *weight_grads_out, summed, kv_rest)
    grad_router, grad_second, grad_first = sums[:experts].T, sums[experts], sums[experts + 1]
    return (
        layer_out,
        grad_inputs,
        grad_first,
        grad_second,
        grad_query,
        grad_key,
        grad_value,
        grad_output,
        grad_router,
        grad_gate.T[None],
        grad_up.T[None],
        grad_down[None],
    )


def solution(mesh):
    experts, tensors = mesh.shape["expert"], mesh.shape["tensor"]
    in_specs = (
        P("expert", None),
        P("expert", None),
        P("expert", None),
        P(),
        P(),
        P(None, "tensor"),
        P(),
        P(),
        P("tensor", None),
        P(),
        P("expert", None, "tensor"),
        P("expert", None, "tensor"),
        P("expert", "tensor", None),
    )
    out_specs = (
        P("expert", None),
        P("expert", None),
        P(),
        P(),
        P(None, "tensor"),
        P(),
        P(),
        P("tensor", None),
        P(),
        P("expert", None, "tensor"),
        P("expert", None, "tensor"),
        P("expert", "tensor", None),
    )

    def run(*arrays):
        return shards(experts, tensors, *arrays)

    return jax.shard_map(run, mesh=mesh, in_specs=in_specs, out_specs=out_specs, check_vma=False)
```
